32 devices in a mesh: slab: 8 (over z, y), led: 4 (over x, core).
Axes of the slice: x: 2, y: 2, z: 4, core: 2. Of those that a mesh axis runs over, the one named last changes fastest.
Arguments:
- spectrum: float32 [2, 2048, 2048], P(None, 'slab'), may hold values from -6 to 6
- led_rows: int32 [8], P('led'), may hold values from 256 to 768
- led_cols: int32 [8], P('led'), may hold values from 0 to 1024
- images: float32 [8, 1024, 1024], P('led', 'slab'), may hold values from 0.05 to 4
Outputs:
- updated: float32 [2, 2048, 2048], P(None, 'slab', 'led')
The draws below stay inside these ranges and needn't reach their ends.
All inputs are finite; a program needn't handle non-finite values.
Results may differ from the reference program's by a relative error of at most 0.0065.
Values may be sent and summed in bfloat16 or wider, within the bound.
No kernel may reach another device: no remote copies, remote signals or barrier semaphores. Data moves between devices by JAX's collectives and lax.ppermute only.
A program may use at most 64 MiB of HBM per device.

```python
import math
import jax
import jax.numpy as jnp
from jax import lax

WIN = 1024
NROW = 2048
NCOL = 2048
LEDS = 8


def plant(values, stream_key, low, high):
    longest = values.shape.index(max(values.shape))
    spots = []
    for shift in (0, 1):
        where = [jax.random.randint(jax.random.fold_in(stream_key, axis), (), 0, length) for axis, length in enumerate(values.shape)]
        where[longest] = (where[longest] + shift) % values.shape[longest]
        spots.append(tuple(where))
    return values.at[spots[0]].set(low).at[spots[1]].set(high)


def levels(stream_key, shape, split, low, top_value):
    loudness = 1.0
    for axis_at, shards_of in split:
        steps = jax.random.uniform(jax.random.fold_in(jax.random.fold_in(stream_key, 6), axis_at), (shards_of,), jnp.float32, low / len(split), top_value / len(split))
        loudness = loudness * jnp.repeat(jnp.exp(steps), shape[axis_at] // shards_of).reshape((-1,) + (1,) * (len(shape) - 1 - axis_at))
    return loudness


def noise(stream_key, extent, scale, most, pieces=(), held_as=jnp.bfloat16):
    result = scale * jax.random.normal(stream_key, extent, jnp.float32)
    if pieces:
        result = result * levels(stream_key, extent, pieces, -0.22, 0.18)
    return jnp.clip(result, -most, most).astype(held_as)


def setup_inputs(seed: int = 0) -> dict:
    keys = jax.random.split(jax.random.key(seed), 5)
    spectrum = noise(keys[0], (2, NROW, NCOL), 1.0, 6.0, ((1, 8),), jnp.float32)
    led_rows = plant(jax.random.randint(keys[1], (LEDS,), (NROW - WIN) // 4, 3 * (NROW - WIN) // 4 + 1), jax.random.fold_in(keys[1], 1), (NROW - WIN) // 4, (3 * (NROW - WIN) // 4 + 1) - 1).astype(jnp.int32)
    led_cols = plant(jax.random.randint(keys[2], (LEDS,), 0, NCOL - WIN + 1), jax.random.fold_in(keys[2], 1), 0, NCOL - WIN).astype(jnp.int32)
    images = jnp.clip(jnp.exp(math.log(4.0) - 4.3820266 * jax.random.uniform(keys[3], (LEDS, WIN, WIN), jnp.float32) ** levels(keys[3], (LEDS, WIN, WIN), ((0, 4), (1, 8)), -0.2, 0.2)), 0.05, 4.0)
    return dict(spectrum=spectrum, led_rows=led_rows, led_cols=led_cols, images=images)


def make_tables(width):
    index = jnp.arange(width, dtype=jnp.int32)
    angle_index = index[:, None] * index[None, :] % width
    angle = angle_index.astype(jnp.float32) * (2.0 * 3.141592653589793 / width)
    scale = 1.0 / jnp.sqrt(jnp.float32(width))
    return ((jnp.cos(angle) * scale).astype(jnp.bfloat16), (jnp.sin(angle) * scale).astype(jnp.bfloat16))

def make_pupil(row_index, col_index, width):
    row_term = (2 * row_index + 1 - width) * (2 * row_index + 1 - width)
    col_term = (2 * col_index + 1 - width) * (2 * col_index + 1 - width)
    return (row_term[:, None] + col_term[None, :] < width * width).astype(jnp.float32)

def product(left, right):
    return jnp.dot(left, right, preferred_element_type=jnp.float32)

def one_window(spec_re, spec_im, row_start, col_start, image, cos_table, sin_table, mask):
    win_re = (lax.dynamic_slice(spec_re, (row_start, col_start), (WIN, WIN)) * mask).astype(jnp.bfloat16)
    win_im = (lax.dynamic_slice(spec_im, (row_start, col_start), (WIN, WIN)) * mask).astype(jnp.bfloat16)
    row_re = (product(win_re, cos_table) + product(win_im, sin_table)).astype(jnp.bfloat16)
    row_im = (product(win_im, cos_table) - product(win_re, sin_table)).astype(jnp.bfloat16)
    field_re = product(row_re.T, cos_table) + product(row_im.T, sin_table)
    field_im = product(row_im.T, cos_table) - product(row_re.T, sin_table)
    factor = jnp.sqrt(image) / jnp.sqrt(field_re * field_re + field_im * field_im + 0.25) - 1.0
    diff_re = (field_re * factor).astype(jnp.bfloat16)
    diff_im = (field_im * factor).astype(jnp.bfloat16)
    back_re = (product(diff_re, cos_table) - product(diff_im, sin_table)).astype(jnp.bfloat16)
    back_im = (product(diff_im, cos_table) + product(diff_re, sin_table)).astype(jnp.bfloat16)
    upd_re = product(back_re.T, cos_table) - product(back_im.T, sin_table)
    upd_im = product(back_im.T, cos_table) + product(back_re.T, sin_table)
    return (upd_re * mask, upd_im * mask)

def reference(spectrum, led_rows, led_cols, images):
    cos_table, sin_table = make_tables(WIN)
    index = jnp.arange(WIN, dtype=jnp.int32)
    mask = make_pupil(index, index, WIN)
    spec_re = spectrum[0]
    spec_im = spectrum[1]
    grad_re = jnp.zeros((NROW, NCOL), jnp.float32)
    grad_im = jnp.zeros((NROW, NCOL), jnp.float32)
    for number in range(LEDS):
        row_start = led_rows[number].astype(jnp.int32)
        col_start = led_cols[number].astype(jnp.int32)
        upd_re, upd_im = one_window(spec_re, spec_im, row_start, col_start, images[number], cos_table, sin_table, mask)
        current_re = lax.dynamic_slice(grad_re, (row_start, col_start), (WIN, WIN))
        current_im = lax.dynamic_slice(grad_im, (row_start, col_start), (WIN, WIN))
        grad_re = lax.dynamic_update_slice(grad_re, current_re + upd_re, (row_start, col_start))
        grad_im = lax.dynamic_update_slice(grad_im, current_im + upd_im, (row_start, col_start))
    return spectrum + jnp.stack([grad_re, grad_im])
```

```python
import functools

import jax
import jax.numpy as jnp
import numpy as np
from jax import lax
from jax.experimental import pallas as pl
from jax.experimental.pallas import tpu as pltpu
from jax.sharding import PartitionSpec as P

LANES = 128


def as_sent(value):
    return jax.tree.map(lambda a: a.astype(jnp.bfloat16) if a.dtype == jnp.float32 else a, value)


def host_tables(width):
    index = np.arange(width, dtype=np.int64)
    angle_index = (index[:, None] * index[None, :] % width).astype(np.float32)
    angle = angle_index * np.float32(2.0 * 3.141592653589793 / width)
    scale = np.float32(1.0) / np.sqrt(np.float32(width))
    return (
        (np.cos(angle) * scale).astype(jnp.bfloat16),
        (np.sin(angle) * scale).astype(jnp.bfloat16),
    )


def make_pupil(row_index, col_index, width):
    row_term = (2 * row_index + 1 - width) * (2 * row_index + 1 - width)
    col_term = (2 * col_index + 1 - width) * (2 * col_index + 1 - width)
    return (row_term[:, None] + col_term[None, :] < width * width).astype(jnp.float32)


def contract(form, left, right):
    return jnp.einsum(form, left, right, preferred_element_type=jnp.float32)


def take_rows(strip, start, width):
    return lax.dynamic_slice_in_dim(strip, start, width, 1)


def place_rows(block, start, total, axis_dim):
    shape = list(block.shape)
    shape[axis_dim] = total
    holder = jnp.zeros(tuple(shape), block.dtype)
    return lax.dynamic_update_slice_in_dim(holder, block, start, axis_dim)


def modulus_step(field_in_re, field_in_im, image, cos_table, sin_table):
    field_re = contract("lka,am->lkm", field_in_re, cos_table) + contract(
        "lka,am->lkm", field_in_im, sin_table
    )
    field_im = contract("lka,am->lkm", field_in_im, cos_table) - contract(
        "lka,am->lkm", field_in_re, sin_table
    )
    factor = jnp.sqrt(image) / jnp.sqrt(field_re * field_re + field_im * field_im + 0.25) - 1.0
    diff_re = (field_re * factor).astype(jnp.bfloat16)
    diff_im = (field_im * factor).astype(jnp.bfloat16)
    back_re = (
        contract("lkm,ma->lka", diff_re, cos_table) - contract("lkm,ma->lka", diff_im, sin_table)
    ).astype(jnp.bfloat16)
    back_im = (
        contract("lkm,ma->lka", diff_im, cos_table) + contract("lkm,ma->lka", diff_re, sin_table)
    ).astype(jnp.bfloat16)
    return (back_re, back_im)


def body_any(spectrum, led_rows, led_cols, images):
    width = images.shape[2]
    slab_rows = spectrum.shape[1]
    columns = spectrum.shape[2]
    slabs = lax.axis_size("slab")
    total_rows = slab_rows * slabs
    position = lax.axis_index("slab")
    cos_table, sin_table = (jnp.asarray(t) for t in host_tables(width))
    own_rows = position * slab_rows + jnp.arange(slab_rows, dtype=jnp.int32)
    col_index = jnp.arange(width, dtype=jnp.int32)

    def take_cols(start):
        return lax.dynamic_slice_in_dim(spectrum, start, width, 2)

    def owner_mask(start):
        return make_pupil(own_rows - start, col_index, width)

    windows = jax.vmap(take_cols)(led_cols)
    masks = jax.vmap(owner_mask)(led_rows)
    win_re = (windows[:, 0] * masks).astype(jnp.bfloat16)
    win_im = (windows[:, 1] * masks).astype(jnp.bfloat16)

    def slice_strip(block, start):
        return take_rows(block, start, width)

    row_re = (
        contract("lgb,bk->lkg", win_re, cos_table) + contract("lgb,bk->lkg", win_im, sin_table)
    ).astype(jnp.bfloat16)
    row_im = (
        contract("lgb,bk->lkg", win_im, cos_table) - contract("lgb,bk->lkg", win_re, sin_table)
    ).astype(jnp.bfloat16)
    col_re, col_im = (
        lax.all_to_all(row_re, "slab", split_axis=1, concat_axis=2, tiled=True),
        lax.all_to_all(row_im, "slab", split_axis=1, concat_axis=2, tiled=True),
    )
    field_in_re = jax.vmap(slice_strip)(col_re, led_rows)
    field_in_im = jax.vmap(slice_strip)(col_im, led_rows)
    back_re, back_im = modulus_step(field_in_re, field_in_im, images, cos_table, sin_table)

    def place_strip(block, start):
        return place_rows(block, start, total_rows, 1)

    full_re = jax.vmap(place_strip)(back_re, led_rows)
    full_im = jax.vmap(place_strip)(back_im, led_rows)
    home_re, home_im = (
        lax.all_to_all(as_sent(full_re), "slab", split_axis=2, concat_axis=1, tiled=True).astype(
            full_re.dtype
        ),
        lax.all_to_all(as_sent(full_im), "slab", split_axis=2, concat_axis=1, tiled=True).astype(
            full_im.dtype
        ),
    )
    upd_re = contract("lkg,kb->lgb", home_re, cos_table) - contract(
        "lkg,kb->lgb", home_im, sin_table
    )
    upd_im = contract("lkg,kb->lgb", home_im, cos_table) + contract(
        "lkg,kb->lgb", home_re, sin_table
    )
    upd_re = upd_re * masks
    upd_im = upd_im * masks

    def add_window(number, gradient):
        start = led_cols[number]
        piece = jnp.stack([upd_re[number], upd_im[number]])
        current = lax.dynamic_slice_in_dim(gradient, start, width, 2)
        return lax.dynamic_update_slice_in_dim(gradient, current + piece, start, 2)

    gradient = lax.fori_loop(
        0, led_rows.shape[0], add_window, jnp.zeros((2, slab_rows, columns), jnp.float32)
    )
    summed = lax.psum_scatter(gradient, "led", scatter_dimension=2, tiled=True)
    share = summed.shape[2]
    own_part = lax.dynamic_slice_in_dim(spectrum, lax.axis_index("led") * share, share, 2)
    return own_part + summed


def dot(left, right):
    return jnp.dot(left, right, preferred_element_type=jnp.float32)


def window_mask(first_row, row_start, col_start, rows, first_col, cols, width):
    shape = (rows, cols)
    at_row = lax.broadcasted_iota(jnp.int32, shape, 0) + (first_row - row_start)
    at_col = lax.broadcasted_iota(jnp.int32, shape, 1) + (first_col - col_start)
    wraps = at_col < 0
    at_col = jnp.where(wraps, at_col + width, at_col)
    row_term = 2 * at_row + 1 - width
    col_term = 2 * at_col + 1 - width
    return row_term * row_term + col_term * col_term < width * width, wraps


def rows_kernel(slabs, scalars, spectrum, table_any, *rest):
    outs = rest[:slabs]
    win_re, win_im, table, sems = rest[slabs:]
    position = scalars[0]
    rows = spectrum.shape[1]
    width = win_re.shape[1]
    leds = win_re.shape[0] // rows
    copies = [
        pltpu.make_async_copy(
            table_any.at[lax.rem(position + d, slabs)], table.at[d], sems.at[d]
        )
        for d in range(slabs)
    ]
    for copy in copies:
        copy.start()
    for led in range(leds):
        inside, wraps = window_mask(
            position * rows, scalars[1 + led], scalars[1 + leds + led], rows, 0, width, width
        )
        here = pl.ds(led * rows, rows)
        for plane, window in enumerate((win_re, win_im)):
            value = jnp.where(wraps, spectrum[plane, :, width:], spectrum[plane, :, :width])
            window[here, :] = jnp.where(inside, value, 0.0).astype(jnp.bfloat16)
    for d in range(slabs):
        copies[d].wait()
        from_re = dot(win_re[...], table[d])
        from_im = dot(win_im[...], table[d])
        row_re = (from_re[:, :LANES] + from_im[:, LANES:]).astype(jnp.bfloat16)
        row_im = (from_im[:, :LANES] - from_re[:, LANES:]).astype(jnp.bfloat16)
        for led in range(leds):
            outs[d][led] = row_re[led * rows : (led + 1) * rows]
            outs[d][leds + led] = row_im[led * rows : (led + 1) * rows]


def field_kernel(slabs, scalars, amplitude, table_any, *rest):
    blocks = rest[:slabs]
    period = slabs // 2
    outs = rest[slabs : slabs + period]
    field_in, diff, table, sems = rest[slabs + period :]
    position = scalars[0]
    parts, rows, _ = blocks[0].shape
    half = parts // 2 * LANES
    width = field_in.shape[0]
    steps = width // LANES
    copies = [
        pltpu.make_async_copy(table_any.at[j], table.at[j], sems.at[j]) for j in range(steps)
    ]
    for copy in copies:
        copy.start()
    for d in range(period):
        at = pl.multiple_of(lax.rem(position - d + slabs, period) * rows, rows)
        for part in range(parts):
            field_in[pl.ds(at, rows), part * LANES : (part + 1) * LANES] = (
                blocks[d][part] + blocks[d + period][part]
            )
    for j in range(steps):
        copies[j].wait()
        both = dot(table[j], field_in[...])
        field_re = both[:LANES, :half] + both[LANES:, half:]
        field_im = both[:LANES, half:] - both[LANES:, :half]
        here = pl.ds(j * LANES, LANES)
        factor = (
            amplitude[here, :] * lax.rsqrt(field_re * field_re + field_im * field_im + 0.25) - 1.0
        )
        diff[here, :half] = (field_re * factor).astype(jnp.bfloat16)
        diff[here, half:] = (field_im * factor).astype(jnp.bfloat16)
    for i in range(period):
        for h in range(rows // LANES):
            j = lax.rem(position + i, period) * (rows // LANES) + h
            both = dot(table[j], diff[...])
            back_re = (both[:LANES, :half] - both[LANES:, half:]).astype(jnp.bfloat16)
            back_im = (both[:LANES, half:] + both[LANES:, :half]).astype(jnp.bfloat16)
            here = pl.ds(h * LANES, LANES)
            for part in range(parts // 2):
                cols = slice(part * LANES, (part + 1) * LANES)
                outs[i][part, here, :] = back_re[:, cols]
                outs[i][parts // 2 + part, here, :] = back_im[:, cols]


def update_kernel(slabs, scalars, table_any, *rest):
    blocks = rest[:slabs]
    sent, kept = rest[slabs : slabs + 2]
    back_re, back_im, table, sems = rest[slabs + 2 :]
    position = scalars[0]
    core = scalars[5]
    parts, rows, _ = blocks[0].shape
    leds = parts // 2
    width = back_re.shape[1]
    steps = width // LANES
    group = steps // 2

    def block_of(n):
        owner = 1 - core if n < group else core
        return owner * group + n % group

    copies = [
        pltpu.make_async_copy(table_any.at[block_of(n)], table.at[n], sems.at[n])
        for n in range(steps)
    ]
    for copy in copies:
        copy.start()
    for d in range(slabs):
        at = pl.multiple_of(lax.rem(position - d + slabs, slabs) * LANES, LANES)
        for led in range(leds):
            here = slice(led * rows, (led + 1) * rows)
            back_re[here, pl.ds(at, LANES)] = blocks[d][led]
            back_im[here, pl.ds(at, LANES)] = blocks[d][leds + led]
    for n in range(steps):
        copies[n].wait()
        from_re = dot(back_re[...], table[n])
        from_im = dot(back_im[...], table[n])
        update = (
            from_re[:, :LANES] - from_im[:, LANES:],
            from_im[:, :LANES] + from_re[:, LANES:],
        )
        low = [0.0, 0.0]
        high = [0.0, 0.0]
        for led in range(leds):
            inside, wraps = window_mask(
                position * rows,
                scalars[1 + led],
                scalars[1 + leds + led],
                rows,
                block_of(n) * LANES,
                LANES,
                width,
            )
            for plane in range(2):
                piece = jnp.where(inside, update[plane][led * rows : (led + 1) * rows], 0.0)
                low[plane] += jnp.where(wraps, 0.0, piece)
                high[plane] += jnp.where(wraps, piece, 0.0)
        out = sent if n < group else kept
        cols = slice(n % group * LANES, (n % group + 1) * LANES)
        for plane in range(2):
            out[plane, 0, :, cols] = low[plane].astype(out.dtype)
            out[plane, 1, :, cols] = high[plane].astype(out.dtype)


def local_call(kernel, out_shape, in_vmem, scratch, flops, moved, name, tables_at):
    vmem = pl.BlockSpec(memory_space=pltpu.VMEM)
    specs = [pl.BlockSpec(memory_space=pltpu.SMEM)]
    specs += [pl.BlockSpec(memory_space=pl.ANY) if i == tables_at else vmem for i in range(in_vmem)]
    return pl.pallas_call(
        kernel,
        out_shape=out_shape,
        in_specs=specs,
        out_specs=jax.tree.map(lambda _: vmem, out_shape),
        scratch_shapes=scratch,
        compiler_params=pltpu.CompilerParams(vmem_limit_bytes=48 * 2**20),
        cost_estimate=pl.CostEstimate(flops=flops, bytes_accessed=moved, transcendentals=0),
        name=name,
    )


def body_slabs(spectrum, led_rows, led_cols, images):
    leds, block, width = images.shape
    rows = spectrum.shape[1]
    slabs = lax.axis_size("slab")
    position = lax.axis_index("slab")
    led_at = lax.axis_index("led")
    core = lax.rem(led_at, 2)
    plane_x = lax.div(led_at, 2)
    bf16 = jnp.bfloat16
    scalars = jnp.concatenate(
        [position[None], led_rows, led_cols, core[None]], dtype=jnp.int32
    )
    cos_table, sin_table = host_tables(width)
    steps = width // LANES
    by_col = np.stack(
        [
            np.concatenate([t[:, j * LANES : (j + 1) * LANES] for t in (cos_table, sin_table)], 1)
            for j in range(steps)
        ]
    )
    by_row = jnp.asarray(np.ascontiguousarray(by_col.transpose(0, 2, 1)))
    by_col = jnp.asarray(by_col)
    sent_block = jax.ShapeDtypeStruct((2 * leds, rows, LANES), bf16)
    table_col = [pltpu.VMEM(by_col.shape, bf16), pltpu.SemaphoreType.DMA((steps,))]
    table_row = [pltpu.VMEM(by_row.shape, bf16), pltpu.SemaphoreType.DMA((steps,))]

    first_flops = 8 * leds * rows * width * width
    row_blocks = local_call(
        functools.partial(rows_kernel, slabs),
        [sent_block] * slabs,
        2,
        [pltpu.VMEM((leds * rows, width), bf16)] * 2 + table_col,
        first_flops,
        10 * 2**20,
        "row_transform",
        1,
    )(scalars, spectrum, by_col)

    used = range(1, slabs - 1)

    def to_columns(d):
        if d == 0:
            return row_blocks[0]
        pairs = [(s, (s + d) % slabs) for s in used]
        return lax.ppermute(row_blocks[d], "slab", pairs)

    col_blocks = [to_columns(d) for d in range(slabs)]
    amplitude = jnp.sqrt(images).transpose(2, 0, 1).reshape(width, leds * block)
    period = slabs // 2
    back_blocks = local_call(
        functools.partial(field_kernel, slabs),
        [sent_block] * period,
        2 + slabs,
        [pltpu.VMEM((width, 2 * leds * block), bf16)] * 2 + table_row,
        16 * leds * block * width * width,
        8 * 2**20,
        "modulus_step",
        1,
    )(scalars, amplitude, by_row, *col_blocks)

    def to_rows(d):
        if d == 0:
            return back_blocks[0]
        pairs = [(s, (s + d) % slabs) for s in range(slabs) if (s + d) % slabs in used]
        return lax.ppermute(back_blocks[d % period], "slab", pairs)

    home_blocks = [to_rows(d) for d in range(slabs)]
    share = spectrum.shape[2] // 4
    sent, kept = local_call(
        functools.partial(update_kernel, slabs),
        [
            jax.ShapeDtypeStruct((2, 2, rows, share), bf16),
            jax.ShapeDtypeStruct((2, 2, rows, share), jnp.float32),
        ],
        1 + slabs,
        [pltpu.VMEM((leds * rows, width), bf16)] * 2 + table_col,
        first_flops,
        9 * 2**20,
        "row_update",
        0,
    )(scalars, by_col, *home_blocks)
    got = lax.ppermute(sent, "led", [(0, 1), (1, 0), (2, 3), (3, 2)])
    over = lax.dynamic_index_in_dim(kept, 1 - plane_x, 1, False) + lax.dynamic_index_in_dim(
        got, 1 - plane_x, 1, False
    ).astype(jnp.float32)
    got_x = lax.ppermute(over.astype(bf16), "led", [(0, 2), (2, 0), (1, 3), (3, 1)])
    own = lax.dynamic_index_in_dim(kept, plane_x, 1, False) + lax.dynamic_index_in_dim(
        got, plane_x, 1, False
    ).astype(jnp.float32)
    own_part = lax.dynamic_slice_in_dim(spectrum, led_at * share, share, 2)
    return own_part + (own + got_x.astype(jnp.float32))


def solution(mesh):
    placed = (P(None, "slab", None), P("led"), P("led"), P("led", "slab", None))
    fits = mesh.shape["slab"] == 8 and mesh.shape["led"] == 4

    def body(spectrum, led_rows, led_cols, images):
        shapes = (spectrum.shape, images.shape)
        if fits and shapes == ((2, 256, 2048), (2, 128, 1024)):
            return body_slabs(spectrum, led_rows, led_cols, images)
        return body_any(spectrum, led_rows, led_cols, images)

    return jax.shard_map(
        body, mesh=mesh, in_specs=placed, out_specs=P(None, "slab", "led"), check_vma=False
    )
```

```python
import functools

import jax
import jax.numpy as jnp
import numpy as np
from jax import lax
from jax.experimental import pallas as pl
from jax.experimental.pallas import tpu as pltpu
from jax.sharding import PartitionSpec as P

LANES = 128


def as_sent(value):
    return jax.tree.map(lambda a: a.astype(jnp.bfloat16) if a.dtype == jnp.float32 else a, value)


def host_tables(width):
    index = np.arange(width, dtype=np.int64)
    angle_index = (index[:, None] * index[None, :] % width).astype(np.float32)
    angle = angle_index * np.float32(2.0 * 3.141592653589793 / width)
    scale = np.float32(1.0) / np.sqrt(np.float32(width))
    return (
        (np.cos(angle) * scale).astype(jnp.bfloat16),
        (np.sin(angle) * scale).astype(jnp.bfloat16),
    )


def make_pupil(row_index, col_index, width):
    row_term = (2 * row_index + 1 - width) * (2 * row_index + 1 - width)
    col_term = (2 * col_index + 1 - width) * (2 * col_index + 1 - width)
    return (row_term[:, None] + col_term[None, :] < width * width).astype(jnp.float32)


def contract(form, left, right):
    return jnp.einsum(form, left, right, preferred_element_type=jnp.float32)


def take_rows(strip, start, width):
    return lax.dynamic_slice_in_dim(strip, start, width, 1)


def place_rows(block, start, total, axis_dim):
    shape = list(block.shape)
    shape[axis_dim] = total
    holder = jnp.zeros(tuple(shape), block.dtype)
    return lax.dynamic_update_slice_in_dim(holder, block, start, axis_dim)


def modulus_step(field_in_re, field_in_im, image, cos_table, sin_table):
    field_re = contract("lka,am->lkm", field_in_re, cos_table) + contract(
        "lka,am->lkm", field_in_im, sin_table
    )
    field_im = contract("lka,am->lkm", field_in_im, cos_table) - contract(
        "lka,am->lkm", field_in_re, sin_table
    )
    factor = jnp.sqrt(image) / jnp.sqrt(field_re * field_re + field_im * field_im + 0.25) - 1.0
    diff_re = (field_re * factor).astype(jnp.bfloat16)
    diff_im = (field_im * factor).astype(jnp.bfloat16)
    back_re = (
        contract("lkm,ma->lka", diff_re, cos_table) - contract("lkm,ma->lka", diff_im, sin_table)
    ).astype(jnp.bfloat16)
    back_im = (
        contract("lkm,ma->lka", diff_im, cos_table) + contract("lkm,ma->lka", diff_re, sin_table)
    ).astype(jnp.bfloat16)
    return (back_re, back_im)


def body_any(spectrum, led_rows, led_cols, images):
    width = images.shape[2]
    slab_rows = spectrum.shape[1]
    columns = spectrum.shape[2]
    slabs = lax.axis_size("slab")
    total_rows = slab_rows * slabs
    position = lax.axis_index("slab")
    cos_table, sin_table = (jnp.asarray(t) for t in host_tables(width))
    own_rows = position * slab_rows + jnp.arange(slab_rows, dtype=jnp.int32)
    col_index = jnp.arange(width, dtype=jnp.int32)

    def take_cols(start):
        return lax.dynamic_slice_in_dim(spectrum, start, width, 2)

    def owner_mask(start):
        return make_pupil(own_rows - start, col_index, width)

    windows = jax.vmap(take_cols)(led_cols)
    masks = jax.vmap(owner_mask)(led_rows)
    win_re = (windows[:, 0] * masks).astype(jnp.bfloat16)
    win_im = (windows[:, 1] * masks).astype(jnp.bfloat16)

    def slice_strip(block, start):
        return take_rows(block, start, width)

    row_re = (
        contract("lgb,bk->lkg", win_re, cos_table) + contract("lgb,bk->lkg", win_im, sin_table)
    ).astype(jnp.bfloat16)
    row_im = (
        contract("lgb,bk->lkg", win_im, cos_table) - contract("lgb,bk->lkg", win_re, sin_table)
    ).astype(jnp.bfloat16)
    col_re, col_im = (
        lax.all_to_all(row_re, "slab", split_axis=1, concat_axis=2, tiled=True),
        lax.all_to_all(row_im, "slab", split_axis=1, concat_axis=2, tiled=True),
    )
    field_in_re = jax.vmap(slice_strip)(col_re, led_rows)
    field_in_im = jax.vmap(slice_strip)(col_im, led_rows)
    back_re, back_im = modulus_step(field_in_re, field_in_im, images, cos_table, sin_table)

    def place_strip(block, start):
        return place_rows(block, start, total_rows, 1)

    full_re = jax.vmap(place_strip)(back_re, led_rows)
    full_im = jax.vmap(place_strip)(back_im, led_rows)
    home_re, home_im = (
        lax.all_to_all(as_sent(full_re), "slab", split_axis=2, concat_axis=1, tiled=True).astype(
            full_re.dtype
        ),
        lax.all_to_all(as_sent(full_im), "slab", split_axis=2, concat_axis=1, tiled=True).astype(
            full_im.dtype
        ),
    )
    upd_re = contract("lkg,kb->lgb", home_re, cos_table) - contract(
        "lkg,kb->lgb", home_im, sin_table
    )
    upd_im = contract("lkg,kb->lgb", home_im, cos_table) + contract(
        "lkg,kb->lgb", home_re, sin_table
    )
    upd_re = upd_re * masks
    upd_im = upd_im * masks

    def add_window(number, gradient):
        start = led_cols[number]
        piece = jnp.stack([upd_re[number], upd_im[number]])
        current = lax.dynamic_slice_in_dim(gradient, start, width, 2)
        return lax.dynamic_update_slice_in_dim(gradient, current + piece, start, 2)

    gradient = lax.fori_loop(
        0, led_rows.shape[0], add_window, jnp.zeros((2, slab_rows, columns), jnp.float32)
    )
    summed = lax.psum_scatter(gradient, "led", scatter_dimension=2, tiled=True)
    share = summed.shape[2]
    own_part = lax.dynamic_slice_in_dim(spectrum, lax.axis_index("led") * share, share, 2)
    return own_part + summed


def dot(left, right):
    return jnp.dot(left, right, preferred_element_type=jnp.float32)


def window_mask(first_row, row_start, col_start, rows, first_col, cols, width):
    shape = (rows, cols)
    at_row = lax.broadcasted_iota(jnp.int32, shape, 0) + (first_row - row_start)
    at_col = lax.broadcasted_iota(jnp.int32, shape, 1) + (first_col - col_start)
    wraps = at_col < 0
    at_col = jnp.where(wraps, at_col + width, at_col)
    row_term = 2 * at_row + 1 - width
    col_term = 2 * at_col + 1 - width
    return row_term * row_term + col_term * col_term < width * width, wraps


def window_kernel(scalars, spectrum, *windows):
    position = scalars[0]
    leds = len(windows)
    rows = spectrum.shape[1]
    width = windows[0].shape[1]
    for led in range(leds):
        inside, wraps = window_mask(
            position * rows, scalars[1 + led], scalars[1 + leds + led], rows, 0, width, width
        )
        for plane in range(2):
            value = jnp.where(wraps, spectrum[plane, :, width:], spectrum[plane, :, :width])
            windows[led][plane * rows : (plane + 1) * rows, :] = jnp.where(
                inside, value, 0.0
            ).astype(jnp.bfloat16)


def rows_kernel(slabs, scalars, window, table_any, *rest):
    outs = rest[:slabs]
    table, sems = rest[slabs:]
    position = scalars[0]
    rows = window.shape[0] // 2
    copies = [
        pltpu.make_async_copy(
            table_any.at[lax.rem(position + d, slabs)], table.at[d], sems.at[d]
        )
        for d in range(slabs)
    ]
    for copy in copies:
        copy.start()
    for d in range(slabs):
        copies[d].wait()
        both = dot(window[...], table[d])
        outs[d][0] = (both[:rows, :LANES] + both[rows:, LANES:]).astype(jnp.bfloat16)
        outs[d][1] = (both[rows:, :LANES] - both[:rows, LANES:]).astype(jnp.bfloat16)


def field_kernel(slabs, scalars, amplitude, table_any, *rest):
    blocks = rest[:slabs]
    period = slabs // 2
    outs = rest[slabs : slabs + period]
    field_in, diff, table, sems = rest[slabs + period :]
    position = scalars[0]
    rows = blocks[0].shape[1]
    width = field_in.shape[0]
    steps = width // LANES
    group = 4
    copies = [
        pltpu.make_async_copy(table_any.at[j], table.at[j], sems.at[j]) for j in range(steps)
    ]
    for copy in copies:
        copy.start()
    for d in range(period):
        at = pl.multiple_of(lax.rem(position - d + slabs, period) * rows, rows)
        for part in range(2):
            field_in[pl.ds(at, rows), part * LANES : (part + 1) * LANES] = (
                blocks[d][part] + blocks[d + period][part]
            )
    for first in range(0, steps, group):
        for j in range(first, first + group):
            copies[j].wait()
        product = dot(
            table[first : first + group].reshape(group * 2 * LANES, width), field_in[...]
        )
        for j in range(first, first + group):
            both = product[(j - first) * 2 * LANES : (j - first + 1) * 2 * LANES]
            field_re = both[:LANES, :LANES] + both[LANES:, LANES:]
            field_im = both[:LANES, LANES:] - both[LANES:, :LANES]
            here = pl.ds(j * LANES, LANES)
            factor = (
                amplitude[here, :] * lax.rsqrt(field_re * field_re + field_im * field_im + 0.25)
                - 1.0
            )
            diff[here, :LANES] = (field_re * factor).astype(jnp.bfloat16)
            diff[here, LANES:] = (field_im * factor).astype(jnp.bfloat16)
    pieces = rows // LANES
    for i in range(period):
        first = lax.rem(position + i, period) * pieces
        product = dot(
            table[pl.ds(first, pieces)].reshape(pieces * 2 * LANES, width), diff[...]
        )
        for h in range(pieces):
            both = product[h * 2 * LANES : (h + 1) * 2 * LANES]
            here = pl.ds(h * LANES, LANES)
            outs[i][0, here, :] = (both[:LANES, :LANES] - both[LANES:, LANES:]).astype(
                jnp.bfloat16
            )
            outs[i][1, here, :] = (both[:LANES, LANES:] + both[LANES:, :LANES]).astype(
                jnp.bfloat16
            )


def update_kernel(slabs, led, leds, first_step, last_step, scalars, table_any, *rest):
    blocks = rest[:slabs]
    rest = rest[slabs:]
    earlier, rest = (rest[0], rest[1:]) if led else (None, rest)
    out, back, table, sems = rest
    position = scalars[0]
    core = scalars[1 + 2 * leds]
    plane_x = scalars[2 + 2 * leds]
    rows = blocks[0].shape[1]
    width = back.shape[1]
    group = width // LANES // 2

    def block_of(n):
        owner = 1 - core if n < group else core
        return owner * group + n % group

    def mask_of(which, n):
        return window_mask(
            position * rows,
            scalars[1 + which],
            scalars[1 + leds + which],
            rows,
            block_of(n) * LANES,
            LANES,
            width,
        )

    copies = {
        n: pltpu.make_async_copy(
            table_any.at[block_of(n)], table.at[n - first_step], sems.at[n - first_step]
        )
        for n in range(first_step, last_step)
    }
    for copy in copies.values():
        copy.start()
    for d in range(slabs):
        at = pl.multiple_of(lax.rem(position - d + slabs, slabs) * LANES, LANES)
        for plane in range(2):
            back[plane * rows : (plane + 1) * rows, pl.ds(at, LANES)] = blocks[d][plane]
    for n in range(first_step, last_step):
        copies[n].wait()
        both = dot(back[...], table[n - first_step])
        update = (
            both[:rows, :LANES] - both[rows:, LANES:],
            both[rows:, :LANES] + both[:rows, LANES:],
        )
        inside, wraps = mask_of(led, n)
        cols = slice((n - first_step) * LANES, (n - first_step + 1) * LANES)
        if earlier is None:
            for plane in range(2):
                out[plane, :, cols] = jnp.where(inside, update[plane], 0.0)
            continue
        _, wraps_earlier = mask_of(0, n)
        for plane in range(2):
            piece = jnp.where(inside, update[plane], 0.0)
            before = earlier[plane, :, n * LANES : (n + 1) * LANES]
            low = jnp.where(wraps, 0.0, piece) + jnp.where(wraps_earlier, 0.0, before)
            high = jnp.where(wraps, piece, 0.0) + jnp.where(wraps_earlier, before, 0.0)
            out[1 - plane_x, plane, :, cols] = low.astype(out.dtype)
            out[plane_x, plane, :, cols] = high.astype(out.dtype)


def local_call(kernel, out_shape, in_vmem, scratch, flops, moved, name, table_at=None):
    vmem = pl.BlockSpec(memory_space=pltpu.VMEM)
    specs = [pl.BlockSpec(memory_space=pltpu.SMEM)]
    specs += [pl.BlockSpec(memory_space=pl.ANY) if i == table_at else vmem for i in range(in_vmem)]
    return pl.pallas_call(
        kernel,
        out_shape=out_shape,
        in_specs=specs,
        out_specs=jax.tree.map(lambda _: vmem, out_shape),
        scratch_shapes=scratch,
        compiler_params=pltpu.CompilerParams(vmem_limit_bytes=32 * 2**20),
        cost_estimate=pl.CostEstimate(flops=flops, bytes_accessed=moved, transcendentals=0),
        name=name,
    )


def body_slabs(spectrum, led_rows, led_cols, images):
    leds, block, width = images.shape
    rows = spectrum.shape[1]
    slabs = lax.axis_size("slab")
    period = slabs // 2
    used = range(1, slabs - 1)
    position = lax.axis_index("slab")
    led_at = lax.axis_index("led")
    core = lax.rem(led_at, 2)
    plane_x = lax.div(led_at, 2)
    bf16 = jnp.bfloat16
    scalars = jnp.concatenate(
        [position[None], led_rows, led_cols, core[None], plane_x[None]], dtype=jnp.int32
    )
    cos_table, sin_table = host_tables(width)
    steps = width // LANES
    by_col = np.stack(
        [
            np.concatenate([t[:, j * LANES : (j + 1) * LANES] for t in (cos_table, sin_table)], 1)
            for j in range(steps)
        ]
    )
    by_row = jnp.asarray(np.ascontiguousarray(by_col.transpose(0, 2, 1)))
    by_col = jnp.asarray(by_col)
    sent_block = jax.ShapeDtypeStruct((2, rows, LANES), bf16)
    table_col = [pltpu.VMEM(by_col.shape, bf16), pltpu.SemaphoreType.DMA((steps,))]
    table_row = [pltpu.VMEM(by_row.shape, bf16), pltpu.SemaphoreType.DMA((steps,))]
    flops = 8 * rows * width * width

    windows = local_call(
        window_kernel,
        [jax.ShapeDtypeStruct((2 * rows, width), bf16)] * leds,
        1,
        [],
        0,
        6 * 2**20,
        "windows",
    )(scalars, spectrum)
    amplitude = jnp.sqrt(images).transpose(0, 2, 1)

    def to_columns(sent, d):
        if d == 0:
            return sent
        return lax.ppermute(sent, "slab", [(s, (s + d) % slabs) for s in used])

    def to_rows(sent, d):
        if d == 0:
            return sent
        pairs = [(s, (s + d) % slabs) for s in range(slabs) if (s + d) % slabs in used]
        return lax.ppermute(sent, "slab", pairs)

    home = []
    for led in range(leds):
        row_blocks = local_call(
            functools.partial(rows_kernel, slabs),
            [sent_block] * slabs,
            2,
            table_col,
            flops,
            6 * 2**20,
            f"row_transform_{led}",
            1,
        )(scalars, windows[led], by_col)
        col_blocks = [to_columns(row_blocks[d], d) for d in range(slabs)]
        back_blocks = local_call(
            functools.partial(field_kernel, slabs),
            [sent_block] * period,
            2 + slabs,
            [pltpu.VMEM((width, 2 * block), bf16)] * 2 + table_row,
            16 * block * width * width,
            6 * 2**20,
            f"modulus_step_{led}",
            1,
        )(scalars, amplitude[led], by_row, *col_blocks)
        home.append([to_rows(back_blocks[d % period], d) for d in range(slabs)])

    share = width // 2
    back_scratch = [pltpu.VMEM((2 * rows, width), bf16)]

    def update_call(led, first_step, last_step, out_shape, name):
        count = last_step - first_step
        return local_call(
            functools.partial(update_kernel, slabs, led, leds, first_step, last_step),
            out_shape,
            1 + slabs + (1 if led else 0),
            back_scratch
            + [pltpu.VMEM((count,) + by_col.shape[1:], bf16), pltpu.SemaphoreType.DMA((count,))],
            flops * count // steps,
            7 * 2**20,
            name,
            0,
        )

    earlier = update_call(
        0, 0, steps, jax.ShapeDtypeStruct((2, rows, width), jnp.float32), "update_0"
    )(scalars, by_col, *home[0])
    half = steps // 2
    sent = update_call(
        1, 0, half, jax.ShapeDtypeStruct((2, 2, rows, share), bf16), "update_1_sent"
    )(scalars, by_col, *home[1], earlier)
    got = lax.ppermute(sent, "led", [(0, 1), (1, 0), (2, 3), (3, 2)])
    kept = update_call(
        1, half, steps, jax.ShapeDtypeStruct((2, 2, rows, share), jnp.float32), "update_1_kept"
    )(scalars, by_col, *home[1], earlier)
    over = (kept[0] + got[0].astype(jnp.float32)).astype(bf16)
    got_x = lax.ppermute(over, "led", [(0, 2), (2, 0), (1, 3), (3, 1)])
    own_part = lax.dynamic_slice_in_dim(spectrum, led_at * share, share, 2)
    base = own_part + (kept[1] + got[1].astype(jnp.float32))
    base, got_x = lax.optimization_barrier((base, got_x))
    return base + got_x.astype(jnp.float32)


def solution(mesh):
    placed = (P(None, "slab", None), P("led"), P("led"), P("led", "slab", None))
    fits = mesh.shape["slab"] == 8 and mesh.shape["led"] == 4

    def body(spectrum, led_rows, led_cols, images):
        shapes = (spectrum.shape, images.shape)
        if fits and shapes == ((2, 256, 2048), (2, 128, 1024)):
            return body_slabs(spectrum, led_rows, led_cols, images)
        return body_any(spectrum, led_rows, led_cols, images)

    return jax.shard_map(
        body, mesh=mesh, in_specs=placed, out_specs=P(None, "slab", "led"), check_vma=False
    )
```

```python
import functools

import jax
import jax.numpy as jnp
import numpy as np
from jax import lax
from jax.experimental import pallas as pl
from jax.experimental.pallas import tpu as pltpu
from jax.sharding import PartitionSpec as P

LANES = 128


def as_sent(value):
    return jax.tree.map(lambda a: a.astype(jnp.bfloat16) if a.dtype == jnp.float32 else a, value)


def host_tables(width):
    index = np.arange(width, dtype=np.int64)
    angle_index = (index[:, None] * index[None, :] % width).astype(np.float32)
    angle = angle_index * np.float32(2.0 * 3.141592653589793 / width)
    scale = np.float32(1.0) / np.sqrt(np.float32(width))
    return (
        (np.cos(angle) * scale).astype(jnp.bfloat16),
        (np.sin(angle) * scale).astype(jnp.bfloat16),
    )


def make_pupil(row_index, col_index, width):
    row_term = (2 * row_index + 1 - width) * (2 * row_index + 1 - width)
    col_term = (2 * col_index + 1 - width) * (2 * col_index + 1 - width)
    return (row_term[:, None] + col_term[None, :] < width * width).astype(jnp.float32)


def contract(form, left, right):
    return jnp.einsum(form, left, right, preferred_element_type=jnp.float32)


def take_rows(strip, start, width):
    return lax.dynamic_slice_in_dim(strip, start, width, 1)


def place_rows(block, start, total, axis_dim):
    shape = list(block.shape)
    shape[axis_dim] = total
    holder = jnp.zeros(tuple(shape), block.dtype)
    return lax.dynamic_update_slice_in_dim(holder, block, start, axis_dim)


def modulus_step(field_in_re, field_in_im, image, cos_table, sin_table):
    field_re = contract("lka,am->lkm", field_in_re, cos_table) + contract(
        "lka,am->lkm", field_in_im, sin_table
    )
    field_im = contract("lka,am->lkm", field_in_im, cos_table) - contract(
        "lka,am->lkm", field_in_re, sin_table
    )
    factor = jnp.sqrt(image) / jnp.sqrt(field_re * field_re + field_im * field_im + 0.25) - 1.0
    diff_re = (field_re * factor).astype(jnp.bfloat16)
    diff_im = (field_im * factor).astype(jnp.bfloat16)
    back_re = (
        contract("lkm,ma->lka", diff_re, cos_table) - contract("lkm,ma->lka", diff_im, sin_table)
    ).astype(jnp.bfloat16)
    back_im = (
        contract("lkm,ma->lka", diff_im, cos_table) + contract("lkm,ma->lka", diff_re, sin_table)
    ).astype(jnp.bfloat16)
    return (back_re, back_im)


def body_any(spectrum, led_rows, led_cols, images):
    width = images.shape[2]
    slab_rows = spectrum.shape[1]
    columns = spectrum.shape[2]
    slabs = lax.axis_size("slab")
    total_rows = slab_rows * slabs
    position = lax.axis_index("slab")
    cos_table, sin_table = (jnp.asarray(t) for t in host_tables(width))
    own_rows = position * slab_rows + jnp.arange(slab_rows, dtype=jnp.int32)
    col_index = jnp.arange(width, dtype=jnp.int32)

    def take_cols(start):
        return lax.dynamic_slice_in_dim(spectrum, start, width, 2)

    def owner_mask(start):
        return make_pupil(own_rows - start, col_index, width)

    windows = jax.vmap(take_cols)(led_cols)
    masks = jax.vmap(owner_mask)(led_rows)
    win_re = (windows[:, 0] * masks).astype(jnp.bfloat16)
    win_im = (windows[:, 1] * masks).astype(jnp.bfloat16)

    def slice_strip(block, start):
        return take_rows(block, start, width)

    row_re = (
        contract("lgb,bk->lkg", win_re, cos_table) + contract("lgb,bk->lkg", win_im, sin_table)
    ).astype(jnp.bfloat16)
    row_im = (
        contract("lgb,bk->lkg", win_im, cos_table) - contract("lgb,bk->lkg", win_re, sin_table)
    ).astype(jnp.bfloat16)
    col_re, col_im = (
        lax.all_to_all(row_re, "slab", split_axis=1, concat_axis=2, tiled=True),
        lax.all_to_all(row_im, "slab", split_axis=1, concat_axis=2, tiled=True),
    )
    field_in_re = jax.vmap(slice_strip)(col_re, led_rows)
    field_in_im = jax.vmap(slice_strip)(col_im, led_rows)
    back_re, back_im = modulus_step(field_in_re, field_in_im, images, cos_table, sin_table)

    def place_strip(block, start):
        return place_rows(block, start, total_rows, 1)

    full_re = jax.vmap(place_strip)(back_re, led_rows)
    full_im = jax.vmap(place_strip)(back_im, led_rows)
    home_re, home_im = (
        lax.all_to_all(as_sent(full_re), "slab", split_axis=2, concat_axis=1, tiled=True).astype(
            full_re.dtype
        ),
        lax.all_to_all(as_sent(full_im), "slab", split_axis=2, concat_axis=1, tiled=True).astype(
            full_im.dtype
        ),
    )
    upd_re = contract("lkg,kb->lgb", home_re, cos_table) - contract(
        "lkg,kb->lgb", home_im, sin_table
    )
    upd_im = contract("lkg,kb->lgb", home_im, cos_table) + contract(
        "lkg,kb->lgb", home_re, sin_table
    )
    upd_re = upd_re * masks
    upd_im = upd_im * masks

    def add_window(number, gradient):
        start = led_cols[number]
        piece = jnp.stack([upd_re[number], upd_im[number]])
        current = lax.dynamic_slice_in_dim(gradient, start, width, 2)
        return lax.dynamic_update_slice_in_dim(gradient, current + piece, start, 2)

    gradient = lax.fori_loop(
        0, led_rows.shape[0], add_window, jnp.zeros((2, slab_rows, columns), jnp.float32)
    )
    summed = lax.psum_scatter(gradient, "led", scatter_dimension=2, tiled=True)
    share = summed.shape[2]
    own_part = lax.dynamic_slice_in_dim(spectrum, lax.axis_index("led") * share, share, 2)
    return own_part + summed


SLABS = 8
PERIOD = 4
FIRST, LAST = 0, 7
EARLY = (5, 7)
LATE = (0, 1, 2, 3, 4, 6)
PASSED = {4: 0, 6: 1}
PASSED_FROM = {FIRST: 1, LAST: 6}


def dot(left, right):
    return jnp.dot(left, right, preferred_element_type=jnp.float32)


def window_mask(first_row, row_start, col_start, rows, first_col, cols, width):
    shape = (rows, cols)
    at_row = lax.broadcasted_iota(jnp.int32, shape, 0) + (first_row - row_start)
    at_col = lax.broadcasted_iota(jnp.int32, shape, 1) + (first_col - col_start)
    wraps = at_col < 0
    at_col = jnp.where(wraps, at_col + width, at_col)
    row_term = 2 * at_row + 1 - width
    col_term = 2 * at_col + 1 - width
    return row_term * row_term + col_term * col_term < width * width, wraps


def row_block(window, table):
    both = dot(window, table)
    half = both.shape[0] // 2
    row_re = both[:half, :LANES] + both[half:, LANES:]
    row_im = both[half:, :LANES] - both[:half, LANES:]
    return row_re.astype(jnp.bfloat16), row_im.astype(jnp.bfloat16)


def store_parts(out, values):
    per = out.shape[0] // 2
    rows = out.shape[1]
    for plane, value in enumerate(values):
        for led in range(per):
            out[plane * per + led] = value[led * rows : (led + 1) * rows]


def first_kernel(led_rows, led_cols, spectrum_any, table_any, window, *rest):
    outs = rest[: len(EARLY)]
    early, spectrum, table, sems = rest[len(EARLY) :]
    position = lax.axis_index("slab")
    leds = led_rows.shape[0]
    rows = spectrum.shape[1]
    width = window.shape[1]
    chunks = 4
    step = rows // chunks
    fetches = [
        pltpu.make_async_copy(
            spectrum_any.at[:, pl.ds(i * step, step)],
            spectrum.at[:, pl.ds(i * step, step)],
            sems.at[i],
        )
        for i in range(chunks)
    ]
    tables = [
        pltpu.make_async_copy(
            table_any.at[jnp.bitwise_xor(position, d)], table.at[i], sems.at[chunks + i]
        )
        for i, d in enumerate(EARLY)
    ]
    for copy in fetches + tables:
        copy.start()
    for i in range(chunks):
        fetches[i].wait()
        here = slice(i * step, (i + 1) * step)
        for led in range(leds):
            inside, wraps = window_mask(
                position * rows + i * step, led_rows[led], led_cols[led], step, 0, width, width
            )
            for plane in range(2):
                value = jnp.where(
                    wraps, spectrum[plane, here, width:], spectrum[plane, here, :width]
                )
                at = (plane * leds + led) * rows + i * step
                window[at : at + step, :] = jnp.where(inside, value, 0.0).astype(jnp.bfloat16)
    for i in range(len(EARLY)):
        tables[i].wait()
        values = row_block(window[...], table[i])
        store_parts(outs[i], values)
        store_parts(early.at[i], values)


def second_kernel(window, table, *outs):
    position = lax.axis_index("slab")
    for d, out in zip(LATE, outs):
        store_parts(out, row_block(window[...], table[jnp.bitwise_xor(position, d)]))


def field_kernel(amplitude, table, *rest):
    blocks = rest[:SLABS]
    outs = rest[SLABS : SLABS + PERIOD]
    field_in, diff = rest[SLABS + PERIOD :]
    position = lax.axis_index("slab")
    parts, rows, _ = blocks[0].shape
    half = parts // 2 * LANES
    width = field_in.shape[0]
    steps = width // LANES
    group = 4
    for d in range(SLABS):
        source = jnp.bitwise_xor(position, d)
        if d in PASSED:
            for by, origin in PASSED_FROM.items():
                source = jnp.where(source == by, origin, source)
        at = pl.multiple_of(jnp.bitwise_and(source, PERIOD - 1) * rows, rows)
        for part in range(parts):
            where = (pl.ds(at, rows), slice(part * LANES, (part + 1) * LANES))
            if d < PERIOD:
                field_in[where] = blocks[d][part]
            else:
                field_in[where] += blocks[d][part]
    for first in range(0, steps, group):
        product = dot(
            table[first : first + group].reshape(group * 2 * LANES, width), field_in[...]
        )
        for j in range(first, first + group):
            both = product[(j - first) * 2 * LANES : (j - first + 1) * 2 * LANES]
            field_re = both[:LANES, :half] + both[LANES:, half:]
            field_im = both[:LANES, half:] - both[LANES:, :half]
            here = pl.ds(j * LANES, LANES)
            factor = (
                amplitude[here, :] * lax.rsqrt(field_re * field_re + field_im * field_im + 0.25)
                - 1.0
            )
            diff[here, :half] = (field_re * factor).astype(jnp.bfloat16)
            diff[here, half:] = (field_im * factor).astype(jnp.bfloat16)
    pieces = rows // LANES
    for i in range(PERIOD):
        first = jnp.bitwise_and(jnp.bitwise_xor(position, i), PERIOD - 1) * pieces
        product = dot(table[pl.ds(first, pieces)].reshape(pieces * 2 * LANES, width), diff[...])
        for h in range(pieces):
            both = product[h * 2 * LANES : (h + 1) * 2 * LANES]
            here = pl.ds(h * LANES, LANES)
            back_re = (both[:LANES, :half] - both[LANES:, half:]).astype(jnp.bfloat16)
            back_im = (both[:LANES, half:] + both[LANES:, :half]).astype(jnp.bfloat16)
            for part in range(parts // 2):
                cols = slice(part * LANES, (part + 1) * LANES)
                outs[i][part, here, :] = back_re[:, cols]
                outs[i][parts // 2 + part, here, :] = back_im[:, cols]


def update_columns(first_step, last_step, led_rows, led_cols, table, back, out):
    position = lax.axis_index("slab")
    led_at = lax.axis_index("led")
    core = jnp.bitwise_and(led_at, 1)
    plane_x = jnp.right_shift(led_at, 1)
    leds = led_rows.shape[0]
    rows = back.shape[0] // (2 * leds)
    width = back.shape[1]
    group = width // LANES // 2
    for n in range(first_step, last_step):
        owner = 1 - core if n < group else core
        block = owner * group + n % group
        both = dot(back[...], table[block])
        half = leds * rows
        update = (
            both[:half, :LANES] - both[half:, LANES:],
            both[half:, :LANES] + both[:half, LANES:],
        )
        low = [0.0, 0.0]
        high = [0.0, 0.0]
        for led in range(leds):
            inside, wraps = window_mask(
                position * rows, led_rows[led], led_cols[led], rows, block * LANES, LANES, width
            )
            for plane in range(2):
                piece = jnp.where(inside, update[plane][led * rows : (led + 1) * rows], 0.0)
                low[plane] += jnp.where(wraps, 0.0, piece)
                high[plane] += jnp.where(wraps, piece, 0.0)
        cols = slice((n - first_step) * LANES, (n - first_step + 1) * LANES)
        for plane in range(2):
            out[1 - plane_x, plane, :, cols] = low[plane].astype(out.dtype)
            out[plane_x, plane, :, cols] = high[plane].astype(out.dtype)


def sent_kernel(led_rows, led_cols, table, *rest):
    blocks = rest[:SLABS]
    out, back = rest[SLABS:]
    position = lax.axis_index("slab")
    parts, rows, _ = blocks[0].shape
    for d in range(SLABS):
        at = pl.multiple_of(jnp.bitwise_xor(position, d) * LANES, LANES)
        for part in range(parts):
            back[part * rows : (part + 1) * rows, pl.ds(at, LANES)] = blocks[d][part]
    half = back.shape[1] // LANES // 2
    update_columns(0, half, led_rows, led_cols, table, back, out)


def kept_kernel(led_rows, led_cols, table, back, out):
    half = back.shape[1] // LANES // 2
    update_columns(half, 2 * half, led_rows, led_cols, table, back, out)


def local_call(kernel, out_shape, spaces, scratch, flops, moved, name):
    return pl.pallas_call(
        kernel,
        out_shape=out_shape,
        in_specs=[pl.BlockSpec(memory_space=space) for space in spaces],
        out_specs=jax.tree.map(lambda _: pl.BlockSpec(memory_space=pltpu.VMEM), out_shape),
        scratch_shapes=scratch,
        compiler_params=pltpu.CompilerParams(vmem_limit_bytes=32 * 2**20),
        cost_estimate=pl.CostEstimate(flops=flops, bytes_accessed=moved, transcendentals=0),
        name=name,
    )


def body_slabs(spectrum, led_rows, led_cols, images):
    leds, block, width = images.shape
    rows = spectrum.shape[1]
    led_at = lax.axis_index("led")
    bf16 = jnp.bfloat16
    vmem, smem, hbm = pltpu.VMEM, pltpu.SMEM, pltpu.HBM
    cos_table, sin_table = host_tables(width)
    steps = width // LANES
    by_col = np.stack(
        [
            np.concatenate([t[:, j * LANES : (j + 1) * LANES] for t in (cos_table, sin_table)], 1)
            for j in range(steps)
        ]
    )
    by_row = jnp.asarray(np.ascontiguousarray(by_col.transpose(0, 2, 1)))
    by_col = jnp.asarray(by_col)
    parts = 2 * leds
    sent_block = jax.ShapeDtypeStruct((parts, rows, LANES), bf16)
    flops = 8 * leds * rows * width * width

    window, *outs, early = local_call(
        first_kernel,
        [
            jax.ShapeDtypeStruct((parts * rows, width), bf16),
            *[sent_block] * len(EARLY),
            jax.ShapeDtypeStruct((len(EARLY),) + sent_block.shape, bf16),
        ],
        [smem, smem, hbm, hbm],
        [
            pltpu.VMEM(spectrum.shape, jnp.float32),
            pltpu.VMEM((len(EARLY),) + by_col.shape[1:], bf16),
            pltpu.SemaphoreType.DMA((4 + len(EARLY),)),
        ],
        flops // 4,
        8 * 2**20,
        "windows_and_early_rows",
    )(led_rows, led_cols, spectrum, by_col)
    passed = lax.ppermute(early, "slab", [(s, by) for by, s in PASSED_FROM.items()])
    windowed = range(FIRST + 1, LAST)
    col_blocks = {}
    for d, sent in zip(EARLY, outs):
        pairs = [(s, s ^ d) for s in windowed if s not in PASSED_FROM.values()]
        col_blocks[d] = lax.ppermute(sent, "slab", pairs)
    row_blocks = local_call(
        second_kernel,
        [sent_block] * len(LATE),
        [vmem, vmem],
        [],
        3 * flops // 4,
        8 * 2**20,
        "late_rows",
    )(window, by_col)
    for d, sent in zip(LATE, row_blocks):
        if d == 0:
            col_blocks[d] = sent
        elif d in PASSED:
            pairs = [(s, s ^ d) for s in range(SLABS)]
            col_blocks[d] = lax.ppermute(sent + passed[PASSED[d]], "slab", pairs)
        else:
            col_blocks[d] = lax.ppermute(sent, "slab", [(s, s ^ d) for s in windowed])

    amplitude = jnp.sqrt(images).transpose(2, 0, 1).reshape(width, leds * block)
    back_blocks = local_call(
        field_kernel,
        [sent_block] * PERIOD,
        [vmem] * (2 + SLABS),
        [pltpu.VMEM((width, parts * block), bf16)] * 2,
        16 * leds * block * width * width,
        12 * 2**20,
        "modulus_step",
    )(amplitude, by_row, *[col_blocks[d] for d in range(SLABS)])

    def to_rows(d):
        sent = back_blocks[d % PERIOD]
        if d == 0:
            return sent
        return lax.ppermute(sent, "slab", [(s, s ^ d) for s in range(SLABS) if s ^ d in windowed])

    home = [to_rows(d) for d in range(SLABS)]
    share = width // 2
    sent, back = local_call(
        sent_kernel,
        [
            jax.ShapeDtypeStruct((2, 2, rows, share), bf16),
            jax.ShapeDtypeStruct((parts * rows, width), bf16),
        ],
        [smem, smem] + [vmem] * (1 + SLABS),
        [],
        flops // 2,
        8 * 2**20,
        "update_sent",
    )(led_rows, led_cols, by_col, *home)
    got = lax.ppermute(sent, "led", [(0, 1), (1, 0), (2, 3), (3, 2)])
    kept = local_call(
        kept_kernel,
        jax.ShapeDtypeStruct((2, 2, rows, share), jnp.float32),
        [smem, smem, vmem, vmem],
        [],
        flops // 2,
        8 * 2**20,
        "update_kept",
    )(led_rows, led_cols, by_col, back)
    over = (kept[0] + got[0].astype(jnp.float32)).astype(bf16)
    got_x = lax.ppermute(over, "led", [(0, 2), (2, 0), (1, 3), (3, 1)])
    own_part = lax.dynamic_slice_in_dim(spectrum, led_at * share, share, 2)
    base = own_part + (kept[1] + got[1].astype(jnp.float32))
    base, got_x = lax.optimization_barrier((base, got_x))
    return base + got_x.astype(jnp.float32)


def solution(mesh):
    placed = (P(None, "slab", None), P("led"), P("led"), P("led", "slab", None))
    fits = mesh.shape["slab"] == 8 and mesh.shape["led"] == 4

    def body(spectrum, led_rows, led_cols, images):
        shapes = (spectrum.shape, images.shape)
        if fits and shapes == ((2, 256, 2048), (2, 128, 1024)):
            return body_slabs(spectrum, led_rows, led_cols, images)
        return body_any(spectrum, led_rows, led_cols, images)

    return jax.shard_map(
        body, mesh=mesh, in_specs=placed, out_specs=P(None, "slab", "led"), check_vma=False
    )
```

```python
import functools

import jax
import jax.numpy as jnp
import numpy as np
from jax import lax
from jax.experimental import pallas as pl
from jax.experimental.pallas import tpu as pltpu
from jax.sharding import PartitionSpec as P

LANES = 128


def as_sent(value):
    return jax.tree.map(lambda a: a.astype(jnp.bfloat16) if a.dtype == jnp.float32 else a, value)


def host_tables(width):
    index = np.arange(width, dtype=np.int64)
    angle_index = (index[:, None] * index[None, :] % width).astype(np.float32)
    angle = angle_index * np.float32(2.0 * 3.141592653589793 / width)
    scale = np.float32(1.0) / np.sqrt(np.float32(width))
    return (
        (np.cos(angle) * scale).astype(jnp.bfloat16),
        (np.sin(angle) * scale).astype(jnp.bfloat16),
    )


def make_pupil(row_index, col_index, width):
    row_term = (2 * row_index + 1 - width) * (2 * row_index + 1 - width)
    col_term = (2 * col_index + 1 - width) * (2 * col_index + 1 - width)
    return (row_term[:, None] + col_term[None, :] < width * width).astype(jnp.float32)


def contract(form, left, right):
    return jnp.einsum(form, left, right, preferred_element_type=jnp.float32)


def take_rows(strip, start, width):
    return lax.dynamic_slice_in_dim(strip, start, width, 1)


def place_rows(block, start, total, axis_dim):
    shape = list(block.shape)
    shape[axis_dim] = total
    holder = jnp.zeros(tuple(shape), block.dtype)
    return lax.dynamic_update_slice_in_dim(holder, block, start, axis_dim)


def modulus_step(field_in_re, field_in_im, image, cos_table, sin_table):
    field_re = contract("lka,am->lkm", field_in_re, cos_table) + contract(
        "lka,am->lkm", field_in_im, sin_table
    )
    field_im = contract("lka,am->lkm", field_in_im, cos_table) - contract(
        "lka,am->lkm", field_in_re, sin_table
    )
    factor = jnp.sqrt(image) / jnp.sqrt(field_re * field_re + field_im * field_im + 0.25) - 1.0
    diff_re = (field_re * factor).astype(jnp.bfloat16)
    diff_im = (field_im * factor).astype(jnp.bfloat16)
    back_re = (
        contract("lkm,ma->lka", diff_re, cos_table) - contract("lkm,ma->lka", diff_im, sin_table)
    ).astype(jnp.bfloat16)
    back_im = (
        contract("lkm,ma->lka", diff_im, cos_table) + contract("lkm,ma->lka", diff_re, sin_table)
    ).astype(jnp.bfloat16)
    return (back_re, back_im)


def body_any(spectrum, led_rows, led_cols, images):
    width = images.shape[2]
    slab_rows = spectrum.shape[1]
    columns = spectrum.shape[2]
    slabs = lax.axis_size("slab")
    total_rows = slab_rows * slabs
    position = lax.axis_index("slab")
    cos_table, sin_table = (jnp.asarray(t) for t in host_tables(width))
    own_rows = position * slab_rows + jnp.arange(slab_rows, dtype=jnp.int32)
    col_index = jnp.arange(width, dtype=jnp.int32)

    def take_cols(start):
        return lax.dynamic_slice_in_dim(spectrum, start, width, 2)

    def owner_mask(start):
        return make_pupil(own_rows - start, col_index, width)

    windows = jax.vmap(take_cols)(led_cols)
    masks = jax.vmap(owner_mask)(led_rows)
    win_re = (windows[:, 0] * masks).astype(jnp.bfloat16)
    win_im = (windows[:, 1] * masks).astype(jnp.bfloat16)

    def slice_strip(block, start):
        return take_rows(block, start, width)

    row_re = (
        contract("lgb,bk->lkg", win_re, cos_table) + contract("lgb,bk->lkg", win_im, sin_table)
    ).astype(jnp.bfloat16)
    row_im = (
        contract("lgb,bk->lkg", win_im, cos_table) - contract("lgb,bk->lkg", win_re, sin_table)
    ).astype(jnp.bfloat16)
    col_re, col_im = (
        lax.all_to_all(row_re, "slab", split_axis=1, concat_axis=2, tiled=True),
        lax.all_to_all(row_im, "slab", split_axis=1, concat_axis=2, tiled=True),
    )
    field_in_re = jax.vmap(slice_strip)(col_re, led_rows)
    field_in_im = jax.vmap(slice_strip)(col_im, led_rows)
    back_re, back_im = modulus_step(field_in_re, field_in_im, images, cos_table, sin_table)

    def place_strip(block, start):
        return place_rows(block, start, total_rows, 1)

    full_re = jax.vmap(place_strip)(back_re, led_rows)
    full_im = jax.vmap(place_strip)(back_im, led_rows)
    home_re, home_im = (
        lax.all_to_all(as_sent(full_re), "slab", split_axis=2, concat_axis=1, tiled=True).astype(
            full_re.dtype
        ),
        lax.all_to_all(as_sent(full_im), "slab", split_axis=2, concat_axis=1, tiled=True).astype(
            full_im.dtype
        ),
    )
    upd_re = contract("lkg,kb->lgb", home_re, cos_table) - contract(
        "lkg,kb->lgb", home_im, sin_table
    )
    upd_im = contract("lkg,kb->lgb", home_im, cos_table) + contract(
        "lkg,kb->lgb", home_re, sin_table
    )
    upd_re = upd_re * masks
    upd_im = upd_im * masks

    def add_window(number, gradient):
        start = led_cols[number]
        piece = jnp.stack([upd_re[number], upd_im[number]])
        current = lax.dynamic_slice_in_dim(gradient, start, width, 2)
        return lax.dynamic_update_slice_in_dim(gradient, current + piece, start, 2)

    gradient = lax.fori_loop(
        0, led_rows.shape[0], add_window, jnp.zeros((2, slab_rows, columns), jnp.float32)
    )
    summed = lax.psum_scatter(gradient, "led", scatter_dimension=2, tiled=True)
    share = summed.shape[2]
    own_part = lax.dynamic_slice_in_dim(spectrum, lax.axis_index("led") * share, share, 2)
    return own_part + summed


SLABS = 8
PERIOD = 4
FIRST, LAST = 0, 7
EARLY = (5, 7)
LATE = (0, 1, 2, 3, 4, 6)
PASSED = {4: 0, 6: 1}
PASSED_FROM = {FIRST: 1, LAST: 6}


class Stream:
    def __init__(self, source, target, sems, blocks):
        self.target = target
        self.copies = [
            pltpu.make_async_copy(source.at[block], target.at[i], sems.at[i])
            for i, block in enumerate(blocks)
        ]
        self.started = 0
        self.taken = 0
        self.start()
        self.start()

    def start(self):
        if self.started < len(self.copies):
            self.copies[self.started].start()
            self.started += 1

    def take(self):
        self.copies[self.taken].wait()
        self.start()
        self.taken += 1
        return self.target[self.taken - 1]


def dot(left, right):
    return jnp.dot(left, right, preferred_element_type=jnp.float32)


def window_mask(first_row, row_start, col_start, rows, first_col, cols, width):
    shape = (rows, cols)
    at_row = lax.broadcasted_iota(jnp.int32, shape, 0) + (first_row - row_start)
    at_col = lax.broadcasted_iota(jnp.int32, shape, 1) + (first_col - col_start)
    wraps = at_col < 0
    at_col = jnp.where(wraps, at_col + width, at_col)
    row_term = 2 * at_row + 1 - width
    col_term = 2 * at_col + 1 - width
    return row_term * row_term + col_term * col_term < width * width, wraps


def row_block(window, table):
    both = dot(window, table)
    half = both.shape[0] // 2
    row_re = both[:half, :LANES] + both[half:, LANES:]
    row_im = both[half:, :LANES] - both[:half, LANES:]
    return row_re.astype(jnp.bfloat16), row_im.astype(jnp.bfloat16)


def store_parts(out, values):
    per = out.shape[0] // 2
    rows = out.shape[1]
    for plane, value in enumerate(values):
        for led in range(per):
            out[plane * per + led] = value[led * rows : (led + 1) * rows]


def first_kernel(starts, spectrum_any, table_any, window, *rest):
    outs = rest[: len(EARLY)]
    early, table, spectrum, sems, table_sems = rest[len(EARLY) :]
    position = lax.axis_index("slab")
    leds = starts.shape[0] // 2
    rows = spectrum.shape[1]
    width = window.shape[1]
    chunks = 4
    step = rows // chunks
    fetches = [
        pltpu.make_async_copy(
            spectrum_any.at[:, pl.ds(i * step, step)],
            spectrum.at[:, pl.ds(i * step, step)],
            sems.at[i],
        )
        for i in range(chunks)
    ]
    for copy in fetches:
        copy.start()
    for i in range(chunks):
        fetches[i].wait()
        if i == chunks - 1:
            blocks = [jnp.bitwise_xor(position, d) for d in EARLY]
            tables = Stream(table_any, table, table_sems, blocks)
        here = slice(i * step, (i + 1) * step)
        for led in range(leds):
            inside, wraps = window_mask(
                position * rows + i * step, starts[led], starts[leds + led], step, 0, width, width
            )
            for plane in range(2):
                value = jnp.where(
                    wraps, spectrum[plane, here, width:], spectrum[plane, here, :width]
                )
                at = (plane * leds + led) * rows + i * step
                window[at : at + step, :] = jnp.where(inside, value, 0.0).astype(jnp.bfloat16)
    for i in range(len(EARLY)):
        values = row_block(window[...], tables.take())
        store_parts(outs[i], values)
        store_parts(early.at[i], values)


def second_kernel(window, table_any, *rest):
    outs = rest[: len(LATE)]
    position = lax.axis_index("slab")
    tables = Stream(table_any, *rest[len(LATE) :], [jnp.bitwise_xor(position, d) for d in LATE])
    for out in outs:
        store_parts(out, row_block(window[...], tables.take()))


def field_kernel(amplitude, table_any, *rest):
    blocks = rest[:SLABS]
    outs = rest[SLABS : SLABS + PERIOD]
    field_in, diff, table, sems = rest[SLABS + PERIOD :]
    position = lax.axis_index("slab")
    parts, rows, _ = blocks[0].shape
    half = parts // 2 * LANES
    width = field_in.shape[0]
    steps = width // LANES
    group = 4
    tables = Stream(table_any, table, sems, range(steps))
    for d in range(SLABS):
        source = jnp.bitwise_xor(position, d)
        if d in PASSED:
            for by, origin in PASSED_FROM.items():
                source = jnp.where(source == by, origin, source)
        at = pl.multiple_of(jnp.bitwise_and(source, PERIOD - 1) * rows, rows)
        for part in range(parts):
            where = (pl.ds(at, rows), slice(part * LANES, (part + 1) * LANES))
            if d < PERIOD:
                field_in[where] = blocks[d][part]
            else:
                field_in[where] += blocks[d][part]
    for first in range(0, steps, group):
        for _ in range(group):
            tables.take()
        product = dot(
            table[first : first + group].reshape(group * 2 * LANES, width), field_in[...]
        )
        for j in range(first, first + group):
            both = product[(j - first) * 2 * LANES : (j - first + 1) * 2 * LANES]
            field_re = both[:LANES, :half] + both[LANES:, half:]
            field_im = both[:LANES, half:] - both[LANES:, :half]
            here = pl.ds(j * LANES, LANES)
            factor = (
                amplitude[here, :] * lax.rsqrt(field_re * field_re + field_im * field_im + 0.25)
                - 1.0
            )
            diff[here, :half] = (field_re * factor).astype(jnp.bfloat16)
            diff[here, half:] = (field_im * factor).astype(jnp.bfloat16)
    pieces = rows // LANES
    for i in range(PERIOD):
        first = lax.rem(position + i, PERIOD) * pieces
        product = dot(table[pl.ds(first, pieces)].reshape(pieces * 2 * LANES, width), diff[...])
        for h in range(pieces):
            both = product[h * 2 * LANES : (h + 1) * 2 * LANES]
            here = pl.ds(h * LANES, LANES)
            back_re = (both[:LANES, :half] - both[LANES:, half:]).astype(jnp.bfloat16)
            back_im = (both[:LANES, half:] + both[LANES:, :half]).astype(jnp.bfloat16)
            for part in range(parts // 2):
                cols = slice(part * LANES, (part + 1) * LANES)
                outs[i][part, here, :] = back_re[:, cols]
                outs[i][parts // 2 + part, here, :] = back_im[:, cols]


def update_columns(first_step, last_step, starts, table_any, back, out, table, sems, fill=None):
    position = lax.axis_index("slab")
    led_at = lax.axis_index("led")
    core = jnp.bitwise_and(led_at, 1)
    plane_x = jnp.right_shift(led_at, 1)
    leds = starts.shape[0] // 2
    rows = back.shape[0] // (2 * leds)
    width = back.shape[1]
    group = width // LANES // 2
    blocks = [
        (1 - core if n < group else core) * group + n % group for n in range(first_step, last_step)
    ]
    tables = Stream(table_any, table, sems, blocks)
    if fill is not None:
        fill()
    for n in range(first_step, last_step):
        block = blocks[n - first_step]
        both = dot(back[...], tables.take())
        half = leds * rows
        update = (
            both[:half, :LANES] - both[half:, LANES:],
            both[half:, :LANES] + both[:half, LANES:],
        )
        low = [0.0, 0.0]
        high = [0.0, 0.0]
        for led in range(leds):
            inside, wraps = window_mask(
                position * rows, starts[led], starts[leds + led], rows, block * LANES, LANES, width
            )
            for plane in range(2):
                piece = jnp.where(inside, update[plane][led * rows : (led + 1) * rows], 0.0)
                low[plane] += jnp.where(wraps, 0.0, piece)
                high[plane] += jnp.where(wraps, piece, 0.0)
        cols = slice((n - first_step) * LANES, (n - first_step + 1) * LANES)
        for plane in range(2):
            out[1 - plane_x, plane, :, cols] = low[plane].astype(out.dtype)
            out[plane_x, plane, :, cols] = high[plane].astype(out.dtype)


def sent_kernel(starts, table_any, *rest):
    blocks = rest[:SLABS]
    out, back, table, sems = rest[SLABS:]
    position = lax.axis_index("slab")
    parts, rows, _ = blocks[0].shape
    half = back.shape[1] // LANES // 2

    def fill():
        for d in range(SLABS):
            at = pl.multiple_of(lax.rem(position + SLABS - d, SLABS) * LANES, LANES)
            for part in range(parts):
                back[part * rows : (part + 1) * rows, pl.ds(at, LANES)] = blocks[d][part]

    update_columns(0, half, starts, table_any, back, out, table, sems, fill)


def kept_kernel(starts, table_any, back, out, table, sems):
    half = back.shape[1] // LANES // 2
    update_columns(half, 2 * half, starts, table_any, back, out, table, sems)


def local_call(kernel, out_shape, spaces, scratch, flops, moved, name):
    return pl.pallas_call(
        kernel,
        out_shape=out_shape,
        in_specs=[pl.BlockSpec(memory_space=space) for space in spaces],
        out_specs=jax.tree.map(lambda _: pl.BlockSpec(memory_space=pltpu.VMEM), out_shape),
        scratch_shapes=scratch,
        compiler_params=pltpu.CompilerParams(vmem_limit_bytes=48 * 2**20),
        cost_estimate=pl.CostEstimate(flops=flops, bytes_accessed=moved, transcendentals=0),
        name=name,
    )


def table_scratch(table, count):
    return [
        pltpu.VMEM((count,) + table.shape[1:], table.dtype),
        pltpu.SemaphoreType.DMA((count,)),
    ]


def body_slabs(spectrum, led_rows, led_cols, images):
    leds, block, width = images.shape
    rows = spectrum.shape[1]
    led_at = lax.axis_index("led")
    bf16 = jnp.bfloat16
    vmem, smem = pltpu.VMEM, pltpu.SMEM
    cos_table, sin_table = host_tables(width)
    steps = width // LANES
    by_col = np.stack(
        [
            np.concatenate([t[:, j * LANES : (j + 1) * LANES] for t in (cos_table, sin_table)], 1)
            for j in range(steps)
        ]
    )
    by_row = jnp.asarray(np.ascontiguousarray(by_col.transpose(0, 2, 1)))
    by_col = jnp.asarray(by_col)
    parts = 2 * leds
    sent_block = jax.ShapeDtypeStruct((parts, rows, LANES), bf16)
    flops = 8 * leds * rows * width * width

    starts = jnp.concatenate([led_rows, led_cols]).astype(jnp.int32)
    window, *outs, early = local_call(
        first_kernel,
        [
            jax.ShapeDtypeStruct((parts * rows, width), bf16),
            *[sent_block] * len(EARLY),
            jax.ShapeDtypeStruct((len(EARLY),) + sent_block.shape, bf16),
        ],
        [smem, pl.ANY, pl.ANY],
        [
            pltpu.VMEM((len(EARLY),) + by_col.shape[1:], bf16),
            pltpu.VMEM(spectrum.shape, jnp.float32),
            pltpu.SemaphoreType.DMA((4,)),
            pltpu.SemaphoreType.DMA((len(EARLY),)),
        ],
        flops // 4,
        8 * 2**20,
        "windows_and_early_rows",
    )(starts, spectrum, by_col)
    passed = lax.ppermute(early, "slab", [(s, by) for by, s in PASSED_FROM.items()])
    windowed = range(FIRST + 1, LAST)
    col_blocks = {}
    for d, sent in zip(EARLY, outs):
        pairs = [(s, s ^ d) for s in windowed if s not in PASSED_FROM.values()]
        col_blocks[d] = lax.ppermute(sent, "slab", pairs)
    row_blocks = local_call(
        second_kernel,
        [sent_block] * len(LATE),
        [vmem, pl.ANY],
        table_scratch(by_col, len(LATE)),
        3 * flops // 4,
        8 * 2**20,
        "late_rows",
    )(window, by_col)
    passed, col_blocks, *row_blocks = lax.optimization_barrier((passed, col_blocks, *row_blocks))
    row_blocks = dict(zip(LATE, row_blocks))
    col_blocks[0] = row_blocks[0]
    for d in PASSED:
        pairs = [(s, s ^ d) for s in range(SLABS)]
        col_blocks[d] = lax.ppermute(row_blocks[d] + passed[PASSED[d]], "slab", pairs)
    col_blocks[2] = lax.ppermute(row_blocks[2], "slab", [(s, s ^ 2) for s in windowed])
    col_blocks[2], row_blocks[1], row_blocks[3] = lax.optimization_barrier(
        (col_blocks[2], row_blocks[1], row_blocks[3])
    )
    for d in (1, 3):
        col_blocks[d] = lax.ppermute(row_blocks[d], "slab", [(s, s ^ d) for s in windowed])

    amplitude = jnp.sqrt(images).transpose(2, 0, 1).reshape(width, leds * block)
    back_blocks = local_call(
        field_kernel,
        [sent_block] * PERIOD,
        [vmem, pl.ANY] + [vmem] * SLABS,
        [pltpu.VMEM((width, parts * block), bf16)] * 2 + table_scratch(by_row, steps),
        16 * leds * block * width * width,
        12 * 2**20,
        "modulus_step",
    )(amplitude, by_row, *[col_blocks[d] for d in range(SLABS)])

    def to_rows(d):
        sent = back_blocks[d % PERIOD]
        if d == 0:
            return sent
        pairs = [(s, (s + d) % SLABS) for s in range(SLABS) if (s + d) % SLABS in windowed]
        return lax.ppermute(sent, "slab", pairs)

    home = [to_rows(d) for d in range(SLABS)]
    share = width // 2
    sent, back = local_call(
        sent_kernel,
        [
            jax.ShapeDtypeStruct((2, 2, rows, share), bf16),
            jax.ShapeDtypeStruct((parts * rows, width), bf16),
        ],
        [smem, pl.ANY] + [vmem] * SLABS,
        table_scratch(by_col, steps // 2),
        flops // 2,
        8 * 2**20,
        "update_sent",
    )(starts, by_col, *home)
    got = lax.ppermute(sent, "led", [(0, 1), (1, 0), (2, 3), (3, 2)])
    kept = local_call(
        kept_kernel,
        jax.ShapeDtypeStruct((2, 2, rows, share), jnp.float32),
        [smem, pl.ANY, vmem],
        table_scratch(by_col, steps // 2),
        flops // 2,
        8 * 2**20,
        "update_kept",
    )(starts, by_col, back)
    over = (kept[0] + got[0].astype(jnp.float32)).astype(bf16)
    got_x = lax.ppermute(over, "led", [(0, 2), (2, 0), (1, 3), (3, 1)])
    own_part = lax.dynamic_slice_in_dim(spectrum, led_at * share, share, 2)
    base = own_part + (kept[1] + got[1].astype(jnp.float32))
    base, got_x = lax.optimization_barrier((base, got_x))
    return base + got_x.astype(jnp.float32)


def solution(mesh):
    placed = (P(None, "slab", None), P("led"), P("led"), P("led", "slab", None))
    fits = mesh.shape["slab"] == 8 and mesh.shape["led"] == 4

    def body(spectrum, led_rows, led_cols, images):
        shapes = (spectrum.shape, images.shape)
        if fits and shapes == ((2, 256, 2048), (2, 128, 1024)):
            return body_slabs(spectrum, led_rows, led_cols, images)
        return body_any(spectrum, led_rows, led_cols, images)

    return jax.shard_map(
        body, mesh=mesh, in_specs=placed, out_specs=P(None, "slab", "led"), check_vma=False
    )
```

```python
import functools

import jax
import jax.numpy as jnp
import numpy as np
from jax import lax
from jax.experimental import pallas as pl
from jax.experimental.pallas import tpu as pltpu
from jax.sharding import PartitionSpec as P

LANES = 128


def as_sent(value):
    return jax.tree.map(lambda a: a.astype(jnp.bfloat16) if a.dtype == jnp.float32 else a, value)


def host_tables(width):
    index = np.arange(width, dtype=np.int64)
    angle_index = (index[:, None] * index[None, :] % width).astype(np.float32)
    angle = angle_index * np.float32(2.0 * 3.141592653589793 / width)
    scale = np.float32(1.0) / np.sqrt(np.float32(width))
    return (
        (np.cos(angle) * scale).astype(jnp.bfloat16),
        (np.sin(angle) * scale).astype(jnp.bfloat16),
    )


def make_pupil(row_index, col_index, width):
    row_term = (2 * row_index + 1 - width) * (2 * row_index + 1 - width)
    col_term = (2 * col_index + 1 - width) * (2 * col_index + 1 - width)
    return (row_term[:, None] + col_term[None, :] < width * width).astype(jnp.float32)


def contract(form, left, right):
    return jnp.einsum(form, left, right, preferred_element_type=jnp.float32)


def take_rows(strip, start, width):
    return lax.dynamic_slice_in_dim(strip, start, width, 1)


def place_rows(block, start, total, axis_dim):
    shape = list(block.shape)
    shape[axis_dim] = total
    holder = jnp.zeros(tuple(shape), block.dtype)
    return lax.dynamic_update_slice_in_dim(holder, block, start, axis_dim)


def modulus_step(field_in_re, field_in_im, image, cos_table, sin_table):
    field_re = contract("lka,am->lkm", field_in_re, cos_table) + contract(
        "lka,am->lkm", field_in_im, sin_table
    )
    field_im = contract("lka,am->lkm", field_in_im, cos_table) - contract(
        "lka,am->lkm", field_in_re, sin_table
    )
    factor = jnp.sqrt(image) / jnp.sqrt(field_re * field_re + field_im * field_im + 0.25) - 1.0
    diff_re = (field_re * factor).astype(jnp.bfloat16)
    diff_im = (field_im * factor).astype(jnp.bfloat16)
    back_re = (
        contract("lkm,ma->lka", diff_re, cos_table) - contract("lkm,ma->lka", diff_im, sin_table)
    ).astype(jnp.bfloat16)
    back_im = (
        contract("lkm,ma->lka", diff_im, cos_table) + contract("lkm,ma->lka", diff_re, sin_table)
    ).astype(jnp.bfloat16)
    return (back_re, back_im)


def body_any(spectrum, led_rows, led_cols, images):
    width = images.shape[2]
    slab_rows = spectrum.shape[1]
    columns = spectrum.shape[2]
    slabs = lax.axis_size("slab")
    total_rows = slab_rows * slabs
    position = lax.axis_index("slab")
    cos_table, sin_table = (jnp.asarray(t) for t in host_tables(width))
    own_rows = position * slab_rows + jnp.arange(slab_rows, dtype=jnp.int32)
    col_index = jnp.arange(width, dtype=jnp.int32)

    def take_cols(start):
        return lax.dynamic_slice_in_dim(spectrum, start, width, 2)

    def owner_mask(start):
        return make_pupil(own_rows - start, col_index, width)

    windows = jax.vmap(take_cols)(led_cols)
    masks = jax.vmap(owner_mask)(led_rows)
    win_re = (windows[:, 0] * masks).astype(jnp.bfloat16)
    win_im = (windows[:, 1] * masks).astype(jnp.bfloat16)

    def slice_strip(block, start):
        return take_rows(block, start, width)

    row_re = (
        contract("lgb,bk->lkg", win_re, cos_table) + contract("lgb,bk->lkg", win_im, sin_table)
    ).astype(jnp.bfloat16)
    row_im = (
        contract("lgb,bk->lkg", win_im, cos_table) - contract("lgb,bk->lkg", win_re, sin_table)
    ).astype(jnp.bfloat16)
    col_re, col_im = (
        lax.all_to_all(row_re, "slab", split_axis=1, concat_axis=2, tiled=True),
        lax.all_to_all(row_im, "slab", split_axis=1, concat_axis=2, tiled=True),
    )
    field_in_re = jax.vmap(slice_strip)(col_re, led_rows)
    field_in_im = jax.vmap(slice_strip)(col_im, led_rows)
    back_re, back_im = modulus_step(field_in_re, field_in_im, images, cos_table, sin_table)

    def place_strip(block, start):
        return place_rows(block, start, total_rows, 1)

    full_re = jax.vmap(place_strip)(back_re, led_rows)
    full_im = jax.vmap(place_strip)(back_im, led_rows)
    home_re, home_im = (
        lax.all_to_all(as_sent(full_re), "slab", split_axis=2, concat_axis=1, tiled=True).astype(
            full_re.dtype
        ),
        lax.all_to_all(as_sent(full_im), "slab", split_axis=2, concat_axis=1, tiled=True).astype(
            full_im.dtype
        ),
    )
    upd_re = contract("lkg,kb->lgb", home_re, cos_table) - contract(
        "lkg,kb->lgb", home_im, sin_table
    )
    upd_im = contract("lkg,kb->lgb", home_im, cos_table) + contract(
        "lkg,kb->lgb", home_re, sin_table
    )
    upd_re = upd_re * masks
    upd_im = upd_im * masks

    def add_window(number, gradient):
        start = led_cols[number]
        piece = jnp.stack([upd_re[number], upd_im[number]])
        current = lax.dynamic_slice_in_dim(gradient, start, width, 2)
        return lax.dynamic_update_slice_in_dim(gradient, current + piece, start, 2)

    gradient = lax.fori_loop(
        0, led_rows.shape[0], add_window, jnp.zeros((2, slab_rows, columns), jnp.float32)
    )
    summed = lax.psum_scatter(gradient, "led", scatter_dimension=2, tiled=True)
    share = summed.shape[2]
    own_part = lax.dynamic_slice_in_dim(spectrum, lax.axis_index("led") * share, share, 2)
    return own_part + summed


SLABS = 8
HALF = 4
FIRST, LAST = 0, 7
CROSS = (4, 5, 6, 7)
LATE = (5, 7)
PASSED = {1: 0, 6: 7}
PIECES = 4


class Stream:
    def __init__(self, source, target, sems, blocks):
        self.target = target
        step = source.shape[1] // PIECES
        self.copies = [
            [
                pltpu.make_async_copy(
                    source.at[block, pl.ds(piece * step, step)],
                    target.at[i, pl.ds(piece * step, step)],
                    sems.at[i, piece],
                )
                for piece in range(PIECES)
            ]
            for i, block in enumerate(blocks)
        ]
        for copies in self.copies:
            for copy in copies:
                copy.start()

    def take(self, i):
        for copy in self.copies[i]:
            copy.wait()
        return self.target[i]


def dot(left, right):
    return jnp.dot(left, right, preferred_element_type=jnp.float32)


def window_mask(first_row, row_start, col_start, rows, first_col, cols, width):
    shape = (rows, cols)
    at_row = lax.broadcasted_iota(jnp.int32, shape, 0) + (first_row - row_start)
    at_col = lax.broadcasted_iota(jnp.int32, shape, 1) + (first_col - col_start)
    wraps = at_col < 0
    at_col = jnp.where(wraps, at_col + width, at_col)
    row_term = 2 * at_row + 1 - width
    col_term = 2 * at_col + 1 - width
    return row_term * row_term + col_term * col_term < width * width, wraps


def row_block(window, table):
    both = dot(window, table)
    half = both.shape[0] // 2
    row_re = both[:half, :LANES] + both[half:, LANES:]
    row_im = both[half:, :LANES] - both[:half, LANES:]
    return row_re.astype(jnp.bfloat16), row_im.astype(jnp.bfloat16)


def store_parts(out, values):
    per = out.shape[0] // 2
    rows = out.shape[1]
    for plane, value in enumerate(values):
        for led in range(per):
            out[plane * per + led] = value[led * rows : (led + 1) * rows]


def first_kernel(starts, spectrum_any, table_any, window, *rest):
    outs = rest[: len(CROSS)]
    late, spectrum, sems, table, table_sems = rest[len(CROSS) :]
    position = lax.axis_index("slab")
    leds = starts.shape[0] // 2
    rows = spectrum.shape[1]
    width = window.shape[1]
    chunks = sems.shape[0]
    step = rows // chunks
    fetches = [
        [
            pltpu.make_async_copy(
                spectrum_any.at[plane, pl.ds(i * step, step)],
                spectrum.at[plane, pl.ds(i * step, step)],
                sems.at[i, plane],
            )
            for plane in range(2)
        ]
        for i in range(chunks)
    ]
    for pair in fetches:
        for copy in pair:
            copy.start()
    tables = Stream(
        table_any, table, table_sems, [jnp.bitwise_xor(position, d) for d in CROSS]
    )
    for i in range(chunks):
        for copy in fetches[i]:
            copy.wait()
        here = slice(i * step, (i + 1) * step)
        for led in range(leds):
            inside, wraps = window_mask(
                position * rows + i * step, starts[led], starts[leds + led], step, 0, width, width
            )
            for plane in range(2):
                value = jnp.where(
                    wraps, spectrum[plane, here, width:], spectrum[plane, here, :width]
                )
                at = (plane * leds + led) * rows + i * step
                window[at : at + step, :] = jnp.where(inside, value, 0.0).astype(jnp.bfloat16)
    for i, d in enumerate(CROSS):
        values = row_block(window[...], tables.take(i))
        store_parts(outs[i], values)
        if d in LATE:
            store_parts(late.at[LATE.index(d)], values)


def second_kernel(window, table_any, out, table, sems):
    position = lax.axis_index("slab")
    base = position - jnp.bitwise_and(position, HALF - 1)
    tables = Stream(table_any, table, sems, [base + i for i in range(HALF)])
    for i in range(HALF):
        store_parts(out.at[i], row_block(window[...], tables.take(i)))


def field_kernel(amplitude, table_any, near, *rest):
    far = rest[: len(CROSS)]
    near_out = rest[len(CROSS)]
    far_out = rest[len(CROSS) + 1 : 2 * len(CROSS) + 1]
    field_in, diff, table, sems = rest[2 * len(CROSS) + 1 :]
    position = lax.axis_index("slab")
    _, parts, rows, _ = near.shape
    half = parts // 2 * LANES
    width = field_in.shape[0]
    steps = width // LANES
    group = 4
    tables = Stream(table_any, table, sems, range(steps))
    for i in range(HALF):
        for part in range(parts):
            cols = slice(part * LANES, (part + 1) * LANES)
            field_in[i * rows : (i + 1) * rows, cols] = near[i, part]
    for d, block in zip(CROSS, far):
        source = jnp.bitwise_and(jnp.bitwise_xor(position, d), HALF - 1)
        at = pl.multiple_of(source * rows, rows)
        for part in range(parts):
            cols = slice(part * LANES, (part + 1) * LANES)
            field_in[pl.ds(at, rows), cols] += block[part]
    for first in range(0, steps, group):
        for j in range(first, first + group):
            tables.take(j)
        product = dot(
            table[first : first + group].reshape(group * 2 * LANES, width), field_in[...]
        )
        for j in range(first, first + group):
            both = product[(j - first) * 2 * LANES : (j - first + 1) * 2 * LANES]
            field_re = both[:LANES, :half] + both[LANES:, half:]
            field_im = both[:LANES, half:] - both[LANES:, :half]
            here = pl.ds(j * LANES, LANES)
            factor = (
                amplitude[here, :] * lax.rsqrt(field_re * field_re + field_im * field_im + 0.25)
                - 1.0
            )
            diff[here, :half] = (field_re * factor).astype(jnp.bfloat16)
            diff[here, half:] = (field_im * factor).astype(jnp.bfloat16)
    pieces = rows // LANES
    for i in range(HALF):
        product = dot(
            table[i * pieces : (i + 1) * pieces].reshape(pieces * 2 * LANES, width), diff[...]
        )
        for h in range(pieces):
            both = product[h * 2 * LANES : (h + 1) * 2 * LANES]
            here = pl.ds(h * LANES, LANES)
            back_re = (both[:LANES, :half] - both[LANES:, half:]).astype(jnp.bfloat16)
            back_im = (both[:LANES, half:] + both[LANES:, :half]).astype(jnp.bfloat16)
            for part in range(parts // 2):
                cols = slice(part * LANES, (part + 1) * LANES)
                near_out[i, part, here, :] = back_re[:, cols]
                near_out[i, parts // 2 + part, here, :] = back_im[:, cols]
    for d, out in zip(CROSS, far_out):
        out[...] = near_out[jnp.bitwise_and(jnp.bitwise_xor(position, d), HALF - 1)]


def update_columns(first_step, last_step, starts, table_any, back, out, table, sems, fill=None):
    position = lax.axis_index("slab")
    led_at = lax.axis_index("led")
    core = jnp.bitwise_and(led_at, 1)
    plane_x = jnp.right_shift(led_at, 1)
    leds = starts.shape[0] // 2
    rows = back.shape[0] // (2 * leds)
    width = back.shape[1]
    group = width // LANES // 2
    blocks = [
        (1 - core if n < group else core) * group + n % group for n in range(first_step, last_step)
    ]
    tables = Stream(table_any, table, sems, blocks)
    if fill is not None:
        fill()
    for n in range(first_step, last_step):
        block = blocks[n - first_step]
        both = dot(back[...], tables.take(n - first_step))
        half = leds * rows
        update = (
            both[:half, :LANES] - both[half:, LANES:],
            both[half:, :LANES] + both[:half, LANES:],
        )
        low = [0.0, 0.0]
        high = [0.0, 0.0]
        for led in range(leds):
            inside, wraps = window_mask(
                position * rows, starts[led], starts[leds + led], rows, block * LANES, LANES, width
            )
            for plane in range(2):
                piece = jnp.where(inside, update[plane][led * rows : (led + 1) * rows], 0.0)
                low[plane] += jnp.where(wraps, 0.0, piece)
                high[plane] += jnp.where(wraps, piece, 0.0)
        cols = slice((n - first_step) * LANES, (n - first_step + 1) * LANES)
        for plane in range(2):
            out[1 - plane_x, plane, :, cols] = low[plane].astype(out.dtype)
            out[plane_x, plane, :, cols] = high[plane].astype(out.dtype)


def sent_kernel(starts, table_any, near, *rest):
    far = rest[: len(CROSS)]
    out, back, table, sems = rest[len(CROSS) :]
    position = lax.axis_index("slab")
    base = position - jnp.bitwise_and(position, HALF - 1)
    _, parts, rows, _ = near.shape
    half = back.shape[1] // LANES // 2

    def fill():
        for i in range(HALF):
            at = pl.multiple_of((base + i) * LANES, LANES)
            for part in range(parts):
                back[part * rows : (part + 1) * rows, pl.ds(at, LANES)] = near[i, part]
        for d, block in zip(CROSS, far):
            at = pl.multiple_of(jnp.bitwise_xor(position, d) * LANES, LANES)
            for part in range(parts):
                back[part * rows : (part + 1) * rows, pl.ds(at, LANES)] = block[part]

    update_columns(0, half, starts, table_any, back, out, table, sems, fill)


def kept_kernel(starts, table_any, back, out, table, sems):
    half = back.shape[1] // LANES // 2
    update_columns(half, 2 * half, starts, table_any, back, out, table, sems)


def local_call(kernel, out_shape, spaces, scratch, flops, moved, name):
    return pl.pallas_call(
        kernel,
        out_shape=out_shape,
        in_specs=[pl.BlockSpec(memory_space=space) for space in spaces],
        out_specs=jax.tree.map(lambda _: pl.BlockSpec(memory_space=pltpu.VMEM), out_shape),
        scratch_shapes=scratch,
        compiler_params=pltpu.CompilerParams(vmem_limit_bytes=48 * 2**20),
        cost_estimate=pl.CostEstimate(flops=flops, bytes_accessed=moved, transcendentals=0),
        name=name,
    )


def table_scratch(table, count):
    return [
        pltpu.VMEM((count,) + table.shape[1:], table.dtype),
        pltpu.SemaphoreType.DMA((count, PIECES)),
    ]


def body_slabs(spectrum, led_rows, led_cols, images):
    leds, block, width = images.shape
    rows = spectrum.shape[1]
    led_at = lax.axis_index("led")
    bf16 = jnp.bfloat16
    vmem, smem = pltpu.VMEM, pltpu.SMEM
    cos_table, sin_table = host_tables(width)
    steps = width // LANES
    by_col = np.stack(
        [
            np.concatenate([t[:, j * LANES : (j + 1) * LANES] for t in (cos_table, sin_table)], 1)
            for j in range(steps)
        ]
    )
    by_row = jnp.asarray(np.ascontiguousarray(by_col.transpose(0, 2, 1)))
    by_col = jnp.asarray(by_col)
    parts = 2 * leds
    sent_block = jax.ShapeDtypeStruct((parts, rows, LANES), bf16)
    near_block = jax.ShapeDtypeStruct((HALF,) + sent_block.shape, bf16)
    flops = 8 * leds * rows * width * width

    starts = jnp.concatenate([led_rows, led_cols]).astype(jnp.int32)
    window, *outs, late = local_call(
        first_kernel,
        [
            jax.ShapeDtypeStruct((parts * rows, width), bf16),
            *[sent_block] * len(CROSS),
            jax.ShapeDtypeStruct((len(LATE),) + sent_block.shape, bf16),
        ],
        [smem, pl.ANY, pl.ANY],
        [pltpu.VMEM(spectrum.shape, jnp.float32), pltpu.SemaphoreType.DMA((8, 2))]
        + table_scratch(by_col, len(CROSS)),
        flops // 2,
        8 * 2**20,
        "windows_and_far_rows",
    )(starts, spectrum, by_col)
    outs = dict(zip(CROSS, outs))
    passed = lax.ppermute(late, "slab", list(PASSED.items()))
    windowed = range(FIRST + 1, LAST)
    columns = {}
    for d in CROSS:
        if d not in LATE:
            columns[d] = lax.ppermute(outs[d], "slab", [(s, s ^ d) for s in windowed])
    near_rows = local_call(
        second_kernel,
        near_block,
        [vmem, pl.ANY],
        table_scratch(by_col, HALF),
        flops // 2,
        5 * 2**20,
        "near_rows",
    )(window, by_col)
    passed, near_rows = lax.optimization_barrier((passed, near_rows))
    for i, d in enumerate(LATE):
        pairs = [(PASSED.get(s, s), s ^ d) for s in windowed]
        columns[d] = lax.ppermute(outs[d] + passed[i], "slab", pairs)
    halves = [list(range(HALF)), list(range(HALF, SLABS))]

    def within_half(blocks):
        return lax.all_to_all(
            blocks, "slab", split_axis=0, concat_axis=0, axis_index_groups=halves, tiled=True
        )

    near_columns = within_half(near_rows)
    amplitude = jnp.sqrt(images).transpose(2, 0, 1).reshape(width, leds * block)
    near_strips, *far_strips = local_call(
        field_kernel,
        [near_block] + [sent_block] * len(CROSS),
        [vmem, pl.ANY, vmem] + [vmem] * len(CROSS),
        [pltpu.VMEM((width, parts * block), bf16)] * 2 + table_scratch(by_row, steps),
        16 * leds * block * width * width,
        12 * 2**20,
        "modulus_step",
    )(amplitude, by_row, near_columns, *[columns[d] for d in CROSS])
    far_home = [
        lax.ppermute(sent, "slab", [(s, s ^ d) for s in range(SLABS) if s ^ d in windowed])
        for d, sent in zip(CROSS, far_strips)
    ]
    near_home = within_half(near_strips)
    share = width // 2
    sent, back = local_call(
        sent_kernel,
        [
            jax.ShapeDtypeStruct((2, 2, rows, share), bf16),
            jax.ShapeDtypeStruct((parts * rows, width), bf16),
        ],
        [smem, pl.ANY, vmem] + [vmem] * len(CROSS),
        table_scratch(by_col, steps // 2),
        flops // 2,
        8 * 2**20,
        "update_sent",
    )(starts, by_col, near_home, *far_home)
    got = lax.ppermute(sent, "led", [(0, 1), (1, 0), (2, 3), (3, 2)])
    kept = local_call(
        kept_kernel,
        jax.ShapeDtypeStruct((2, 2, rows, share), jnp.float32),
        [smem, pl.ANY, vmem],
        table_scratch(by_col, steps // 2),
        flops // 2,
        8 * 2**20,
        "update_kept",
    )(starts, by_col, back)
    over = (kept[0] + got[0].astype(jnp.float32)).astype(bf16)
    got_x = lax.ppermute(over, "led", [(0, 2), (2, 0), (1, 3), (3, 1)])
    own_part = lax.dynamic_slice_in_dim(spectrum, led_at * share, share, 2)
    base = own_part + (kept[1] + got[1].astype(jnp.float32))
    base, got_x = lax.optimization_barrier((base, got_x))
    return base + got_x.astype(jnp.float32)


def solution(mesh):
    placed = (P(None, "slab", None), P("led"), P("led"), P("led", "slab", None))
    fits = mesh.shape["slab"] == 8 and mesh.shape["led"] == 4

    def body(spectrum, led_rows, led_cols, images):
        shapes = (spectrum.shape, images.shape)
        if fits and shapes == ((2, 256, 2048), (2, 128, 1024)):
            return body_slabs(spectrum, led_rows, led_cols, images)
        return body_any(spectrum, led_rows, led_cols, images)

    return jax.shard_map(
        body, mesh=mesh, in_specs=placed, out_specs=P(None, "slab", "led"), check_vma=False
    )
```

```python
import functools

import jax
import jax.numpy as jnp
import numpy as np
from jax import lax
from jax.experimental import pallas as pl
from jax.experimental.pallas import tpu as pltpu
from jax.sharding import PartitionSpec as P

LANES = 128


def as_sent(value):
    return jax.tree.map(lambda a: a.astype(jnp.bfloat16) if a.dtype == jnp.float32 else a, value)


def host_tables(width):
    index = np.arange(width, dtype=np.int64)
    angle_index = (index[:, None] * index[None, :] % width).astype(np.float32)
    angle = angle_index * np.float32(2.0 * 3.141592653589793 / width)
    scale = np.float32(1.0) / np.sqrt(np.float32(width))
    return (
        (np.cos(angle) * scale).astype(jnp.bfloat16),
        (np.sin(angle) * scale).astype(jnp.bfloat16),
    )


def make_pupil(row_index, col_index, width):
    row_term = (2 * row_index + 1 - width) * (2 * row_index + 1 - width)
    col_term = (2 * col_index + 1 - width) * (2 * col_index + 1 - width)
    return (row_term[:, None] + col_term[None, :] < width * width).astype(jnp.float32)


def contract(form, left, right):
    return jnp.einsum(form, left, right, preferred_element_type=jnp.float32)


def take_rows(strip, start, width):
    return lax.dynamic_slice_in_dim(strip, start, width, 1)


def place_rows(block, start, total, axis_dim):
    shape = list(block.shape)
    shape[axis_dim] = total
    holder = jnp.zeros(tuple(shape), block.dtype)
    return lax.dynamic_update_slice_in_dim(holder, block, start, axis_dim)


def modulus_step(field_in_re, field_in_im, image, cos_table, sin_table):
    field_re = contract("lka,am->lkm", field_in_re, cos_table) + contract(
        "lka,am->lkm", field_in_im, sin_table
    )
    field_im = contract("lka,am->lkm", field_in_im, cos_table) - contract(
        "lka,am->lkm", field_in_re, sin_table
    )
    factor = jnp.sqrt(image) / jnp.sqrt(field_re * field_re + field_im * field_im + 0.25) - 1.0
    diff_re = (field_re * factor).astype(jnp.bfloat16)
    diff_im = (field_im * factor).astype(jnp.bfloat16)
    back_re = (
        contract("lkm,ma->lka", diff_re, cos_table) - contract("lkm,ma->lka", diff_im, sin_table)
    ).astype(jnp.bfloat16)
    back_im = (
        contract("lkm,ma->lka", diff_im, cos_table) + contract("lkm,ma->lka", diff_re, sin_table)
    ).astype(jnp.bfloat16)
    return (back_re, back_im)


def body_any(spectrum, led_rows, led_cols, images):
    width = images.shape[2]
    slab_rows = spectrum.shape[1]
    columns = spectrum.shape[2]
    slabs = lax.axis_size("slab")
    total_rows = slab_rows * slabs
    position = lax.axis_index("slab")
    cos_table, sin_table = (jnp.asarray(t) for t in host_tables(width))
    own_rows = position * slab_rows + jnp.arange(slab_rows, dtype=jnp.int32)
    col_index = jnp.arange(width, dtype=jnp.int32)

    def take_cols(start):
        return lax.dynamic_slice_in_dim(spectrum, start, width, 2)

    def owner_mask(start):
        return make_pupil(own_rows - start, col_index, width)

    windows = jax.vmap(take_cols)(led_cols)
    masks = jax.vmap(owner_mask)(led_rows)
    win_re = (windows[:, 0] * masks).astype(jnp.bfloat16)
    win_im = (windows[:, 1] * masks).astype(jnp.bfloat16)

    def slice_strip(block, start):
        return take_rows(block, start, width)

    row_re = (
        contract("lgb,bk->lkg", win_re, cos_table) + contract("lgb,bk->lkg", win_im, sin_table)
    ).astype(jnp.bfloat16)
    row_im = (
        contract("lgb,bk->lkg", win_im, cos_table) - contract("lgb,bk->lkg", win_re, sin_table)
    ).astype(jnp.bfloat16)
    col_re, col_im = (
        lax.all_to_all(row_re, "slab", split_axis=1, concat_axis=2, tiled=True),
        lax.all_to_all(row_im, "slab", split_axis=1, concat_axis=2, tiled=True),
    )
    field_in_re = jax.vmap(slice_strip)(col_re, led_rows)
    field_in_im = jax.vmap(slice_strip)(col_im, led_rows)
    back_re, back_im = modulus_step(field_in_re, field_in_im, images, cos_table, sin_table)

    def place_strip(block, start):
        return place_rows(block, start, total_rows, 1)

    full_re = jax.vmap(place_strip)(back_re, led_rows)
    full_im = jax.vmap(place_strip)(back_im, led_rows)
    home_re, home_im = (
        lax.all_to_all(as_sent(full_re), "slab", split_axis=2, concat_axis=1, tiled=True).astype(
            full_re.dtype
        ),
        lax.all_to_all(as_sent(full_im), "slab", split_axis=2, concat_axis=1, tiled=True).astype(
            full_im.dtype
        ),
    )
    upd_re = contract("lkg,kb->lgb", home_re, cos_table) - contract(
        "lkg,kb->lgb", home_im, sin_table
    )
    upd_im = contract("lkg,kb->lgb", home_im, cos_table) + contract(
        "lkg,kb->lgb", home_re, sin_table
    )
    upd_re = upd_re * masks
    upd_im = upd_im * masks

    def add_window(number, gradient):
        start = led_cols[number]
        piece = jnp.stack([upd_re[number], upd_im[number]])
        current = lax.dynamic_slice_in_dim(gradient, start, width, 2)
        return lax.dynamic_update_slice_in_dim(gradient, current + piece, start, 2)

    gradient = lax.fori_loop(
        0, led_rows.shape[0], add_window, jnp.zeros((2, slab_rows, columns), jnp.float32)
    )
    summed = lax.psum_scatter(gradient, "led", scatter_dimension=2, tiled=True)
    share = summed.shape[2]
    own_part = lax.dynamic_slice_in_dim(spectrum, lax.axis_index("led") * share, share, 2)
    return own_part + summed


SLABS = 8
HALF = 4
FIRST, LAST = 0, 7
CROSS = (4, 5, 6, 7)
PASSED = {1: 0, 6: 7}
INNER = (2, 3, 4, 5)


def dot(left, right):
    return jnp.dot(left, right, preferred_element_type=jnp.float32)


def window_mask(first_row, row_start, col_start, rows, first_col, cols, width):
    shape = (rows, cols)
    at_row = lax.broadcasted_iota(jnp.int32, shape, 0) + (first_row - row_start)
    at_col = lax.broadcasted_iota(jnp.int32, shape, 1) + (first_col - col_start)
    wraps = at_col < 0
    at_col = jnp.where(wraps, at_col + width, at_col)
    row_term = 2 * at_row + 1 - width
    col_term = 2 * at_col + 1 - width
    return row_term * row_term + col_term * col_term < width * width, wraps


def row_block(window, table):
    both = dot(window, table)
    half = both.shape[0] // 2
    row_re = both[:half, :LANES] + both[half:, LANES:]
    row_im = both[half:, :LANES] - both[:half, LANES:]
    return row_re.astype(jnp.bfloat16), row_im.astype(jnp.bfloat16)


def store_parts(out, values):
    per = out.shape[0] // 2
    rows = out.shape[1]
    for plane, value in enumerate(values):
        for led in range(per):
            out[plane * per + led] = value[led * rows : (led + 1) * rows]


def is_one_of(position, slabs):
    return functools.reduce(jnp.logical_or, [position == slab for slab in slabs])


def window_kernel(starts, spectrum, window):
    position = lax.axis_index("slab")
    leds = starts.shape[0] // 2
    rows = spectrum.shape[1]
    width = window.shape[1]
    for led in range(leds):
        inside, wraps = window_mask(
            position * rows, starts[led], starts[leds + led], rows, 0, width, width
        )
        for plane in range(2):
            value = jnp.where(wraps, spectrum[plane, :, width:], spectrum[plane, :, :width])
            at = (plane * leds + led) * rows
            window[at : at + rows, :] = jnp.where(inside, value, 0.0).astype(jnp.bfloat16)


def far_kernel(window, table, *outs):
    position = lax.axis_index("slab")
    hands_over = is_one_of(position, PASSED)
    classes = (jnp.where(hands_over, 5, 6), 7, 2, 4, jnp.where(hands_over, 6, 5))
    for out, d in zip(outs, classes):
        store_parts(out, row_block(window[...], table[jnp.bitwise_xor(position, d)]))


def near_kernel(window, table, *outs):
    position = lax.axis_index("slab")
    for out, d in zip(outs, (0, 1, 3)):
        store_parts(out, row_block(window[...], table[jnp.bitwise_xor(position, d)]))


def field_kernel(amplitude, table, *rest):
    near, far = rest[:HALF], rest[HALF : HALF + 5]
    outs = rest[HALF + 5 : 2 * HALF + 5]
    field_in, diff, strips = rest[2 * HALF + 5 :]
    position = lax.axis_index("slab")
    parts, rows, _ = near[0].shape
    half = parts // 2 * LANES
    width = field_in.shape[0]
    steps = width // LANES
    group = 4
    for d, block in enumerate(near):
        at = pl.multiple_of(jnp.bitwise_and(jnp.bitwise_xor(position, d), HALF - 1) * rows, rows)
        for part in range(parts):
            cols = slice(part * LANES, (part + 1) * LANES)
            field_in[pl.ds(at, rows), cols] = block[part]

    def add(block, origin):
        at = pl.multiple_of(jnp.bitwise_and(origin, HALF - 1) * rows, rows)
        for part in range(parts):
            cols = slice(part * LANES, (part + 1) * LANES)
            field_in[pl.ds(at, rows), cols] += block[part]

    passes = is_one_of(position, PASSED.values())
    hands_over = is_one_of(position, PASSED)
    ends = is_one_of(position, [to ^ 4 for to in PASSED.values()])

    @pl.when(is_one_of(position, INNER))
    def _():
        add(far[0], jnp.bitwise_xor(position, 6))
        add(far[1], jnp.bitwise_xor(position, 7))
        add(far[2], jnp.bitwise_xor(position, jnp.where(ends, 5, 4)))

    @pl.when(jnp.logical_or(passes, hands_over))
    def _():
        add(far[2], jnp.bitwise_xor(position, 4))
        add(far[3], jnp.bitwise_xor(position, jnp.where(hands_over, 7, 6)))
        add(far[4], jnp.bitwise_xor(position, 5))

    for first in range(0, steps, group):
        product = dot(
            table[first : first + group].reshape(group * 2 * LANES, width), field_in[...]
        )
        for j in range(first, first + group):
            both = product[(j - first) * 2 * LANES : (j - first + 1) * 2 * LANES]
            field_re = both[:LANES, :half] + both[LANES:, half:]
            field_im = both[:LANES, half:] - both[LANES:, :half]
            here = pl.ds(j * LANES, LANES)
            factor = (
                amplitude[here, :] * lax.rsqrt(field_re * field_re + field_im * field_im + 0.25)
                - 1.0
            )
            diff[here, :half] = (field_re * factor).astype(jnp.bfloat16)
            diff[here, half:] = (field_im * factor).astype(jnp.bfloat16)
    pieces = rows // LANES
    for i in range(HALF):
        product = dot(
            table[i * pieces : (i + 1) * pieces].reshape(pieces * 2 * LANES, width), diff[...]
        )
        for h in range(pieces):
            both = product[h * 2 * LANES : (h + 1) * 2 * LANES]
            here = pl.ds(h * LANES, LANES)
            back_re = (both[:LANES, :half] - both[LANES:, half:]).astype(jnp.bfloat16)
            back_im = (both[:LANES, half:] + both[LANES:, :half]).astype(jnp.bfloat16)
            for part in range(parts // 2):
                cols = slice(part * LANES, (part + 1) * LANES)
                strips[i, part, here, :] = back_re[:, cols]
                strips[i, parts // 2 + part, here, :] = back_im[:, cols]
    for d, out in enumerate(outs):
        out[...] = strips[jnp.bitwise_and(jnp.bitwise_xor(position, d), HALF - 1)]


def update_columns(first_step, last_step, starts, table, back, out):
    position = lax.axis_index("slab")
    led_at = lax.axis_index("led")
    core = jnp.bitwise_and(led_at, 1)
    plane_x = jnp.right_shift(led_at, 1)
    leds = starts.shape[0] // 2
    rows = back.shape[0] // (2 * leds)
    width = back.shape[1]
    group = width // LANES // 2
    blocks = [
        (1 - core if n < group else core) * group + n % group for n in range(first_step, last_step)
    ]
    for n in range(first_step, last_step):
        block = blocks[n - first_step]
        both = dot(back[...], table[block])
        half = leds * rows
        update = (
            both[:half, :LANES] - both[half:, LANES:],
            both[half:, :LANES] + both[:half, LANES:],
        )
        low = [0.0, 0.0]
        high = [0.0, 0.0]
        for led in range(leds):
            inside, wraps = window_mask(
                position * rows, starts[led], starts[leds + led], rows, block * LANES, LANES, width
            )
            for plane in range(2):
                piece = jnp.where(inside, update[plane][led * rows : (led + 1) * rows], 0.0)
                low[plane] += jnp.where(wraps, 0.0, piece)
                high[plane] += jnp.where(wraps, piece, 0.0)
        cols = slice((n - first_step) * LANES, (n - first_step + 1) * LANES)
        for plane in range(2):
            out[1 - plane_x, plane, :, cols] = low[plane].astype(out.dtype)
            out[plane_x, plane, :, cols] = high[plane].astype(out.dtype)


def sent_kernel(starts, table, *rest):
    blocks = rest[:SLABS]
    out, back = rest[SLABS:]
    position = lax.axis_index("slab")
    parts, rows, _ = blocks[0].shape
    half = back.shape[1] // LANES // 2
    for d, block in enumerate(blocks):
        at = pl.multiple_of(jnp.bitwise_xor(position, d) * LANES, LANES)
        for part in range(parts):
            back[part * rows : (part + 1) * rows, pl.ds(at, LANES)] = block[part]
    update_columns(0, half, starts, table, back, out)


def kept_kernel(starts, table, back, out):
    half = back.shape[1] // LANES // 2
    update_columns(half, 2 * half, starts, table, back, out)


def local_call(kernel, out_shape, spaces, scratch, flops, moved, name):
    return pl.pallas_call(
        kernel,
        out_shape=out_shape,
        in_specs=[pl.BlockSpec(memory_space=space) for space in spaces],
        out_specs=jax.tree.map(lambda _: pl.BlockSpec(memory_space=pltpu.VMEM), out_shape),
        scratch_shapes=scratch,
        compiler_params=pltpu.CompilerParams(vmem_limit_bytes=32 * 2**20),
        cost_estimate=pl.CostEstimate(flops=flops, bytes_accessed=moved, transcendentals=0),
        name=name,
    )


def body_slabs(spectrum, led_rows, led_cols, images):
    leds, block, width = images.shape
    rows = spectrum.shape[1]
    led_at = lax.axis_index("led")
    bf16 = jnp.bfloat16
    vmem, smem = pltpu.VMEM, pltpu.SMEM
    cos_table, sin_table = host_tables(width)
    steps = width // LANES
    by_col = np.stack(
        [
            np.concatenate([t[:, j * LANES : (j + 1) * LANES] for t in (cos_table, sin_table)], 1)
            for j in range(steps)
        ]
    )
    by_row = jnp.asarray(np.ascontiguousarray(by_col.transpose(0, 2, 1)))
    by_col = jnp.asarray(by_col)
    parts = 2 * leds
    sent_block = jax.ShapeDtypeStruct((parts, rows, LANES), bf16)
    flops = 8 * leds * rows * width * width

    starts = jnp.concatenate([led_rows, led_cols]).astype(jnp.int32)
    window = local_call(
        window_kernel,
        jax.ShapeDtypeStruct((parts * rows, width), bf16),
        [smem, vmem],
        [],
        0,
        6 * 2**20,
        "windows",
    )(starts, spectrum)
    first_a, first_b, near_2, second_a, second_b = local_call(
        far_kernel,
        [sent_block] * 5,
        [vmem, vmem],
        [],
        flops * 5 // 8,
        5 * 2**20,
        "far_rows",
    )(window, by_col)

    def permute(sent, pairs):
        return lax.ppermute(sent, "slab", pairs)

    handed = list(PASSED.items())
    windowed = range(FIRST + 1, LAST)
    got_a = permute(first_a, [(s, s ^ 6) for s in INNER] + handed)
    got_b = permute(first_b, [(s, s ^ 7) for s in INNER] + handed)
    near_2 = permute(near_2, [(s, s ^ 2) for s in windowed])
    near_0, near_1, near_3 = local_call(
        near_kernel,
        [sent_block] * 3,
        [vmem, vmem],
        [],
        flops * 3 // 8,
        5 * 2**20,
        "near_rows",
    )(window, by_col)
    got_a, got_b, second_a, second_b, near_1, near_2, near_3 = lax.optimization_barrier(
        (got_a, got_b, second_a, second_b, near_1, near_2, near_3)
    )
    passes = is_one_of(lax.axis_index("slab"), PASSED.values())
    outer_pairs = [(s, s ^ 6) for s in range(SLABS) if s not in INNER]
    far_columns = [
        got_a,
        got_b,
        permute(jnp.where(passes, got_a, second_a), [(s, s ^ 4) for s in range(SLABS)]),
        permute(jnp.where(passes, got_b, second_b), outer_pairs),
        permute(second_b, [(s, s ^ 5) for s in INNER]),
    ]
    near_1 = permute(near_1, [(s, s ^ 1) for s in windowed])
    near_3 = permute(near_3, [(s, s ^ 3) for s in windowed])
    near_columns = [near_0, near_1, near_2, near_3]
    amplitude = jnp.sqrt(images).transpose(2, 0, 1).reshape(width, leds * block)
    strips = local_call(
        field_kernel,
        [sent_block] * HALF,
        [vmem] * 11,
        [pltpu.VMEM((width, parts * block), bf16)] * 2
        + [pltpu.VMEM((HALF,) + sent_block.shape, bf16)],
        16 * leds * block * width * width,
        12 * 2**20,
        "modulus_step",
    )(amplitude, by_row, *near_columns, *far_columns)

    def send_home(sent, d):
        return permute(sent, [(s, s ^ d) for s in range(SLABS) if FIRST < s ^ d < LAST])

    far_home = [send_home(strips[d % HALF], d) for d in CROSS]
    far_home[0], *late_strips = lax.optimization_barrier((far_home[0], *strips[1:]))
    near_home = [send_home(sent, d) for d, sent in enumerate(late_strips, 1)]
    home = [strips[0], *near_home, *far_home]
    share = width // 2
    sent, back = local_call(
        sent_kernel,
        [
            jax.ShapeDtypeStruct((2, 2, rows, share), bf16),
            jax.ShapeDtypeStruct((parts * rows, width), bf16),
        ],
        [smem] + [vmem] * (1 + SLABS),
        [],
        flops // 2,
        8 * 2**20,
        "update_sent",
    )(starts, by_col, *home)
    got = lax.ppermute(sent, "led", [(0, 1), (1, 0), (2, 3), (3, 2)])
    kept = local_call(
        kept_kernel,
        jax.ShapeDtypeStruct((2, 2, rows, share), jnp.float32),
        [smem, vmem, vmem],
        [],
        flops // 2,
        8 * 2**20,
        "update_kept",
    )(starts, by_col, back)
    over = (kept[0] + got[0].astype(jnp.float32)).astype(bf16)
    got_x = lax.ppermute(over, "led", [(0, 2), (2, 0), (1, 3), (3, 1)])
    own_part = lax.dynamic_slice_in_dim(spectrum, led_at * share, share, 2)
    base = own_part + (kept[1] + got[1].astype(jnp.float32))
    base, got_x = lax.optimization_barrier((base, got_x))
    return base + got_x.astype(jnp.float32)


def solution(mesh):
    placed = (P(None, "slab", None), P("led"), P("led"), P("led", "slab", None))
    fits = mesh.shape["slab"] == 8 and mesh.shape["led"] == 4

    def body(spectrum, led_rows, led_cols, images):
        shapes = (spectrum.shape, images.shape)
        if fits and shapes == ((2, 256, 2048), (2, 128, 1024)):
            return body_slabs(spectrum, led_rows, led_cols, images)
        return body_any(spectrum, led_rows, led_cols, images)

    return jax.shard_map(
        body, mesh=mesh, in_specs=placed, out_specs=P(None, "slab", "led"), check_vma=False
    )
```

```python
import functools

import jax
import jax.numpy as jnp
import numpy as np
from jax import lax
from jax.experimental import pallas as pl
from jax.experimental.pallas import tpu as pltpu
from jax.sharding import PartitionSpec as P

LANES = 128


def as_sent(value):
    return jax.tree.map(lambda a: a.astype(jnp.bfloat16) if a.dtype == jnp.float32 else a, value)


def host_tables(width):
    index = np.arange(width, dtype=np.int64)
    angle_index = (index[:, None] * index[None, :] % width).astype(np.float32)
    angle = angle_index * np.float32(2.0 * 3.141592653589793 / width)
    scale = np.float32(1.0) / np.sqrt(np.float32(width))
    return (
        (np.cos(angle) * scale).astype(jnp.bfloat16),
        (np.sin(angle) * scale).astype(jnp.bfloat16),
    )


def make_pupil(row_index, col_index, width):
    row_term = (2 * row_index + 1 - width) * (2 * row_index + 1 - width)
    col_term = (2 * col_index + 1 - width) * (2 * col_index + 1 - width)
    return (row_term[:, None] + col_term[None, :] < width * width).astype(jnp.float32)


def contract(form, left, right):
    return jnp.einsum(form, left, right, preferred_element_type=jnp.float32)


def take_rows(strip, start, width):
    return lax.dynamic_slice_in_dim(strip, start, width, 1)


def place_rows(block, start, total, axis_dim):
    shape = list(block.shape)
    shape[axis_dim] = total
    holder = jnp.zeros(tuple(shape), block.dtype)
    return lax.dynamic_update_slice_in_dim(holder, block, start, axis_dim)


def modulus_step(field_in_re, field_in_im, image, cos_table, sin_table):
    field_re = contract("lka,am->lkm", field_in_re, cos_table) + contract(
        "lka,am->lkm", field_in_im, sin_table
    )
    field_im = contract("lka,am->lkm", field_in_im, cos_table) - contract(
        "lka,am->lkm", field_in_re, sin_table
    )
    factor = jnp.sqrt(image) / jnp.sqrt(field_re * field_re + field_im * field_im + 0.25) - 1.0
    diff_re = (field_re * factor).astype(jnp.bfloat16)
    diff_im = (field_im * factor).astype(jnp.bfloat16)
    back_re = (
        contract("lkm,ma->lka", diff_re, cos_table) - contract("lkm,ma->lka", diff_im, sin_table)
    ).astype(jnp.bfloat16)
    back_im = (
        contract("lkm,ma->lka", diff_im, cos_table) + contract("lkm,ma->lka", diff_re, sin_table)
    ).astype(jnp.bfloat16)
    return (back_re, back_im)


def body_any(spectrum, led_rows, led_cols, images):
    width = images.shape[2]
    slab_rows = spectrum.shape[1]
    columns = spectrum.shape[2]
    slabs = lax.axis_size("slab")
    total_rows = slab_rows * slabs
    position = lax.axis_index("slab")
    cos_table, sin_table = (jnp.asarray(t) for t in host_tables(width))
    own_rows = position * slab_rows + jnp.arange(slab_rows, dtype=jnp.int32)
    col_index = jnp.arange(width, dtype=jnp.int32)

    def take_cols(start):
        return lax.dynamic_slice_in_dim(spectrum, start, width, 2)

    def owner_mask(start):
        return make_pupil(own_rows - start, col_index, width)

    windows = jax.vmap(take_cols)(led_cols)
    masks = jax.vmap(owner_mask)(led_rows)
    win_re = (windows[:, 0] * masks).astype(jnp.bfloat16)
    win_im = (windows[:, 1] * masks).astype(jnp.bfloat16)

    def slice_strip(block, start):
        return take_rows(block, start, width)

    row_re = (
        contract("lgb,bk->lkg", win_re, cos_table) + contract("lgb,bk->lkg", win_im, sin_table)
    ).astype(jnp.bfloat16)
    row_im = (
        contract("lgb,bk->lkg", win_im, cos_table) - contract("lgb,bk->lkg", win_re, sin_table)
    ).astype(jnp.bfloat16)
    col_re, col_im = (
        lax.all_to_all(row_re, "slab", split_axis=1, concat_axis=2, tiled=True),
        lax.all_to_all(row_im, "slab", split_axis=1, concat_axis=2, tiled=True),
    )
    field_in_re = jax.vmap(slice_strip)(col_re, led_rows)
    field_in_im = jax.vmap(slice_strip)(col_im, led_rows)
    back_re, back_im = modulus_step(field_in_re, field_in_im, images, cos_table, sin_table)

    def place_strip(block, start):
        return place_rows(block, start, total_rows, 1)

    full_re = jax.vmap(place_strip)(back_re, led_rows)
    full_im = jax.vmap(place_strip)(back_im, led_rows)
    home_re, home_im = (
        lax.all_to_all(as_sent(full_re), "slab", split_axis=2, concat_axis=1, tiled=True).astype(
            full_re.dtype
        ),
        lax.all_to_all(as_sent(full_im), "slab", split_axis=2, concat_axis=1, tiled=True).astype(
            full_im.dtype
        ),
    )
    upd_re = contract("lkg,kb->lgb", home_re, cos_table) - contract(
        "lkg,kb->lgb", home_im, sin_table
    )
    upd_im = contract("lkg,kb->lgb", home_im, cos_table) + contract(
        "lkg,kb->lgb", home_re, sin_table
    )
    upd_re = upd_re * masks
    upd_im = upd_im * masks

    def add_window(number, gradient):
        start = led_cols[number]
        piece = jnp.stack([upd_re[number], upd_im[number]])
        current = lax.dynamic_slice_in_dim(gradient, start, width, 2)
        return lax.dynamic_update_slice_in_dim(gradient, current + piece, start, 2)

    gradient = lax.fori_loop(
        0, led_rows.shape[0], add_window, jnp.zeros((2, slab_rows, columns), jnp.float32)
    )
    summed = lax.psum_scatter(gradient, "led", scatter_dimension=2, tiled=True)
    share = summed.shape[2]
    own_part = lax.dynamic_slice_in_dim(spectrum, lax.axis_index("led") * share, share, 2)
    return own_part + summed


SLABS = 8
HALF = 4
FIRST, LAST = 0, 7
CROSS = (4, 5, 6, 7)
PASSED = {1: 0, 6: 7}
INNER = (2, 3, 4, 5)


def dot(left, right):
    return jnp.dot(left, right, preferred_element_type=jnp.float32)


def window_mask(first_row, row_start, col_start, rows, first_col, cols, width):
    shape = (rows, cols)
    at_row = lax.broadcasted_iota(jnp.int32, shape, 0) + (first_row - row_start)
    at_col = lax.broadcasted_iota(jnp.int32, shape, 1) + (first_col - col_start)
    wraps = at_col < 0
    at_col = jnp.where(wraps, at_col + width, at_col)
    row_term = 2 * at_row + 1 - width
    col_term = 2 * at_col + 1 - width
    return row_term * row_term + col_term * col_term < width * width, wraps


def dot_t(left, right):
    return lax.dot_general(
        left, right, (((1,), (1,)), ((), ())), preferred_element_type=jnp.float32
    )


def row_block(window, table):
    both = dot_t(window, table)
    half = both.shape[0] // 2
    row_re = both[:half, :LANES] + both[half:, LANES:]
    row_im = both[half:, :LANES] - both[:half, LANES:]
    return row_re.astype(jnp.bfloat16), row_im.astype(jnp.bfloat16)


def store_parts(out, values):
    per = out.shape[0] // 2
    rows = out.shape[1]
    for plane, value in enumerate(values):
        for led in range(per):
            out[plane * per + led] = value[led * rows : (led + 1) * rows]


def is_one_of(position, slabs):
    return functools.reduce(jnp.logical_or, [position == slab for slab in slabs])


def window_kernel(starts, spectrum, window):
    position = lax.axis_index("slab")
    leds = starts.shape[0] // 2
    rows = spectrum.shape[1]
    width = window.shape[1]
    for led in range(leds):
        inside, wraps = window_mask(
            position * rows, starts[led], starts[leds + led], rows, 0, width, width
        )
        for plane in range(2):
            value = jnp.where(wraps, spectrum[plane, :, width:], spectrum[plane, :, :width])
            at = (plane * leds + led) * rows
            window[at : at + rows, :] = jnp.where(inside, value, 0.0).astype(jnp.bfloat16)


def classes_of(position):
    hands_over = is_one_of(position, PASSED)
    return (jnp.where(hands_over, 5, 6), 7, 2, 4, jnp.where(hands_over, 6, 5), 0, 1, 3)


def rows_kernel(which, window, table, *outs):
    position = lax.axis_index("slab")
    for out, d in zip(outs, classes_of(position)[which]):
        store_parts(out, row_block(window[...], table[jnp.bitwise_xor(position, d)]))


def field_kernel(amplitude, table, *rest):
    near, far = rest[:HALF], rest[HALF : HALF + 5]
    outs = rest[HALF + 5 : 2 * HALF + 5]
    field_in, diff, strips = rest[2 * HALF + 5 :]
    position = lax.axis_index("slab")
    parts, rows, _ = near[0].shape
    half = parts // 2 * LANES
    width = field_in.shape[0]
    steps = width // LANES
    group = 4
    for d, block in enumerate(near):
        at = pl.multiple_of(jnp.bitwise_and(jnp.bitwise_xor(position, d), HALF - 1) * rows, rows)
        for part in range(parts):
            cols = slice(part * LANES, (part + 1) * LANES)
            field_in[pl.ds(at, rows), cols] = block[part]

    def add(block, origin):
        at = pl.multiple_of(jnp.bitwise_and(origin, HALF - 1) * rows, rows)
        for part in range(parts):
            cols = slice(part * LANES, (part + 1) * LANES)
            field_in[pl.ds(at, rows), cols] += block[part]

    passes = is_one_of(position, PASSED.values())
    hands_over = is_one_of(position, PASSED)
    ends = is_one_of(position, [to ^ 4 for to in PASSED.values()])

    @pl.when(is_one_of(position, INNER))
    def _():
        add(far[0], jnp.bitwise_xor(position, 6))
        add(far[1], jnp.bitwise_xor(position, 7))
        add(far[2], jnp.bitwise_xor(position, jnp.where(ends, 5, 4)))

    @pl.when(jnp.logical_or(passes, hands_over))
    def _():
        add(far[2], jnp.bitwise_xor(position, 4))
        add(far[3], jnp.bitwise_xor(position, jnp.where(hands_over, 7, 6)))
        add(far[4], jnp.bitwise_xor(position, 5))

    for first in range(0, steps, group):
        product = dot(
            table[first : first + group].reshape(group * 2 * LANES, width), field_in[...]
        )
        for j in range(first, first + group):
            both = product[(j - first) * 2 * LANES : (j - first + 1) * 2 * LANES]
            field_re = both[:LANES, :half] + both[LANES:, half:]
            field_im = both[:LANES, half:] - both[LANES:, :half]
            here = pl.ds(j * LANES, LANES)
            factor = (
                amplitude[here, :] * lax.rsqrt(field_re * field_re + field_im * field_im + 0.25)
                - 1.0
            )
            diff[here, :half] = (field_re * factor).astype(jnp.bfloat16)
            diff[here, half:] = (field_im * factor).astype(jnp.bfloat16)
    pieces = rows // LANES
    for i in range(HALF):
        product = dot(
            table[i * pieces : (i + 1) * pieces].reshape(pieces * 2 * LANES, width), diff[...]
        )
        for h in range(pieces):
            both = product[h * 2 * LANES : (h + 1) * 2 * LANES]
            here = pl.ds(h * LANES, LANES)
            back_re = (both[:LANES, :half] - both[LANES:, half:]).astype(jnp.bfloat16)
            back_im = (both[:LANES, half:] + both[LANES:, :half]).astype(jnp.bfloat16)
            for part in range(parts // 2):
                cols = slice(part * LANES, (part + 1) * LANES)
                strips[i, part, here, :] = back_re[:, cols]
                strips[i, parts // 2 + part, here, :] = back_im[:, cols]
    for d, out in enumerate(outs):
        out[...] = strips[jnp.bitwise_and(jnp.bitwise_xor(position, d), HALF - 1)]


def layout_kernel(*refs):
    position = lax.axis_index("slab")
    for d, strip in enumerate(refs[:-1]):
        refs[-1][jnp.bitwise_and(jnp.bitwise_xor(position, d), HALF - 1)] = strip[...]


def update_columns(first_step, last_step, starts, table, back, out):
    position = lax.axis_index("slab")
    led_at = lax.axis_index("led")
    core = jnp.bitwise_and(led_at, 1)
    plane_x = jnp.right_shift(led_at, 1)
    leds = starts.shape[0] // 2
    rows = back.shape[0] // (2 * leds)
    width = back.shape[1]
    group = width // LANES // 2
    blocks = [
        (1 - core if n < group else core) * group + n % group for n in range(first_step, last_step)
    ]
    for n in range(first_step, last_step):
        block = blocks[n - first_step]
        both = dot_t(back[...], table[block])
        half = leds * rows
        update = (
            both[:half, :LANES] - both[half:, LANES:],
            both[half:, :LANES] + both[:half, LANES:],
        )
        low = [0.0, 0.0]
        high = [0.0, 0.0]
        for led in range(leds):
            inside, wraps = window_mask(
                position * rows, starts[led], starts[leds + led], rows, block * LANES, LANES, width
            )
            for plane in range(2):
                piece = jnp.where(inside, update[plane][led * rows : (led + 1) * rows], 0.0)
                low[plane] += jnp.where(wraps, 0.0, piece)
                high[plane] += jnp.where(wraps, piece, 0.0)
        cols = slice((n - first_step) * LANES, (n - first_step + 1) * LANES)
        for plane in range(2):
            out[1 - plane_x, plane, :, cols] = low[plane].astype(out.dtype)
            out[plane_x, plane, :, cols] = high[plane].astype(out.dtype)


def sent_kernel(starts, table, near, *rest):
    far = rest[: len(CROSS)]
    out, back = rest[len(CROSS) :]
    position = lax.axis_index("slab")
    base = position - jnp.bitwise_and(position, HALF - 1)
    _, parts, rows, _ = near.shape
    half = back.shape[1] // LANES // 2
    blocks = [(base + i, near.at[i]) for i in range(HALF)]
    blocks += [(jnp.bitwise_xor(position, d), block) for d, block in zip(CROSS, far)]
    for source, block in blocks:
        at = pl.multiple_of(source * LANES, LANES)
        for part in range(parts):
            back[part * rows : (part + 1) * rows, pl.ds(at, LANES)] = block[part]
    update_columns(0, half, starts, table, back, out)


def kept_kernel(starts, table, back, out):
    half = back.shape[1] // LANES // 2
    update_columns(half, 2 * half, starts, table, back, out)


def local_call(kernel, out_shape, spaces, scratch, flops, moved, limit, name):
    return pl.pallas_call(
        kernel,
        out_shape=out_shape,
        in_specs=[pl.BlockSpec(memory_space=space) for space in spaces],
        out_specs=jax.tree.map(lambda _: pl.BlockSpec(memory_space=pltpu.VMEM), out_shape),
        scratch_shapes=scratch,
        compiler_params=pltpu.CompilerParams(vmem_limit_bytes=limit * 2**20),
        cost_estimate=pl.CostEstimate(flops=flops, bytes_accessed=moved, transcendentals=0),
        name=name,
    )


def body_slabs(spectrum, led_rows, led_cols, images):
    leds, block, width = images.shape
    rows = spectrum.shape[1]
    led_at = lax.axis_index("led")
    bf16 = jnp.bfloat16
    vmem, smem = pltpu.VMEM, pltpu.SMEM
    cos_table, sin_table = host_tables(width)
    steps = width // LANES
    table = jnp.asarray(
        np.stack(
            [
                np.concatenate([t[j * LANES : (j + 1) * LANES] for t in (cos_table, sin_table)])
                for j in range(steps)
            ]
        )
    )
    parts = 2 * leds
    sent_block = jax.ShapeDtypeStruct((parts, rows, LANES), bf16)
    flops = 8 * leds * rows * width * width

    starts = jnp.concatenate([led_rows, led_cols]).astype(jnp.int32)
    window = local_call(
        window_kernel,
        jax.ShapeDtypeStruct((parts * rows, width), bf16),
        [smem, vmem],
        [],
        0,
        6 * 2**20,
        12,
        "windows",
    )(starts, spectrum)

    def rows_call(which, name):
        count = which.stop - which.start
        return local_call(
            functools.partial(rows_kernel, which),
            [sent_block] * count,
            [vmem, vmem],
            [],
            flops * count // SLABS,
            5 * 2**20,
            16,
            name,
        )(window, table)

    first_a, first_b, near_2 = rows_call(slice(0, 3), "rows_round_1")
    def permute(sent, pairs):
        return lax.ppermute(sent, "slab", pairs)

    handed = list(PASSED.items())
    windowed = range(FIRST + 1, LAST)
    got_a = permute(first_a, [(s, s ^ 6) for s in INNER] + handed)
    got_b = permute(first_b, [(s, s ^ 7) for s in INNER] + handed)
    near_2 = permute(near_2, [(s, s ^ 2) for s in windowed])
    second_a, second_b, near_0, near_1, near_3 = rows_call(slice(3, SLABS), "rows_round_2")
    got_a, got_b, second_a, second_b, near_1, near_2, near_3 = lax.optimization_barrier(
        (got_a, got_b, second_a, second_b, near_1, near_2, near_3)
    )
    passes = is_one_of(lax.axis_index("slab"), PASSED.values())
    outer_pairs = [(s, s ^ 6) for s in range(SLABS) if s not in INNER]
    far_columns = [
        got_a,
        got_b,
        permute(jnp.where(passes, got_a, second_a), [(s, s ^ 4) for s in range(SLABS)]),
        permute(jnp.where(passes, got_b, second_b), outer_pairs),
        permute(second_b, [(s, s ^ 5) for s in INNER]),
    ]
    near_1 = permute(near_1, [(s, s ^ 1) for s in windowed])
    near_3 = permute(near_3, [(s, s ^ 3) for s in windowed])
    near_columns = [near_0, near_1, near_2, near_3]
    amplitude = jnp.sqrt(images).transpose(2, 0, 1).reshape(width, leds * block)
    strips = local_call(
        field_kernel,
        [sent_block] * HALF,
        [vmem] * 11,
        [pltpu.VMEM((width, parts * block), bf16)] * 2
        + [pltpu.VMEM((HALF,) + sent_block.shape, bf16)],
        16 * leds * block * width * width,
        12 * 2**20,
        20,
        "modulus_step",
    )(amplitude, table, *near_columns, *far_columns)

    def send_home(sent, d):
        return permute(sent, [(s, s ^ d) for s in range(SLABS) if FIRST < s ^ d < LAST])

    far_home = [send_home(strips[d % HALF], d) for d in CROSS]
    near_strips = local_call(
        layout_kernel,
        jax.ShapeDtypeStruct((HALF,) + sent_block.shape, bf16),
        [vmem] * HALF,
        [],
        0,
        12 * 2**20,
        8,
        "near_strips",
    )(*strips)
    near_home = lax.all_to_all(
        near_strips,
        "slab",
        split_axis=0,
        concat_axis=0,
        axis_index_groups=[list(range(HALF)), list(range(HALF, SLABS))],
        tiled=True,
    )
    share = width // 2
    sent, back = local_call(
        sent_kernel,
        [
            jax.ShapeDtypeStruct((2, 2, rows, share), bf16),
            jax.ShapeDtypeStruct((parts * rows, width), bf16),
        ],
        [smem] + [vmem] * (2 + len(CROSS)),
        [],
        flops // 2,
        8 * 2**20,
        20,
        "update_sent",
    )(starts, table, near_home, *far_home)
    got = lax.ppermute(sent, "led", [(0, 1), (1, 0), (2, 3), (3, 2)])
    kept = local_call(
        kept_kernel,
        jax.ShapeDtypeStruct((2, 2, rows, share), jnp.float32),
        [smem, vmem, vmem],
        [],
        flops // 2,
        8 * 2**20,
        20,
        "update_kept",
    )(starts, table, back)
    over = (kept[0] + got[0].astype(jnp.float32)).astype(bf16)
    got_x = lax.ppermute(over, "led", [(0, 2), (2, 0), (1, 3), (3, 1)])
    own_part = lax.dynamic_slice_in_dim(spectrum, led_at * share, share, 2)
    base = own_part + (kept[1] + got[1].astype(jnp.float32))
    base, got_x = lax.optimization_barrier((base, got_x))
    return base + got_x.astype(jnp.float32)


def solution(mesh):
    placed = (P(None, "slab", None), P("led"), P("led"), P("led", "slab", None))
    fits = mesh.shape["slab"] == 8 and mesh.shape["led"] == 4

    def body(spectrum, led_rows, led_cols, images):
        shapes = (spectrum.shape, images.shape)
        if fits and shapes == ((2, 256, 2048), (2, 128, 1024)):
            return body_slabs(spectrum, led_rows, led_cols, images)
        return body_any(spectrum, led_rows, led_cols, images)

    return jax.shard_map(
        body, mesh=mesh, in_specs=placed, out_specs=P(None, "slab", "led"), check_vma=False
    )
```

```python
import functools

import jax
import jax.numpy as jnp
import numpy as np
from jax import lax
from jax.experimental import pallas as pl
from jax.experimental.pallas import tpu as pltpu
from jax.sharding import PartitionSpec as P

LANES = 128


def as_sent(value):
    return jax.tree.map(lambda a: a.astype(jnp.bfloat16) if a.dtype == jnp.float32 else a, value)


def host_tables(width):
    index = np.arange(width, dtype=np.int64)
    angle_index = (index[:, None] * index[None, :] % width).astype(np.float32)
    angle = angle_index * np.float32(2.0 * 3.141592653589793 / width)
    scale = np.float32(1.0) / np.sqrt(np.float32(width))
    return (
        (np.cos(angle) * scale).astype(jnp.bfloat16),
        (np.sin(angle) * scale).astype(jnp.bfloat16),
    )


def make_pupil(row_index, col_index, width):
    row_term = (2 * row_index + 1 - width) * (2 * row_index + 1 - width)
    col_term = (2 * col_index + 1 - width) * (2 * col_index + 1 - width)
    return (row_term[:, None] + col_term[None, :] < width * width).astype(jnp.float32)


def contract(form, left, right):
    return jnp.einsum(form, left, right, preferred_element_type=jnp.float32)


def take_rows(strip, start, width):
    return lax.dynamic_slice_in_dim(strip, start, width, 1)


def place_rows(block, start, total, axis_dim):
    shape = list(block.shape)
    shape[axis_dim] = total
    holder = jnp.zeros(tuple(shape), block.dtype)
    return lax.dynamic_update_slice_in_dim(holder, block, start, axis_dim)


def modulus_step(field_in_re, field_in_im, image, cos_table, sin_table):
    field_re = contract("lka,am->lkm", field_in_re, cos_table) + contract(
        "lka,am->lkm", field_in_im, sin_table
    )
    field_im = contract("lka,am->lkm", field_in_im, cos_table) - contract(
        "lka,am->lkm", field_in_re, sin_table
    )
    factor = jnp.sqrt(image) / jnp.sqrt(field_re * field_re + field_im * field_im + 0.25) - 1.0
    diff_re = (field_re * factor).astype(jnp.bfloat16)
    diff_im = (field_im * factor).astype(jnp.bfloat16)
    back_re = (
        contract("lkm,ma->lka", diff_re, cos_table) - contract("lkm,ma->lka", diff_im, sin_table)
    ).astype(jnp.bfloat16)
    back_im = (
        contract("lkm,ma->lka", diff_im, cos_table) + contract("lkm,ma->lka", diff_re, sin_table)
    ).astype(jnp.bfloat16)
    return (back_re, back_im)


def body_any(spectrum, led_rows, led_cols, images):
    width = images.shape[2]
    slab_rows = spectrum.shape[1]
    columns = spectrum.shape[2]
    slabs = lax.axis_size("slab")
    total_rows = slab_rows * slabs
    position = lax.axis_index("slab")
    cos_table, sin_table = (jnp.asarray(t) for t in host_tables(width))
    own_rows = position * slab_rows + jnp.arange(slab_rows, dtype=jnp.int32)
    col_index = jnp.arange(width, dtype=jnp.int32)

    def take_cols(start):
        return lax.dynamic_slice_in_dim(spectrum, start, width, 2)

    def owner_mask(start):
        return make_pupil(own_rows - start, col_index, width)

    windows = jax.vmap(take_cols)(led_cols)
    masks = jax.vmap(owner_mask)(led_rows)
    win_re = (windows[:, 0] * masks).astype(jnp.bfloat16)
    win_im = (windows[:, 1] * masks).astype(jnp.bfloat16)

    def slice_strip(block, start):
        return take_rows(block, start, width)

    row_re = (
        contract("lgb,bk->lkg", win_re, cos_table) + contract("lgb,bk->lkg", win_im, sin_table)
    ).astype(jnp.bfloat16)
    row_im = (
        contract("lgb,bk->lkg", win_im, cos_table) - contract("lgb,bk->lkg", win_re, sin_table)
    ).astype(jnp.bfloat16)
    col_re, col_im = (
        lax.all_to_all(row_re, "slab", split_axis=1, concat_axis=2, tiled=True),
        lax.all_to_all(row_im, "slab", split_axis=1, concat_axis=2, tiled=True),
    )
    field_in_re = jax.vmap(slice_strip)(col_re, led_rows)
    field_in_im = jax.vmap(slice_strip)(col_im, led_rows)
    back_re, back_im = modulus_step(field_in_re, field_in_im, images, cos_table, sin_table)

    def place_strip(block, start):
        return place_rows(block, start, total_rows, 1)

    full_re = jax.vmap(place_strip)(back_re, led_rows)
    full_im = jax.vmap(place_strip)(back_im, led_rows)
    home_re, home_im = (
        lax.all_to_all(as_sent(full_re), "slab", split_axis=2, concat_axis=1, tiled=True).astype(
            full_re.dtype
        ),
        lax.all_to_all(as_sent(full_im), "slab", split_axis=2, concat_axis=1, tiled=True).astype(
            full_im.dtype
        ),
    )
    upd_re = contract("lkg,kb->lgb", home_re, cos_table) - contract(
        "lkg,kb->lgb", home_im, sin_table
    )
    upd_im = contract("lkg,kb->lgb", home_im, cos_table) + contract(
        "lkg,kb->lgb", home_re, sin_table
    )
    upd_re = upd_re * masks
    upd_im = upd_im * masks

    def add_window(number, gradient):
        start = led_cols[number]
        piece = jnp.stack([upd_re[number], upd_im[number]])
        current = lax.dynamic_slice_in_dim(gradient, start, width, 2)
        return lax.dynamic_update_slice_in_dim(gradient, current + piece, start, 2)

    gradient = lax.fori_loop(
        0, led_rows.shape[0], add_window, jnp.zeros((2, slab_rows, columns), jnp.float32)
    )
    summed = lax.psum_scatter(gradient, "led", scatter_dimension=2, tiled=True)
    share = summed.shape[2]
    own_part = lax.dynamic_slice_in_dim(spectrum, lax.axis_index("led") * share, share, 2)
    return own_part + summed


SLABS = 8
HALF = 4
FIRST, LAST = 0, 7
CROSS = (4, 5, 6, 7)
PASSED = {1: 0, 6: 7}
INNER = (2, 3, 4, 5)


def dot(left, right):
    return jnp.dot(left, right, preferred_element_type=jnp.float32)


def window_mask(first_row, row_start, col_start, rows, first_col, cols, width):
    shape = (rows, cols)
    at_row = lax.broadcasted_iota(jnp.int32, shape, 0) + (first_row - row_start)
    at_col = lax.broadcasted_iota(jnp.int32, shape, 1) + (first_col - col_start)
    wraps = at_col < 0
    at_col = jnp.where(wraps, at_col + width, at_col)
    row_term = 2 * at_row + 1 - width
    col_term = 2 * at_col + 1 - width
    return row_term * row_term + col_term * col_term < width * width, wraps


def row_block(window, table):
    both = dot(window, table)
    half = both.shape[0] // 2
    row_re = both[:half, :LANES] + both[half:, LANES:]
    row_im = both[half:, :LANES] - both[:half, LANES:]
    return row_re.astype(jnp.bfloat16), row_im.astype(jnp.bfloat16)


def store_parts(out, values):
    per = out.shape[0] // 2
    rows = out.shape[1]
    for plane, value in enumerate(values):
        for led in range(per):
            out[plane * per + led] = value[led * rows : (led + 1) * rows]


def is_one_of(position, slabs):
    return functools.reduce(jnp.logical_or, [position == slab for slab in slabs])


def window_kernel(starts, spectrum, window):
    position = lax.axis_index("slab")
    leds = starts.shape[0] // 2
    rows = spectrum.shape[1]
    width = window.shape[1]
    for led in range(leds):
        inside, wraps = window_mask(
            position * rows, starts[led], starts[leds + led], rows, 0, width, width
        )
        for plane in range(2):
            value = jnp.where(wraps, spectrum[plane, :, width:], spectrum[plane, :, :width])
            at = (plane * leds + led) * rows
            window[at : at + rows, :] = jnp.where(inside, value, 0.0).astype(jnp.bfloat16)


def classes_of(position):
    hands_over = is_one_of(position, PASSED)
    return (jnp.where(hands_over, 5, 6), 7, 2, 4, jnp.where(hands_over, 6, 5), 0, 1, 3)


def rows_kernel(which, window, table, *outs):
    position = lax.axis_index("slab")
    for out, d in zip(outs, classes_of(position)[which]):
        store_parts(out, row_block(window[...], table[jnp.bitwise_xor(position, d)]))


def choose_kernel(got_a, got_b, own_a, own_b, out_a, out_b):
    passes = is_one_of(lax.axis_index("slab"), PASSED.values())

    @pl.when(passes)
    def _():
        out_a[...] = got_a[...]
        out_b[...] = got_b[...]

    @pl.when(jnp.logical_not(passes))
    def _():
        out_a[...] = own_a[...]
        out_b[...] = own_b[...]


def amplitude_kernel(images, table, out, table_out):
    leds, block, width = images.shape
    for led in range(leds):
        for j in range(width // LANES):
            piece = jnp.sqrt(images[led, :, j * LANES : (j + 1) * LANES])
            out[j * LANES : (j + 1) * LANES, led * block : (led + 1) * block] = piece.T
    table_out[...] = table[...]


def field_kernel(amplitude, table, *rest):
    far, near = rest[:5], rest[5 : HALF + 5]
    outs = rest[HALF + 5 : 2 * HALF + 5]
    field_in, diff, strips = rest[2 * HALF + 5 :]
    position = lax.axis_index("slab")
    parts, rows, _ = near[0].shape
    half = parts // 2 * LANES
    width = field_in.shape[0]
    steps = width // LANES
    group = 4
    for d, block in enumerate(near):
        at = pl.multiple_of(jnp.bitwise_and(jnp.bitwise_xor(position, d), HALF - 1) * rows, rows)
        for part in range(parts):
            cols = slice(part * LANES, (part + 1) * LANES)
            field_in[pl.ds(at, rows), cols] = block[part]

    def add(block, origin):
        at = pl.multiple_of(jnp.bitwise_and(origin, HALF - 1) * rows, rows)
        for part in range(parts):
            cols = slice(part * LANES, (part + 1) * LANES)
            field_in[pl.ds(at, rows), cols] += block[part]

    passes = is_one_of(position, PASSED.values())
    hands_over = is_one_of(position, PASSED)
    ends = is_one_of(position, [to ^ 4 for to in PASSED.values()])

    @pl.when(is_one_of(position, INNER))
    def _():
        add(far[0], jnp.bitwise_xor(position, 6))
        add(far[1], jnp.bitwise_xor(position, 7))
        add(far[2], jnp.bitwise_xor(position, jnp.where(ends, 5, 4)))

    @pl.when(jnp.logical_or(passes, hands_over))
    def _():
        add(far[2], jnp.bitwise_xor(position, 4))
        add(far[3], jnp.bitwise_xor(position, jnp.where(hands_over, 7, 6)))
        add(far[4], jnp.bitwise_xor(position, 5))

    for first in range(0, steps, group):
        product = dot(
            table[first : first + group].reshape(group * 2 * LANES, width), field_in[...]
        )
        for j in range(first, first + group):
            both = product[(j - first) * 2 * LANES : (j - first + 1) * 2 * LANES]
            field_re = both[:LANES, :half] + both[LANES:, half:]
            field_im = both[:LANES, half:] - both[LANES:, :half]
            here = pl.ds(j * LANES, LANES)
            factor = (
                amplitude[here, :] * lax.rsqrt(field_re * field_re + field_im * field_im + 0.25)
                - 1.0
            )
            diff[here, :half] = (field_re * factor).astype(jnp.bfloat16)
            diff[here, half:] = (field_im * factor).astype(jnp.bfloat16)
    pieces = rows // LANES
    for i in range(HALF):
        product = dot(
            table[i * pieces : (i + 1) * pieces].reshape(pieces * 2 * LANES, width), diff[...]
        )
        for h in range(pieces):
            both = product[h * 2 * LANES : (h + 1) * 2 * LANES]
            here = pl.ds(h * LANES, LANES)
            back_re = (both[:LANES, :half] - both[LANES:, half:]).astype(jnp.bfloat16)
            back_im = (both[:LANES, half:] + both[LANES:, :half]).astype(jnp.bfloat16)
            for part in range(parts // 2):
                cols = slice(part * LANES, (part + 1) * LANES)
                strips[i, part, here, :] = back_re[:, cols]
                strips[i, parts // 2 + part, here, :] = back_im[:, cols]
    for d, out in enumerate(outs):
        out[...] = strips[jnp.bitwise_and(position + d, HALF - 1)]


def update_columns(first_step, last_step, starts, table, back, out):
    position = lax.axis_index("slab")
    led_at = lax.axis_index("led")
    core = jnp.bitwise_and(led_at, 1)
    plane_x = jnp.right_shift(led_at, 1)
    leds = starts.shape[0] // 2
    rows = back.shape[0] // (2 * leds)
    width = back.shape[1]
    group = width // LANES // 2
    blocks = [
        (1 - core if n < group else core) * group + n % group for n in range(first_step, last_step)
    ]
    for n in range(first_step, last_step):
        block = blocks[n - first_step]
        both = dot(back[...], table[block])
        half = leds * rows
        update = (
            both[:half, :LANES] - both[half:, LANES:],
            both[half:, :LANES] + both[:half, LANES:],
        )
        low = [0.0, 0.0]
        high = [0.0, 0.0]
        for led in range(leds):
            inside, wraps = window_mask(
                position * rows, starts[led], starts[leds + led], rows, block * LANES, LANES, width
            )
            for plane in range(2):
                piece = jnp.where(inside, update[plane][led * rows : (led + 1) * rows], 0.0)
                low[plane] += jnp.where(wraps, 0.0, piece)
                high[plane] += jnp.where(wraps, piece, 0.0)
        cols = slice((n - first_step) * LANES, (n - first_step + 1) * LANES)
        for plane in range(2):
            out[1 - plane_x, plane, :, cols] = low[plane].astype(out.dtype)
            out[plane_x, plane, :, cols] = high[plane].astype(out.dtype)


def sent_kernel(starts, table, *rest):
    blocks = rest[:SLABS]
    out, back = rest[SLABS:]
    position = lax.axis_index("slab")
    parts, rows, _ = blocks[0].shape
    half = back.shape[1] // LANES // 2
    for d, block in enumerate(blocks):
        at = pl.multiple_of(lax.rem(position + SLABS - d, SLABS) * LANES, LANES)
        for part in range(parts):
            back[part * rows : (part + 1) * rows, pl.ds(at, LANES)] = block[part]
    update_columns(0, half, starts, table, back, out)


def kept_kernel(starts, table, back, out):
    half = back.shape[1] // LANES // 2
    update_columns(half, 2 * half, starts, table, back, out)


def local_call(kernel, out_shape, spaces, scratch, flops, moved, name):
    return pl.pallas_call(
        kernel,
        out_shape=out_shape,
        in_specs=[pl.BlockSpec(memory_space=space) for space in spaces],
        out_specs=jax.tree.map(lambda _: pl.BlockSpec(memory_space=pltpu.VMEM), out_shape),
        scratch_shapes=scratch,
        compiler_params=pltpu.CompilerParams(vmem_limit_bytes=32 * 2**20),
        cost_estimate=pl.CostEstimate(flops=flops, bytes_accessed=moved, transcendentals=0),
        name=name,
    )


def body_slabs(spectrum, led_rows, led_cols, images):
    leds, block, width = images.shape
    rows = spectrum.shape[1]
    led_at = lax.axis_index("led")
    bf16 = jnp.bfloat16
    vmem, smem = pltpu.VMEM, pltpu.SMEM
    cos_table, sin_table = host_tables(width)
    steps = width // LANES
    by_col = np.stack(
        [
            np.concatenate([t[:, j * LANES : (j + 1) * LANES] for t in (cos_table, sin_table)], 1)
            for j in range(steps)
        ]
    )
    by_row = jnp.asarray(np.ascontiguousarray(by_col.transpose(0, 2, 1)))
    by_col = jnp.asarray(by_col)
    parts = 2 * leds
    sent_block = jax.ShapeDtypeStruct((parts, rows, LANES), bf16)
    flops = 8 * leds * rows * width * width

    starts = jnp.concatenate([led_rows, led_cols]).astype(jnp.int32)
    window = local_call(
        window_kernel,
        jax.ShapeDtypeStruct((parts * rows, width), bf16),
        [smem, vmem],
        [],
        0,
        6 * 2**20,
        "windows",
    )(starts, spectrum)

    def rows_call(which, name):
        count = which.stop - which.start
        return local_call(
            functools.partial(rows_kernel, which),
            [sent_block] * count,
            [vmem, vmem],
            [],
            flops * count // SLABS,
            5 * 2**20,
            name,
        )(window, by_col)

    first_a, first_b, near_2 = rows_call(slice(0, 3), "rows_round_1")

    def permute(sent, pairs):
        return lax.ppermute(sent, "slab", pairs)

    handed = list(PASSED.items())
    windowed = range(FIRST + 1, LAST)
    got_a = permute(first_a, [(s, s ^ 6) for s in INNER] + handed)
    got_b = permute(first_b, [(s, s ^ 7) for s in INNER] + handed)
    near_2 = permute(near_2, [(s, s ^ 2) for s in windowed])
    second_a, second_b, near_0, near_1, near_3 = rows_call(slice(3, SLABS), "rows_round_2")
    inner_b = second_b
    second_a, second_b = local_call(
        choose_kernel,
        [sent_block] * 2,
        [vmem] * 4,
        [],
        0,
        2**20,
        "round_2_blocks",
    )(got_a, got_b, second_a, second_b)
    second_a, second_b, inner_b, near_1, near_2, near_3, images = lax.optimization_barrier(
        (second_a, second_b, inner_b, near_1, near_2, near_3, images)
    )
    outer_pairs = [(s, s ^ 6) for s in range(SLABS) if s not in INNER]
    far_columns = [
        got_a,
        got_b,
        permute(second_a, [(s, s ^ 4) for s in range(SLABS)]),
        permute(second_b, outer_pairs),
        permute(inner_b, [(s, s ^ 5) for s in INNER]),
    ]
    near_1 = permute(near_1, [(s, s ^ 1) for s in windowed])
    near_3 = permute(near_3, [(s, s ^ 3) for s in windowed])
    near_columns = [near_0, near_1, near_2, near_3]
    amplitude, by_row = local_call(
        amplitude_kernel,
        [
            jax.ShapeDtypeStruct((width, leds * block), jnp.float32),
            jax.ShapeDtypeStruct(by_row.shape, bf16),
        ],
        [vmem] * 2,
        [],
        0,
        10 * 2**20,
        "amplitude",
    )(images, by_row)
    strips = local_call(
        field_kernel,
        [sent_block] * HALF,
        [vmem] * 11,
        [pltpu.VMEM((width, parts * block), bf16)] * 2
        + [pltpu.VMEM((HALF,) + sent_block.shape, bf16)],
        16 * leds * block * width * width,
        12 * 2**20,
        "modulus_step",
    )(amplitude, by_row, *far_columns, *near_columns)

    def send_home(d):
        pairs = [(s, (s + d) % SLABS) for s in range(SLABS) if FIRST < (s + d) % SLABS < LAST]
        return permute(strips[d % HALF], pairs)

    strips = list(strips)
    home = {0: strips[0]}
    for d in (4, 5, 1, 6, 2):
        home[d] = send_home(d)
    for d, before in ((7, 4), (3, 5)):
        home[before], strips[3] = lax.optimization_barrier((home[before], strips[3]))
        home[d] = send_home(d)
    home = [home[d] for d in range(SLABS)]
    share = width // 2
    sent, back = local_call(
        sent_kernel,
        [
            jax.ShapeDtypeStruct((2, 2, rows, share), bf16),
            jax.ShapeDtypeStruct((parts * rows, width), bf16),
        ],
        [smem] + [vmem] * (1 + SLABS),
        [],
        flops // 2,
        8 * 2**20,
        "update_sent",
    )(starts, by_col, *home)
    got = lax.ppermute(sent, "led", [(0, 1), (1, 0), (2, 3), (3, 2)])
    kept = local_call(
        kept_kernel,
        jax.ShapeDtypeStruct((2, 2, rows, share), jnp.float32),
        [smem, vmem, vmem],
        [],
        flops // 2,
        8 * 2**20,
        "update_kept",
    )(starts, by_col, back)
    over = (kept[0] + got[0].astype(jnp.float32)).astype(bf16)
    got_x = lax.ppermute(over, "led", [(0, 2), (2, 0), (1, 3), (3, 1)])
    own_part = lax.dynamic_slice_in_dim(spectrum, led_at * share, share, 2)
    base = own_part + (kept[1] + got[1].astype(jnp.float32))
    base, got_x = lax.optimization_barrier((base, got_x))
    return base + got_x.astype(jnp.float32)


def solution(mesh):
    placed = (P(None, "slab", None), P("led"), P("led"), P("led", "slab", None))
    fits = mesh.shape["slab"] == 8 and mesh.shape["led"] == 4

    def body(spectrum, led_rows, led_cols, images):
        shapes = (spectrum.shape, images.shape)
        if fits and shapes == ((2, 256, 2048), (2, 128, 1024)):
            return body_slabs(spectrum, led_rows, led_cols, images)
        return body_any(spectrum, led_rows, led_cols, images)

    return jax.shard_map(
        body, mesh=mesh, in_specs=placed, out_specs=P(None, "slab", "led"), check_vma=False
    )
```

```python
import functools

import jax
import jax.numpy as jnp
import numpy as np
from jax import lax
from jax.experimental import pallas as pl
from jax.experimental.pallas import tpu as pltpu
from jax.sharding import PartitionSpec as P

LANES = 128


def as_sent(value):
    return jax.tree.map(lambda a: a.astype(jnp.bfloat16) if a.dtype == jnp.float32 else a, value)


def host_tables(width):
    index = np.arange(width, dtype=np.int64)
    angle_index = (index[:, None] * index[None, :] % width).astype(np.float32)
    angle = angle_index * np.float32(2.0 * 3.141592653589793 / width)
    scale = np.float32(1.0) / np.sqrt(np.float32(width))
    return (
        (np.cos(angle) * scale).astype(jnp.bfloat16),
        (np.sin(angle) * scale).astype(jnp.bfloat16),
    )


def make_pupil(row_index, col_index, width):
    row_term = (2 * row_index + 1 - width) * (2 * row_index + 1 - width)
    col_term = (2 * col_index + 1 - width) * (2 * col_index + 1 - width)
    return (row_term[:, None] + col_term[None, :] < width * width).astype(jnp.float32)


def contract(form, left, right):
    return jnp.einsum(form, left, right, preferred_element_type=jnp.float32)


def take_rows(strip, start, width):
    return lax.dynamic_slice_in_dim(strip, start, width, 1)


def place_rows(block, start, total, axis_dim):
    shape = list(block.shape)
    shape[axis_dim] = total
    holder = jnp.zeros(tuple(shape), block.dtype)
    return lax.dynamic_update_slice_in_dim(holder, block, start, axis_dim)


def modulus_step(field_in_re, field_in_im, image, cos_table, sin_table):
    field_re = contract("lka,am->lkm", field_in_re, cos_table) + contract(
        "lka,am->lkm", field_in_im, sin_table
    )
    field_im = contract("lka,am->lkm", field_in_im, cos_table) - contract(
        "lka,am->lkm", field_in_re, sin_table
    )
    factor = jnp.sqrt(image) / jnp.sqrt(field_re * field_re + field_im * field_im + 0.25) - 1.0
    diff_re = (field_re * factor).astype(jnp.bfloat16)
    diff_im = (field_im * factor).astype(jnp.bfloat16)
    back_re = (
        contract("lkm,ma->lka", diff_re, cos_table) - contract("lkm,ma->lka", diff_im, sin_table)
    ).astype(jnp.bfloat16)
    back_im = (
        contract("lkm,ma->lka", diff_im, cos_table) + contract("lkm,ma->lka", diff_re, sin_table)
    ).astype(jnp.bfloat16)
    return (back_re, back_im)


def body_any(spectrum, led_rows, led_cols, images):
    width = images.shape[2]
    slab_rows = spectrum.shape[1]
    columns = spectrum.shape[2]
    slabs = lax.axis_size("slab")
    total_rows = slab_rows * slabs
    position = lax.axis_index("slab")
    cos_table, sin_table = (jnp.asarray(t) for t in host_tables(width))
    own_rows = position * slab_rows + jnp.arange(slab_rows, dtype=jnp.int32)
    col_index = jnp.arange(width, dtype=jnp.int32)

    def take_cols(start):
        return lax.dynamic_slice_in_dim(spectrum, start, width, 2)

    def owner_mask(start):
        return make_pupil(own_rows - start, col_index, width)

    windows = jax.vmap(take_cols)(led_cols)
    masks = jax.vmap(owner_mask)(led_rows)
    win_re = (windows[:, 0] * masks).astype(jnp.bfloat16)
    win_im = (windows[:, 1] * masks).astype(jnp.bfloat16)

    def slice_strip(block, start):
        return take_rows(block, start, width)

    row_re = (
        contract("lgb,bk->lkg", win_re, cos_table) + contract("lgb,bk->lkg", win_im, sin_table)
    ).astype(jnp.bfloat16)
    row_im = (
        contract("lgb,bk->lkg", win_im, cos_table) - contract("lgb,bk->lkg", win_re, sin_table)
    ).astype(jnp.bfloat16)
    col_re, col_im = (
        lax.all_to_all(row_re, "slab", split_axis=1, concat_axis=2, tiled=True),
        lax.all_to_all(row_im, "slab", split_axis=1, concat_axis=2, tiled=True),
    )
    field_in_re = jax.vmap(slice_strip)(col_re, led_rows)
    field_in_im = jax.vmap(slice_strip)(col_im, led_rows)
    back_re, back_im = modulus_step(field_in_re, field_in_im, images, cos_table, sin_table)

    def place_strip(block, start):
        return place_rows(block, start, total_rows, 1)

    full_re = jax.vmap(place_strip)(back_re, led_rows)
    full_im = jax.vmap(place_strip)(back_im, led_rows)
    home_re, home_im = (
        lax.all_to_all(as_sent(full_re), "slab", split_axis=2, concat_axis=1, tiled=True).astype(
            full_re.dtype
        ),
        lax.all_to_all(as_sent(full_im), "slab", split_axis=2, concat_axis=1, tiled=True).astype(
            full_im.dtype
        ),
    )
    upd_re = contract("lkg,kb->lgb", home_re, cos_table) - contract(
        "lkg,kb->lgb", home_im, sin_table
    )
    upd_im = contract("lkg,kb->lgb", home_im, cos_table) + contract(
        "lkg,kb->lgb", home_re, sin_table
    )
    upd_re = upd_re * masks
    upd_im = upd_im * masks

    def add_window(number, gradient):
        start = led_cols[number]
        piece = jnp.stack([upd_re[number], upd_im[number]])
        current = lax.dynamic_slice_in_dim(gradient, start, width, 2)
        return lax.dynamic_update_slice_in_dim(gradient, current + piece, start, 2)

    gradient = lax.fori_loop(
        0, led_rows.shape[0], add_window, jnp.zeros((2, slab_rows, columns), jnp.float32)
    )
    summed = lax.psum_scatter(gradient, "led", scatter_dimension=2, tiled=True)
    share = summed.shape[2]
    own_part = lax.dynamic_slice_in_dim(spectrum, lax.axis_index("led") * share, share, 2)
    return own_part + summed


SLABS = 8
HALF = 4
FIRST, LAST = 0, 7
CROSS = (4, 5, 6, 7)
PASSED = {1: 0, 6: 7}
INNER = (2, 3, 4, 5)


def dot(left, right):
    return jnp.dot(left, right, preferred_element_type=jnp.float32)


def window_mask(first_row, row_start, col_start, rows, first_col, cols, width):
    shape = (rows, cols)
    at_row = lax.broadcasted_iota(jnp.int32, shape, 0) + (first_row - row_start)
    at_col = lax.broadcasted_iota(jnp.int32, shape, 1) + (first_col - col_start)
    wraps = at_col < 0
    at_col = jnp.where(wraps, at_col + width, at_col)
    row_term = 2 * at_row + 1 - width
    col_term = 2 * at_col + 1 - width
    return row_term * row_term + col_term * col_term < width * width, wraps


def row_block(window, table):
    both = dot(window, table)
    half = both.shape[0] // 2
    row_re = both[:half, :LANES] + both[half:, LANES:]
    row_im = both[half:, :LANES] - both[:half, LANES:]
    return row_re.astype(jnp.bfloat16), row_im.astype(jnp.bfloat16)


def store_parts(out, values):
    per = out.shape[0] // 2
    rows = out.shape[1]
    for plane, value in enumerate(values):
        for led in range(per):
            out[plane * per + led] = value[led * rows : (led + 1) * rows]


def is_one_of(position, slabs):
    return functools.reduce(jnp.logical_or, [position == slab for slab in slabs])


def window_kernel(starts, spectrum, window):
    position = lax.axis_index("slab")
    leds = starts.shape[0] // 2
    rows = spectrum.shape[1]
    width = window.shape[1]
    for led in range(leds):
        inside, wraps = window_mask(
            position * rows, starts[led], starts[leds + led], rows, 0, width, width
        )
        for plane in range(2):
            value = jnp.where(wraps, spectrum[plane, :, width:], spectrum[plane, :, :width])
            at = (plane * leds + led) * rows
            window[at : at + rows, :] = jnp.where(inside, value, 0.0).astype(jnp.bfloat16)


def classes_of(position):
    hands_over = is_one_of(position, PASSED)
    return (jnp.where(hands_over, 5, 6), 7, 2, 4, jnp.where(hands_over, 6, 5), 0, 1, 3)


def rows_kernel(which, window, table, *outs):
    position = lax.axis_index("slab")
    for out, d in zip(outs, classes_of(position)[which]):
        store_parts(out, row_block(window[...], table[jnp.bitwise_xor(position, d)]))


def choose_kernel(got, own, out):
    passes = is_one_of(lax.axis_index("slab"), PASSED.values())

    @pl.when(passes)
    def _():
        out[...] = got[...]

    @pl.when(jnp.logical_not(passes))
    def _():
        out[...] = own[...]


def partner_at(position, d):
    return 1 - jnp.bitwise_and(position if d == 1 else jnp.right_shift(position, 1), 1)


def amplitude_kernel(images, table, out, table_out):
    leds, block, width = images.shape
    for led in range(leds):
        for j in range(width // LANES):
            piece = jnp.sqrt(images[led, :, j * LANES : (j + 1) * LANES])
            out[j * LANES : (j + 1) * LANES, led * block : (led + 1) * block] = piece.T
    table_out[...] = table[...]


def field_kernel(amplitude, table, *rest):
    far, near = rest[:5], rest[5 : HALF + 5]
    outs = rest[HALF + 5 : 2 * HALF + 5]
    field_in, diff, strips = rest[2 * HALF + 5 :]
    position = lax.axis_index("slab")
    parts, rows, _ = near[0].shape
    half = parts // 2 * LANES
    width = field_in.shape[0]
    steps = width // LANES
    group = 4
    for d, block in enumerate(near):
        block = block.at[partner_at(position, d)] if d else block
        at = pl.multiple_of(jnp.bitwise_and(jnp.bitwise_xor(position, d), HALF - 1) * rows, rows)
        for part in range(parts):
            cols = slice(part * LANES, (part + 1) * LANES)
            field_in[pl.ds(at, rows), cols] = block[part]

    def add(block, origin):
        at = pl.multiple_of(jnp.bitwise_and(origin, HALF - 1) * rows, rows)
        for part in range(parts):
            cols = slice(part * LANES, (part + 1) * LANES)
            field_in[pl.ds(at, rows), cols] += block[part]

    passes = is_one_of(position, PASSED.values())
    hands_over = is_one_of(position, PASSED)
    ends = is_one_of(position, [to ^ 4 for to in PASSED.values()])

    @pl.when(is_one_of(position, INNER))
    def _():
        add(far[0], jnp.bitwise_xor(position, 6))
        add(far[1], jnp.bitwise_xor(position, 7))
        add(far[2], jnp.bitwise_xor(position, jnp.where(ends, 5, 4)))

    @pl.when(jnp.logical_or(passes, hands_over))
    def _():
        add(far[2], jnp.bitwise_xor(position, 4))
        add(far[3], jnp.bitwise_xor(position, jnp.where(hands_over, 7, 6)))
        add(far[4], jnp.bitwise_xor(position, 5))

    for first in range(0, steps, group):
        product = dot(
            table[first : first + group].reshape(group * 2 * LANES, width), field_in[...]
        )
        for j in range(first, first + group):
            both = product[(j - first) * 2 * LANES : (j - first + 1) * 2 * LANES]
            field_re = both[:LANES, :half] + both[LANES:, half:]
            field_im = both[:LANES, half:] - both[LANES:, :half]
            here = pl.ds(j * LANES, LANES)
            factor = (
                amplitude[here, :] * lax.rsqrt(field_re * field_re + field_im * field_im + 0.25)
                - 1.0
            )
            diff[here, :half] = (field_re * factor).astype(jnp.bfloat16)
            diff[here, half:] = (field_im * factor).astype(jnp.bfloat16)
    pieces = rows // LANES
    for i in range(HALF):
        product = dot(
            table[i * pieces : (i + 1) * pieces].reshape(pieces * 2 * LANES, width), diff[...]
        )
        for h in range(pieces):
            both = product[h * 2 * LANES : (h + 1) * 2 * LANES]
            here = pl.ds(h * LANES, LANES)
            back_re = (both[:LANES, :half] - both[LANES:, half:]).astype(jnp.bfloat16)
            back_im = (both[:LANES, half:] + both[LANES:, :half]).astype(jnp.bfloat16)
            for part in range(parts // 2):
                cols = slice(part * LANES, (part + 1) * LANES)
                strips[i, part, here, :] = back_re[:, cols]
                strips[i, parts // 2 + part, here, :] = back_im[:, cols]
    for d, out in enumerate(outs):
        out[...] = strips[jnp.bitwise_and(jnp.bitwise_xor(position, d), HALF - 1)]


def update_columns(first_step, last_step, starts, table, back, out):
    position = lax.axis_index("slab")
    led_at = lax.axis_index("led")
    core = jnp.bitwise_and(led_at, 1)
    plane_x = jnp.right_shift(led_at, 1)
    leds = starts.shape[0] // 2
    rows = back.shape[0] // (2 * leds)
    width = back.shape[1]
    group = width // LANES // 2
    blocks = [
        (1 - core if n < group else core) * group + n % group for n in range(first_step, last_step)
    ]
    for n in range(first_step, last_step):
        block = blocks[n - first_step]
        both = dot(back[...], table[block])
        half = leds * rows
        update = (
            both[:half, :LANES] - both[half:, LANES:],
            both[half:, :LANES] + both[:half, LANES:],
        )
        low = [0.0, 0.0]
        high = [0.0, 0.0]
        for led in range(leds):
            inside, wraps = window_mask(
                position * rows, starts[led], starts[leds + led], rows, block * LANES, LANES, width
            )
            for plane in range(2):
                piece = jnp.where(inside, update[plane][led * rows : (led + 1) * rows], 0.0)
                low[plane] += jnp.where(wraps, 0.0, piece)
                high[plane] += jnp.where(wraps, piece, 0.0)
        cols = slice((n - first_step) * LANES, (n - first_step + 1) * LANES)
        for plane in range(2):
            out[1 - plane_x, plane, :, cols] = low[plane].astype(out.dtype)
            out[plane_x, plane, :, cols] = high[plane].astype(out.dtype)


def sent_kernel(starts, table, *rest):
    blocks = rest[:SLABS]
    out, back = rest[SLABS:]
    position = lax.axis_index("slab")
    parts, rows, _ = blocks[0].shape
    half = back.shape[1] // LANES // 2
    for d, block in enumerate(blocks):
        block = block.at[partner_at(position, d)] if 0 < d < HALF else block
        at = pl.multiple_of(jnp.bitwise_xor(position, d) * LANES, LANES)
        for part in range(parts):
            back[part * rows : (part + 1) * rows, pl.ds(at, LANES)] = block[part]
    update_columns(0, half, starts, table, back, out)


def kept_kernel(starts, table, back, out):
    half = back.shape[1] // LANES // 2
    update_columns(half, 2 * half, starts, table, back, out)


def local_call(kernel, out_shape, spaces, scratch, flops, moved, name):
    return pl.pallas_call(
        kernel,
        out_shape=out_shape,
        in_specs=[pl.BlockSpec(memory_space=space) for space in spaces],
        out_specs=jax.tree.map(lambda _: pl.BlockSpec(memory_space=pltpu.VMEM), out_shape),
        scratch_shapes=scratch,
        compiler_params=pltpu.CompilerParams(vmem_limit_bytes=32 * 2**20),
        cost_estimate=pl.CostEstimate(flops=flops, bytes_accessed=moved, transcendentals=0),
        name=name,
    )


def body_slabs(spectrum, led_rows, led_cols, images):
    leds, block, width = images.shape
    rows = spectrum.shape[1]
    led_at = lax.axis_index("led")
    bf16 = jnp.bfloat16
    vmem, smem = pltpu.VMEM, pltpu.SMEM
    cos_table, sin_table = host_tables(width)
    steps = width // LANES
    by_col = np.stack(
        [
            np.concatenate([t[:, j * LANES : (j + 1) * LANES] for t in (cos_table, sin_table)], 1)
            for j in range(steps)
        ]
    )
    by_row = jnp.asarray(np.ascontiguousarray(by_col.transpose(0, 2, 1)))
    by_col = jnp.asarray(by_col)
    parts = 2 * leds
    sent_block = jax.ShapeDtypeStruct((parts, rows, LANES), bf16)
    flops = 8 * leds * rows * width * width

    starts = jnp.concatenate([led_rows, led_cols]).astype(jnp.int32)
    window = local_call(
        window_kernel,
        jax.ShapeDtypeStruct((parts * rows, width), bf16),
        [smem, vmem],
        [],
        0,
        6 * 2**20,
        "windows",
    )(starts, spectrum)

    def rows_call(which, name):
        count = which.stop - which.start
        return local_call(
            functools.partial(rows_kernel, which),
            [sent_block] * count,
            [vmem, vmem],
            [],
            flops * count // SLABS,
            5 * 2**20,
            name,
        )(window, by_col)

    first_a, first_b, near_2 = rows_call(slice(0, 3), "rows_round_1")

    def permute(sent, pairs):
        return lax.ppermute(sent, "slab", pairs)

    def swap_near(sent, d):
        pairs = [[s, s ^ d] for s in range(SLABS) if s < s ^ d]
        return lax.all_gather(sent, "slab", axis_index_groups=pairs)

    def choose(got, own, name):
        return local_call(
            choose_kernel, sent_block, [vmem] * 2, [], 0, 2**19, name
        )(got, own)

    handed = list(PASSED.items())
    got_a = permute(first_a, [(s, s ^ 6) for s in INNER] + handed)
    got_b = permute(first_b, [(s, s ^ 7) for s in INNER] + handed)
    near_2 = swap_near(near_2, 2)
    second_a, second_b, near_0, near_1, near_3 = rows_call(slice(3, SLABS), "rows_round_2")
    got_a, second_a, second_b, near_1, near_3, images = lax.optimization_barrier(
        (got_a, second_a, second_b, near_1, near_3, images)
    )
    outer_pairs = [(s, s ^ 6) for s in range(SLABS) if s not in INNER]
    far_columns = [
        got_a,
        got_b,
        permute(choose(got_a, second_a, "class_4_blocks"), [(s, s ^ 4) for s in range(SLABS)]),
        permute(choose(got_b, second_b, "class_6_blocks"), outer_pairs),
        permute(second_b, [(s, s ^ 5) for s in INNER]),
    ]
    near_columns = [near_0, swap_near(near_1, 1), near_2, swap_near(near_3, 3)]
    amplitude, by_row = local_call(
        amplitude_kernel,
        [
            jax.ShapeDtypeStruct((width, leds * block), jnp.float32),
            jax.ShapeDtypeStruct(by_row.shape, bf16),
        ],
        [vmem] * 2,
        [],
        0,
        10 * 2**20,
        "amplitude",
    )(images, by_row)
    strips = local_call(
        field_kernel,
        [sent_block] * HALF,
        [vmem] * 11,
        [pltpu.VMEM((width, parts * block), bf16)] * 2
        + [pltpu.VMEM((HALF,) + sent_block.shape, bf16)],
        16 * leds * block * width * width,
        12 * 2**20,
        "modulus_step",
    )(amplitude, by_row, *far_columns, *near_columns)

    home = [strips[0]]
    home += [swap_near(strips[d], d) for d in range(1, HALF)]
    home += [
        permute(strips[d % HALF], [(s, s ^ d) for s in range(SLABS) if FIRST < s ^ d < LAST])
        for d in CROSS
    ]
    share = width // 2
    sent, back = local_call(
        sent_kernel,
        [
            jax.ShapeDtypeStruct((2, 2, rows, share), bf16),
            jax.ShapeDtypeStruct((parts * rows, width), bf16),
        ],
        [smem] + [vmem] * (1 + SLABS),
        [],
        flops // 2,
        8 * 2**20,
        "update_sent",
    )(starts, by_col, *home)
    got = lax.ppermute(sent, "led", [(0, 1), (1, 0), (2, 3), (3, 2)])
    kept = local_call(
        kept_kernel,
        jax.ShapeDtypeStruct((2, 2, rows, share), jnp.float32),
        [smem, vmem, vmem],
        [],
        flops // 2,
        8 * 2**20,
        "update_kept",
    )(starts, by_col, back)
    over = (kept[0] + got[0].astype(jnp.float32)).astype(bf16)
    got_x = lax.ppermute(over, "led", [(0, 2), (2, 0), (1, 3), (3, 1)])
    own_part = lax.dynamic_slice_in_dim(spectrum, led_at * share, share, 2)
    base = own_part + (kept[1] + got[1].astype(jnp.float32))
    base, got_x = lax.optimization_barrier((base, got_x))
    return base + got_x.astype(jnp.float32)


def solution(mesh):
    placed = (P(None, "slab", None), P("led"), P("led"), P("led", "slab", None))
    fits = mesh.shape["slab"] == 8 and mesh.shape["led"] == 4

    def body(spectrum, led_rows, led_cols, images):
        shapes = (spectrum.shape, images.shape)
        if fits and shapes == ((2, 256, 2048), (2, 128, 1024)):
            return body_slabs(spectrum, led_rows, led_cols, images)
        return body_any(spectrum, led_rows, led_cols, images)

    return jax.shard_map(
        body, mesh=mesh, in_specs=placed, out_specs=P(None, "slab", "led"), check_vma=False
    )
```

```python
import functools

import jax
import jax.numpy as jnp
import numpy as np
from jax import lax
from jax.experimental import pallas as pl
from jax.experimental.pallas import tpu as pltpu
from jax.sharding import PartitionSpec as P

LANES = 128


def as_sent(value):
    return jax.tree.map(lambda a: a.astype(jnp.bfloat16) if a.dtype == jnp.float32 else a, value)


def host_tables(width):
    index = np.arange(width, dtype=np.int64)
    angle_index = (index[:, None] * index[None, :] % width).astype(np.float32)
    angle = angle_index * np.float32(2.0 * 3.141592653589793 / width)
    scale = np.float32(1.0) / np.sqrt(np.float32(width))
    return (
        (np.cos(angle) * scale).astype(jnp.bfloat16),
        (np.sin(angle) * scale).astype(jnp.bfloat16),
    )


def make_pupil(row_index, col_index, width):
    row_term = (2 * row_index + 1 - width) * (2 * row_index + 1 - width)
    col_term = (2 * col_index + 1 - width) * (2 * col_index + 1 - width)
    return (row_term[:, None] + col_term[None, :] < width * width).astype(jnp.float32)


def contract(form, left, right):
    return jnp.einsum(form, left, right, preferred_element_type=jnp.float32)


def take_rows(strip, start, width):
    return lax.dynamic_slice_in_dim(strip, start, width, 1)


def place_rows(block, start, total, axis_dim):
    shape = list(block.shape)
    shape[axis_dim] = total
    holder = jnp.zeros(tuple(shape), block.dtype)
    return lax.dynamic_update_slice_in_dim(holder, block, start, axis_dim)


def modulus_step(field_in_re, field_in_im, image, cos_table, sin_table):
    field_re = contract("lka,am->lkm", field_in_re, cos_table) + contract(
        "lka,am->lkm", field_in_im, sin_table
    )
    field_im = contract("lka,am->lkm", field_in_im, cos_table) - contract(
        "lka,am->lkm", field_in_re, sin_table
    )
    factor = jnp.sqrt(image) / jnp.sqrt(field_re * field_re + field_im * field_im + 0.25) - 1.0
    diff_re = (field_re * factor).astype(jnp.bfloat16)
    diff_im = (field_im * factor).astype(jnp.bfloat16)
    back_re = (
        contract("lkm,ma->lka", diff_re, cos_table) - contract("lkm,ma->lka", diff_im, sin_table)
    ).astype(jnp.bfloat16)
    back_im = (
        contract("lkm,ma->lka", diff_im, cos_table) + contract("lkm,ma->lka", diff_re, sin_table)
    ).astype(jnp.bfloat16)
    return (back_re, back_im)


def body_any(spectrum, led_rows, led_cols, images):
    width = images.shape[2]
    slab_rows = spectrum.shape[1]
    columns = spectrum.shape[2]
    slabs = lax.axis_size("slab")
    total_rows = slab_rows * slabs
    position = lax.axis_index("slab")
    cos_table, sin_table = (jnp.asarray(t) for t in host_tables(width))
    own_rows = position * slab_rows + jnp.arange(slab_rows, dtype=jnp.int32)
    col_index = jnp.arange(width, dtype=jnp.int32)

    def take_cols(start):
        return lax.dynamic_slice_in_dim(spectrum, start, width, 2)

    def owner_mask(start):
        return make_pupil(own_rows - start, col_index, width)

    windows = jax.vmap(take_cols)(led_cols)
    masks = jax.vmap(owner_mask)(led_rows)
    win_re = (windows[:, 0] * masks).astype(jnp.bfloat16)
    win_im = (windows[:, 1] * masks).astype(jnp.bfloat16)

    def slice_strip(block, start):
        return take_rows(block, start, width)

    row_re = (
        contract("lgb,bk->lkg", win_re, cos_table) + contract("lgb,bk->lkg", win_im, sin_table)
    ).astype(jnp.bfloat16)
    row_im = (
        contract("lgb,bk->lkg", win_im, cos_table) - contract("lgb,bk->lkg", win_re, sin_table)
    ).astype(jnp.bfloat16)
    col_re, col_im = (
        lax.all_to_all(row_re, "slab", split_axis=1, concat_axis=2, tiled=True),
        lax.all_to_all(row_im, "slab", split_axis=1, concat_axis=2, tiled=True),
    )
    field_in_re = jax.vmap(slice_strip)(col_re, led_rows)
    field_in_im = jax.vmap(slice_strip)(col_im, led_rows)
    back_re, back_im = modulus_step(field_in_re, field_in_im, images, cos_table, sin_table)

    def place_strip(block, start):
        return place_rows(block, start, total_rows, 1)

    full_re = jax.vmap(place_strip)(back_re, led_rows)
    full_im = jax.vmap(place_strip)(back_im, led_rows)
    home_re, home_im = (
        lax.all_to_all(as_sent(full_re), "slab", split_axis=2, concat_axis=1, tiled=True).astype(
            full_re.dtype
        ),
        lax.all_to_all(as_sent(full_im), "slab", split_axis=2, concat_axis=1, tiled=True).astype(
            full_im.dtype
        ),
    )
    upd_re = contract("lkg,kb->lgb", home_re, cos_table) - contract(
        "lkg,kb->lgb", home_im, sin_table
    )
    upd_im = contract("lkg,kb->lgb", home_im, cos_table) + contract(
        "lkg,kb->lgb", home_re, sin_table
    )
    upd_re = upd_re * masks
    upd_im = upd_im * masks

    def add_window(number, gradient):
        start = led_cols[number]
        piece = jnp.stack([upd_re[number], upd_im[number]])
        current = lax.dynamic_slice_in_dim(gradient, start, width, 2)
        return lax.dynamic_update_slice_in_dim(gradient, current + piece, start, 2)

    gradient = lax.fori_loop(
        0, led_rows.shape[0], add_window, jnp.zeros((2, slab_rows, columns), jnp.float32)
    )
    summed = lax.psum_scatter(gradient, "led", scatter_dimension=2, tiled=True)
    share = summed.shape[2]
    own_part = lax.dynamic_slice_in_dim(spectrum, lax.axis_index("led") * share, share, 2)
    return own_part + summed


SLABS = 8
HALF = 4
FIRST, LAST = 0, 7
PASSED = {1: 0, 6: 7}
INNER = (2, 3, 4, 5)


def dot(left, right):
    return jnp.dot(left, right, preferred_element_type=jnp.float32)


def window_mask(first_row, row_start, col_start, rows, first_col, cols, width):
    shape = (rows, cols)
    at_row = lax.broadcasted_iota(jnp.int32, shape, 0) + (first_row - row_start)
    at_col = lax.broadcasted_iota(jnp.int32, shape, 1) + (first_col - col_start)
    wraps = at_col < 0
    at_col = jnp.where(wraps, at_col + width, at_col)
    row_term = 2 * at_row + 1 - width
    col_term = 2 * at_col + 1 - width
    return row_term * row_term + col_term * col_term < width * width, wraps


def row_block(window, table):
    both = dot(window, table)
    half = both.shape[0] // 2
    row_re = both[:half, :LANES] + both[half:, LANES:]
    row_im = both[half:, :LANES] - both[:half, LANES:]
    return row_re.astype(jnp.bfloat16), row_im.astype(jnp.bfloat16)


def store_parts(out, values):
    per = out.shape[0] // 2
    rows = out.shape[1]
    for plane, value in enumerate(values):
        for led in range(per):
            out[plane * per + led] = value[led * rows : (led + 1) * rows]


def is_one_of(position, slabs):
    return functools.reduce(jnp.logical_or, [position == slab for slab in slabs])


def window_kernel(starts, spectrum, window):
    position = lax.axis_index("slab")
    leds = starts.shape[0] // 2
    rows = spectrum.shape[1]
    width = window.shape[1]
    for led in range(leds):
        inside, wraps = window_mask(
            position * rows, starts[led], starts[leds + led], rows, 0, width, width
        )
        for plane in range(2):
            value = jnp.where(wraps, spectrum[plane, :, width:], spectrum[plane, :, :width])
            at = (plane * leds + led) * rows
            window[at : at + rows, :] = jnp.where(inside, value, 0.0).astype(jnp.bfloat16)


def classes_of(position):
    hands_over = is_one_of(position, PASSED)
    return (jnp.where(hands_over, 5, 6), 7, 2, 4, jnp.where(hands_over, 6, 5), 0, 1, 3)


def rows_kernel(which, window, table, *outs):
    position = lax.axis_index("slab")
    for out, d in zip(outs, classes_of(position)[which]):
        store_parts(out, row_block(window[...], table[jnp.bitwise_xor(position, d)]))


def choose_kernel(got, own, out):
    passes = is_one_of(lax.axis_index("slab"), PASSED.values())

    @pl.when(passes)
    def _():
        out[...] = got[...]

    @pl.when(jnp.logical_not(passes))
    def _():
        out[...] = own[...]


def amplitude_kernel(images, table, out, table_out):
    leds, block, width = images.shape
    for led in range(leds):
        for j in range(width // LANES):
            piece = jnp.sqrt(images[led, :, j * LANES : (j + 1) * LANES])
            out[j * LANES : (j + 1) * LANES, led * block : (led + 1) * block] = piece.T
    table_out[...] = table[...]


def field_kernel(amplitude, table, *rest):
    far, near = rest[:5], rest[5 : HALF + 5]
    outs = rest[HALF + 5 : 2 * HALF + 5]
    field_in, diff, strips = rest[2 * HALF + 5 :]
    position = lax.axis_index("slab")
    parts, rows, _ = near[0].shape
    half = parts // 2 * LANES
    width = field_in.shape[0]
    steps = width // LANES
    group = 4
    for d, block in enumerate(near):
        at = pl.multiple_of(jnp.bitwise_and(jnp.bitwise_xor(position, d), HALF - 1) * rows, rows)
        for part in range(parts):
            cols = slice(part * LANES, (part + 1) * LANES)
            field_in[pl.ds(at, rows), cols] = block[part]

    def add(block, origin):
        at = pl.multiple_of(jnp.bitwise_and(origin, HALF - 1) * rows, rows)
        for part in range(parts):
            cols = slice(part * LANES, (part + 1) * LANES)
            field_in[pl.ds(at, rows), cols] += block[part]

    passes = is_one_of(position, PASSED.values())
    hands_over = is_one_of(position, PASSED)
    ends = is_one_of(position, [to ^ 4 for to in PASSED.values()])

    @pl.when(is_one_of(position, INNER))
    def _():
        add(far[0], jnp.bitwise_xor(position, 6))
        add(far[1], jnp.bitwise_xor(position, 7))
        add(far[2], jnp.bitwise_xor(position, jnp.where(ends, 5, 4)))

    @pl.when(jnp.logical_or(passes, hands_over))
    def _():
        add(far[2], jnp.bitwise_xor(position, 4))
        add(far[3], jnp.bitwise_xor(position, jnp.where(hands_over, 7, 6)))
        add(far[4], jnp.bitwise_xor(position, 5))

    for first in range(0, steps, group):
        product = dot(
            table[first : first + group].reshape(group * 2 * LANES, width), field_in[...]
        )
        for j in range(first, first + group):
            both = product[(j - first) * 2 * LANES : (j - first + 1) * 2 * LANES]
            field_re = both[:LANES, :half] + both[LANES:, half:]
            field_im = both[:LANES, half:] - both[LANES:, :half]
            here = pl.ds(j * LANES, LANES)
            factor = (
                amplitude[here, :] * lax.rsqrt(field_re * field_re + field_im * field_im + 0.25)
                - 1.0
            )
            diff[here, :half] = (field_re * factor).astype(jnp.bfloat16)
            diff[here, half:] = (field_im * factor).astype(jnp.bfloat16)
    pieces = rows // LANES
    for i in range(HALF):
        product = dot(
            table[i * pieces : (i + 1) * pieces].reshape(pieces * 2 * LANES, width), diff[...]
        )
        for h in range(pieces):
            both = product[h * 2 * LANES : (h + 1) * 2 * LANES]
            here = pl.ds(h * LANES, LANES)
            back_re = (both[:LANES, :half] - both[LANES:, half:]).astype(jnp.bfloat16)
            back_im = (both[:LANES, half:] + both[LANES:, :half]).astype(jnp.bfloat16)
            for part in range(parts // 2):
                cols = slice(part * LANES, (part + 1) * LANES)
                strips[i, part, here, :] = back_re[:, cols]
                strips[i, parts // 2 + part, here, :] = back_im[:, cols]
    for d, out in enumerate(outs):
        out[...] = strips[jnp.bitwise_and(jnp.bitwise_xor(position, d), HALF - 1)]


def update_columns(own_core, starts, table, back, outs):
    position = lax.axis_index("slab")
    led_at = lax.axis_index("led")
    core = jnp.bitwise_and(led_at, 1)
    plane_x = jnp.right_shift(led_at, 1)
    which_half = jnp.right_shift(position, 2)
    first_row = jnp.bitwise_and(position, HALF - 1)
    leds = starts.shape[0] // 2
    rows = back.shape[0] // (2 * leds)
    depth = back.shape[1]
    width = table.shape[1]
    group = width // LANES // 2
    owner = core if own_core else 1 - core
    shape = (rows, LANES)
    for n in range(group):
        block = owner * group + n
        both = dot(
            back[...], table[block, pl.ds(pl.multiple_of(which_half * depth, depth), depth)]
        )
        half = leds * rows
        update = (
            both[:half, :LANES] - both[half:, LANES:],
            both[half:, :LANES] + both[:half, LANES:],
        )
        sums = [[0.0, 0.0] for _ in outs]
        for led in range(leds):
            at_row = lax.broadcasted_iota(jnp.int32, shape, 0) + (
                first_row * rows - starts[led]
            )
            at_col = lax.broadcasted_iota(jnp.int32, shape, 1) + (
                block * LANES - starts[leds + led]
            )
            row_term = 2 * jnp.where(at_row < 0, at_row + width, at_row) + 1 - width
            col_term = 2 * jnp.where(at_col < 0, at_col + width, at_col) + 1 - width
            inside = row_term * row_term + col_term * col_term < width * width
            this_slab = jnp.where(at_row < 0, 1, 0) == which_half
            this_x = jnp.where(at_col < 0, 1, 0) == plane_x
            for plane in range(2):
                piece = jnp.where(inside, update[plane][led * rows : (led + 1) * rows], 0.0)
                for i, at_slab in enumerate(
                    (jnp.where(this_slab, piece, 0.0), jnp.where(this_slab, 0.0, piece))
                ):
                    sums[2 * i][plane] += jnp.where(this_x, at_slab, 0.0)
                    sums[2 * i + 1][plane] += jnp.where(this_x, 0.0, at_slab)
        cols = slice(n * LANES, (n + 1) * LANES)
        for out, both_planes in zip(outs, sums):
            for plane in range(2):
                out[plane, :, cols] = both_planes[plane].astype(out.dtype)


def sent_kernel(starts, table, *rest):
    blocks = rest[:HALF]
    this_slab, that_slab, back = rest[HALF:]
    position = lax.axis_index("slab")
    parts, rows, _ = blocks[0].shape
    for d, block in enumerate(blocks):
        source = jnp.bitwise_and(jnp.bitwise_xor(position, d), HALF - 1)
        at = pl.multiple_of(source * LANES, LANES)
        for part in range(parts):
            back[part * rows : (part + 1) * rows, pl.ds(at, LANES)] = block[part]
    outs = [out.at[i] for out in (this_slab, that_slab) for i in range(2)]
    update_columns(False, starts, table, back, outs)


def kept_kernel(starts, table, back, *outs):
    update_columns(True, starts, table, back, outs)


def local_call(kernel, out_shape, spaces, scratch, flops, moved, name):
    return pl.pallas_call(
        kernel,
        out_shape=out_shape,
        in_specs=[pl.BlockSpec(memory_space=space) for space in spaces],
        out_specs=jax.tree.map(lambda _: pl.BlockSpec(memory_space=pltpu.VMEM), out_shape),
        scratch_shapes=scratch,
        compiler_params=pltpu.CompilerParams(vmem_limit_bytes=32 * 2**20),
        cost_estimate=pl.CostEstimate(flops=flops, bytes_accessed=moved, transcendentals=0),
        name=name,
    )


def body_slabs(spectrum, led_rows, led_cols, images):
    leds, block, width = images.shape
    rows = spectrum.shape[1]
    led_at = lax.axis_index("led")
    bf16 = jnp.bfloat16
    vmem, smem = pltpu.VMEM, pltpu.SMEM
    cos_table, sin_table = host_tables(width)
    steps = width // LANES
    by_col = np.stack(
        [
            np.concatenate([t[:, j * LANES : (j + 1) * LANES] for t in (cos_table, sin_table)], 1)
            for j in range(steps)
        ]
    )
    by_row = jnp.asarray(np.ascontiguousarray(by_col.transpose(0, 2, 1)))
    by_col = jnp.asarray(by_col)
    parts = 2 * leds
    sent_block = jax.ShapeDtypeStruct((parts, rows, LANES), bf16)
    flops = 8 * leds * rows * width * width

    starts = jnp.concatenate([led_rows, led_cols]).astype(jnp.int32)
    window = local_call(
        window_kernel,
        jax.ShapeDtypeStruct((parts * rows, width), bf16),
        [smem, vmem],
        [],
        0,
        6 * 2**20,
        "windows",
    )(starts, spectrum)

    def rows_call(which, name):
        count = which.stop - which.start
        return local_call(
            functools.partial(rows_kernel, which),
            [sent_block] * count,
            [vmem, vmem],
            [],
            flops * count // SLABS,
            5 * 2**20,
            name,
        )(window, by_col)

    first_a, first_b, near_2 = rows_call(slice(0, 3), "rows_round_1")

    def permute(sent, pairs):
        return lax.ppermute(sent, "slab", pairs)

    def choose(got, own, name):
        return local_call(
            choose_kernel, sent_block, [vmem] * 2, [], 0, 2**19, name
        )(got, own)

    handed = list(PASSED.items())
    windowed = range(FIRST + 1, LAST)
    got_a = permute(first_a, [(s, s ^ 6) for s in INNER] + handed)
    got_b = permute(first_b, [(s, s ^ 7) for s in INNER] + handed)
    near_2 = permute(near_2, [(s, s ^ 2) for s in windowed])
    second_a, second_b, near_0, near_1, near_3 = rows_call(slice(3, SLABS), "rows_round_2")
    got_a, second_a, second_b, near_1, near_3, images = lax.optimization_barrier(
        (got_a, second_a, second_b, near_1, near_3, images)
    )
    outer_pairs = [(s, s ^ 6) for s in range(SLABS) if s not in INNER]
    far_columns = [
        got_a,
        got_b,
        permute(choose(got_a, second_a, "class_4_blocks"), [(s, s ^ 4) for s in range(SLABS)]),
        permute(choose(got_b, second_b, "class_6_blocks"), outer_pairs),
        permute(second_b, [(s, s ^ 5) for s in INNER]),
    ]
    near_1 = permute(near_1, [(s, s ^ 1) for s in windowed])
    near_3 = permute(near_3, [(s, s ^ 3) for s in windowed])
    near_columns = [near_0, near_1, near_2, near_3]
    amplitude, by_row = local_call(
        amplitude_kernel,
        [
            jax.ShapeDtypeStruct((width, leds * block), jnp.float32),
            jax.ShapeDtypeStruct(by_row.shape, bf16),
        ],
        [vmem] * 2,
        [],
        0,
        10 * 2**20,
        "amplitude",
    )(images, by_row)
    strips = local_call(
        field_kernel,
        [sent_block] * HALF,
        [vmem] * 11,
        [pltpu.VMEM((width, parts * block), bf16)] * 2
        + [pltpu.VMEM((HALF,) + sent_block.shape, bf16)],
        16 * leds * block * width * width,
        12 * 2**20,
        "modulus_step",
    )(amplitude, by_row, *far_columns, *near_columns)

    def send_home(d):
        pairs = [(s, (s + d) % SLABS) for s in range(SLABS) if FIRST < (s + d) % SLABS < LAST]
        return permute(strips[d % HALF], pairs)

    home = [strips[0]]
    home += [
        permute(strips[d], [(s, s ^ d) for s in range(SLABS)]) for d in range(1, HALF)
    ]
    share = width // 2
    piece = (2, rows, share)
    sent_this, sent_that, back = local_call(
        sent_kernel,
        [
            jax.ShapeDtypeStruct((2,) + piece, bf16),
            jax.ShapeDtypeStruct((2,) + piece, bf16),
            jax.ShapeDtypeStruct((parts * rows, HALF * LANES), bf16),
        ],
        [smem] + [vmem] * (1 + HALF),
        [],
        flops // 4,
        8 * 2**20,
        "update_sent",
    )(starts, by_col, *home)
    cores = [(0, 1), (1, 0), (2, 3), (3, 2)]
    planes = [(0, 2), (2, 0), (1, 3), (3, 1)]
    got_that = lax.ppermute(sent_that, "led", cores)
    got_this = lax.ppermute(sent_this, "led", cores)
    this_near, this_far, that_near, that_far = local_call(
        kept_kernel,
        [jax.ShapeDtypeStruct(piece, jnp.float32)] * 4,
        [smem, vmem, vmem],
        [],
        flops // 4,
        10 * 2**20,
        "update_kept",
    )(starts, by_col, back)

    def summed(*values):
        return sum(value.astype(jnp.float32) for value in values)

    across = [(s, s ^ 4) for s in range(SLABS) if FIRST < s ^ 4 < LAST]
    from_x = []
    for i in range(2):
        here = slice(i * rows // 2, (i + 1) * rows // 2)
        over = summed(that_far[:, here], got_that[1, :, here]).astype(bf16)
        from_x.append((here, lax.ppermute(over, "led", planes)))
    from_z = []
    over = None
    over_this = summed(this_far, got_this[1]).astype(bf16)
    for here, got in from_x:
        if over is None:
            got, over_this = lax.optimization_barrier((got, over_this))
        else:
            over, got = lax.optimization_barrier((over, got))
        over = summed(that_near[:, here], got_that[0, :, here], got).astype(bf16)
        from_z.append(permute(over, across))
    over_this = lax.ppermute(over_this, "led", planes)
    own_part = lax.dynamic_slice_in_dim(spectrum, led_at * share, share, 2)
    base = own_part + summed(this_near, got_this[0], over_this)
    base, *from_z = lax.optimization_barrier((base, *from_z))
    return base + summed(jnp.concatenate(from_z, 1))


def solution(mesh):
    placed = (P(None, "slab", None), P("led"), P("led"), P("led", "slab", None))
    fits = mesh.shape["slab"] == 8 and mesh.shape["led"] == 4

    def body(spectrum, led_rows, led_cols, images):
        shapes = (spectrum.shape, images.shape)
        if fits and shapes == ((2, 256, 2048), (2, 128, 1024)):
            return body_slabs(spectrum, led_rows, led_cols, images)
        return body_any(spectrum, led_rows, led_cols, images)

    return jax.shard_map(
        body, mesh=mesh, in_specs=placed, out_specs=P(None, "slab", "led"), check_vma=False
    )
```

```python
import functools

import jax
import jax.numpy as jnp
import numpy as np
from jax import lax
from jax.experimental import pallas as pl
from jax.experimental.pallas import tpu as pltpu
from jax.sharding import PartitionSpec as P

LANES = 128


def as_sent(value):
    return jax.tree.map(lambda a: a.astype(jnp.bfloat16) if a.dtype == jnp.float32 else a, value)


def host_tables(width):
    index = np.arange(width, dtype=np.int64)
    angle_index = (index[:, None] * index[None, :] % width).astype(np.float32)
    angle = angle_index * np.float32(2.0 * 3.141592653589793 / width)
    scale = np.float32(1.0) / np.sqrt(np.float32(width))
    return (
        (np.cos(angle) * scale).astype(jnp.bfloat16),
        (np.sin(angle) * scale).astype(jnp.bfloat16),
    )


def make_pupil(row_index, col_index, width):
    row_term = (2 * row_index + 1 - width) * (2 * row_index + 1 - width)
    col_term = (2 * col_index + 1 - width) * (2 * col_index + 1 - width)
    return (row_term[:, None] + col_term[None, :] < width * width).astype(jnp.float32)


def contract(form, left, right):
    return jnp.einsum(form, left, right, preferred_element_type=jnp.float32)


def take_rows(strip, start, width):
    return lax.dynamic_slice_in_dim(strip, start, width, 1)


def place_rows(block, start, total, axis_dim):
    shape = list(block.shape)
    shape[axis_dim] = total
    holder = jnp.zeros(tuple(shape), block.dtype)
    return lax.dynamic_update_slice_in_dim(holder, block, start, axis_dim)


def modulus_step(field_in_re, field_in_im, image, cos_table, sin_table):
    field_re = contract("lka,am->lkm", field_in_re, cos_table) + contract(
        "lka,am->lkm", field_in_im, sin_table
    )
    field_im = contract("lka,am->lkm", field_in_im, cos_table) - contract(
        "lka,am->lkm", field_in_re, sin_table
    )
    factor = jnp.sqrt(image) / jnp.sqrt(field_re * field_re + field_im * field_im + 0.25) - 1.0
    diff_re = (field_re * factor).astype(jnp.bfloat16)
    diff_im = (field_im * factor).astype(jnp.bfloat16)
    back_re = (
        contract("lkm,ma->lka", diff_re, cos_table) - contract("lkm,ma->lka", diff_im, sin_table)
    ).astype(jnp.bfloat16)
    back_im = (
        contract("lkm,ma->lka", diff_im, cos_table) + contract("lkm,ma->lka", diff_re, sin_table)
    ).astype(jnp.bfloat16)
    return (back_re, back_im)


def body_any(spectrum, led_rows, led_cols, images):
    width = images.shape[2]
    slab_rows = spectrum.shape[1]
    columns = spectrum.shape[2]
    slabs = lax.axis_size("slab")
    total_rows = slab_rows * slabs
    position = lax.axis_index("slab")
    cos_table, sin_table = (jnp.asarray(t) for t in host_tables(width))
    own_rows = position * slab_rows + jnp.arange(slab_rows, dtype=jnp.int32)
    col_index = jnp.arange(width, dtype=jnp.int32)

    def take_cols(start):
        return lax.dynamic_slice_in_dim(spectrum, start, width, 2)

    def owner_mask(start):
        return make_pupil(own_rows - start, col_index, width)

    windows = jax.vmap(take_cols)(led_cols)
    masks = jax.vmap(owner_mask)(led_rows)
    win_re = (windows[:, 0] * masks).astype(jnp.bfloat16)
    win_im = (windows[:, 1] * masks).astype(jnp.bfloat16)

    def slice_strip(block, start):
        return take_rows(block, start, width)

    row_re = (
        contract("lgb,bk->lkg", win_re, cos_table) + contract("lgb,bk->lkg", win_im, sin_table)
    ).astype(jnp.bfloat16)
    row_im = (
        contract("lgb,bk->lkg", win_im, cos_table) - contract("lgb,bk->lkg", win_re, sin_table)
    ).astype(jnp.bfloat16)
    col_re, col_im = (
        lax.all_to_all(row_re, "slab", split_axis=1, concat_axis=2, tiled=True),
        lax.all_to_all(row_im, "slab", split_axis=1, concat_axis=2, tiled=True),
    )
    field_in_re = jax.vmap(slice_strip)(col_re, led_rows)
    field_in_im = jax.vmap(slice_strip)(col_im, led_rows)
    back_re, back_im = modulus_step(field_in_re, field_in_im, images, cos_table, sin_table)

    def place_strip(block, start):
        return place_rows(block, start, total_rows, 1)

    full_re = jax.vmap(place_strip)(back_re, led_rows)
    full_im = jax.vmap(place_strip)(back_im, led_rows)
    home_re, home_im = (
        lax.all_to_all(as_sent(full_re), "slab", split_axis=2, concat_axis=1, tiled=True).astype(
            full_re.dtype
        ),
        lax.all_to_all(as_sent(full_im), "slab", split_axis=2, concat_axis=1, tiled=True).astype(
            full_im.dtype
        ),
    )
    upd_re = contract("lkg,kb->lgb", home_re, cos_table) - contract(
        "lkg,kb->lgb", home_im, sin_table
    )
    upd_im = contract("lkg,kb->lgb", home_im, cos_table) + contract(
        "lkg,kb->lgb", home_re, sin_table
    )
    upd_re = upd_re * masks
    upd_im = upd_im * masks

    def add_window(number, gradient):
        start = led_cols[number]
        piece = jnp.stack([upd_re[number], upd_im[number]])
        current = lax.dynamic_slice_in_dim(gradient, start, width, 2)
        return lax.dynamic_update_slice_in_dim(gradient, current + piece, start, 2)

    gradient = lax.fori_loop(
        0, led_rows.shape[0], add_window, jnp.zeros((2, slab_rows, columns), jnp.float32)
    )
    summed = lax.psum_scatter(gradient, "led", scatter_dimension=2, tiled=True)
    share = summed.shape[2]
    own_part = lax.dynamic_slice_in_dim(spectrum, lax.axis_index("led") * share, share, 2)
    return own_part + summed


SLABS = 8
HALF = 4
FIRST, LAST = 0, 7
HANDED = {1: (0, 4), 6: (7, 3)}
FAR = (
    {1: 4, 2: 4, 3: 5, 4: 2, 5: 3, 6: 3},
    {1: 6, 2: 7, 3: 4, 4: 3, 5: 0, 6: 1},
    {1: 7, 2: 5, 3: 6, 4: 1, 5: 2, 6: 0},
    {1: 5, 2: 6, 3: 7, 4: 0, 5: 1, 6: 2},
)


def look_up(position, table):
    return sum(jnp.where(position == slab, value, 0) for slab, value in table.items())


def origins(far):
    table = {to: slab for slab, to in far.items()}
    if far is FAR[0]:
        table = {to: slab for slab, to in far.items() if slab not in HANDED}
    if far is FAR[-1]:
        table.update({to: slab for slab, (_, to) in HANDED.items()})
    return table


def dot(left, right):
    return jnp.dot(left, right, preferred_element_type=jnp.float32)


def window_mask(first_row, row_start, col_start, rows, first_col, cols, width):
    shape = (rows, cols)
    at_row = lax.broadcasted_iota(jnp.int32, shape, 0) + (first_row - row_start)
    at_col = lax.broadcasted_iota(jnp.int32, shape, 1) + (first_col - col_start)
    wraps = at_col < 0
    at_col = jnp.where(wraps, at_col + width, at_col)
    row_term = 2 * at_row + 1 - width
    col_term = 2 * at_col + 1 - width
    return row_term * row_term + col_term * col_term < width * width, wraps


def row_block(window, table):
    both = dot(window, table)
    half = both.shape[0] // 2
    row_re = both[:half, :LANES] + both[half:, LANES:]
    row_im = both[half:, :LANES] - both[:half, LANES:]
    return row_re.astype(jnp.bfloat16), row_im.astype(jnp.bfloat16)


def store_parts(out, values):
    per = out.shape[0] // 2
    rows = out.shape[1]
    for plane, value in enumerate(values):
        for led in range(per):
            out[plane * per + led] = value[led * rows : (led + 1) * rows]


def is_one_of(position, slabs):
    return functools.reduce(jnp.logical_or, [position == slab for slab in slabs])


def window_kernel(starts, spectrum, window):
    position = lax.axis_index("slab")
    leds = starts.shape[0] // 2
    rows = spectrum.shape[1]
    width = window.shape[1]
    for led in range(leds):
        inside, wraps = window_mask(
            position * rows, starts[led], starts[leds + led], rows, 0, width, width
        )
        for plane in range(2):
            value = jnp.where(wraps, spectrum[plane, :, width:], spectrum[plane, :, :width])
            at = (plane * leds + led) * rows
            window[at : at + rows, :] = jnp.where(inside, value, 0.0).astype(jnp.bfloat16)


def rows_kernel(which, window, table, *outs):
    position = lax.axis_index("slab")
    blocks = [look_up(position, far) for far in FAR]
    blocks += [jnp.bitwise_xor(position, d) for d in (0, 2, 1, 3)]
    for out, block in zip(outs, blocks[which]):
        store_parts(out, row_block(window[...], table[block]))


def choose_kernel(got, own, out):
    passes = is_one_of(lax.axis_index("slab"), [by for by, _ in HANDED.values()])

    @pl.when(passes)
    def _():
        out[...] = got[...]

    @pl.when(jnp.logical_not(passes))
    def _():
        out[...] = own[...]


def amplitude_kernel(images, table, out, table_out):
    leds, block, width = images.shape
    for led in range(leds):
        for j in range(width // LANES):
            piece = jnp.sqrt(images[led, :, j * LANES : (j + 1) * LANES])
            out[j * LANES : (j + 1) * LANES, led * block : (led + 1) * block] = piece.T
    table_out[...] = table[...]


def field_kernel(amplitude, table, *rest):
    far, near = rest[: len(FAR)], rest[len(FAR) : len(FAR) + HALF]
    outs = rest[len(FAR) + HALF : len(FAR) + 2 * HALF]
    field_in, diff, strips = rest[len(FAR) + 2 * HALF :]
    position = lax.axis_index("slab")
    parts, rows, _ = near[0].shape
    half = parts // 2 * LANES
    width = field_in.shape[0]
    steps = width // LANES
    group = 4
    for d, block in enumerate(near):
        at = pl.multiple_of(jnp.bitwise_and(jnp.bitwise_xor(position, d), HALF - 1) * rows, rows)
        for part in range(parts):
            cols = slice(part * LANES, (part + 1) * LANES)
            field_in[pl.ds(at, rows), cols] = block[part]

    def add(block, origin):
        at = pl.multiple_of(jnp.bitwise_and(origin, HALF - 1) * rows, rows)
        for part in range(parts):
            cols = slice(part * LANES, (part + 1) * LANES)
            field_in[pl.ds(at, rows), cols] += block[part]

    for block, permute in zip(far, FAR):
        table_of = origins(permute)

        @pl.when(is_one_of(position, table_of))
        def _():
            add(block, look_up(position, table_of))

    for first in range(0, steps, group):
        product = dot(
            table[first : first + group].reshape(group * 2 * LANES, width), field_in[...]
        )
        for j in range(first, first + group):
            both = product[(j - first) * 2 * LANES : (j - first + 1) * 2 * LANES]
            field_re = both[:LANES, :half] + both[LANES:, half:]
            field_im = both[:LANES, half:] - both[LANES:, :half]
            here = pl.ds(j * LANES, LANES)
            factor = (
                amplitude[here, :] * lax.rsqrt(field_re * field_re + field_im * field_im + 0.25)
                - 1.0
            )
            diff[here, :half] = (field_re * factor).astype(jnp.bfloat16)
            diff[here, half:] = (field_im * factor).astype(jnp.bfloat16)
    pieces = rows // LANES
    for i in range(HALF):
        product = dot(
            table[i * pieces : (i + 1) * pieces].reshape(pieces * 2 * LANES, width), diff[...]
        )
        for h in range(pieces):
            both = product[h * 2 * LANES : (h + 1) * 2 * LANES]
            here = pl.ds(h * LANES, LANES)
            back_re = (both[:LANES, :half] - both[LANES:, half:]).astype(jnp.bfloat16)
            back_im = (both[:LANES, half:] + both[LANES:, :half]).astype(jnp.bfloat16)
            for part in range(parts // 2):
                cols = slice(part * LANES, (part + 1) * LANES)
                strips[i, part, here, :] = back_re[:, cols]
                strips[i, parts // 2 + part, here, :] = back_im[:, cols]
    for d, out in enumerate(outs):
        out[...] = strips[jnp.bitwise_and(jnp.bitwise_xor(position, d), HALF - 1)]


def update_columns(own_core, row_half, starts, table, back, outs):
    position = lax.axis_index("slab")
    led_at = lax.axis_index("led")
    core = jnp.bitwise_and(led_at, 1)
    plane_x = jnp.right_shift(led_at, 1)
    which_half = jnp.right_shift(position, 2)
    leds = starts.shape[0] // 2
    rows = back.shape[0] // (2 * leds)
    first_row = (jnp.bitwise_and(position, HALF - 1) * 2 + row_half) * rows
    depth = back.shape[1]
    width = table.shape[1]
    group = width // LANES // 2
    owner = core if own_core else 1 - core
    shape = (rows, LANES)
    for n in range(group):
        block = owner * group + n
        both = dot(
            back[...], table[block, pl.ds(pl.multiple_of(which_half * depth, depth), depth)]
        )
        half = leds * rows
        update = (
            both[:half, :LANES] - both[half:, LANES:],
            both[half:, :LANES] + both[:half, LANES:],
        )
        sums = [[0.0, 0.0] for _ in outs]
        for led in range(leds):
            at_row = lax.broadcasted_iota(jnp.int32, shape, 0) + (first_row - starts[led])
            at_col = lax.broadcasted_iota(jnp.int32, shape, 1) + (
                block * LANES - starts[leds + led]
            )
            row_term = 2 * jnp.where(at_row < 0, at_row + width, at_row) + 1 - width
            col_term = 2 * jnp.where(at_col < 0, at_col + width, at_col) + 1 - width
            inside = row_term * row_term + col_term * col_term < width * width
            this_slab = jnp.where(at_row < 0, 1, 0) == which_half
            this_x = jnp.where(at_col < 0, 1, 0) == plane_x
            for plane in range(2):
                piece = jnp.where(inside, update[plane][led * rows : (led + 1) * rows], 0.0)
                for i, at_slab in enumerate(
                    (jnp.where(this_slab, piece, 0.0), jnp.where(this_slab, 0.0, piece))
                ):
                    sums[2 * i][plane] += jnp.where(this_x, at_slab, 0.0)
                    sums[2 * i + 1][plane] += jnp.where(this_x, 0.0, at_slab)
        cols = slice(n * LANES, (n + 1) * LANES)
        for out, both_planes in zip(outs, sums):
            for plane in range(2):
                out[plane, :, cols] = both_planes[plane].astype(out.dtype)


def sent_kernel(row_half, starts, table, *rest):
    blocks = rest[:HALF]
    this_slab, that_slab, back = rest[HALF:]
    position = lax.axis_index("slab")
    parts, rows, _ = blocks[0].shape
    rows = rows // 2
    for d, block in enumerate(blocks):
        source = jnp.bitwise_and(jnp.bitwise_xor(position, d), HALF - 1)
        at = pl.multiple_of(source * LANES, LANES)
        for part in range(parts):
            back[part * rows : (part + 1) * rows, pl.ds(at, LANES)] = block[
                part, row_half * rows : (row_half + 1) * rows
            ]
    outs = [out.at[i] for out in (this_slab, that_slab) for i in range(2)]
    update_columns(False, row_half, starts, table, back, outs)


def kept_kernel(row_half, starts, table, back, *outs):
    update_columns(True, row_half, starts, table, back, outs)


def sum_kernel(picks, *refs):
    total = 0.0
    for ref, pick in zip(refs, picks):
        value = ref[...] if pick is None else ref[pick]
        total = total + value.astype(jnp.float32)
    refs[-1][...] = total.astype(refs[-1].dtype)


def final_kernel(*refs):
    base, got, out = refs[-3:]
    out[...] = base[...] + got[...].astype(jnp.float32)


def final_call(row_half, before, base, got):
    planes, rows, share = base.shape
    vmem = pl.BlockSpec(memory_space=pltpu.VMEM)
    first = before is None
    return pl.pallas_call(
        final_kernel,
        out_shape=jax.ShapeDtypeStruct((planes, 2 * rows, share), base.dtype),
        grid=(1,),
        in_specs=([] if first else [pl.BlockSpec(memory_space=pl.ANY)]) + [vmem] * 2,
        out_specs=pl.BlockSpec((planes, rows, share), lambda _: (0, row_half, 0)),
        input_output_aliases={} if first else {0: 0},
        cost_estimate=pl.CostEstimate(flops=0, bytes_accessed=2**20, transcendentals=0),
        name=f"updated_{row_half}",
    )(*([] if first else [before]), base, got)


def local_call(kernel, out_shape, spaces, scratch, flops, moved, name):
    return pl.pallas_call(
        kernel,
        out_shape=out_shape,
        in_specs=[pl.BlockSpec(memory_space=space) for space in spaces],
        out_specs=jax.tree.map(lambda _: pl.BlockSpec(memory_space=pltpu.VMEM), out_shape),
        scratch_shapes=scratch,
        compiler_params=pltpu.CompilerParams(vmem_limit_bytes=32 * 2**20),
        cost_estimate=pl.CostEstimate(flops=flops, bytes_accessed=moved, transcendentals=0),
        name=name,
    )


def body_slabs(spectrum, led_rows, led_cols, images):
    leds, block, width = images.shape
    rows = spectrum.shape[1]
    led_at = lax.axis_index("led")
    bf16 = jnp.bfloat16
    vmem, smem = pltpu.VMEM, pltpu.SMEM
    cos_table, sin_table = host_tables(width)
    steps = width // LANES
    by_col = np.stack(
        [
            np.concatenate([t[:, j * LANES : (j + 1) * LANES] for t in (cos_table, sin_table)], 1)
            for j in range(steps)
        ]
    )
    by_row = jnp.asarray(np.ascontiguousarray(by_col.transpose(0, 2, 1)))
    by_col = jnp.asarray(by_col)
    parts = 2 * leds
    sent_block = jax.ShapeDtypeStruct((parts, rows, LANES), bf16)
    flops = 8 * leds * rows * width * width

    starts = jnp.concatenate([led_rows, led_cols]).astype(jnp.int32)
    window = local_call(
        window_kernel,
        jax.ShapeDtypeStruct((parts * rows, width), bf16),
        [smem, vmem],
        [],
        0,
        6 * 2**20,
        "windows",
    )(starts, spectrum)

    def rows_call(which, name):
        count = which.stop - which.start
        return local_call(
            functools.partial(rows_kernel, which),
            [sent_block] * count,
            [vmem, vmem],
            [],
            flops * count // SLABS,
            5 * 2**20,
            name,
        )(window, by_col)

    far_sent = list(rows_call(slice(0, 3), "rows_far"))

    def permute(sent, pairs):
        return lax.ppermute(sent, "slab", pairs)

    def choose(got, own, name):
        return local_call(
            choose_kernel, sent_block, [vmem] * 2, [], 0, 2**19, name
        )(got, own)

    windowed = range(FIRST + 1, LAST)
    far_columns = []
    for far, sent in zip(FAR, far_sent):
        pairs = dict(far)
        if far is FAR[0]:
            pairs.update({slab: by for slab, (by, _) in HANDED.items()})
        far_columns.append(permute(sent, list(pairs.items())))
    last, near_0, near_2, near_1, near_3 = rows_call(slice(3, SLABS), "rows_near")
    near_2 = permute(near_2, [(s, s ^ 2) for s in windowed])
    far_columns[0], last, near_1, near_3, images = lax.optimization_barrier(
        (far_columns[0], last, near_1, near_3, images)
    )
    last = local_call(
        choose_kernel, sent_block, [vmem] * 2, [], 0, 2**19, "last_far_blocks"
    )(far_columns[0], last)
    pairs = list(FAR[-1].items()) + list(HANDED.values())
    far_columns.append(permute(last, pairs))
    near_1 = permute(near_1, [(s, s ^ 1) for s in windowed])
    near_3 = permute(near_3, [(s, s ^ 3) for s in windowed])
    near_columns = [near_0, near_1, near_2, near_3]
    amplitude, by_row = local_call(
        amplitude_kernel,
        [
            jax.ShapeDtypeStruct((width, leds * block), jnp.float32),
            jax.ShapeDtypeStruct(by_row.shape, bf16),
        ],
        [vmem] * 2,
        [],
        0,
        10 * 2**20,
        "amplitude",
    )(images, by_row)
    strips = local_call(
        field_kernel,
        [sent_block] * HALF,
        [vmem] * (2 + len(FAR) + HALF),
        [pltpu.VMEM((width, parts * block), bf16)] * 2
        + [pltpu.VMEM((HALF,) + sent_block.shape, bf16)],
        16 * leds * block * width * width,
        12 * 2**20,
        "modulus_step",
    )(amplitude, by_row, *far_columns, *near_columns)

    def send_home(d):
        pairs = [(s, (s + d) % SLABS) for s in range(SLABS) if FIRST < (s + d) % SLABS < LAST]
        return permute(strips[d % HALF], pairs)

    home = [strips[0]]
    home += [
        permute(strips[d], [(s, s ^ d) for s in range(SLABS)]) for d in range(1, HALF)
    ]
    share = width // 2
    piece = (2, rows // 2, share)
    cores = [(0, 1), (1, 0), (2, 3), (3, 2)]
    planes = [(0, 2), (2, 0), (1, 3), (3, 1)]

    def summed(*values):
        return sum(value.astype(jnp.float32) for value in values)

    def sum_call(values, picks, name):
        return local_call(
            functools.partial(sum_kernel, picks),
            jax.ShapeDtypeStruct(piece, bf16),
            [vmem] * len(values),
            [],
            0,
            2**20,
            name,
        )(*values)

    halves = []
    for i in range(2):
        sent_this, sent_that, back = local_call(
            functools.partial(sent_kernel, i),
            [
                jax.ShapeDtypeStruct((2,) + piece, bf16),
                jax.ShapeDtypeStruct((2,) + piece, bf16),
                jax.ShapeDtypeStruct((parts * rows // 2, HALF * LANES), bf16),
            ],
            [smem] + [vmem] * (1 + HALF),
            [],
            flops // 8,
            6 * 2**20,
            f"update_sent_{i}",
        )(starts, by_col, *home)
        got_that = lax.ppermute(sent_that, "led", cores)
        halves.append((back, sent_this, got_that))
    across = [(s, s ^ 4) for s in range(SLABS) if FIRST < s ^ 4 < LAST]
    own_part = lax.dynamic_slice_in_dim(spectrum, led_at * share, share, 2)
    from_z = []
    base = []
    over_x = None
    for i, (back, sent_this, got_that) in enumerate(halves):
        if i:
            over_x, back = lax.optimization_barrier((over_x, back))
        this_near, this_far, that_near, that_far = local_call(
            functools.partial(kept_kernel, i),
            [jax.ShapeDtypeStruct(piece, jnp.float32)] * 4,
            [smem, vmem, vmem],
            [],
            flops // 8,
            8 * 2**20,
            f"update_kept_{i}",
        )(starts, by_col, back)
        over_x = sum_call((that_far, got_that), (None, 1), f"over_x_{i}")
        got_x = lax.ppermute(over_x, "led", planes)
        if i:
            from_z[0], got_x = lax.optimization_barrier((from_z[0], got_x))
        over_z = sum_call((that_near, got_that, got_x), (None, 0, None), f"over_z_{i}")
        from_z.append(permute(over_z, across))
        got_this = lax.ppermute(sent_this, "led", cores)
        over_this = sum_call((this_far, got_this), (None, 1), f"over_this_{i}")
        over_this, _ = lax.optimization_barrier((over_this, over_z))
        got_x = lax.ppermute(over_this, "led", planes)
        here = slice(i * rows // 2, (i + 1) * rows // 2)
        base.append(own_part[:, here] + summed(this_near, got_this[0], got_x))
    updated = None
    for i in range(2):
        updated = final_call(i, updated, base[i], from_z[i])
    return updated


def solution(mesh):
    placed = (P(None, "slab", None), P("led"), P("led"), P("led", "slab", None))
    fits = mesh.shape["slab"] == 8 and mesh.shape["led"] == 4

    def body(spectrum, led_rows, led_cols, images):
        shapes = (spectrum.shape, images.shape)
        if fits and shapes == ((2, 256, 2048), (2, 128, 1024)):
            return body_slabs(spectrum, led_rows, led_cols, images)
        return body_any(spectrum, led_rows, led_cols, images)

    return jax.shard_map(
        body, mesh=mesh, in_specs=placed, out_specs=P(None, "slab", "led"), check_vma=False
    )
```

```python
import functools

import jax
import jax.numpy as jnp
import numpy as np
from jax import lax
from jax.experimental import pallas as pl
from jax.experimental.pallas import tpu as pltpu
from jax.sharding import PartitionSpec as P

LANES = 128


def as_sent(value):
    return jax.tree.map(lambda a: a.astype(jnp.bfloat16) if a.dtype == jnp.float32 else a, value)


def host_tables(width):
    index = np.arange(width, dtype=np.int64)
    angle_index = (index[:, None] * index[None, :] % width).astype(np.float32)
    angle = angle_index * np.float32(2.0 * 3.141592653589793 / width)
    scale = np.float32(1.0) / np.sqrt(np.float32(width))
    return (
        (np.cos(angle) * scale).astype(jnp.bfloat16),
        (np.sin(angle) * scale).astype(jnp.bfloat16),
    )


def make_pupil(row_index, col_index, width):
    row_term = (2 * row_index + 1 - width) * (2 * row_index + 1 - width)
    col_term = (2 * col_index + 1 - width) * (2 * col_index + 1 - width)
    return (row_term[:, None] + col_term[None, :] < width * width).astype(jnp.float32)


def contract(form, left, right):
    return jnp.einsum(form, left, right, preferred_element_type=jnp.float32)


def take_rows(strip, start, width):
    return lax.dynamic_slice_in_dim(strip, start, width, 1)


def place_rows(block, start, total, axis_dim):
    shape = list(block.shape)
    shape[axis_dim] = total
    holder = jnp.zeros(tuple(shape), block.dtype)
    return lax.dynamic_update_slice_in_dim(holder, block, start, axis_dim)


def modulus_step(field_in_re, field_in_im, image, cos_table, sin_table):
    field_re = contract("lka,am->lkm", field_in_re, cos_table) + contract(
        "lka,am->lkm", field_in_im, sin_table
    )
    field_im = contract("lka,am->lkm", field_in_im, cos_table) - contract(
        "lka,am->lkm", field_in_re, sin_table
    )
    factor = jnp.sqrt(image) / jnp.sqrt(field_re * field_re + field_im * field_im + 0.25) - 1.0
    diff_re = (field_re * factor).astype(jnp.bfloat16)
    diff_im = (field_im * factor).astype(jnp.bfloat16)
    back_re = (
        contract("lkm,ma->lka", diff_re, cos_table) - contract("lkm,ma->lka", diff_im, sin_table)
    ).astype(jnp.bfloat16)
    back_im = (
        contract("lkm,ma->lka", diff_im, cos_table) + contract("lkm,ma->lka", diff_re, sin_table)
    ).astype(jnp.bfloat16)
    return (back_re, back_im)


def body_any(spectrum, led_rows, led_cols, images):
    width = images.shape[2]
    slab_rows = spectrum.shape[1]
    columns = spectrum.shape[2]
    slabs = lax.axis_size("slab")
    total_rows = slab_rows * slabs
    position = lax.axis_index("slab")
    cos_table, sin_table = (jnp.asarray(t) for t in host_tables(width))
    own_rows = position * slab_rows + jnp.arange(slab_rows, dtype=jnp.int32)
    col_index = jnp.arange(width, dtype=jnp.int32)

    def take_cols(start):
        return lax.dynamic_slice_in_dim(spectrum, start, width, 2)

    def owner_mask(start):
        return make_pupil(own_rows - start, col_index, width)

    windows = jax.vmap(take_cols)(led_cols)
    masks = jax.vmap(owner_mask)(led_rows)
    win_re = (windows[:, 0] * masks).astype(jnp.bfloat16)
    win_im = (windows[:, 1] * masks).astype(jnp.bfloat16)

    def slice_strip(block, start):
        return take_rows(block, start, width)

    row_re = (
        contract("lgb,bk->lkg", win_re, cos_table) + contract("lgb,bk->lkg", win_im, sin_table)
    ).astype(jnp.bfloat16)
    row_im = (
        contract("lgb,bk->lkg", win_im, cos_table) - contract("lgb,bk->lkg", win_re, sin_table)
    ).astype(jnp.bfloat16)
    col_re, col_im = (
        lax.all_to_all(row_re, "slab", split_axis=1, concat_axis=2, tiled=True),
        lax.all_to_all(row_im, "slab", split_axis=1, concat_axis=2, tiled=True),
    )
    field_in_re = jax.vmap(slice_strip)(col_re, led_rows)
    field_in_im = jax.vmap(slice_strip)(col_im, led_rows)
    back_re, back_im = modulus_step(field_in_re, field_in_im, images, cos_table, sin_table)

    def place_strip(block, start):
        return place_rows(block, start, total_rows, 1)

    full_re = jax.vmap(place_strip)(back_re, led_rows)
    full_im = jax.vmap(place_strip)(back_im, led_rows)
    home_re, home_im = (
        lax.all_to_all(as_sent(full_re), "slab", split_axis=2, concat_axis=1, tiled=True).astype(
            full_re.dtype
        ),
        lax.all_to_all(as_sent(full_im), "slab", split_axis=2, concat_axis=1, tiled=True).astype(
            full_im.dtype
        ),
    )
    upd_re = contract("lkg,kb->lgb", home_re, cos_table) - contract(
        "lkg,kb->lgb", home_im, sin_table
    )
    upd_im = contract("lkg,kb->lgb", home_im, cos_table) + contract(
        "lkg,kb->lgb", home_re, sin_table
    )
    upd_re = upd_re * masks
    upd_im = upd_im * masks

    def add_window(number, gradient):
        start = led_cols[number]
        piece = jnp.stack([upd_re[number], upd_im[number]])
        current = lax.dynamic_slice_in_dim(gradient, start, width, 2)
        return lax.dynamic_update_slice_in_dim(gradient, current + piece, start, 2)

    gradient = lax.fori_loop(
        0, led_rows.shape[0], add_window, jnp.zeros((2, slab_rows, columns), jnp.float32)
    )
    summed = lax.psum_scatter(gradient, "led", scatter_dimension=2, tiled=True)
    share = summed.shape[2]
    own_part = lax.dynamic_slice_in_dim(spectrum, lax.axis_index("led") * share, share, 2)
    return own_part + summed


SLABS = 8
HALF = 4
FIRST, LAST = 0, 7
HANDED = {1: (0, 4), 6: (7, 3)}
FAR = (
    {1: 4, 2: 4, 3: 5, 4: 2, 5: 3, 6: 3},
    {1: 6, 2: 7, 3: 4, 4: 3, 5: 0, 6: 1},
    {1: 7, 2: 5, 3: 6, 4: 1, 5: 2, 6: 0},
    {1: 5, 2: 6, 3: 7, 4: 0, 5: 1, 6: 2},
)


def look_up(position, table):
    return sum(jnp.where(position == slab, value, 0) for slab, value in table.items())


def origins(far):
    table = {to: slab for slab, to in far.items()}
    if far is FAR[0]:
        table = {to: slab for slab, to in far.items() if slab not in HANDED}
    if far is FAR[-1]:
        table.update({to: slab for slab, (_, to) in HANDED.items()})
    return table


def dot(left, right):
    return jnp.dot(left, right, preferred_element_type=jnp.float32)


def window_mask(first_row, row_start, col_start, rows, first_col, cols, width):
    shape = (rows, cols)
    at_row = lax.broadcasted_iota(jnp.int32, shape, 0) + (first_row - row_start)
    at_col = lax.broadcasted_iota(jnp.int32, shape, 1) + (first_col - col_start)
    wraps = at_col < 0
    at_col = jnp.where(wraps, at_col + width, at_col)
    row_term = 2 * at_row + 1 - width
    col_term = 2 * at_col + 1 - width
    return row_term * row_term + col_term * col_term < width * width, wraps


def row_block(window, table):
    both = dot(window, table)
    half = both.shape[0] // 2
    row_re = both[:half, :LANES] + both[half:, LANES:]
    row_im = both[half:, :LANES] - both[:half, LANES:]
    return row_re.astype(jnp.bfloat16), row_im.astype(jnp.bfloat16)


def store_parts(out, values):
    per = out.shape[0] // 2
    rows = out.shape[1]
    for plane, value in enumerate(values):
        for led in range(per):
            out[plane * per + led] = value[led * rows : (led + 1) * rows]


def is_one_of(position, slabs):
    return functools.reduce(jnp.logical_or, [position == slab for slab in slabs])


def window_kernel(starts, spectrum, window):
    position = lax.axis_index("slab")
    leds = starts.shape[0] // 2
    rows = spectrum.shape[1]
    width = window.shape[1]
    for led in range(leds):
        inside, wraps = window_mask(
            position * rows, starts[led], starts[leds + led], rows, 0, width, width
        )
        for plane in range(2):
            value = jnp.where(wraps, spectrum[plane, :, width:], spectrum[plane, :, :width])
            at = (plane * leds + led) * rows
            window[at : at + rows, :] = jnp.where(inside, value, 0.0).astype(jnp.bfloat16)


def rows_kernel(which, window, table, *outs):
    position = lax.axis_index("slab")
    blocks = [look_up(position, far) for far in FAR]
    blocks += [jnp.bitwise_xor(position, d) for d in (0, 2, 1, 3)]
    for out, block in zip(outs, blocks[which]):
        store_parts(out, row_block(window[...], table[block]))


def choose_kernel(got, own, out):
    passes = is_one_of(lax.axis_index("slab"), [by for by, _ in HANDED.values()])

    @pl.when(passes)
    def _():
        out[...] = got[...]

    @pl.when(jnp.logical_not(passes))
    def _():
        out[...] = own[...]


def amplitude_kernel(images, table, out, table_out):
    leds, block, width = images.shape
    for led in range(leds):
        for j in range(width // LANES):
            piece = jnp.sqrt(images[led, :, j * LANES : (j + 1) * LANES])
            out[j * LANES : (j + 1) * LANES, led * block : (led + 1) * block] = piece.T
    table_out[...] = table[...]


def field_kernel(amplitude, table, *rest):
    far, near = rest[: len(FAR)], rest[len(FAR) : len(FAR) + HALF]
    outs = rest[len(FAR) + HALF : len(FAR) + 2 * HALF]
    field_in, diff, strips = rest[len(FAR) + 2 * HALF :]
    position = lax.axis_index("slab")
    parts, rows, _ = near[0].shape
    half = parts // 2 * LANES
    width = field_in.shape[0]
    steps = width // LANES
    group = 4
    for d, block in enumerate(near):
        at = pl.multiple_of(jnp.bitwise_and(jnp.bitwise_xor(position, d), HALF - 1) * rows, rows)
        for part in range(parts):
            cols = slice(part * LANES, (part + 1) * LANES)
            field_in[pl.ds(at, rows), cols] = block[part]

    def add(block, origin):
        at = pl.multiple_of(jnp.bitwise_and(origin, HALF - 1) * rows, rows)
        for part in range(parts):
            cols = slice(part * LANES, (part + 1) * LANES)
            field_in[pl.ds(at, rows), cols] += block[part]

    for block, permute in zip(far, FAR):
        table_of = origins(permute)

        @pl.when(is_one_of(position, table_of))
        def _():
            add(block, look_up(position, table_of))

    for first in range(0, steps, group):
        product = dot(
            table[first : first + group].reshape(group * 2 * LANES, width), field_in[...]
        )
        for j in range(first, first + group):
            both = product[(j - first) * 2 * LANES : (j - first + 1) * 2 * LANES]
            field_re = both[:LANES, :half] + both[LANES:, half:]
            field_im = both[:LANES, half:] - both[LANES:, :half]
            here = pl.ds(j * LANES, LANES)
            factor = (
                amplitude[here, :] * lax.rsqrt(field_re * field_re + field_im * field_im + 0.25)
                - 1.0
            )
            diff[here, :half] = (field_re * factor).astype(jnp.bfloat16)
            diff[here, half:] = (field_im * factor).astype(jnp.bfloat16)
    pieces = rows // LANES
    for i in range(HALF):
        product = dot(
            table[i * pieces : (i + 1) * pieces].reshape(pieces * 2 * LANES, width), diff[...]
        )
        for h in range(pieces):
            both = product[h * 2 * LANES : (h + 1) * 2 * LANES]
            here = pl.ds(h * LANES, LANES)
            back_re = (both[:LANES, :half] - both[LANES:, half:]).astype(jnp.bfloat16)
            back_im = (both[:LANES, half:] + both[LANES:, :half]).astype(jnp.bfloat16)
            for part in range(parts // 2):
                cols = slice(part * LANES, (part + 1) * LANES)
                strips[i, part, here, :] = back_re[:, cols]
                strips[i, parts // 2 + part, here, :] = back_im[:, cols]
    for d, out in enumerate(outs):
        out[...] = strips[jnp.bitwise_and(jnp.bitwise_xor(position, d), HALF - 1)]


def update_columns(own_core, starts, table, back, outs):
    position = lax.axis_index("slab")
    led_at = lax.axis_index("led")
    core = jnp.bitwise_and(led_at, 1)
    plane_x = jnp.right_shift(led_at, 1)
    which_half = jnp.right_shift(position, 2)
    first_row = jnp.bitwise_and(position, HALF - 1)
    leds = starts.shape[0] // 2
    rows = back.shape[0] // (2 * leds)
    depth = back.shape[1]
    width = table.shape[1]
    group = width // LANES // 2
    owner = core if own_core else 1 - core
    shape = (rows, LANES)
    for n in range(group):
        block = owner * group + n
        both = dot(
            back[...], table[block, pl.ds(pl.multiple_of(which_half * depth, depth), depth)]
        )
        half = leds * rows
        update = (
            both[:half, :LANES] - both[half:, LANES:],
            both[half:, :LANES] + both[:half, LANES:],
        )
        sums = [[0.0, 0.0] for _ in outs]
        for led in range(leds):
            at_row = lax.broadcasted_iota(jnp.int32, shape, 0) + (
                first_row * rows - starts[led]
            )
            at_col = lax.broadcasted_iota(jnp.int32, shape, 1) + (
                block * LANES - starts[leds + led]
            )
            row_term = 2 * jnp.where(at_row < 0, at_row + width, at_row) + 1 - width
            col_term = 2 * jnp.where(at_col < 0, at_col + width, at_col) + 1 - width
            inside = row_term * row_term + col_term * col_term < width * width
            this_slab = jnp.where(at_row < 0, 1, 0) == which_half
            this_x = jnp.where(at_col < 0, 1, 0) == plane_x
            for plane in range(2):
                piece = jnp.where(inside, update[plane][led * rows : (led + 1) * rows], 0.0)
                for i, at_slab in enumerate(
                    (jnp.where(this_slab, piece, 0.0), jnp.where(this_slab, 0.0, piece))
                ):
                    sums[2 * i][plane] += jnp.where(this_x, at_slab, 0.0)
                    sums[2 * i + 1][plane] += jnp.where(this_x, 0.0, at_slab)
        cols = slice(n * LANES, (n + 1) * LANES)
        for out, both_planes in zip(outs, sums):
            for plane in range(2):
                out[plane, :, cols] = both_planes[plane].astype(out.dtype)


def sent_kernel(starts, table, *rest):
    blocks = rest[:HALF]
    this_slab, that_slab, back = rest[HALF:]
    position = lax.axis_index("slab")
    parts, rows, _ = blocks[0].shape
    for d, block in enumerate(blocks):
        source = jnp.bitwise_and(jnp.bitwise_xor(position, d), HALF - 1)
        at = pl.multiple_of(source * LANES, LANES)
        for part in range(parts):
            back[part * rows : (part + 1) * rows, pl.ds(at, LANES)] = block[part]
    outs = [out.at[i] for out in (this_slab, that_slab) for i in range(2)]
    update_columns(False, starts, table, back, outs)


def kept_kernel(starts, table, back, *outs):
    update_columns(True, starts, table, back, outs)


def z_first_kernel(that_near, that_far, got_that, out):
    cols = out.shape[3]
    for i, kept in enumerate((that_near, that_far)):
        total = kept[:, :, :cols] + got_that[i, :, :, :cols].astype(jnp.float32)
        out[i] = total.astype(out.dtype)


def x_first_kernel(that_far, got_that, out):
    cols = that_far.shape[2] - out.shape[2]
    total = that_far[:, :, cols:] + got_that[1, :, :, cols:].astype(jnp.float32)
    out[...] = total.astype(out.dtype)


def z_second_kernel(that_near, got_that, got_x, out):
    cols = that_near.shape[2] - out.shape[2]
    total = that_near[:, :, cols:] + got_that[0, :, :, cols:].astype(jnp.float32)
    out[...] = (total + got_x[...].astype(jnp.float32)).astype(out.dtype)


def x_second_kernel(this_far, got_this, got_z, out):
    cols = got_z.shape[3]
    total = this_far[...] + got_this[1].astype(jnp.float32)
    out[:, :, cols:] = total[:, :, cols:].astype(out.dtype)
    out[:, :, :cols] = (total[:, :, :cols] + got_z[1].astype(jnp.float32)).astype(out.dtype)


def local_call(kernel, out_shape, spaces, scratch, flops, moved, name):
    return pl.pallas_call(
        kernel,
        out_shape=out_shape,
        in_specs=[pl.BlockSpec(memory_space=space) for space in spaces],
        out_specs=jax.tree.map(lambda _: pl.BlockSpec(memory_space=pltpu.VMEM), out_shape),
        scratch_shapes=scratch,
        compiler_params=pltpu.CompilerParams(vmem_limit_bytes=32 * 2**20),
        cost_estimate=pl.CostEstimate(flops=flops, bytes_accessed=moved, transcendentals=0),
        name=name,
    )


def body_slabs(spectrum, led_rows, led_cols, images):
    leds, block, width = images.shape
    rows = spectrum.shape[1]
    led_at = lax.axis_index("led")
    bf16 = jnp.bfloat16
    vmem, smem = pltpu.VMEM, pltpu.SMEM
    cos_table, sin_table = host_tables(width)
    steps = width // LANES
    by_col = np.stack(
        [
            np.concatenate([t[:, j * LANES : (j + 1) * LANES] for t in (cos_table, sin_table)], 1)
            for j in range(steps)
        ]
    )
    by_row = jnp.asarray(np.ascontiguousarray(by_col.transpose(0, 2, 1)))
    by_col = jnp.asarray(by_col)
    parts = 2 * leds
    sent_block = jax.ShapeDtypeStruct((parts, rows, LANES), bf16)
    flops = 8 * leds * rows * width * width

    starts = jnp.concatenate([led_rows, led_cols]).astype(jnp.int32)
    window = local_call(
        window_kernel,
        jax.ShapeDtypeStruct((parts * rows, width), bf16),
        [smem, vmem],
        [],
        0,
        6 * 2**20,
        "windows",
    )(starts, spectrum)

    def rows_call(which, name, window):
        count = which.stop - which.start
        return local_call(
            functools.partial(rows_kernel, which),
            [sent_block] * count,
            [vmem, vmem],
            [],
            flops * count // SLABS,
            5 * 2**20,
            name,
        )(window, by_col)

    *far_sent, last = rows_call(slice(0, 4), "rows_far", window)

    def permute(sent, pairs):
        return lax.ppermute(sent, "slab", pairs)

    def choose(got, own, name):
        return local_call(
            choose_kernel, sent_block, [vmem] * 2, [], 0, 2**19, name
        )(got, own)

    windowed = range(FIRST + 1, LAST)
    far_columns = []
    for far, sent in zip(FAR, far_sent):
        pairs = dict(far)
        if far is FAR[0]:
            pairs.update({slab: by for slab, (by, _) in HANDED.items()})
        far_columns.append(permute(sent, list(pairs.items())))
    far_columns[0], window, images = lax.optimization_barrier((far_columns[0], window, images))
    last = local_call(
        choose_kernel, sent_block, [vmem] * 2, [], 0, 2**19, "last_far_blocks"
    )(far_columns[0], last)
    near_0, near_2, near_1, near_3 = rows_call(slice(4, SLABS), "rows_near", window)
    pairs = list(FAR[-1].items()) + list(HANDED.values())
    far_columns.append(permute(last, pairs))
    near_2 = permute(near_2, [(s, s ^ 2) for s in windowed])
    near_1 = permute(near_1, [(s, s ^ 1) for s in windowed])
    near_3 = permute(near_3, [(s, s ^ 3) for s in windowed])
    near_columns = [near_0, near_1, near_2, near_3]
    amplitude, by_row = local_call(
        amplitude_kernel,
        [
            jax.ShapeDtypeStruct((width, leds * block), jnp.float32),
            jax.ShapeDtypeStruct(by_row.shape, bf16),
        ],
        [vmem] * 2,
        [],
        0,
        10 * 2**20,
        "amplitude",
    )(images, by_row)
    strips = local_call(
        field_kernel,
        [sent_block] * HALF,
        [vmem] * (2 + len(FAR) + HALF),
        [pltpu.VMEM((width, parts * block), bf16)] * 2
        + [pltpu.VMEM((HALF,) + sent_block.shape, bf16)],
        16 * leds * block * width * width,
        12 * 2**20,
        "modulus_step",
    )(amplitude, by_row, *far_columns, *near_columns)

    def send_home(d):
        pairs = [(s, (s + d) % SLABS) for s in range(SLABS) if FIRST < (s + d) % SLABS < LAST]
        return permute(strips[d % HALF], pairs)

    home = [strips[0]]
    home += [
        permute(strips[d], [(s, s ^ d) for s in range(SLABS)]) for d in range(1, HALF)
    ]
    share = width // 2
    first = share // 4
    piece = (2, rows, share)
    cores = [(0, 1), (1, 0), (2, 3), (3, 2)]
    planes = [(0, 2), (2, 0), (1, 3), (3, 1)]
    across = [(s, s ^ 4) for s in range(SLABS) if FIRST < s ^ 4 < LAST]
    sent_this, sent_that, back = local_call(
        sent_kernel,
        [
            jax.ShapeDtypeStruct((2,) + piece, bf16),
            jax.ShapeDtypeStruct((2,) + piece, bf16),
            jax.ShapeDtypeStruct((parts * rows, HALF * LANES), bf16),
        ],
        [smem] + [vmem] * (1 + HALF),
        [],
        flops // 4,
        8 * 2**20,
        "update_sent",
    )(starts, by_col, *home)
    got_that = lax.ppermute(sent_that, "led", cores)
    got_this = lax.ppermute(sent_this, "led", cores)
    this_near, this_far, that_near, that_far = local_call(
        kept_kernel,
        [jax.ShapeDtypeStruct(piece, jnp.float32)] * 4,
        [smem, vmem, vmem],
        [],
        flops // 4,
        10 * 2**20,
        "update_kept",
    )(starts, by_col, back)

    def sum_call(kernel, shape, *values):
        out_shape = jax.ShapeDtypeStruct(shape, bf16)
        specs = [vmem] * len(values)
        return local_call(kernel, out_shape, specs, [], 0, 2**20, kernel.__name__)(*values)

    over = sum_call(z_first_kernel, (2, 2, rows, first), that_near, that_far, got_that)
    got_z_first = permute(over, across)
    over = sum_call(x_first_kernel, (2, rows, share - first), that_far, got_that)
    got_x = lax.ppermute(over, "led", planes)
    over = sum_call(z_second_kernel, (2, rows, share - first), that_near, got_that, got_x)
    got_z_second = permute(over, across)
    over = sum_call(x_second_kernel, piece, this_far, got_this, got_z_first)
    got_x = lax.ppermute(over, "led", planes)

    def widen(value, before):
        after = share - before - value.shape[2]
        return jnp.pad(value.astype(jnp.float32), ((0, 0), (0, 0), (before, after)))

    base = lax.dynamic_slice_in_dim(spectrum, led_at * share, share, 2)
    base += this_near + got_this[0].astype(jnp.float32) + got_x.astype(jnp.float32)
    base += widen(got_z_first[0], 0)
    base, got_z_second = lax.optimization_barrier((base, got_z_second))
    return base + widen(got_z_second, first)


def solution(mesh):
    placed = (P(None, "slab", None), P("led"), P("led"), P("led", "slab", None))
    fits = mesh.shape["slab"] == 8 and mesh.shape["led"] == 4

    def body(spectrum, led_rows, led_cols, images):
        shapes = (spectrum.shape, images.shape)
        if fits and shapes == ((2, 256, 2048), (2, 128, 1024)):
            return body_slabs(spectrum, led_rows, led_cols, images)
        return body_any(spectrum, led_rows, led_cols, images)

    return jax.shard_map(
        body, mesh=mesh, in_specs=placed, out_specs=P(None, "slab", "led"), check_vma=False
    )
```

```python
import functools

import jax
import jax.numpy as jnp
import numpy as np
from jax import lax
from jax.experimental import pallas as pl
from jax.experimental.pallas import tpu as pltpu
from jax.sharding import PartitionSpec as P

LANES = 128


def as_sent(value):
    return jax.tree.map(lambda a: a.astype(jnp.bfloat16) if a.dtype == jnp.float32 else a, value)


def host_tables(width):
    index = np.arange(width, dtype=np.int64)
    angle_index = (index[:, None] * index[None, :] % width).astype(np.float32)
    angle = angle_index * np.float32(2.0 * 3.141592653589793 / width)
    scale = np.float32(1.0) / np.sqrt(np.float32(width))
    return (
        (np.cos(angle) * scale).astype(jnp.bfloat16),
        (np.sin(angle) * scale).astype(jnp.bfloat16),
    )


def make_pupil(row_index, col_index, width):
    row_term = (2 * row_index + 1 - width) * (2 * row_index + 1 - width)
    col_term = (2 * col_index + 1 - width) * (2 * col_index + 1 - width)
    return (row_term[:, None] + col_term[None, :] < width * width).astype(jnp.float32)


def contract(form, left, right):
    return jnp.einsum(form, left, right, preferred_element_type=jnp.float32)


def take_rows(strip, start, width):
    return lax.dynamic_slice_in_dim(strip, start, width, 1)


def place_rows(block, start, total, axis_dim):
    shape = list(block.shape)
    shape[axis_dim] = total
    holder = jnp.zeros(tuple(shape), block.dtype)
    return lax.dynamic_update_slice_in_dim(holder, block, start, axis_dim)


def modulus_step(field_in_re, field_in_im, image, cos_table, sin_table):
    field_re = contract("lka,am->lkm", field_in_re, cos_table) + contract(
        "lka,am->lkm", field_in_im, sin_table
    )
    field_im = contract("lka,am->lkm", field_in_im, cos_table) - contract(
        "lka,am->lkm", field_in_re, sin_table
    )
    factor = jnp.sqrt(image) / jnp.sqrt(field_re * field_re + field_im * field_im + 0.25) - 1.0
    diff_re = (field_re * factor).astype(jnp.bfloat16)
    diff_im = (field_im * factor).astype(jnp.bfloat16)
    back_re = (
        contract("lkm,ma->lka", diff_re, cos_table) - contract("lkm,ma->lka", diff_im, sin_table)
    ).astype(jnp.bfloat16)
    back_im = (
        contract("lkm,ma->lka", diff_im, cos_table) + contract("lkm,ma->lka", diff_re, sin_table)
    ).astype(jnp.bfloat16)
    return (back_re, back_im)


def body_any(spectrum, led_rows, led_cols, images):
    width = images.shape[2]
    slab_rows = spectrum.shape[1]
    columns = spectrum.shape[2]
    slabs = lax.axis_size("slab")
    total_rows = slab_rows * slabs
    position = lax.axis_index("slab")
    cos_table, sin_table = (jnp.asarray(t) for t in host_tables(width))
    own_rows = position * slab_rows + jnp.arange(slab_rows, dtype=jnp.int32)
    col_index = jnp.arange(width, dtype=jnp.int32)

    def take_cols(start):
        return lax.dynamic_slice_in_dim(spectrum, start, width, 2)

    def owner_mask(start):
        return make_pupil(own_rows - start, col_index, width)

    windows = jax.vmap(take_cols)(led_cols)
    masks = jax.vmap(owner_mask)(led_rows)
    win_re = (windows[:, 0] * masks).astype(jnp.bfloat16)
    win_im = (windows[:, 1] * masks).astype(jnp.bfloat16)

    def slice_strip(block, start):
        return take_rows(block, start, width)

    row_re = (
        contract("lgb,bk->lkg", win_re, cos_table) + contract("lgb,bk->lkg", win_im, sin_table)
    ).astype(jnp.bfloat16)
    row_im = (
        contract("lgb,bk->lkg", win_im, cos_table) - contract("lgb,bk->lkg", win_re, sin_table)
    ).astype(jnp.bfloat16)
    col_re, col_im = (
        lax.all_to_all(row_re, "slab", split_axis=1, concat_axis=2, tiled=True),
        lax.all_to_all(row_im, "slab", split_axis=1, concat_axis=2, tiled=True),
    )
    field_in_re = jax.vmap(slice_strip)(col_re, led_rows)
    field_in_im = jax.vmap(slice_strip)(col_im, led_rows)
    back_re, back_im = modulus_step(field_in_re, field_in_im, images, cos_table, sin_table)

    def place_strip(block, start):
        return place_rows(block, start, total_rows, 1)

    full_re = jax.vmap(place_strip)(back_re, led_rows)
    full_im = jax.vmap(place_strip)(back_im, led_rows)
    home_re, home_im = (
        lax.all_to_all(as_sent(full_re), "slab", split_axis=2, concat_axis=1, tiled=True).astype(
            full_re.dtype
        ),
        lax.all_to_all(as_sent(full_im), "slab", split_axis=2, concat_axis=1, tiled=True).astype(
            full_im.dtype
        ),
    )
    upd_re = contract("lkg,kb->lgb", home_re, cos_table) - contract(
        "lkg,kb->lgb", home_im, sin_table
    )
    upd_im = contract("lkg,kb->lgb", home_im, cos_table) + contract(
        "lkg,kb->lgb", home_re, sin_table
    )
    upd_re = upd_re * masks
    upd_im = upd_im * masks

    def add_window(number, gradient):
        start = led_cols[number]
        piece = jnp.stack([upd_re[number], upd_im[number]])
        current = lax.dynamic_slice_in_dim(gradient, start, width, 2)
        return lax.dynamic_update_slice_in_dim(gradient, current + piece, start, 2)

    gradient = lax.fori_loop(
        0, led_rows.shape[0], add_window, jnp.zeros((2, slab_rows, columns), jnp.float32)
    )
    summed = lax.psum_scatter(gradient, "led", scatter_dimension=2, tiled=True)
    share = summed.shape[2]
    own_part = lax.dynamic_slice_in_dim(spectrum, lax.axis_index("led") * share, share, 2)
    return own_part + summed


SLABS = 8
HALF = 4
FIRST, LAST = 0, 7
HANDED = {1: (0, 4), 6: (7, 3)}
FAR = (
    {1: 4, 2: 4, 3: 5, 4: 2, 5: 3, 6: 3},
    {1: 6, 2: 7, 3: 4, 4: 3, 5: 0, 6: 1},
    {1: 7, 2: 5, 3: 6, 4: 1, 5: 2, 6: 0},
    {1: 5, 2: 6, 3: 7, 4: 0, 5: 1, 6: 2},
)


def look_up(position, table):
    return sum(jnp.where(position == slab, value, 0) for slab, value in table.items())


def origins(far):
    table = {to: slab for slab, to in far.items()}
    if far is FAR[0]:
        table = {to: slab for slab, to in far.items() if slab not in HANDED}
    if far is FAR[-1]:
        table.update({to: slab for slab, (_, to) in HANDED.items()})
    return table


def dot(left, right):
    return jnp.dot(left, right, preferred_element_type=jnp.float32)


def window_mask(first_row, row_start, col_start, rows, first_col, cols, width):
    shape = (rows, cols)
    at_row = lax.broadcasted_iota(jnp.int32, shape, 0) + (first_row - row_start)
    at_col = lax.broadcasted_iota(jnp.int32, shape, 1) + (first_col - col_start)
    wraps = at_col < 0
    at_col = jnp.where(wraps, at_col + width, at_col)
    row_term = 2 * at_row + 1 - width
    col_term = 2 * at_col + 1 - width
    return row_term * row_term + col_term * col_term < width * width, wraps


def row_block(window, table):
    both = dot(window, table)
    half = both.shape[0] // 2
    row_re = both[:half, :LANES] + both[half:, LANES:]
    row_im = both[half:, :LANES] - both[:half, LANES:]
    return row_re.astype(jnp.bfloat16), row_im.astype(jnp.bfloat16)


def store_parts(out, values):
    per = out.shape[0] // 2
    rows = out.shape[1]
    for plane, value in enumerate(values):
        for led in range(per):
            out[plane * per + led] = value[led * rows : (led + 1) * rows]


def is_one_of(position, slabs):
    return functools.reduce(jnp.logical_or, [position == slab for slab in slabs])


def window_kernel(starts, spectrum, window):
    position = lax.axis_index("slab")
    leds = starts.shape[0] // 2
    rows = spectrum.shape[1]
    width = window.shape[1]
    for led in range(leds):
        inside, wraps = window_mask(
            position * rows, starts[led], starts[leds + led], rows, 0, width, width
        )
        for plane in range(2):
            value = jnp.where(wraps, spectrum[plane, :, width:], spectrum[plane, :, :width])
            at = (plane * leds + led) * rows
            window[at : at + rows, :] = jnp.where(inside, value, 0.0).astype(jnp.bfloat16)


def rows_kernel(which, window, table, *outs):
    position = lax.axis_index("slab")
    blocks = [jnp.bitwise_xor(position, 2)]
    blocks += [look_up(position, far) for far in FAR]
    blocks += [jnp.bitwise_xor(position, d) for d in (0, 1, 3)]
    for out, block in zip(outs, blocks[which]):
        store_parts(out, row_block(window[...], table[block]))


def choose_kernel(got, own, out):
    passes = is_one_of(lax.axis_index("slab"), [by for by, _ in HANDED.values()])

    @pl.when(passes)
    def _():
        out[...] = got[...]

    @pl.when(jnp.logical_not(passes))
    def _():
        out[...] = own[...]


def amplitude_kernel(images, table, out, table_out):
    leds, block, width = images.shape
    for led in range(leds):
        for j in range(width // LANES):
            piece = jnp.sqrt(images[led, :, j * LANES : (j + 1) * LANES])
            out[j * LANES : (j + 1) * LANES, led * block : (led + 1) * block] = piece.T
    table_out[...] = table[...]


def field_kernel(amplitude, table, *rest):
    far, near = rest[: len(FAR)], rest[len(FAR) : len(FAR) + HALF]
    outs = rest[len(FAR) + HALF : len(FAR) + 2 * HALF]
    field_in, diff, strips = rest[len(FAR) + 2 * HALF :]
    position = lax.axis_index("slab")
    parts, rows, _ = near[0].shape
    half = parts // 2 * LANES
    width = field_in.shape[0]
    steps = width // LANES
    group = 4
    for d, block in enumerate(near):
        at = pl.multiple_of(jnp.bitwise_and(jnp.bitwise_xor(position, d), HALF - 1) * rows, rows)
        for part in range(parts):
            cols = slice(part * LANES, (part + 1) * LANES)
            field_in[pl.ds(at, rows), cols] = block[part]

    def add(block, origin):
        at = pl.multiple_of(jnp.bitwise_and(origin, HALF - 1) * rows, rows)
        for part in range(parts):
            cols = slice(part * LANES, (part + 1) * LANES)
            field_in[pl.ds(at, rows), cols] += block[part]

    for block, permute in zip(far, FAR):
        table_of = origins(permute)

        @pl.when(is_one_of(position, table_of))
        def _():
            add(block, look_up(position, table_of))

    for first in range(0, steps, group):
        product = dot(
            table[first : first + group].reshape(group * 2 * LANES, width), field_in[...]
        )
        for j in range(first, first + group):
            both = product[(j - first) * 2 * LANES : (j - first + 1) * 2 * LANES]
            field_re = both[:LANES, :half] + both[LANES:, half:]
            field_im = both[:LANES, half:] - both[LANES:, :half]
            here = pl.ds(j * LANES, LANES)
            factor = (
                amplitude[here, :] * lax.rsqrt(field_re * field_re + field_im * field_im + 0.25)
                - 1.0
            )
            diff[here, :half] = (field_re * factor).astype(jnp.bfloat16)
            diff[here, half:] = (field_im * factor).astype(jnp.bfloat16)
    pieces = rows // LANES
    for i in range(HALF):
        product = dot(
            table[i * pieces : (i + 1) * pieces].reshape(pieces * 2 * LANES, width), diff[...]
        )
        for h in range(pieces):
            both = product[h * 2 * LANES : (h + 1) * 2 * LANES]
            here = pl.ds(h * LANES, LANES)
            back_re = (both[:LANES, :half] - both[LANES:, half:]).astype(jnp.bfloat16)
            back_im = (both[:LANES, half:] + both[LANES:, :half]).astype(jnp.bfloat16)
            for part in range(parts // 2):
                cols = slice(part * LANES, (part + 1) * LANES)
                strips[i, part, here, :] = back_re[:, cols]
                strips[i, parts // 2 + part, here, :] = back_im[:, cols]
    for d, out in enumerate(outs):
        out[...] = strips[jnp.bitwise_and(jnp.bitwise_xor(position, d), HALF - 1)]


def update_columns(own_core, starts, table, back, outs):
    position = lax.axis_index("slab")
    led_at = lax.axis_index("led")
    core = jnp.bitwise_and(led_at, 1)
    plane_x = jnp.right_shift(led_at, 1)
    which_half = jnp.right_shift(position, 2)
    first_row = jnp.bitwise_and(position, HALF - 1)
    leds = starts.shape[0] // 2
    rows = back.shape[0] // (2 * leds)
    depth = back.shape[1]
    width = table.shape[1]
    group = width // LANES // 2
    owner = core if own_core else 1 - core
    shape = (rows, LANES)
    for n in range(group):
        block = owner * group + n
        both = dot(
            back[...], table[block, pl.ds(pl.multiple_of(which_half * depth, depth), depth)]
        )
        half = leds * rows
        update = (
            both[:half, :LANES] - both[half:, LANES:],
            both[half:, :LANES] + both[:half, LANES:],
        )
        sums = [[0.0, 0.0] for _ in outs]
        for led in range(leds):
            at_row = lax.broadcasted_iota(jnp.int32, shape, 0) + (
                first_row * rows - starts[led]
            )
            at_col = lax.broadcasted_iota(jnp.int32, shape, 1) + (
                block * LANES - starts[leds + led]
            )
            row_term = 2 * jnp.where(at_row < 0, at_row + width, at_row) + 1 - width
            col_term = 2 * jnp.where(at_col < 0, at_col + width, at_col) + 1 - width
            inside = row_term * row_term + col_term * col_term < width * width
            this_slab = jnp.where(at_row < 0, 1, 0) == which_half
            this_x = jnp.where(at_col < 0, 1, 0) == plane_x
            for plane in range(2):
                piece = jnp.where(inside, update[plane][led * rows : (led + 1) * rows], 0.0)
                for i, at_slab in enumerate(
                    (jnp.where(this_slab, piece, 0.0), jnp.where(this_slab, 0.0, piece))
                ):
                    sums[2 * i][plane] += jnp.where(this_x, at_slab, 0.0)
                    sums[2 * i + 1][plane] += jnp.where(this_x, 0.0, at_slab)
        cols = slice(n * LANES, (n + 1) * LANES)
        for out, both_planes in zip(outs, sums):
            for plane in range(2):
                out[plane, :, cols] = both_planes[plane].astype(out.dtype)


def sent_kernel(starts, table, *rest):
    blocks = rest[:HALF]
    this_slab, that_slab, back = rest[HALF:]
    position = lax.axis_index("slab")
    parts, rows, _ = blocks[0].shape
    for d, block in enumerate(blocks):
        source = jnp.bitwise_and(jnp.bitwise_xor(position, d), HALF - 1)
        at = pl.multiple_of(source * LANES, LANES)
        for part in range(parts):
            back[part * rows : (part + 1) * rows, pl.ds(at, LANES)] = block[part]
    outs = [out.at[i] for out in (this_slab, that_slab) for i in range(2)]
    update_columns(False, starts, table, back, outs)


def kept_kernel(starts, table, back, *outs):
    update_columns(True, starts, table, back, outs)


def z_first_kernel(that_near, that_far, got_that, out):
    cols = out.shape[3]
    for i, kept in enumerate((that_near, that_far)):
        total = kept[:, :, :cols] + got_that[i, :, :, :cols].astype(jnp.float32)
        out[i] = total.astype(out.dtype)


def x_first_kernel(that_far, got_that, out):
    cols = that_far.shape[2] - out.shape[2]
    total = that_far[:, :, cols:] + got_that[1, :, :, cols:].astype(jnp.float32)
    out[...] = total.astype(out.dtype)


def z_second_kernel(that_near, got_that, got_x, out):
    cols = that_near.shape[2] - out.shape[2]
    total = that_near[:, :, cols:] + got_that[0, :, :, cols:].astype(jnp.float32)
    out[...] = (total + got_x[...].astype(jnp.float32)).astype(out.dtype)


def x_second_kernel(this_far, got_this, got_z, out):
    cols = got_z.shape[3]
    total = this_far[...] + got_this[1].astype(jnp.float32)
    out[:, :, cols:] = total[:, :, cols:].astype(out.dtype)
    out[:, :, :cols] = (total[:, :, :cols] + got_z[1].astype(jnp.float32)).astype(out.dtype)


def local_call(kernel, out_shape, spaces, scratch, flops, moved, name):
    return pl.pallas_call(
        kernel,
        out_shape=out_shape,
        in_specs=[pl.BlockSpec(memory_space=space) for space in spaces],
        out_specs=jax.tree.map(lambda _: pl.BlockSpec(memory_space=pltpu.VMEM), out_shape),
        scratch_shapes=scratch,
        compiler_params=pltpu.CompilerParams(vmem_limit_bytes=32 * 2**20),
        cost_estimate=pl.CostEstimate(flops=flops, bytes_accessed=moved, transcendentals=0),
        name=name,
    )


def body_slabs(spectrum, led_rows, led_cols, images):
    leds, block, width = images.shape
    rows = spectrum.shape[1]
    led_at = lax.axis_index("led")
    bf16 = jnp.bfloat16
    vmem, smem = pltpu.VMEM, pltpu.SMEM
    cos_table, sin_table = host_tables(width)
    steps = width // LANES
    by_col = np.stack(
        [
            np.concatenate([t[:, j * LANES : (j + 1) * LANES] for t in (cos_table, sin_table)], 1)
            for j in range(steps)
        ]
    )
    by_row = jnp.asarray(np.ascontiguousarray(by_col.transpose(0, 2, 1)))
    by_col = jnp.asarray(by_col)
    parts = 2 * leds
    sent_block = jax.ShapeDtypeStruct((parts, rows, LANES), bf16)
    flops = 8 * leds * rows * width * width

    starts = jnp.concatenate([led_rows, led_cols]).astype(jnp.int32)
    window = local_call(
        window_kernel,
        jax.ShapeDtypeStruct((parts * rows, width), bf16),
        [smem, vmem],
        [],
        0,
        6 * 2**20,
        "windows",
    )(starts, spectrum)

    def rows_call(which, name, window):
        count = which.stop - which.start
        return local_call(
            functools.partial(rows_kernel, which),
            [sent_block] * count,
            [vmem, vmem],
            [],
            flops * count // SLABS,
            5 * 2**20,
            name,
        )(window, by_col)

    near_2, *far_sent = rows_call(slice(0, 5), "rows_far", window)

    def permute(sent, pairs):
        return lax.ppermute(sent, "slab", pairs)

    def choose(got, own, name):
        return local_call(
            choose_kernel, sent_block, [vmem] * 2, [], 0, 2**19, name
        )(got, own)

    windowed = range(FIRST + 1, LAST)
    far_columns = []
    for far, sent in zip(FAR[:2], far_sent):
        pairs = dict(far)
        if far is FAR[0]:
            pairs.update({slab: by for slab, (by, _) in HANDED.items()})
        far_columns.append(permute(sent, list(pairs.items())))
    near_2 = permute(near_2, [(s, s ^ 2) for s in windowed])
    third, last = far_sent[2:]
    far_columns[0], third, window, images = lax.optimization_barrier(
        (far_columns[0], third, window, images)
    )
    last = local_call(
        choose_kernel, sent_block, [vmem] * 2, [], 0, 2**19, "last_far_blocks"
    )(far_columns[0], last)
    near_0, near_1, near_3 = rows_call(slice(5, SLABS), "rows_near", window)
    far_columns.append(permute(third, list(FAR[2].items())))
    far_columns.append(permute(last, list(FAR[3].items()) + list(HANDED.values())))
    near_1 = permute(near_1, [(s, s ^ 1) for s in windowed])
    near_3 = permute(near_3, [(s, s ^ 3) for s in windowed])
    near_columns = [near_0, near_1, near_2, near_3]
    amplitude, by_row = local_call(
        amplitude_kernel,
        [
            jax.ShapeDtypeStruct((width, leds * block), jnp.float32),
            jax.ShapeDtypeStruct(by_row.shape, bf16),
        ],
        [vmem] * 2,
        [],
        0,
        10 * 2**20,
        "amplitude",
    )(images, by_row)
    strips = local_call(
        field_kernel,
        [sent_block] * HALF,
        [vmem] * (2 + len(FAR) + HALF),
        [pltpu.VMEM((width, parts * block), bf16)] * 2
        + [pltpu.VMEM((HALF,) + sent_block.shape, bf16)],
        16 * leds * block * width * width,
        12 * 2**20,
        "modulus_step",
    )(amplitude, by_row, *far_columns, *near_columns)

    def send_home(d):
        pairs = [(s, (s + d) % SLABS) for s in range(SLABS) if FIRST < (s + d) % SLABS < LAST]
        return permute(strips[d % HALF], pairs)

    home = [strips[0]]
    home += [
        permute(strips[d], [(s, s ^ d) for s in range(SLABS)]) for d in range(1, HALF)
    ]
    share = width // 2
    first = share // 4
    piece = (2, rows, share)
    cores = [(0, 1), (1, 0), (2, 3), (3, 2)]
    planes = [(0, 2), (2, 0), (1, 3), (3, 1)]
    across = [(s, s ^ 4) for s in range(SLABS) if FIRST < s ^ 4 < LAST]
    sent_this, sent_that, back = local_call(
        sent_kernel,
        [
            jax.ShapeDtypeStruct((2,) + piece, bf16),
            jax.ShapeDtypeStruct((2,) + piece, bf16),
            jax.ShapeDtypeStruct((parts * rows, HALF * LANES), bf16),
        ],
        [smem] + [vmem] * (1 + HALF),
        [],
        flops // 4,
        8 * 2**20,
        "update_sent",
    )(starts, by_col, *home)
    got_that = lax.ppermute(sent_that, "led", cores)
    got_this = lax.ppermute(sent_this, "led", cores)
    this_near, this_far, that_near, that_far = local_call(
        kept_kernel,
        [jax.ShapeDtypeStruct(piece, jnp.float32)] * 4,
        [smem, vmem, vmem],
        [],
        flops // 4,
        10 * 2**20,
        "update_kept",
    )(starts, by_col, back)

    def sum_call(kernel, shape, *values):
        out_shape = jax.ShapeDtypeStruct(shape, bf16)
        specs = [vmem] * len(values)
        return local_call(kernel, out_shape, specs, [], 0, 2**20, kernel.__name__)(*values)

    over = sum_call(z_first_kernel, (2, 2, rows, first), that_near, that_far, got_that)
    got_z_first = permute(over, across)
    over = sum_call(x_first_kernel, (2, rows, share - first), that_far, got_that)
    got_x = lax.ppermute(over, "led", planes)
    over = sum_call(z_second_kernel, (2, rows, share - first), that_near, got_that, got_x)
    got_z_second = permute(over, across)
    got_z_first, _ = lax.optimization_barrier((got_z_first, over))
    over = sum_call(x_second_kernel, piece, this_far, got_this, got_z_first)
    got_x = lax.ppermute(over, "led", planes)

    def widen(value, before):
        after = share - before - value.shape[2]
        return jnp.pad(value.astype(jnp.float32), ((0, 0), (0, 0), (before, after)))

    base = lax.dynamic_slice_in_dim(spectrum, led_at * share, share, 2)
    base += this_near + got_this[0].astype(jnp.float32) + got_x.astype(jnp.float32)
    base += widen(got_z_first[0], 0)
    base, got_z_second = lax.optimization_barrier((base, got_z_second))
    return base + widen(got_z_second, first)


def solution(mesh):
    placed = (P(None, "slab", None), P("led"), P("led"), P("led", "slab", None))
    fits = mesh.shape["slab"] == 8 and mesh.shape["led"] == 4

    def body(spectrum, led_rows, led_cols, images):
        shapes = (spectrum.shape, images.shape)
        if fits and shapes == ((2, 256, 2048), (2, 128, 1024)):
            return body_slabs(spectrum, led_rows, led_cols, images)
        return body_any(spectrum, led_rows, led_cols, images)

    return jax.shard_map(
        body, mesh=mesh, in_specs=placed, out_specs=P(None, "slab", "led"), check_vma=False
    )
```

```python
import functools

import jax
import jax.numpy as jnp
import numpy as np
from jax import lax
from jax.experimental import pallas as pl
from jax.experimental.pallas import tpu as pltpu
from jax.sharding import PartitionSpec as P

LANES = 128


def as_sent(value):
    return jax.tree.map(lambda a: a.astype(jnp.bfloat16) if a.dtype == jnp.float32 else a, value)


def host_tables(width):
    index = np.arange(width, dtype=np.int64)
    angle_index = (index[:, None] * index[None, :] % width).astype(np.float32)
    angle = angle_index * np.float32(2.0 * 3.141592653589793 / width)
    scale = np.float32(1.0) / np.sqrt(np.float32(width))
    return (
        (np.cos(angle) * scale).astype(jnp.bfloat16),
        (np.sin(angle) * scale).astype(jnp.bfloat16),
    )


def make_pupil(row_index, col_index, width):
    row_term = (2 * row_index + 1 - width) * (2 * row_index + 1 - width)
    col_term = (2 * col_index + 1 - width) * (2 * col_index + 1 - width)
    return (row_term[:, None] + col_term[None, :] < width * width).astype(jnp.float32)


def contract(form, left, right):
    return jnp.einsum(form, left, right, preferred_element_type=jnp.float32)


def take_rows(strip, start, width):
    return lax.dynamic_slice_in_dim(strip, start, width, 1)


def place_rows(block, start, total, axis_dim):
    shape = list(block.shape)
    shape[axis_dim] = total
    holder = jnp.zeros(tuple(shape), block.dtype)
    return lax.dynamic_update_slice_in_dim(holder, block, start, axis_dim)


def modulus_step(field_in_re, field_in_im, image, cos_table, sin_table):
    field_re = contract("lka,am->lkm", field_in_re, cos_table) + contract(
        "lka,am->lkm", field_in_im, sin_table
    )
    field_im = contract("lka,am->lkm", field_in_im, cos_table) - contract(
        "lka,am->lkm", field_in_re, sin_table
    )
    factor = jnp.sqrt(image) / jnp.sqrt(field_re * field_re + field_im * field_im + 0.25) - 1.0
    diff_re = (field_re * factor).astype(jnp.bfloat16)
    diff_im = (field_im * factor).astype(jnp.bfloat16)
    back_re = (
        contract("lkm,ma->lka", diff_re, cos_table) - contract("lkm,ma->lka", diff_im, sin_table)
    ).astype(jnp.bfloat16)
    back_im = (
        contract("lkm,ma->lka", diff_im, cos_table) + contract("lkm,ma->lka", diff_re, sin_table)
    ).astype(jnp.bfloat16)
    return (back_re, back_im)


def body_any(spectrum, led_rows, led_cols, images):
    width = images.shape[2]
    slab_rows = spectrum.shape[1]
    columns = spectrum.shape[2]
    slabs = lax.axis_size("slab")
    total_rows = slab_rows * slabs
    position = lax.axis_index("slab")
    cos_table, sin_table = (jnp.asarray(t) for t in host_tables(width))
    own_rows = position * slab_rows + jnp.arange(slab_rows, dtype=jnp.int32)
    col_index = jnp.arange(width, dtype=jnp.int32)

    def take_cols(start):
        return lax.dynamic_slice_in_dim(spectrum, start, width, 2)

    def owner_mask(start):
        return make_pupil(own_rows - start, col_index, width)

    windows = jax.vmap(take_cols)(led_cols)
    masks = jax.vmap(owner_mask)(led_rows)
    win_re = (windows[:, 0] * masks).astype(jnp.bfloat16)
    win_im = (windows[:, 1] * masks).astype(jnp.bfloat16)

    def slice_strip(block, start):
        return take_rows(block, start, width)

    row_re = (
        contract("lgb,bk->lkg", win_re, cos_table) + contract("lgb,bk->lkg", win_im, sin_table)
    ).astype(jnp.bfloat16)
    row_im = (
        contract("lgb,bk->lkg", win_im, cos_table) - contract("lgb,bk->lkg", win_re, sin_table)
    ).astype(jnp.bfloat16)
    col_re, col_im = (
        lax.all_to_all(row_re, "slab", split_axis=1, concat_axis=2, tiled=True),
        lax.all_to_all(row_im, "slab", split_axis=1, concat_axis=2, tiled=True),
    )
    field_in_re = jax.vmap(slice_strip)(col_re, led_rows)
    field_in_im = jax.vmap(slice_strip)(col_im, led_rows)
    back_re, back_im = modulus_step(field_in_re, field_in_im, images, cos_table, sin_table)

    def place_strip(block, start):
        return place_rows(block, start, total_rows, 1)

    full_re = jax.vmap(place_strip)(back_re, led_rows)
    full_im = jax.vmap(place_strip)(back_im, led_rows)
    home_re, home_im = (
        lax.all_to_all(as_sent(full_re), "slab", split_axis=2, concat_axis=1, tiled=True).astype(
            full_re.dtype
        ),
        lax.all_to_all(as_sent(full_im), "slab", split_axis=2, concat_axis=1, tiled=True).astype(
            full_im.dtype
        ),
    )
    upd_re = contract("lkg,kb->lgb", home_re, cos_table) - contract(
        "lkg,kb->lgb", home_im, sin_table
    )
    upd_im = contract("lkg,kb->lgb", home_im, cos_table) + contract(
        "lkg,kb->lgb", home_re, sin_table
    )
    upd_re = upd_re * masks
    upd_im = upd_im * masks

    def add_window(number, gradient):
        start = led_cols[number]
        piece = jnp.stack([upd_re[number], upd_im[number]])
        current = lax.dynamic_slice_in_dim(gradient, start, width, 2)
        return lax.dynamic_update_slice_in_dim(gradient, current + piece, start, 2)

    gradient = lax.fori_loop(
        0, led_rows.shape[0], add_window, jnp.zeros((2, slab_rows, columns), jnp.float32)
    )
    summed = lax.psum_scatter(gradient, "led", scatter_dimension=2, tiled=True)
    share = summed.shape[2]
    own_part = lax.dynamic_slice_in_dim(spectrum, lax.axis_index("led") * share, share, 2)
    return own_part + summed


SLABS = 8
HALF = 4
FIRST, LAST = 0, 7
PASSED = {1: 0, 6: 7}
INNER = (2, 3, 4, 5)


def dot(left, right):
    return jnp.dot(left, right, preferred_element_type=jnp.float32)


def window_mask(first_row, row_start, col_start, rows, first_col, cols, width):
    shape = (rows, cols)
    at_row = lax.broadcasted_iota(jnp.int32, shape, 0) + (first_row - row_start)
    at_col = lax.broadcasted_iota(jnp.int32, shape, 1) + (first_col - col_start)
    wraps = at_col < 0
    at_col = jnp.where(wraps, at_col + width, at_col)
    row_term = 2 * at_row + 1 - width
    col_term = 2 * at_col + 1 - width
    return row_term * row_term + col_term * col_term < width * width, wraps


def row_block(window, table):
    both = dot(window, table)
    half = both.shape[0] // 2
    row_re = both[:half, :LANES] + both[half:, LANES:]
    row_im = both[half:, :LANES] - both[:half, LANES:]
    return row_re.astype(jnp.bfloat16), row_im.astype(jnp.bfloat16)


def store_parts(out, values):
    per = out.shape[0] // 2
    rows = out.shape[1]
    for plane, value in enumerate(values):
        for led in range(per):
            out[plane * per + led] = value[led * rows : (led + 1) * rows]


def is_one_of(position, slabs):
    return functools.reduce(jnp.logical_or, [position == slab for slab in slabs])


def window_kernel(starts, spectrum, window):
    position = lax.axis_index("slab")
    leds = starts.shape[0] // 2
    rows = spectrum.shape[1]
    width = window.shape[1]
    for led in range(leds):
        inside, wraps = window_mask(
            position * rows, starts[led], starts[leds + led], rows, 0, width, width
        )
        for plane in range(2):
            value = jnp.where(wraps, spectrum[plane, :, width:], spectrum[plane, :, :width])
            at = (plane * leds + led) * rows
            window[at : at + rows, :] = jnp.where(inside, value, 0.0).astype(jnp.bfloat16)


def classes_of(position):
    hands_over = is_one_of(position, PASSED)
    return (jnp.where(hands_over, 5, 6), 7, 2, 4, jnp.where(hands_over, 6, 5), 0, 1, 3)


def rows_kernel(which, window, table, *outs):
    position = lax.axis_index("slab")
    for out, d in zip(outs, classes_of(position)[which]):
        store_parts(out, row_block(window[...], table[jnp.bitwise_xor(position, d)]))


def choose_kernel(got, own, out):
    passes = is_one_of(lax.axis_index("slab"), PASSED.values())

    @pl.when(passes)
    def _():
        out[...] = got[...]

    @pl.when(jnp.logical_not(passes))
    def _():
        out[...] = own[...]


def amplitude_kernel(images, table, out, table_out):
    leds, block, width = images.shape
    for led in range(leds):
        for j in range(width // LANES):
            piece = jnp.sqrt(images[led, :, j * LANES : (j + 1) * LANES])
            out[j * LANES : (j + 1) * LANES, led * block : (led + 1) * block] = piece.T
    table_out[...] = table[...]


def field_kernel(amplitude, table, *rest):
    far, near = rest[:5], rest[5 : HALF + 5]
    outs = rest[HALF + 5 : 2 * HALF + 5]
    field_in, diff, strips = rest[2 * HALF + 5 :]
    position = lax.axis_index("slab")
    parts, rows, _ = near[0].shape
    half = parts // 2 * LANES
    width = field_in.shape[0]
    steps = width // LANES
    group = 4
    for d, block in enumerate(near):
        at = pl.multiple_of(jnp.bitwise_and(jnp.bitwise_xor(position, d), HALF - 1) * rows, rows)
        for part in range(parts):
            cols = slice(part * LANES, (part + 1) * LANES)
            field_in[pl.ds(at, rows), cols] = block[part]

    def add(block, origin):
        at = pl.multiple_of(jnp.bitwise_and(origin, HALF - 1) * rows, rows)
        for part in range(parts):
            cols = slice(part * LANES, (part + 1) * LANES)
            field_in[pl.ds(at, rows), cols] += block[part]

    passes = is_one_of(position, PASSED.values())
    hands_over = is_one_of(position, PASSED)
    ends = is_one_of(position, [to ^ 4 for to in PASSED.values()])

    @pl.when(is_one_of(position, INNER))
    def _():
        add(far[0], jnp.bitwise_xor(position, 6))
        add(far[1], jnp.bitwise_xor(position, 7))
        add(far[2], jnp.bitwise_xor(position, jnp.where(ends, 5, 4)))

    @pl.when(jnp.logical_or(passes, hands_over))
    def _():
        add(far[2], jnp.bitwise_xor(position, 4))
        add(far[3], jnp.bitwise_xor(position, jnp.where(hands_over, 7, 6)))
        add(far[4], jnp.bitwise_xor(position, 5))

    for first in range(0, steps, group):
        product = dot(
            table[first : first + group].reshape(group * 2 * LANES, width), field_in[...]
        )
        for j in range(first, first + group):
            both = product[(j - first) * 2 * LANES : (j - first + 1) * 2 * LANES]
            field_re = both[:LANES, :half] + both[LANES:, half:]
            field_im = both[:LANES, half:] - both[LANES:, :half]
            here = pl.ds(j * LANES, LANES)
            factor = (
                amplitude[here, :] * lax.rsqrt(field_re * field_re + field_im * field_im + 0.25)
                - 1.0
            )
            diff[here, :half] = (field_re * factor).astype(jnp.bfloat16)
            diff[here, half:] = (field_im * factor).astype(jnp.bfloat16)
    pieces = rows // LANES
    for i in range(HALF):
        product = dot(
            table[i * pieces : (i + 1) * pieces].reshape(pieces * 2 * LANES, width), diff[...]
        )
        for h in range(pieces):
            both = product[h * 2 * LANES : (h + 1) * 2 * LANES]
            here = pl.ds(h * LANES, LANES)
            back_re = (both[:LANES, :half] - both[LANES:, half:]).astype(jnp.bfloat16)
            back_im = (both[:LANES, half:] + both[LANES:, :half]).astype(jnp.bfloat16)
            for part in range(parts // 2):
                cols = slice(part * LANES, (part + 1) * LANES)
                strips[i, part, here, :] = back_re[:, cols]
                strips[i, parts // 2 + part, here, :] = back_im[:, cols]
    for d, out in enumerate(outs):
        out[...] = strips[jnp.bitwise_and(jnp.bitwise_xor(position, d), HALF - 1)]


def update_columns(own_core, starts, table, back, outs):
    position = lax.axis_index("slab")
    led_at = lax.axis_index("led")
    core = jnp.bitwise_and(led_at, 1)
    plane_x = jnp.right_shift(led_at, 1)
    which_half = jnp.right_shift(position, 2)
    first_row = jnp.bitwise_and(position, HALF - 1)
    leds = starts.shape[0] // 2
    rows = back.shape[0] // (2 * leds)
    depth = back.shape[1]
    width = table.shape[1]
    group = width // LANES // 2
    owner = core if own_core else 1 - core
    shape = (rows, LANES)
    for n in range(group):
        block = owner * group + n
        both = dot(
            back[...], table[block, pl.ds(pl.multiple_of(which_half * depth, depth), depth)]
        )
        half = leds * rows
        update = (
            both[:half, :LANES] - both[half:, LANES:],
            both[half:, :LANES] + both[:half, LANES:],
        )
        sums = [[0.0, 0.0] for _ in outs]
        for led in range(leds):
            at_row = lax.broadcasted_iota(jnp.int32, shape, 0) + (
                first_row * rows - starts[led]
            )
            at_col = lax.broadcasted_iota(jnp.int32, shape, 1) + (
                block * LANES - starts[leds + led]
            )
            row_term = 2 * jnp.where(at_row < 0, at_row + width, at_row) + 1 - width
            col_term = 2 * jnp.where(at_col < 0, at_col + width, at_col) + 1 - width
            inside = row_term * row_term + col_term * col_term < width * width
            this_slab = jnp.where(at_row < 0, 1, 0) == which_half
            this_x = jnp.where(at_col < 0, 1, 0) == plane_x
            for plane in range(2):
                piece = jnp.where(inside, update[plane][led * rows : (led + 1) * rows], 0.0)
                for i, at_slab in enumerate(
                    (jnp.where(this_slab, piece, 0.0), jnp.where(this_slab, 0.0, piece))
                ):
                    sums[2 * i][plane] += jnp.where(this_x, at_slab, 0.0)
                    sums[2 * i + 1][plane] += jnp.where(this_x, 0.0, at_slab)
        cols = slice(n * LANES, (n + 1) * LANES)
        for out, both_planes in zip(outs, sums):
            for plane in range(2):
                out[plane, :, cols] = both_planes[plane].astype(out.dtype)


def sent_kernel(starts, table, *rest):
    blocks = rest[:HALF]
    this_slab, that_slab, back = rest[HALF:]
    position = lax.axis_index("slab")
    parts, rows, _ = blocks[0].shape
    for d, block in enumerate(blocks):
        source = jnp.bitwise_and(jnp.bitwise_xor(position, d), HALF - 1)
        at = pl.multiple_of(source * LANES, LANES)
        for part in range(parts):
            back[part * rows : (part + 1) * rows, pl.ds(at, LANES)] = block[part]
    outs = [out.at[i] for out in (this_slab, that_slab) for i in range(2)]
    update_columns(False, starts, table, back, outs)


def kept_kernel(starts, table, back, *outs):
    update_columns(True, starts, table, back, outs)


def z_first_kernel(that_near, that_far, got_that, out):
    cols = out.shape[3]
    for i, kept in enumerate((that_near, that_far)):
        total = kept[:, :, :cols] + got_that[i, :, :, :cols].astype(jnp.float32)
        out[i] = total.astype(out.dtype)


def x_first_kernel(that_far, got_that, out):
    cols = that_far.shape[2] - out.shape[2]
    total = that_far[:, :, cols:] + got_that[1, :, :, cols:].astype(jnp.float32)
    out[...] = total.astype(out.dtype)


def z_second_kernel(that_near, got_that, got_x, out):
    cols = that_near.shape[2] - out.shape[2]
    total = that_near[:, :, cols:] + got_that[0, :, :, cols:].astype(jnp.float32)
    out[...] = (total + got_x[...].astype(jnp.float32)).astype(out.dtype)


def x_second_kernel(this_far, got_this, got_z, out):
    cols = got_z.shape[3]
    total = this_far[...] + got_this[1].astype(jnp.float32)
    out[:, :, cols:] = total[:, :, cols:].astype(out.dtype)
    out[:, :, :cols] = (total[:, :, :cols] + got_z[1].astype(jnp.float32)).astype(out.dtype)


def local_call(kernel, out_shape, spaces, scratch, flops, moved, name):
    return pl.pallas_call(
        kernel,
        out_shape=out_shape,
        in_specs=[pl.BlockSpec(memory_space=space) for space in spaces],
        out_specs=jax.tree.map(lambda _: pl.BlockSpec(memory_space=pltpu.VMEM), out_shape),
        scratch_shapes=scratch,
        compiler_params=pltpu.CompilerParams(vmem_limit_bytes=32 * 2**20),
        cost_estimate=pl.CostEstimate(flops=flops, bytes_accessed=moved, transcendentals=0),
        name=name,
    )


def body_slabs(spectrum, led_rows, led_cols, images):
    leds, block, width = images.shape
    rows = spectrum.shape[1]
    led_at = lax.axis_index("led")
    bf16 = jnp.bfloat16
    vmem, smem = pltpu.VMEM, pltpu.SMEM
    cos_table, sin_table = host_tables(width)
    steps = width // LANES
    by_col = np.stack(
        [
            np.concatenate([t[:, j * LANES : (j + 1) * LANES] for t in (cos_table, sin_table)], 1)
            for j in range(steps)
        ]
    )
    by_row = jnp.asarray(np.ascontiguousarray(by_col.transpose(0, 2, 1)))
    by_col = jnp.asarray(by_col)
    parts = 2 * leds
    sent_block = jax.ShapeDtypeStruct((parts, rows, LANES), bf16)
    flops = 8 * leds * rows * width * width

    starts = jnp.concatenate([led_rows, led_cols]).astype(jnp.int32)
    window = local_call(
        window_kernel,
        jax.ShapeDtypeStruct((parts * rows, width), bf16),
        [smem, vmem],
        [],
        0,
        6 * 2**20,
        "windows",
    )(starts, spectrum)

    def rows_call(which, name):
        count = which.stop - which.start
        return local_call(
            functools.partial(rows_kernel, which),
            [sent_block] * count,
            [vmem, vmem],
            [],
            flops * count // SLABS,
            5 * 2**20,
            name,
        )(window, by_col)

    first_a, first_b, near_2 = rows_call(slice(0, 3), "rows_round_1")

    def permute(sent, pairs):
        return lax.ppermute(sent, "slab", pairs)

    def choose(got, own, name):
        return local_call(
            choose_kernel, sent_block, [vmem] * 2, [], 0, 2**19, name
        )(got, own)

    handed = list(PASSED.items())
    windowed = range(FIRST + 1, LAST)
    got_a = permute(first_a, [(s, s ^ 6) for s in INNER] + handed)
    got_b = permute(first_b, [(s, s ^ 7) for s in INNER] + handed)
    near_2 = permute(near_2, [(s, s ^ 2) for s in windowed])
    second_a, second_b, near_0, near_1, near_3 = rows_call(slice(3, SLABS), "rows_round_2")
    got_a, second_a, second_b, near_1, near_3, images = lax.optimization_barrier(
        (got_a, second_a, second_b, near_1, near_3, images)
    )
    outer_pairs = [(s, s ^ 6) for s in range(SLABS) if s not in INNER]
    far_columns = [
        got_a,
        got_b,
        permute(choose(got_a, second_a, "class_4_blocks"), [(s, s ^ 4) for s in range(SLABS)]),
        permute(choose(got_b, second_b, "class_6_blocks"), outer_pairs),
        permute(second_b, [(s, s ^ 5) for s in INNER]),
    ]
    near_1 = permute(near_1, [(s, s ^ 1) for s in windowed])
    near_3 = permute(near_3, [(s, s ^ 3) for s in windowed])
    near_columns = [near_0, near_1, near_2, near_3]
    amplitude, by_row = local_call(
        amplitude_kernel,
        [
            jax.ShapeDtypeStruct((width, leds * block), jnp.float32),
            jax.ShapeDtypeStruct(by_row.shape, bf16),
        ],
        [vmem] * 2,
        [],
        0,
        10 * 2**20,
        "amplitude",
    )(images, by_row)
    strips = local_call(
        field_kernel,
        [sent_block] * HALF,
        [vmem] * 11,
        [pltpu.VMEM((width, parts * block), bf16)] * 2
        + [pltpu.VMEM((HALF,) + sent_block.shape, bf16)],
        16 * leds * block * width * width,
        12 * 2**20,
        "modulus_step",
    )(amplitude, by_row, *far_columns, *near_columns)

    def send_home(d):
        pairs = [(s, (s + d) % SLABS) for s in range(SLABS) if FIRST < (s + d) % SLABS < LAST]
        return permute(strips[d % HALF], pairs)

    home = [strips[0]]
    home += [
        permute(strips[d], [(s, s ^ d) for s in range(SLABS)]) for d in range(1, HALF)
    ]
    share = width // 2
    first = share // 4
    piece = (2, rows, share)
    cores = [(0, 1), (1, 0), (2, 3), (3, 2)]
    planes = [(0, 2), (2, 0), (1, 3), (3, 1)]
    across = [(s, s ^ 4) for s in range(SLABS) if FIRST < s ^ 4 < LAST]
    sent_this, sent_that, back = local_call(
        sent_kernel,
        [
            jax.ShapeDtypeStruct((2,) + piece, bf16),
            jax.ShapeDtypeStruct((2,) + piece, bf16),
            jax.ShapeDtypeStruct((parts * rows, HALF * LANES), bf16),
        ],
        [smem] + [vmem] * (1 + HALF),
        [],
        flops // 4,
        8 * 2**20,
        "update_sent",
    )(starts, by_col, *home)
    got_that = lax.ppermute(sent_that, "led", cores)
    got_this = lax.ppermute(sent_this, "led", cores)
    this_near, this_far, that_near, that_far = local_call(
        kept_kernel,
        [jax.ShapeDtypeStruct(piece, jnp.float32)] * 4,
        [smem, vmem, vmem],
        [],
        flops // 4,
        10 * 2**20,
        "update_kept",
    )(starts, by_col, back)

    def sum_call(kernel, shape, *values):
        out_shape = jax.ShapeDtypeStruct(shape, bf16)
        specs = [vmem] * len(values)
        return local_call(kernel, out_shape, specs, [], 0, 2**20, kernel.__name__)(*values)

    over = sum_call(z_first_kernel, (2, 2, rows, first), that_near, that_far, got_that)
    got_z_first = permute(over, across)
    over = sum_call(x_first_kernel, (2, rows, share - first), that_far, got_that)
    got_x = lax.ppermute(over, "led", planes)
    over = sum_call(z_second_kernel, (2, rows, share - first), that_near, got_that, got_x)
    got_z_second = permute(over, across)
    over = sum_call(x_second_kernel, piece, this_far, got_this, got_z_first)
    got_x = lax.ppermute(over, "led", planes)

    def widen(value, before):
        after = share - before - value.shape[2]
        return jnp.pad(value.astype(jnp.float32), ((0, 0), (0, 0), (before, after)))

    base = lax.dynamic_slice_in_dim(spectrum, led_at * share, share, 2)
    base += this_near + got_this[0].astype(jnp.float32) + got_x.astype(jnp.float32)
    base += widen(got_z_first[0], 0)
    base, got_z_second = lax.optimization_barrier((base, got_z_second))
    return base + widen(got_z_second, first)


def solution(mesh):
    placed = (P(None, "slab", None), P("led"), P("led"), P("led", "slab", None))
    fits = mesh.shape["slab"] == 8 and mesh.shape["led"] == 4

    def body(spectrum, led_rows, led_cols, images):
        shapes = (spectrum.shape, images.shape)
        if fits and shapes == ((2, 256, 2048), (2, 128, 1024)):
            return body_slabs(spectrum, led_rows, led_cols, images)
        return body_any(spectrum, led_rows, led_cols, images)

    return jax.shard_map(
        body, mesh=mesh, in_specs=placed, out_specs=P(None, "slab", "led"), check_vma=False
    )
```

```python
import functools

import jax
import jax.numpy as jnp
import numpy as np
from jax import lax
from jax.experimental import pallas as pl
from jax.experimental.pallas import tpu as pltpu
from jax.sharding import PartitionSpec as P

LANES = 128


def as_sent(value):
    return jax.tree.map(lambda a: a.astype(jnp.bfloat16) if a.dtype == jnp.float32 else a, value)


def host_tables(width):
    index = np.arange(width, dtype=np.int64)
    angle_index = (index[:, None] * index[None, :] % width).astype(np.float32)
    angle = angle_index * np.float32(2.0 * 3.141592653589793 / width)
    scale = np.float32(1.0) / np.sqrt(np.float32(width))
    return (
        (np.cos(angle) * scale).astype(jnp.bfloat16),
        (np.sin(angle) * scale).astype(jnp.bfloat16),
    )


def make_pupil(row_index, col_index, width):
    row_term = (2 * row_index + 1 - width) * (2 * row_index + 1 - width)
    col_term = (2 * col_index + 1 - width) * (2 * col_index + 1 - width)
    return (row_term[:, None] + col_term[None, :] < width * width).astype(jnp.float32)


def contract(form, left, right):
    return jnp.einsum(form, left, right, preferred_element_type=jnp.float32)


def take_rows(strip, start, width):
    return lax.dynamic_slice_in_dim(strip, start, width, 1)


def place_rows(block, start, total, axis_dim):
    shape = list(block.shape)
    shape[axis_dim] = total
    holder = jnp.zeros(tuple(shape), block.dtype)
    return lax.dynamic_update_slice_in_dim(holder, block, start, axis_dim)


def modulus_step(field_in_re, field_in_im, image, cos_table, sin_table):
    field_re = contract("lka,am->lkm", field_in_re, cos_table) + contract(
        "lka,am->lkm", field_in_im, sin_table
    )
    field_im = contract("lka,am->lkm", field_in_im, cos_table) - contract(
        "lka,am->lkm", field_in_re, sin_table
    )
    factor = jnp.sqrt(image) / jnp.sqrt(field_re * field_re + field_im * field_im + 0.25) - 1.0
    diff_re = (field_re * factor).astype(jnp.bfloat16)
    diff_im = (field_im * factor).astype(jnp.bfloat16)
    back_re = (
        contract("lkm,ma->lka", diff_re, cos_table) - contract("lkm,ma->lka", diff_im, sin_table)
    ).astype(jnp.bfloat16)
    back_im = (
        contract("lkm,ma->lka", diff_im, cos_table) + contract("lkm,ma->lka", diff_re, sin_table)
    ).astype(jnp.bfloat16)
    return (back_re, back_im)


def body_any(spectrum, led_rows, led_cols, images):
    width = images.shape[2]
    slab_rows = spectrum.shape[1]
    columns = spectrum.shape[2]
    slabs = lax.axis_size("slab")
    total_rows = slab_rows * slabs
    position = lax.axis_index("slab")
    cos_table, sin_table = (jnp.asarray(t) for t in host_tables(width))
    own_rows = position * slab_rows + jnp.arange(slab_rows, dtype=jnp.int32)
    col_index = jnp.arange(width, dtype=jnp.int32)

    def take_cols(start):
        return lax.dynamic_slice_in_dim(spectrum, start, width, 2)

    def owner_mask(start):
        return make_pupil(own_rows - start, col_index, width)

    windows = jax.vmap(take_cols)(led_cols)
    masks = jax.vmap(owner_mask)(led_rows)
    win_re = (windows[:, 0] * masks).astype(jnp.bfloat16)
    win_im = (windows[:, 1] * masks).astype(jnp.bfloat16)

    def slice_strip(block, start):
        return take_rows(block, start, width)

    row_re = (
        contract("lgb,bk->lkg", win_re, cos_table) + contract("lgb,bk->lkg", win_im, sin_table)
    ).astype(jnp.bfloat16)
    row_im = (
        contract("lgb,bk->lkg", win_im, cos_table) - contract("lgb,bk->lkg", win_re, sin_table)
    ).astype(jnp.bfloat16)
    col_re, col_im = (
        lax.all_to_all(row_re, "slab", split_axis=1, concat_axis=2, tiled=True),
        lax.all_to_all(row_im, "slab", split_axis=1, concat_axis=2, tiled=True),
    )
    field_in_re = jax.vmap(slice_strip)(col_re, led_rows)
    field_in_im = jax.vmap(slice_strip)(col_im, led_rows)
    back_re, back_im = modulus_step(field_in_re, field_in_im, images, cos_table, sin_table)

    def place_strip(block, start):
        return place_rows(block, start, total_rows, 1)

    full_re = jax.vmap(place_strip)(back_re, led_rows)
    full_im = jax.vmap(place_strip)(back_im, led_rows)
    home_re, home_im = (
        lax.all_to_all(as_sent(full_re), "slab", split_axis=2, concat_axis=1, tiled=True).astype(
            full_re.dtype
        ),
        lax.all_to_all(as_sent(full_im), "slab", split_axis=2, concat_axis=1, tiled=True).astype(
            full_im.dtype
        ),
    )
    upd_re = contract("lkg,kb->lgb", home_re, cos_table) - contract(
        "lkg,kb->lgb", home_im, sin_table
    )
    upd_im = contract("lkg,kb->lgb", home_im, cos_table) + contract(
        "lkg,kb->lgb", home_re, sin_table
    )
    upd_re = upd_re * masks
    upd_im = upd_im * masks

    def add_window(number, gradient):
        start = led_cols[number]
        piece = jnp.stack([upd_re[number], upd_im[number]])
        current = lax.dynamic_slice_in_dim(gradient, start, width, 2)
        return lax.dynamic_update_slice_in_dim(gradient, current + piece, start, 2)

    gradient = lax.fori_loop(
        0, led_rows.shape[0], add_window, jnp.zeros((2, slab_rows, columns), jnp.float32)
    )
    summed = lax.psum_scatter(gradient, "led", scatter_dimension=2, tiled=True)
    share = summed.shape[2]
    own_part = lax.dynamic_slice_in_dim(spectrum, lax.axis_index("led") * share, share, 2)
    return own_part + summed


SLABS = 8
HALF = 4
FIRST, LAST = 0, 7
PASSED = {1: 0, 6: 7}
INNER = (2, 3, 4, 5)


def dot(left, right):
    return jnp.dot(left, right, preferred_element_type=jnp.float32)


def window_mask(first_row, row_start, col_start, rows, first_col, cols, width):
    shape = (rows, cols)
    at_row = lax.broadcasted_iota(jnp.int32, shape, 0) + (first_row - row_start)
    at_col = lax.broadcasted_iota(jnp.int32, shape, 1) + (first_col - col_start)
    wraps = at_col < 0
    at_col = jnp.where(wraps, at_col + width, at_col)
    row_term = 2 * at_row + 1 - width
    col_term = 2 * at_col + 1 - width
    return row_term * row_term + col_term * col_term < width * width, wraps


def row_block(window, table):
    both = dot(window, table)
    half = both.shape[0] // 2
    row_re = both[:half, :LANES] + both[half:, LANES:]
    row_im = both[half:, :LANES] - both[:half, LANES:]
    return row_re.astype(jnp.bfloat16), row_im.astype(jnp.bfloat16)


def store_parts(out, values):
    per = out.shape[0] // 2
    rows = out.shape[1]
    for plane, value in enumerate(values):
        for led in range(per):
            out[plane * per + led] = value[led * rows : (led + 1) * rows]


def is_one_of(position, slabs):
    return functools.reduce(jnp.logical_or, [position == slab for slab in slabs])


def window_kernel(starts, spectrum, window):
    position = lax.axis_index("slab")
    leds = starts.shape[0] // 2
    rows = spectrum.shape[1]
    width = window.shape[1]
    for led in range(leds):
        inside, wraps = window_mask(
            position * rows, starts[led], starts[leds + led], rows, 0, width, width
        )
        for plane in range(2):
            value = jnp.where(wraps, spectrum[plane, :, width:], spectrum[plane, :, :width])
            at = (plane * leds + led) * rows
            window[at : at + rows, :] = jnp.where(inside, value, 0.0).astype(jnp.bfloat16)


def classes_of(position):
    hands_over = is_one_of(position, PASSED)
    return (jnp.where(hands_over, 5, 6), 7, 2, 4, jnp.where(hands_over, 6, 5), 0, 1, 3)


def rows_kernel(which, window, table, *outs):
    position = lax.axis_index("slab")
    for out, d in zip(outs, classes_of(position)[which]):
        store_parts(out, row_block(window[...], table[jnp.bitwise_xor(position, d)]))


def choose_kernel(got, own, out):
    passes = is_one_of(lax.axis_index("slab"), PASSED.values())

    @pl.when(passes)
    def _():
        out[...] = got[...]

    @pl.when(jnp.logical_not(passes))
    def _():
        out[...] = own[...]


def amplitude_kernel(images, table, out, table_out):
    leds, block, width = images.shape
    for led in range(leds):
        for j in range(width // LANES):
            piece = jnp.sqrt(images[led, :, j * LANES : (j + 1) * LANES])
            out[j * LANES : (j + 1) * LANES, led * block : (led + 1) * block] = piece.T
    table_out[...] = table[...]


def field_kernel(amplitude, table, *rest):
    far, near = rest[:5], rest[5 : HALF + 5]
    outs = rest[HALF + 5 : 2 * HALF + 5]
    field_in, diff, strips = rest[2 * HALF + 5 :]
    position = lax.axis_index("slab")
    parts, rows, _ = near[0].shape
    half = parts // 2 * LANES
    width = field_in.shape[0]
    steps = width // LANES
    group = 4
    for d, block in enumerate(near):
        at = pl.multiple_of(jnp.bitwise_and(jnp.bitwise_xor(position, d), HALF - 1) * rows, rows)
        for part in range(parts):
            cols = slice(part * LANES, (part + 1) * LANES)
            field_in[pl.ds(at, rows), cols] = block[part]

    def add(block, origin):
        at = pl.multiple_of(jnp.bitwise_and(origin, HALF - 1) * rows, rows)
        for part in range(parts):
            cols = slice(part * LANES, (part + 1) * LANES)
            field_in[pl.ds(at, rows), cols] += block[part]

    passes = is_one_of(position, PASSED.values())
    hands_over = is_one_of(position, PASSED)
    ends = is_one_of(position, [to ^ 4 for to in PASSED.values()])

    @pl.when(is_one_of(position, INNER))
    def _():
        add(far[0], jnp.bitwise_xor(position, 6))
        add(far[1], jnp.bitwise_xor(position, 7))
        add(far[2], jnp.bitwise_xor(position, jnp.where(ends, 5, 4)))

    @pl.when(jnp.logical_or(passes, hands_over))
    def _():
        add(far[2], jnp.bitwise_xor(position, 4))
        add(far[3], jnp.bitwise_xor(position, jnp.where(hands_over, 7, 6)))
        add(far[4], jnp.bitwise_xor(position, 5))

    for first in range(0, steps, group):
        product = dot(
            table[first : first + group].reshape(group * 2 * LANES, width), field_in[...]
        )
        for j in range(first, first + group):
            both = product[(j - first) * 2 * LANES : (j - first + 1) * 2 * LANES]
            field_re = both[:LANES, :half] + both[LANES:, half:]
            field_im = both[:LANES, half:] - both[LANES:, :half]
            here = pl.ds(j * LANES, LANES)
            factor = (
                amplitude[here, :] * lax.rsqrt(field_re * field_re + field_im * field_im + 0.25)
                - 1.0
            )
            diff[here, :half] = (field_re * factor).astype(jnp.bfloat16)
            diff[here, half:] = (field_im * factor).astype(jnp.bfloat16)
    pieces = rows // LANES
    for i in range(HALF):
        product = dot(
            table[i * pieces : (i + 1) * pieces].reshape(pieces * 2 * LANES, width), diff[...]
        )
        for h in range(pieces):
            both = product[h * 2 * LANES : (h + 1) * 2 * LANES]
            here = pl.ds(h * LANES, LANES)
            back_re = (both[:LANES, :half] - both[LANES:, half:]).astype(jnp.bfloat16)
            back_im = (both[:LANES, half:] + both[LANES:, :half]).astype(jnp.bfloat16)
            for part in range(parts // 2):
                cols = slice(part * LANES, (part + 1) * LANES)
                strips[i, part, here, :] = back_re[:, cols]
                strips[i, parts // 2 + part, here, :] = back_im[:, cols]
    for d, out in enumerate(outs):
        out[...] = strips[jnp.bitwise_and(jnp.bitwise_xor(position, d), HALF - 1)]


def update_columns(own_core, starts, table, back, outs):
    position = lax.axis_index("slab")
    led_at = lax.axis_index("led")
    core = jnp.bitwise_and(led_at, 1)
    plane_x = jnp.right_shift(led_at, 1)
    which_half = jnp.right_shift(position, 2)
    first_row = jnp.bitwise_and(position, HALF - 1)
    leds = starts.shape[0] // 2
    rows = back.shape[0] // (2 * leds)
    depth = back.shape[1]
    width = table.shape[1]
    group = width // LANES // 2
    owner = core if own_core else 1 - core
    shape = (rows, LANES)
    for n in range(group):
        block = owner * group + n
        both = dot(
            back[...], table[block, pl.ds(pl.multiple_of(which_half * depth, depth), depth)]
        )
        half = leds * rows
        update = (
            both[:half, :LANES] - both[half:, LANES:],
            both[half:, :LANES] + both[:half, LANES:],
        )
        sums = [[0.0, 0.0] for _ in outs]
        for led in range(leds):
            at_row = lax.broadcasted_iota(jnp.int32, shape, 0) + (
                first_row * rows - starts[led]
            )
            at_col = lax.broadcasted_iota(jnp.int32, shape, 1) + (
                block * LANES - starts[leds + led]
            )
            row_term = 2 * jnp.where(at_row < 0, at_row + width, at_row) + 1 - width
            col_term = 2 * jnp.where(at_col < 0, at_col + width, at_col) + 1 - width
            inside = row_term * row_term + col_term * col_term < width * width
            this_slab = jnp.where(at_row < 0, 1, 0) == which_half
            this_x = jnp.where(at_col < 0, 1, 0) == plane_x
            for plane in range(2):
                piece = jnp.where(inside, update[plane][led * rows : (led + 1) * rows], 0.0)
                for i, at_slab in enumerate(
                    (jnp.where(this_slab, piece, 0.0), jnp.where(this_slab, 0.0, piece))
                ):
                    sums[2 * i][plane] += jnp.where(this_x, at_slab, 0.0)
                    sums[2 * i + 1][plane] += jnp.where(this_x, 0.0, at_slab)
        cols = slice(n * LANES, (n + 1) * LANES)
        for out, both_planes in zip(outs, sums):
            for plane in range(2):
                out[plane, :, cols] = both_planes[plane].astype(out.dtype)


def sent_kernel(starts, table, *rest):
    blocks = rest[:HALF]
    this_slab, that_slab, back = rest[HALF:]
    position = lax.axis_index("slab")
    parts, rows, _ = blocks[0].shape
    for d, block in enumerate(blocks):
        source = jnp.bitwise_and(jnp.bitwise_xor(position, d), HALF - 1)
        at = pl.multiple_of(source * LANES, LANES)
        for part in range(parts):
            back[part * rows : (part + 1) * rows, pl.ds(at, LANES)] = block[part]
    outs = [out.at[i] for out in (this_slab, that_slab) for i in range(2)]
    update_columns(False, starts, table, back, outs)


def kept_kernel(starts, table, back, *outs):
    update_columns(True, starts, table, back, outs)


def z_first_kernel(that_near, that_far, got_that, out):
    cols = out.shape[3]
    for i, kept in enumerate((that_near, that_far)):
        total = kept[:, :, :cols] + got_that[i, :, :, :cols].astype(jnp.float32)
        out[i] = total.astype(out.dtype)


def x_first_kernel(that_far, got_that, out):
    cols = that_far.shape[2] - out.shape[2]
    total = that_far[:, :, cols:] + got_that[1, :, :, cols:].astype(jnp.float32)
    out[...] = total.astype(out.dtype)


def z_second_kernel(that_near, got_that, got_x, out):
    cols = that_near.shape[2] - out.shape[2]
    total = that_near[:, :, cols:] + got_that[0, :, :, cols:].astype(jnp.float32)
    out[...] = (total + got_x[...].astype(jnp.float32)).astype(out.dtype)


def x_second_kernel(this_far, got_this, got_z, out):
    cols = got_z.shape[3]
    total = this_far[...] + got_this[1].astype(jnp.float32)
    out[:, :, cols:] = total[:, :, cols:].astype(out.dtype)
    out[:, :, :cols] = (total[:, :, :cols] + got_z[1].astype(jnp.float32)).astype(out.dtype)


def local_call(kernel, out_shape, spaces, scratch, flops, moved, name):
    return pl.pallas_call(
        kernel,
        out_shape=out_shape,
        in_specs=[pl.BlockSpec(memory_space=space) for space in spaces],
        out_specs=jax.tree.map(lambda _: pl.BlockSpec(memory_space=pltpu.VMEM), out_shape),
        scratch_shapes=scratch,
        compiler_params=pltpu.CompilerParams(vmem_limit_bytes=32 * 2**20),
        cost_estimate=pl.CostEstimate(flops=flops, bytes_accessed=moved, transcendentals=0),
        name=name,
    )


def body_slabs(spectrum, led_rows, led_cols, images):
    leds, block, width = images.shape
    rows = spectrum.shape[1]
    led_at = lax.axis_index("led")
    bf16 = jnp.bfloat16
    vmem, smem = pltpu.VMEM, pltpu.SMEM
    cos_table, sin_table = host_tables(width)
    steps = width // LANES
    by_col = np.stack(
        [
            np.concatenate([t[:, j * LANES : (j + 1) * LANES] for t in (cos_table, sin_table)], 1)
            for j in range(steps)
        ]
    )
    by_row = jnp.asarray(np.ascontiguousarray(by_col.transpose(0, 2, 1)))
    by_col = jnp.asarray(by_col)
    parts = 2 * leds
    sent_block = jax.ShapeDtypeStruct((parts, rows, LANES), bf16)
    flops = 8 * leds * rows * width * width

    starts = jnp.concatenate([led_rows, led_cols]).astype(jnp.int32)
    window = local_call(
        window_kernel,
        jax.ShapeDtypeStruct((parts * rows, width), bf16),
        [smem, vmem],
        [],
        0,
        6 * 2**20,
        "windows",
    )(starts, spectrum)

    def rows_call(which, name):
        count = which.stop - which.start
        return local_call(
            functools.partial(rows_kernel, which),
            [sent_block] * count,
            [vmem, vmem],
            [],
            flops * count // SLABS,
            5 * 2**20,
            name,
        )(window, by_col)

    first_a, first_b, near_2 = rows_call(slice(0, 3), "rows_round_1")

    def permute(sent, pairs):
        return lax.ppermute(sent, "slab", pairs)

    def choose(got, own, name):
        return local_call(
            choose_kernel, sent_block, [vmem] * 2, [], 0, 2**19, name
        )(got, own)

    handed = list(PASSED.items())
    windowed = range(FIRST + 1, LAST)
    got_a = permute(first_a, [(s, s ^ 6) for s in INNER] + handed)
    got_b = permute(first_b, [(s, s ^ 7) for s in INNER] + handed)
    near_2 = permute(near_2, [(s, s ^ 2) for s in windowed])
    second_a, second_b, near_0, near_1, near_3 = rows_call(slice(3, SLABS), "rows_round_2")
    got_a, near_2, second_a, second_b, near_1, near_3, images = lax.optimization_barrier(
        (got_a, near_2, second_a, second_b, near_1, near_3, images)
    )
    outer_pairs = [(s, s ^ 6) for s in range(SLABS) if s not in INNER]
    near_1 = permute(near_1, [(s, s ^ 1) for s in windowed])
    near_3 = permute(near_3, [(s, s ^ 3) for s in windowed])
    near_1, got_b = lax.optimization_barrier((near_1, got_b))
    far_columns = [
        got_a,
        got_b,
        permute(choose(got_a, second_a, "class_4_blocks"), [(s, s ^ 4) for s in range(SLABS)]),
        permute(choose(got_b, second_b, "class_6_blocks"), outer_pairs),
        permute(second_b, [(s, s ^ 5) for s in INNER]),
    ]
    near_columns = [near_0, near_1, near_2, near_3]
    amplitude, by_row = local_call(
        amplitude_kernel,
        [
            jax.ShapeDtypeStruct((width, leds * block), jnp.float32),
            jax.ShapeDtypeStruct(by_row.shape, bf16),
        ],
        [vmem] * 2,
        [],
        0,
        10 * 2**20,
        "amplitude",
    )(images, by_row)
    strips = local_call(
        field_kernel,
        [sent_block] * HALF,
        [vmem] * 11,
        [pltpu.VMEM((width, parts * block), bf16)] * 2
        + [pltpu.VMEM((HALF,) + sent_block.shape, bf16)],
        16 * leds * block * width * width,
        12 * 2**20,
        "modulus_step",
    )(amplitude, by_row, *far_columns, *near_columns)

    def send_home(d):
        pairs = [(s, (s + d) % SLABS) for s in range(SLABS) if FIRST < (s + d) % SLABS < LAST]
        return permute(strips[d % HALF], pairs)

    home = [strips[0]]
    home += [
        permute(strips[d], [(s, s ^ d) for s in range(SLABS)]) for d in range(1, HALF)
    ]
    share = width // 2
    first = share // 4
    piece = (2, rows, share)
    cores = [(0, 1), (1, 0), (2, 3), (3, 2)]
    planes = [(0, 2), (2, 0), (1, 3), (3, 1)]
    across = [(s, s ^ 4) for s in range(SLABS) if FIRST < s ^ 4 < LAST]
    sent_this, sent_that, back = local_call(
        sent_kernel,
        [
            jax.ShapeDtypeStruct((2,) + piece, bf16),
            jax.ShapeDtypeStruct((2,) + piece, bf16),
            jax.ShapeDtypeStruct((parts * rows, HALF * LANES), bf16),
        ],
        [smem] + [vmem] * (1 + HALF),
        [],
        flops // 4,
        8 * 2**20,
        "update_sent",
    )(starts, by_col, *home)
    got_that = lax.ppermute(sent_that, "led", cores)
    got_this = lax.ppermute(sent_this, "led", cores)
    this_near, this_far, that_near, that_far = local_call(
        kept_kernel,
        [jax.ShapeDtypeStruct(piece, jnp.float32)] * 4,
        [smem, vmem, vmem],
        [],
        flops // 4,
        10 * 2**20,
        "update_kept",
    )(starts, by_col, back)

    def sum_call(kernel, shape, *values):
        out_shape = jax.ShapeDtypeStruct(shape, bf16)
        specs = [vmem] * len(values)
        return local_call(kernel, out_shape, specs, [], 0, 2**20, kernel.__name__)(*values)

    over = sum_call(z_first_kernel, (2, 2, rows, first), that_near, that_far, got_that)
    got_z_first = permute(over, across)
    over = sum_call(x_first_kernel, (2, rows, share - first), that_far, got_that)
    got_x = lax.ppermute(over, "led", planes)
    over = sum_call(z_second_kernel, (2, rows, share - first), that_near, got_that, got_x)
    got_z_second = permute(over, across)
    over = sum_call(x_second_kernel, piece, this_far, got_this, got_z_first)
    got_x = lax.ppermute(over, "led", planes)

    def widen(value, before):
        after = share - before - value.shape[2]
        return jnp.pad(value.astype(jnp.float32), ((0, 0), (0, 0), (before, after)))

    base = lax.dynamic_slice_in_dim(spectrum, led_at * share, share, 2)
    base += this_near + got_this[0].astype(jnp.float32) + widen(got_z_first[0], 0)
    base, got_x = lax.optimization_barrier((base, got_x))
    base += got_x.astype(jnp.float32)
    base, got_z_second = lax.optimization_barrier((base, got_z_second))
    return base + widen(got_z_second, first)


def solution(mesh):
    placed = (P(None, "slab", None), P("led"), P("led"), P("led", "slab", None))
    fits = mesh.shape["slab"] == 8 and mesh.shape["led"] == 4

    def body(spectrum, led_rows, led_cols, images):
        shapes = (spectrum.shape, images.shape)
        if fits and shapes == ((2, 256, 2048), (2, 128, 1024)):
            return body_slabs(spectrum, led_rows, led_cols, images)
        return body_any(spectrum, led_rows, led_cols, images)

    return jax.shard_map(
        body, mesh=mesh, in_specs=placed, out_specs=P(None, "slab", "led"), check_vma=False
    )
```

```python
import functools

import jax
import jax.numpy as jnp
import numpy as np
from jax import lax
from jax.experimental import pallas as pl
from jax.experimental.pallas import tpu as pltpu
from jax.sharding import PartitionSpec as P

LANES = 128


def as_sent(value):
    return jax.tree.map(lambda a: a.astype(jnp.bfloat16) if a.dtype == jnp.float32 else a, value)


def host_tables(width):
    index = np.arange(width, dtype=np.int64)
    angle_index = (index[:, None] * index[None, :] % width).astype(np.float32)
    angle = angle_index * np.float32(2.0 * 3.141592653589793 / width)
    scale = np.float32(1.0) / np.sqrt(np.float32(width))
    return (
        (np.cos(angle) * scale).astype(jnp.bfloat16),
        (np.sin(angle) * scale).astype(jnp.bfloat16),
    )


def make_pupil(row_index, col_index, width):
    row_term = (2 * row_index + 1 - width) * (2 * row_index + 1 - width)
    col_term = (2 * col_index + 1 - width) * (2 * col_index + 1 - width)
    return (row_term[:, None] + col_term[None, :] < width * width).astype(jnp.float32)


def contract(form, left, right):
    return jnp.einsum(form, left, right, preferred_element_type=jnp.float32)


def take_rows(strip, start, width):
    return lax.dynamic_slice_in_dim(strip, start, width, 1)


def place_rows(block, start, total, axis_dim):
    shape = list(block.shape)
    shape[axis_dim] = total
    holder = jnp.zeros(tuple(shape), block.dtype)
    return lax.dynamic_update_slice_in_dim(holder, block, start, axis_dim)


def modulus_step(field_in_re, field_in_im, image, cos_table, sin_table):
    field_re = contract("lka,am->lkm", field_in_re, cos_table) + contract(
        "lka,am->lkm", field_in_im, sin_table
    )
    field_im = contract("lka,am->lkm", field_in_im, cos_table) - contract(
        "lka,am->lkm", field_in_re, sin_table
    )
    factor = jnp.sqrt(image) / jnp.sqrt(field_re * field_re + field_im * field_im + 0.25) - 1.0
    diff_re = (field_re * factor).astype(jnp.bfloat16)
    diff_im = (field_im * factor).astype(jnp.bfloat16)
    back_re = (
        contract("lkm,ma->lka", diff_re, cos_table) - contract("lkm,ma->lka", diff_im, sin_table)
    ).astype(jnp.bfloat16)
    back_im = (
        contract("lkm,ma->lka", diff_im, cos_table) + contract("lkm,ma->lka", diff_re, sin_table)
    ).astype(jnp.bfloat16)
    return (back_re, back_im)


def body_any(spectrum, led_rows, led_cols, images):
    width = images.shape[2]
    slab_rows = spectrum.shape[1]
    columns = spectrum.shape[2]
    slabs = lax.axis_size("slab")
    total_rows = slab_rows * slabs
    position = lax.axis_index("slab")
    cos_table, sin_table = (jnp.asarray(t) for t in host_tables(width))
    own_rows = position * slab_rows + jnp.arange(slab_rows, dtype=jnp.int32)
    col_index = jnp.arange(width, dtype=jnp.int32)

    def take_cols(start):
        return lax.dynamic_slice_in_dim(spectrum, start, width, 2)

    def owner_mask(start):
        return make_pupil(own_rows - start, col_index, width)

    windows = jax.vmap(take_cols)(led_cols)
    masks = jax.vmap(owner_mask)(led_rows)
    win_re = (windows[:, 0] * masks).astype(jnp.bfloat16)
    win_im = (windows[:, 1] * masks).astype(jnp.bfloat16)

    def slice_strip(block, start):
        return take_rows(block, start, width)

    row_re = (
        contract("lgb,bk->lkg", win_re, cos_table) + contract("lgb,bk->lkg", win_im, sin_table)
    ).astype(jnp.bfloat16)
    row_im = (
        contract("lgb,bk->lkg", win_im, cos_table) - contract("lgb,bk->lkg", win_re, sin_table)
    ).astype(jnp.bfloat16)
    col_re, col_im = (
        lax.all_to_all(row_re, "slab", split_axis=1, concat_axis=2, tiled=True),
        lax.all_to_all(row_im, "slab", split_axis=1, concat_axis=2, tiled=True),
    )
    field_in_re = jax.vmap(slice_strip)(col_re, led_rows)
    field_in_im = jax.vmap(slice_strip)(col_im, led_rows)
    back_re, back_im = modulus_step(field_in_re, field_in_im, images, cos_table, sin_table)

    def place_strip(block, start):
        return place_rows(block, start, total_rows, 1)

    full_re = jax.vmap(place_strip)(back_re, led_rows)
    full_im = jax.vmap(place_strip)(back_im, led_rows)
    home_re, home_im = (
        lax.all_to_all(as_sent(full_re), "slab", split_axis=2, concat_axis=1, tiled=True).astype(
            full_re.dtype
        ),
        lax.all_to_all(as_sent(full_im), "slab", split_axis=2, concat_axis=1, tiled=True).astype(
            full_im.dtype
        ),
    )
    upd_re = contract("lkg,kb->lgb", home_re, cos_table) - contract(
        "lkg,kb->lgb", home_im, sin_table
    )
    upd_im = contract("lkg,kb->lgb", home_im, cos_table) + contract(
        "lkg,kb->lgb", home_re, sin_table
    )
    upd_re = upd_re * masks
    upd_im = upd_im * masks

    def add_window(number, gradient):
        start = led_cols[number]
        piece = jnp.stack([upd_re[number], upd_im[number]])
        current = lax.dynamic_slice_in_dim(gradient, start, width, 2)
        return lax.dynamic_update_slice_in_dim(gradient, current + piece, start, 2)

    gradient = lax.fori_loop(
        0, led_rows.shape[0], add_window, jnp.zeros((2, slab_rows, columns), jnp.float32)
    )
    summed = lax.psum_scatter(gradient, "led", scatter_dimension=2, tiled=True)
    share = summed.shape[2]
    own_part = lax.dynamic_slice_in_dim(spectrum, lax.axis_index("led") * share, share, 2)
    return own_part + summed


SLABS = 8
HALF = 4
FIRST, LAST = 0, 7
PASSED = {1: 0, 6: 7}
INNER = (2, 3, 4, 5)


def dot(left, right):
    return jnp.dot(left, right, preferred_element_type=jnp.float32)


def window_mask(first_row, row_start, col_start, rows, first_col, cols, width):
    shape = (rows, cols)
    at_row = lax.broadcasted_iota(jnp.int32, shape, 0) + (first_row - row_start)
    at_col = lax.broadcasted_iota(jnp.int32, shape, 1) + (first_col - col_start)
    wraps = at_col < 0
    at_col = jnp.where(wraps, at_col + width, at_col)
    row_term = 2 * at_row + 1 - width
    col_term = 2 * at_col + 1 - width
    return row_term * row_term + col_term * col_term < width * width, wraps


def row_block(window, table):
    both = dot(window, table)
    half = both.shape[0] // 2
    row_re = both[:half, :LANES] + both[half:, LANES:]
    row_im = both[half:, :LANES] - both[:half, LANES:]
    return row_re.astype(jnp.bfloat16), row_im.astype(jnp.bfloat16)


def store_parts(out, values):
    per = out.shape[0] // 2
    rows = out.shape[1]
    for plane, value in enumerate(values):
        for led in range(per):
            out[plane * per + led] = value[led * rows : (led + 1) * rows]


def is_one_of(position, slabs):
    return functools.reduce(jnp.logical_or, [position == slab for slab in slabs])


def window_kernel(starts, spectrum, window):
    position = lax.axis_index("slab")
    leds = starts.shape[0] // 2
    rows = spectrum.shape[1]
    width = window.shape[1]
    for led in range(leds):
        inside, wraps = window_mask(
            position * rows, starts[led], starts[leds + led], rows, 0, width, width
        )
        for plane in range(2):
            value = jnp.where(wraps, spectrum[plane, :, width:], spectrum[plane, :, :width])
            at = (plane * leds + led) * rows
            window[at : at + rows, :] = jnp.where(inside, value, 0.0).astype(jnp.bfloat16)


def classes_of(position):
    hands_over = is_one_of(position, PASSED)
    return (jnp.where(hands_over, 5, 6), 7, 2, 4, jnp.where(hands_over, 6, 5), 0, 1, 3)


def rows_kernel(which, window, table, *outs):
    position = lax.axis_index("slab")
    for out, d in zip(outs, classes_of(position)[which]):
        store_parts(out, row_block(window[...], table[jnp.bitwise_xor(position, d)]))


def choose_kernel(got, own, out):
    passes = is_one_of(lax.axis_index("slab"), PASSED.values())

    @pl.when(passes)
    def _():
        out[...] = got[...]

    @pl.when(jnp.logical_not(passes))
    def _():
        out[...] = own[...]


def amplitude_kernel(images, table, out, table_out):
    leds, block, width = images.shape
    for led in range(leds):
        for j in range(width // LANES):
            piece = jnp.sqrt(images[led, :, j * LANES : (j + 1) * LANES])
            out[j * LANES : (j + 1) * LANES, led * block : (led + 1) * block] = piece.T
    table_out[...] = table[...]


def field_kernel(amplitude, table, *rest):
    far, near = rest[:5], rest[5 : HALF + 5]
    outs = rest[HALF + 5 : 2 * HALF + 5]
    field_in, diff, strips = rest[2 * HALF + 5 :]
    position = lax.axis_index("slab")
    parts, rows, _ = near[0].shape
    half = parts // 2 * LANES
    width = field_in.shape[0]
    steps = width // LANES
    group = 4
    for d, block in enumerate(near):
        at = pl.multiple_of(jnp.bitwise_and(jnp.bitwise_xor(position, d), HALF - 1) * rows, rows)
        for part in range(parts):
            cols = slice(part * LANES, (part + 1) * LANES)
            field_in[pl.ds(at, rows), cols] = block[part]

    def add(block, origin):
        at = pl.multiple_of(jnp.bitwise_and(origin, HALF - 1) * rows, rows)
        for part in range(parts):
            cols = slice(part * LANES, (part + 1) * LANES)
            field_in[pl.ds(at, rows), cols] += block[part]

    passes = is_one_of(position, PASSED.values())
    hands_over = is_one_of(position, PASSED)
    ends = is_one_of(position, [to ^ 4 for to in PASSED.values()])

    @pl.when(is_one_of(position, INNER))
    def _():
        add(far[0], jnp.bitwise_xor(position, 6))
        add(far[1], jnp.bitwise_xor(position, 7))
        add(far[2], jnp.bitwise_xor(position, jnp.where(ends, 5, 4)))

    @pl.when(jnp.logical_or(passes, hands_over))
    def _():
        add(far[2], jnp.bitwise_xor(position, 4))
        add(far[3], jnp.bitwise_xor(position, jnp.where(hands_over, 7, 6)))
        add(far[4], jnp.bitwise_xor(position, 5))

    for first in range(0, steps, group):
        product = dot(
            table[first : first + group].reshape(group * 2 * LANES, width), field_in[...]
        )
        for j in range(first, first + group):
            both = product[(j - first) * 2 * LANES : (j - first + 1) * 2 * LANES]
            field_re = both[:LANES, :half] + both[LANES:, half:]
            field_im = both[:LANES, half:] - both[LANES:, :half]
            here = pl.ds(j * LANES, LANES)
            factor = (
                amplitude[here, :] * lax.rsqrt(field_re * field_re + field_im * field_im + 0.25)
                - 1.0
            )
            diff[here, :half] = (field_re * factor).astype(jnp.bfloat16)
            diff[here, half:] = (field_im * factor).astype(jnp.bfloat16)
    pieces = rows // LANES
    for i in range(HALF):
        product = dot(
            table[i * pieces : (i + 1) * pieces].reshape(pieces * 2 * LANES, width), diff[...]
        )
        for h in range(pieces):
            both = product[h * 2 * LANES : (h + 1) * 2 * LANES]
            here = pl.ds(h * LANES, LANES)
            back_re = (both[:LANES, :half] - both[LANES:, half:]).astype(jnp.bfloat16)
            back_im = (both[:LANES, half:] + both[LANES:, :half]).astype(jnp.bfloat16)
            for part in range(parts // 2):
                cols = slice(part * LANES, (part + 1) * LANES)
                strips[i, part, here, :] = back_re[:, cols]
                strips[i, parts // 2 + part, here, :] = back_im[:, cols]
    for d, out in enumerate(outs):
        out[...] = strips[jnp.bitwise_and(jnp.bitwise_xor(position, d), HALF - 1)]


def update_columns(own_core, starts, table, back, outs):
    position = lax.axis_index("slab")
    led_at = lax.axis_index("led")
    core = jnp.bitwise_and(led_at, 1)
    plane_x = jnp.right_shift(led_at, 1)
    which_half = jnp.right_shift(position, 2)
    first_row = jnp.bitwise_and(position, HALF - 1)
    leds = starts.shape[0] // 2
    rows = back.shape[0] // (2 * leds)
    depth = back.shape[1]
    width = table.shape[1]
    group = width // LANES // 2
    owner = core if own_core else 1 - core
    shape = (rows, LANES)
    for n in range(group):
        block = owner * group + n
        both = dot(
            back[...], table[block, pl.ds(pl.multiple_of(which_half * depth, depth), depth)]
        )
        half = leds * rows
        update = (
            both[:half, :LANES] - both[half:, LANES:],
            both[half:, :LANES] + both[:half, LANES:],
        )
        sums = [[0.0, 0.0] for _ in outs]
        for led in range(leds):
            at_row = lax.broadcasted_iota(jnp.int32, shape, 0) + (
                first_row * rows - starts[led]
            )
            at_col = lax.broadcasted_iota(jnp.int32, shape, 1) + (
                block * LANES - starts[leds + led]
            )
            row_term = 2 * jnp.where(at_row < 0, at_row + width, at_row) + 1 - width
            col_term = 2 * jnp.where(at_col < 0, at_col + width, at_col) + 1 - width
            inside = row_term * row_term + col_term * col_term < width * width
            this_slab = jnp.where(at_row < 0, 1, 0) == which_half
            this_x = jnp.where(at_col < 0, 1, 0) == plane_x
            for plane in range(2):
                piece = jnp.where(inside, update[plane][led * rows : (led + 1) * rows], 0.0)
                for i, at_slab in enumerate(
                    (jnp.where(this_slab, piece, 0.0), jnp.where(this_slab, 0.0, piece))
                ):
                    sums[2 * i][plane] += jnp.where(this_x, at_slab, 0.0)
                    sums[2 * i + 1][plane] += jnp.where(this_x, 0.0, at_slab)
        cols = slice(n * LANES, (n + 1) * LANES)
        for out, both_planes in zip(outs, sums):
            for plane in range(2):
                out[plane, :, cols] = both_planes[plane].astype(out.dtype)


def sent_kernel(starts, table, *rest):
    blocks = rest[:HALF]
    this_slab, that_slab, back = rest[HALF:]
    position = lax.axis_index("slab")
    parts, rows, _ = blocks[0].shape
    for d, block in enumerate(blocks):
        source = jnp.bitwise_and(jnp.bitwise_xor(position, d), HALF - 1)
        at = pl.multiple_of(source * LANES, LANES)
        for part in range(parts):
            back[part * rows : (part + 1) * rows, pl.ds(at, LANES)] = block[part]
    outs = [out.at[i] for out in (this_slab, that_slab) for i in range(2)]
    update_columns(False, starts, table, back, outs)


def kept_kernel(starts, table, back, *outs):
    update_columns(True, starts, table, back, outs)


def z_first_kernel(that_near, that_far, got_that, out):
    cols = out.shape[3]
    for i, kept in enumerate((that_near, that_far)):
        total = kept[:, :, :cols] + got_that[i, :, :, :cols].astype(jnp.float32)
        out[i] = total.astype(out.dtype)


def x_first_kernel(that_far, got_that, out):
    cols = that_far.shape[2] - out.shape[2]
    total = that_far[:, :, cols:] + got_that[1, :, :, cols:].astype(jnp.float32)
    out[...] = total.astype(out.dtype)


def z_second_kernel(that_near, got_that, got_x, out):
    cols = that_near.shape[2] - out.shape[2]
    total = that_near[:, :, cols:] + got_that[0, :, :, cols:].astype(jnp.float32)
    out[...] = (total + got_x[...].astype(jnp.float32)).astype(out.dtype)


def x_own_kernel(this_far, got_this, out):
    cols = this_far.shape[2] - out.shape[2]
    total = this_far[:, :, cols:] + got_this[1, :, :, cols:].astype(jnp.float32)
    out[...] = total.astype(out.dtype)


def x_last_kernel(this_far, got_this, got_z, out):
    cols = out.shape[2]
    total = this_far[:, :, :cols] + got_this[1, :, :, :cols].astype(jnp.float32)
    out[...] = (total + got_z[1].astype(jnp.float32)).astype(out.dtype)


def local_call(kernel, out_shape, spaces, scratch, flops, moved, name):
    return pl.pallas_call(
        kernel,
        out_shape=out_shape,
        in_specs=[pl.BlockSpec(memory_space=space) for space in spaces],
        out_specs=jax.tree.map(lambda _: pl.BlockSpec(memory_space=pltpu.VMEM), out_shape),
        scratch_shapes=scratch,
        compiler_params=pltpu.CompilerParams(vmem_limit_bytes=32 * 2**20),
        cost_estimate=pl.CostEstimate(flops=flops, bytes_accessed=moved, transcendentals=0),
        name=name,
    )


def body_slabs(spectrum, led_rows, led_cols, images):
    leds, block, width = images.shape
    rows = spectrum.shape[1]
    led_at = lax.axis_index("led")
    bf16 = jnp.bfloat16
    vmem, smem = pltpu.VMEM, pltpu.SMEM
    cos_table, sin_table = host_tables(width)
    steps = width // LANES
    by_col = np.stack(
        [
            np.concatenate([t[:, j * LANES : (j + 1) * LANES] for t in (cos_table, sin_table)], 1)
            for j in range(steps)
        ]
    )
    by_row = jnp.asarray(np.ascontiguousarray(by_col.transpose(0, 2, 1)))
    by_col = jnp.asarray(by_col)
    parts = 2 * leds
    sent_block = jax.ShapeDtypeStruct((parts, rows, LANES), bf16)
    flops = 8 * leds * rows * width * width

    starts = jnp.concatenate([led_rows, led_cols]).astype(jnp.int32)
    window = local_call(
        window_kernel,
        jax.ShapeDtypeStruct((parts * rows, width), bf16),
        [smem, vmem],
        [],
        0,
        6 * 2**20,
        "windows",
    )(starts, spectrum)

    def rows_call(which, name):
        count = which.stop - which.start
        return local_call(
            functools.partial(rows_kernel, which),
            [sent_block] * count,
            [vmem, vmem],
            [],
            flops * count // SLABS,
            5 * 2**20,
            name,
        )(window, by_col)

    first_a, first_b, near_2 = rows_call(slice(0, 3), "rows_round_1")

    def permute(sent, pairs):
        return lax.ppermute(sent, "slab", pairs)

    def choose(got, own, name):
        return local_call(
            choose_kernel, sent_block, [vmem] * 2, [], 0, 2**19, name
        )(got, own)

    handed = list(PASSED.items())
    windowed = range(FIRST + 1, LAST)
    got_a = permute(first_a, [(s, s ^ 6) for s in INNER] + handed)
    got_b = permute(first_b, [(s, s ^ 7) for s in INNER] + handed)
    near_2 = permute(near_2, [(s, s ^ 2) for s in windowed])
    second_a, second_b, near_0, near_1, near_3 = rows_call(slice(3, SLABS), "rows_round_2")
    got_a, near_2, second_a, second_b, near_1, near_3, images = lax.optimization_barrier(
        (got_a, near_2, second_a, second_b, near_1, near_3, images)
    )
    outer_pairs = [(s, s ^ 6) for s in range(SLABS) if s not in INNER]
    near_1 = permute(near_1, [(s, s ^ 1) for s in windowed])
    near_3 = permute(near_3, [(s, s ^ 3) for s in windowed])
    near_1, got_b = lax.optimization_barrier((near_1, got_b))
    far_columns = [
        got_a,
        got_b,
        permute(choose(got_a, second_a, "class_4_blocks"), [(s, s ^ 4) for s in range(SLABS)]),
        permute(choose(got_b, second_b, "class_6_blocks"), outer_pairs),
        permute(second_b, [(s, s ^ 5) for s in INNER]),
    ]
    near_columns = [near_0, near_1, near_2, near_3]
    amplitude, by_row = local_call(
        amplitude_kernel,
        [
            jax.ShapeDtypeStruct((width, leds * block), jnp.float32),
            jax.ShapeDtypeStruct(by_row.shape, bf16),
        ],
        [vmem] * 2,
        [],
        0,
        10 * 2**20,
        "amplitude",
    )(images, by_row)
    strips = local_call(
        field_kernel,
        [sent_block] * HALF,
        [vmem] * 11,
        [pltpu.VMEM((width, parts * block), bf16)] * 2
        + [pltpu.VMEM((HALF,) + sent_block.shape, bf16)],
        16 * leds * block * width * width,
        12 * 2**20,
        "modulus_step",
    )(amplitude, by_row, *far_columns, *near_columns)

    def send_home(d):
        pairs = [(s, (s + d) % SLABS) for s in range(SLABS) if FIRST < (s + d) % SLABS < LAST]
        return permute(strips[d % HALF], pairs)

    home = [strips[0]]
    home += [
        permute(strips[d], [(s, s ^ d) for s in range(SLABS)]) for d in range(1, HALF)
    ]
    share = width // 2
    first = share // 4
    piece = (2, rows, share)
    cores = [(0, 1), (1, 0), (2, 3), (3, 2)]
    planes = [(0, 2), (2, 0), (1, 3), (3, 1)]
    across = [(s, s ^ 4) for s in range(SLABS) if FIRST < s ^ 4 < LAST]
    sent_this, sent_that, back = local_call(
        sent_kernel,
        [
            jax.ShapeDtypeStruct((2,) + piece, bf16),
            jax.ShapeDtypeStruct((2,) + piece, bf16),
            jax.ShapeDtypeStruct((parts * rows, HALF * LANES), bf16),
        ],
        [smem] + [vmem] * (1 + HALF),
        [],
        flops // 4,
        8 * 2**20,
        "update_sent",
    )(starts, by_col, *home)
    got_that = lax.ppermute(sent_that, "led", cores)
    got_this = lax.ppermute(sent_this, "led", cores)
    this_near, this_far, that_near, that_far = local_call(
        kept_kernel,
        [jax.ShapeDtypeStruct(piece, jnp.float32)] * 4,
        [smem, vmem, vmem],
        [],
        flops // 4,
        10 * 2**20,
        "update_kept",
    )(starts, by_col, back)

    def sum_call(kernel, shape, *values):
        out_shape = jax.ShapeDtypeStruct(shape, bf16)
        specs = [vmem] * len(values)
        return local_call(kernel, out_shape, specs, [], 0, 2**20, kernel.__name__)(*values)

    over = sum_call(z_first_kernel, (2, 2, rows, first), that_near, that_far, got_that)
    got_z_first = permute(over, across)
    over = sum_call(x_first_kernel, (2, rows, share - first), that_far, got_that)
    got_x = lax.ppermute(over, "led", planes)
    over_z = sum_call(z_second_kernel, (2, rows, share - first), that_near, got_that, got_x)
    got_z_second = permute(over_z, across)
    over = sum_call(x_own_kernel, (2, rows, share - first), this_far, got_this)
    got_x_own = lax.ppermute(over, "led", planes)
    over, got_z_first = lax.optimization_barrier((over_z, got_z_first))
    over = sum_call(x_last_kernel, (2, rows, first), this_far, got_this, got_z_first)
    got_x_last = lax.ppermute(over, "led", planes)

    def widen(value, before):
        after = share - before - value.shape[2]
        return jnp.pad(value.astype(jnp.float32), ((0, 0), (0, 0), (before, after)))

    base = lax.dynamic_slice_in_dim(spectrum, led_at * share, share, 2)
    base += this_near + got_this[0].astype(jnp.float32) + widen(got_z_first[0], 0)
    base, got_x_own, got_x_last = lax.optimization_barrier((base, got_x_own, got_x_last))
    base += widen(got_x_own, first) + widen(got_x_last, 0)
    base, got_z_second = lax.optimization_barrier((base, got_z_second))
    return base + widen(got_z_second, first)


def solution(mesh):
    placed = (P(None, "slab", None), P("led"), P("led"), P("led", "slab", None))
    fits = mesh.shape["slab"] == 8 and mesh.shape["led"] == 4

    def body(spectrum, led_rows, led_cols, images):
        shapes = (spectrum.shape, images.shape)
        if fits and shapes == ((2, 256, 2048), (2, 128, 1024)):
            return body_slabs(spectrum, led_rows, led_cols, images)
        return body_any(spectrum, led_rows, led_cols, images)

    return jax.shard_map(
        body, mesh=mesh, in_specs=placed, out_specs=P(None, "slab", "led"), check_vma=False
    )
```

```python
import functools

import jax
import jax.numpy as jnp
import numpy as np
from jax import lax
from jax.experimental import pallas as pl
from jax.experimental.pallas import tpu as pltpu
from jax.sharding import PartitionSpec as P

LANES = 128


def as_sent(value):
    return jax.tree.map(lambda a: a.astype(jnp.bfloat16) if a.dtype == jnp.float32 else a, value)


def host_tables(width):
    index = np.arange(width, dtype=np.int64)
    angle_index = (index[:, None] * index[None, :] % width).astype(np.float32)
    angle = angle_index * np.float32(2.0 * 3.141592653589793 / width)
    scale = np.float32(1.0) / np.sqrt(np.float32(width))
    return (
        (np.cos(angle) * scale).astype(jnp.bfloat16),
        (np.sin(angle) * scale).astype(jnp.bfloat16),
    )


def make_pupil(row_index, col_index, width):
    row_term = (2 * row_index + 1 - width) * (2 * row_index + 1 - width)
    col_term = (2 * col_index + 1 - width) * (2 * col_index + 1 - width)
    return (row_term[:, None] + col_term[None, :] < width * width).astype(jnp.float32)


def contract(form, left, right):
    return jnp.einsum(form, left, right, preferred_element_type=jnp.float32)


def take_rows(strip, start, width):
    return lax.dynamic_slice_in_dim(strip, start, width, 1)


def place_rows(block, start, total, axis_dim):
    shape = list(block.shape)
    shape[axis_dim] = total
    holder = jnp.zeros(tuple(shape), block.dtype)
    return lax.dynamic_update_slice_in_dim(holder, block, start, axis_dim)


def modulus_step(field_in_re, field_in_im, image, cos_table, sin_table):
    field_re = contract("lka,am->lkm", field_in_re, cos_table) + contract(
        "lka,am->lkm", field_in_im, sin_table
    )
    field_im = contract("lka,am->lkm", field_in_im, cos_table) - contract(
        "lka,am->lkm", field_in_re, sin_table
    )
    factor = jnp.sqrt(image) / jnp.sqrt(field_re * field_re + field_im * field_im + 0.25) - 1.0
    diff_re = (field_re * factor).astype(jnp.bfloat16)
    diff_im = (field_im * factor).astype(jnp.bfloat16)
    back_re = (
        contract("lkm,ma->lka", diff_re, cos_table) - contract("lkm,ma->lka", diff_im, sin_table)
    ).astype(jnp.bfloat16)
    back_im = (
        contract("lkm,ma->lka", diff_im, cos_table) + contract("lkm,ma->lka", diff_re, sin_table)
    ).astype(jnp.bfloat16)
    return (back_re, back_im)


def body_any(spectrum, led_rows, led_cols, images):
    width = images.shape[2]
    slab_rows = spectrum.shape[1]
    columns = spectrum.shape[2]
    slabs = lax.axis_size("slab")
    total_rows = slab_rows * slabs
    position = lax.axis_index("slab")
    cos_table, sin_table = (jnp.asarray(t) for t in host_tables(width))
    own_rows = position * slab_rows + jnp.arange(slab_rows, dtype=jnp.int32)
    col_index = jnp.arange(width, dtype=jnp.int32)

    def take_cols(start):
        return lax.dynamic_slice_in_dim(spectrum, start, width, 2)

    def owner_mask(start):
        return make_pupil(own_rows - start, col_index, width)

    windows = jax.vmap(take_cols)(led_cols)
    masks = jax.vmap(owner_mask)(led_rows)
    win_re = (windows[:, 0] * masks).astype(jnp.bfloat16)
    win_im = (windows[:, 1] * masks).astype(jnp.bfloat16)

    def slice_strip(block, start):
        return take_rows(block, start, width)

    row_re = (
        contract("lgb,bk->lkg", win_re, cos_table) + contract("lgb,bk->lkg", win_im, sin_table)
    ).astype(jnp.bfloat16)
    row_im = (
        contract("lgb,bk->lkg", win_im, cos_table) - contract("lgb,bk->lkg", win_re, sin_table)
    ).astype(jnp.bfloat16)
    col_re, col_im = (
        lax.all_to_all(row_re, "slab", split_axis=1, concat_axis=2, tiled=True),
        lax.all_to_all(row_im, "slab", split_axis=1, concat_axis=2, tiled=True),
    )
    field_in_re = jax.vmap(slice_strip)(col_re, led_rows)
    field_in_im = jax.vmap(slice_strip)(col_im, led_rows)
    back_re, back_im = modulus_step(field_in_re, field_in_im, images, cos_table, sin_table)

    def place_strip(block, start):
        return place_rows(block, start, total_rows, 1)

    full_re = jax.vmap(place_strip)(back_re, led_rows)
    full_im = jax.vmap(place_strip)(back_im, led_rows)
    home_re, home_im = (
        lax.all_to_all(as_sent(full_re), "slab", split_axis=2, concat_axis=1, tiled=True).astype(
            full_re.dtype
        ),
        lax.all_to_all(as_sent(full_im), "slab", split_axis=2, concat_axis=1, tiled=True).astype(
            full_im.dtype
        ),
    )
    upd_re = contract("lkg,kb->lgb", home_re, cos_table) - contract(
        "lkg,kb->lgb", home_im, sin_table
    )
    upd_im = contract("lkg,kb->lgb", home_im, cos_table) + contract(
        "lkg,kb->lgb", home_re, sin_table
    )
    upd_re = upd_re * masks
    upd_im = upd_im * masks

    def add_window(number, gradient):
        start = led_cols[number]
        piece = jnp.stack([upd_re[number], upd_im[number]])
        current = lax.dynamic_slice_in_dim(gradient, start, width, 2)
        return lax.dynamic_update_slice_in_dim(gradient, current + piece, start, 2)

    gradient = lax.fori_loop(
        0, led_rows.shape[0], add_window, jnp.zeros((2, slab_rows, columns), jnp.float32)
    )
    summed = lax.psum_scatter(gradient, "led", scatter_dimension=2, tiled=True)
    share = summed.shape[2]
    own_part = lax.dynamic_slice_in_dim(spectrum, lax.axis_index("led") * share, share, 2)
    return own_part + summed


SLABS = 8
HALF = 4
FIRST, LAST = 0, 7
PASSED = {1: 0, 6: 7}
INNER = (2, 3, 4, 5)


def dot(left, right):
    return jnp.dot(left, right, preferred_element_type=jnp.float32)


def window_mask(first_row, row_start, col_start, rows, first_col, cols, width):
    shape = (rows, cols)
    at_row = lax.broadcasted_iota(jnp.int32, shape, 0) + (first_row - row_start)
    at_col = lax.broadcasted_iota(jnp.int32, shape, 1) + (first_col - col_start)
    wraps = at_col < 0
    at_col = jnp.where(wraps, at_col + width, at_col)
    row_term = 2 * at_row + 1 - width
    col_term = 2 * at_col + 1 - width
    return row_term * row_term + col_term * col_term < width * width, wraps


def row_block(window, table):
    both = dot(window, table)
    half = both.shape[0] // 2
    row_re = both[:half, :LANES] + both[half:, LANES:]
    row_im = both[half:, :LANES] - both[:half, LANES:]
    return row_re.astype(jnp.bfloat16), row_im.astype(jnp.bfloat16)


def store_parts(out, values):
    per = out.shape[0] // 2
    rows = out.shape[1]
    for plane, value in enumerate(values):
        for led in range(per):
            out[plane * per + led] = value[led * rows : (led + 1) * rows]


def is_one_of(position, slabs):
    return functools.reduce(jnp.logical_or, [position == slab for slab in slabs])


def window_kernel(starts, spectrum, window):
    position = lax.axis_index("slab")
    leds = starts.shape[0] // 2
    rows = spectrum.shape[1]
    width = window.shape[1]
    for led in range(leds):
        inside, wraps = window_mask(
            position * rows, starts[led], starts[leds + led], rows, 0, width, width
        )
        for plane in range(2):
            value = jnp.where(wraps, spectrum[plane, :, width:], spectrum[plane, :, :width])
            at = (plane * leds + led) * rows
            window[at : at + rows, :] = jnp.where(inside, value, 0.0).astype(jnp.bfloat16)


def classes_of(position):
    hands_over = is_one_of(position, PASSED)
    return (jnp.where(hands_over, 5, 6), 7, 2, 4, jnp.where(hands_over, 6, 5), 0, 1, 3)


def rows_kernel(which, window, table, *outs):
    position = lax.axis_index("slab")
    for out, d in zip(outs, classes_of(position)[which]):
        store_parts(out, row_block(window[...], table[jnp.bitwise_xor(position, d)]))


def choose_kernel(got, own, out):
    passes = is_one_of(lax.axis_index("slab"), PASSED.values())

    @pl.when(passes)
    def _():
        out[...] = got[...]

    @pl.when(jnp.logical_not(passes))
    def _():
        out[...] = own[...]


def amplitude_kernel(images, table, out, table_out):
    leds, block, width = images.shape
    for led in range(leds):
        for j in range(width // LANES):
            piece = jnp.sqrt(images[led, :, j * LANES : (j + 1) * LANES])
            out[j * LANES : (j + 1) * LANES, led * block : (led + 1) * block] = piece.T
    table_out[...] = table[...]


def field_kernel(amplitude, table, *rest):
    far, near = rest[:5], rest[5 : HALF + 5]
    outs = rest[HALF + 5 : 2 * HALF + 5]
    field_in, diff, strips = rest[2 * HALF + 5 :]
    position = lax.axis_index("slab")
    parts, rows, _ = near[0].shape
    half = parts // 2 * LANES
    width = field_in.shape[0]
    steps = width // LANES
    group = 4
    for d, block in enumerate(near):
        at = pl.multiple_of(jnp.bitwise_and(jnp.bitwise_xor(position, d), HALF - 1) * rows, rows)
        for part in range(parts):
            cols = slice(part * LANES, (part + 1) * LANES)
            field_in[pl.ds(at, rows), cols] = block[part]

    def add(block, origin):
        at = pl.multiple_of(jnp.bitwise_and(origin, HALF - 1) * rows, rows)
        for part in range(parts):
            cols = slice(part * LANES, (part + 1) * LANES)
            field_in[pl.ds(at, rows), cols] += block[part]

    passes = is_one_of(position, PASSED.values())
    hands_over = is_one_of(position, PASSED)
    ends = is_one_of(position, [to ^ 4 for to in PASSED.values()])

    @pl.when(is_one_of(position, INNER))
    def _():
        add(far[0], jnp.bitwise_xor(position, 6))
        add(far[1], jnp.bitwise_xor(position, 7))
        add(far[2], jnp.bitwise_xor(position, jnp.where(ends, 5, 4)))

    @pl.when(jnp.logical_or(passes, hands_over))
    def _():
        add(far[2], jnp.bitwise_xor(position, 4))
        add(far[3], jnp.bitwise_xor(position, jnp.where(hands_over, 7, 6)))
        add(far[4], jnp.bitwise_xor(position, 5))

    for first in range(0, steps, group):
        product = dot(
            table[first : first + group].reshape(group * 2 * LANES, width), field_in[...]
        )
        for j in range(first, first + group):
            both = product[(j - first) * 2 * LANES : (j - first + 1) * 2 * LANES]
            field_re = both[:LANES, :half] + both[LANES:, half:]
            field_im = both[:LANES, half:] - both[LANES:, :half]
            here = pl.ds(j * LANES, LANES)
            factor = (
                amplitude[here, :] * lax.rsqrt(field_re * field_re + field_im * field_im + 0.25)
                - 1.0
            )
            diff[here, :half] = (field_re * factor).astype(jnp.bfloat16)
            diff[here, half:] = (field_im * factor).astype(jnp.bfloat16)
    pieces = rows // LANES
    for i in range(HALF):
        product = dot(
            table[i * pieces : (i + 1) * pieces].reshape(pieces * 2 * LANES, width), diff[...]
        )
        for h in range(pieces):
            both = product[h * 2 * LANES : (h + 1) * 2 * LANES]
            here = pl.ds(h * LANES, LANES)
            back_re = (both[:LANES, :half] - both[LANES:, half:]).astype(jnp.bfloat16)
            back_im = (both[:LANES, half:] + both[LANES:, :half]).astype(jnp.bfloat16)
            for part in range(parts // 2):
                cols = slice(part * LANES, (part + 1) * LANES)
                strips[i, part, here, :] = back_re[:, cols]
                strips[i, parts // 2 + part, here, :] = back_im[:, cols]
    for d, out in enumerate(outs):
        out[...] = strips[jnp.bitwise_and(jnp.bitwise_xor(position, d), HALF - 1)]


def update_columns(own_core, starts, table, back, outs):
    position = lax.axis_index("slab")
    led_at = lax.axis_index("led")
    core = jnp.bitwise_and(led_at, 1)
    plane_x = jnp.right_shift(led_at, 1)
    which_half = jnp.right_shift(position, 2)
    first_row = jnp.bitwise_and(position, HALF - 1)
    leds = starts.shape[0] // 2
    rows = back.shape[0] // (2 * leds)
    depth = back.shape[1]
    width = table.shape[1]
    group = width // LANES // 2
    owner = core if own_core else 1 - core
    shape = (rows, LANES)
    for n in range(group):
        block = owner * group + n
        both = dot(
            back[...], table[block, pl.ds(pl.multiple_of(which_half * depth, depth), depth)]
        )
        half = leds * rows
        update = (
            both[:half, :LANES] - both[half:, LANES:],
            both[half:, :LANES] + both[:half, LANES:],
        )
        sums = [[0.0, 0.0] for _ in outs]
        for led in range(leds):
            at_row = lax.broadcasted_iota(jnp.int32, shape, 0) + (
                first_row * rows - starts[led]
            )
            at_col = lax.broadcasted_iota(jnp.int32, shape, 1) + (
                block * LANES - starts[leds + led]
            )
            row_term = 2 * jnp.where(at_row < 0, at_row + width, at_row) + 1 - width
            col_term = 2 * jnp.where(at_col < 0, at_col + width, at_col) + 1 - width
            inside = row_term * row_term + col_term * col_term < width * width
            this_slab = jnp.where(at_row < 0, 1, 0) == which_half
            this_x = jnp.where(at_col < 0, 1, 0) == plane_x
            for plane in range(2):
                piece = jnp.where(inside, update[plane][led * rows : (led + 1) * rows], 0.0)
                for i, at_slab in enumerate(
                    (jnp.where(this_slab, piece, 0.0), jnp.where(this_slab, 0.0, piece))
                ):
                    sums[2 * i][plane] += jnp.where(this_x, at_slab, 0.0)
                    sums[2 * i + 1][plane] += jnp.where(this_x, 0.0, at_slab)
        cols = slice(n * LANES, (n + 1) * LANES)
        for out, both_planes in zip(outs, sums):
            for plane in range(2):
                out[plane, :, cols] = both_planes[plane].astype(out.dtype)


def sent_kernel(starts, table, *rest):
    blocks = rest[:HALF]
    this_slab, that_slab, back = rest[HALF:]
    position = lax.axis_index("slab")
    parts, rows, _ = blocks[0].shape
    for d, block in enumerate(blocks):
        source = jnp.bitwise_and(jnp.bitwise_xor(position, d), HALF - 1)
        at = pl.multiple_of(source * LANES, LANES)
        for part in range(parts):
            back[part * rows : (part + 1) * rows, pl.ds(at, LANES)] = block[part]
    outs = [out.at[i] for out in (this_slab, that_slab) for i in range(2)]
    update_columns(False, starts, table, back, outs)


def kept_kernel(starts, table, back, *outs):
    update_columns(True, starts, table, back, outs)


def z_first_kernel(that_near, that_far, got_that, out):
    cols = out.shape[3]
    for i, kept in enumerate((that_near, that_far)):
        total = kept[:, :, :cols] + got_that[i, :, :, :cols].astype(jnp.float32)
        out[i] = total.astype(out.dtype)


def x_first_kernel(that_far, got_that, out):
    cols = that_far.shape[2] - out.shape[2]
    total = that_far[:, :, cols:] + got_that[1, :, :, cols:].astype(jnp.float32)
    out[...] = total.astype(out.dtype)


def z_second_kernel(that_near, got_that, got_x, out):
    cols = that_near.shape[2] - out.shape[2]
    total = that_near[:, :, cols:] + got_that[0, :, :, cols:].astype(jnp.float32)
    out[...] = (total + got_x[...].astype(jnp.float32)).astype(out.dtype)


def x_own_kernel(this_far, got_this, out):
    cols = this_far.shape[2] - out.shape[2]
    total = this_far[:, :, cols:] + got_this[1, :, :, cols:].astype(jnp.float32)
    out[...] = total.astype(out.dtype)


def x_last_kernel(this_far, got_this, got_z, got_by_y, out):
    cols = out.shape[2]
    total = this_far[:, :, :cols] + got_this[1, :, :, :cols].astype(jnp.float32)
    for got in (got_z, got_by_y):
        total += got[1].astype(jnp.float32)
    out[...] = total.astype(out.dtype)


def local_call(kernel, out_shape, spaces, scratch, flops, moved, name):
    return pl.pallas_call(
        kernel,
        out_shape=out_shape,
        in_specs=[pl.BlockSpec(memory_space=space) for space in spaces],
        out_specs=jax.tree.map(lambda _: pl.BlockSpec(memory_space=pltpu.VMEM), out_shape),
        scratch_shapes=scratch,
        compiler_params=pltpu.CompilerParams(vmem_limit_bytes=32 * 2**20),
        cost_estimate=pl.CostEstimate(flops=flops, bytes_accessed=moved, transcendentals=0),
        name=name,
    )


def body_slabs(spectrum, led_rows, led_cols, images):
    leds, block, width = images.shape
    rows = spectrum.shape[1]
    led_at = lax.axis_index("led")
    bf16 = jnp.bfloat16
    vmem, smem = pltpu.VMEM, pltpu.SMEM
    cos_table, sin_table = host_tables(width)
    steps = width // LANES
    by_col = np.stack(
        [
            np.concatenate([t[:, j * LANES : (j + 1) * LANES] for t in (cos_table, sin_table)], 1)
            for j in range(steps)
        ]
    )
    by_row = jnp.asarray(np.ascontiguousarray(by_col.transpose(0, 2, 1)))
    by_col = jnp.asarray(by_col)
    parts = 2 * leds
    sent_block = jax.ShapeDtypeStruct((parts, rows, LANES), bf16)
    flops = 8 * leds * rows * width * width

    starts = jnp.concatenate([led_rows, led_cols]).astype(jnp.int32)
    window = local_call(
        window_kernel,
        jax.ShapeDtypeStruct((parts * rows, width), bf16),
        [smem, vmem],
        [],
        0,
        6 * 2**20,
        "windows",
    )(starts, spectrum)

    def rows_call(which, name):
        count = which.stop - which.start
        return local_call(
            functools.partial(rows_kernel, which),
            [sent_block] * count,
            [vmem, vmem],
            [],
            flops * count // SLABS,
            5 * 2**20,
            name,
        )(window, by_col)

    first_a, first_b, near_2 = rows_call(slice(0, 3), "rows_round_1")

    def permute(sent, pairs):
        return lax.ppermute(sent, "slab", pairs)

    def choose(got, own, name):
        return local_call(
            choose_kernel, sent_block, [vmem] * 2, [], 0, 2**19, name
        )(got, own)

    handed = list(PASSED.items())
    windowed = range(FIRST + 1, LAST)
    got_a = permute(first_a, [(s, s ^ 6) for s in INNER] + handed)
    got_b = permute(first_b, [(s, s ^ 7) for s in INNER] + handed)
    near_2 = permute(near_2, [(s, s ^ 2) for s in windowed])
    second_a, second_b, near_0, near_1, near_3 = rows_call(slice(3, SLABS), "rows_round_2")
    got_a, near_2, second_a, second_b, near_1, near_3, images = lax.optimization_barrier(
        (got_a, near_2, second_a, second_b, near_1, near_3, images)
    )
    outer_pairs = [(s, s ^ 6) for s in range(SLABS) if s not in INNER]
    near_1 = permute(near_1, [(s, s ^ 1) for s in windowed])
    near_3 = permute(near_3, [(s, s ^ 3) for s in windowed])
    near_1, got_b = lax.optimization_barrier((near_1, got_b))
    far_columns = [
        got_a,
        got_b,
        permute(choose(got_a, second_a, "class_4_blocks"), [(s, s ^ 4) for s in range(SLABS)]),
        permute(choose(got_b, second_b, "class_6_blocks"), outer_pairs),
        permute(second_b, [(s, s ^ 5) for s in INNER]),
    ]
    near_columns = [near_0, near_1, near_2, near_3]
    amplitude, by_row = local_call(
        amplitude_kernel,
        [
            jax.ShapeDtypeStruct((width, leds * block), jnp.float32),
            jax.ShapeDtypeStruct(by_row.shape, bf16),
        ],
        [vmem] * 2,
        [],
        0,
        10 * 2**20,
        "amplitude",
    )(images, by_row)
    strips = local_call(
        field_kernel,
        [sent_block] * HALF,
        [vmem] * 11,
        [pltpu.VMEM((width, parts * block), bf16)] * 2
        + [pltpu.VMEM((HALF,) + sent_block.shape, bf16)],
        16 * leds * block * width * width,
        12 * 2**20,
        "modulus_step",
    )(amplitude, by_row, *far_columns, *near_columns)

    def send_home(d):
        pairs = [(s, (s + d) % SLABS) for s in range(SLABS) if FIRST < (s + d) % SLABS < LAST]
        return permute(strips[d % HALF], pairs)

    home = [strips[0]]
    home += [
        permute(strips[d], [(s, s ^ d) for s in range(SLABS)]) for d in range(1, HALF)
    ]
    share = width // 2
    first = share // 4
    piece = (2, rows, share)
    cores = [(0, 1), (1, 0), (2, 3), (3, 2)]
    planes = [(0, 2), (2, 0), (1, 3), (3, 1)]
    across = [(s, s ^ 4) for s in range(SLABS) if FIRST < s ^ 4 < LAST]
    sent_this, sent_that, back = local_call(
        sent_kernel,
        [
            jax.ShapeDtypeStruct((2,) + piece, bf16),
            jax.ShapeDtypeStruct((2,) + piece, bf16),
            jax.ShapeDtypeStruct((parts * rows, HALF * LANES), bf16),
        ],
        [smem] + [vmem] * (1 + HALF),
        [],
        flops // 4,
        8 * 2**20,
        "update_sent",
    )(starts, by_col, *home)
    got_that = lax.ppermute(sent_that, "led", cores)
    got_this = lax.ppermute(sent_this, "led", cores)
    this_near, this_far, that_near, that_far = local_call(
        kept_kernel,
        [jax.ShapeDtypeStruct(piece, jnp.float32)] * 4,
        [smem, vmem, vmem],
        [],
        flops // 4,
        10 * 2**20,
        "update_kept",
    )(starts, by_col, back)

    def sum_call(kernel, shape, *values):
        out_shape = jax.ShapeDtypeStruct(shape, bf16)
        specs = [vmem] * len(values)
        return local_call(kernel, out_shape, specs, [], 0, 2**20, kernel.__name__)(*values)

    over = sum_call(z_first_kernel, (2, 2, rows, first), that_near, that_far, got_that)
    by_y = {2: 3, 5: 4}
    relayed = permute(over, list(by_y.items()))
    got_z_first = (
        permute(over, [(s, to) for s, to in across if s not in by_y]),
        permute(relayed, [(by, s ^ 4) for s, by in by_y.items()]),
    )
    over = sum_call(x_first_kernel, (2, rows, share - first), that_far, got_that)
    got_x = lax.ppermute(over, "led", planes)
    over_z = sum_call(z_second_kernel, (2, rows, share - first), that_near, got_that, got_x)
    got_z_second = permute(over_z, across)
    over = sum_call(x_own_kernel, (2, rows, share - first), this_far, got_this)
    got_x_own = lax.ppermute(over, "led", planes)
    over, got_z_first = lax.optimization_barrier((over_z, got_z_first))
    over = sum_call(x_last_kernel, (2, rows, first), this_far, got_this, *got_z_first)
    got_x_last = lax.ppermute(over, "led", planes)

    def widen(value, before):
        after = share - before - value.shape[2]
        return jnp.pad(value.astype(jnp.float32), ((0, 0), (0, 0), (before, after)))

    base = lax.dynamic_slice_in_dim(spectrum, led_at * share, share, 2)
    base += this_near + got_this[0].astype(jnp.float32)
    base += widen(sum(got[0].astype(jnp.float32) for got in got_z_first), 0)
    base, got_x_own, got_x_last = lax.optimization_barrier((base, got_x_own, got_x_last))
    base += widen(got_x_own, first) + widen(got_x_last, 0)
    base, got_z_second = lax.optimization_barrier((base, got_z_second))
    return base + widen(got_z_second, first)


def solution(mesh):
    placed = (P(None, "slab", None), P("led"), P("led"), P("led", "slab", None))
    fits = mesh.shape["slab"] == 8 and mesh.shape["led"] == 4

    def body(spectrum, led_rows, led_cols, images):
        shapes = (spectrum.shape, images.shape)
        if fits and shapes == ((2, 256, 2048), (2, 128, 1024)):
            return body_slabs(spectrum, led_rows, led_cols, images)
        return body_any(spectrum, led_rows, led_cols, images)

    return jax.shard_map(
        body, mesh=mesh, in_specs=placed, out_specs=P(None, "slab", "led"), check_vma=False
    )
```

```python
import functools

import jax
import jax.numpy as jnp
import numpy as np
from jax import lax
from jax.experimental import pallas as pl
from jax.experimental.pallas import tpu as pltpu
from jax.sharding import PartitionSpec as P

LANES = 128


def as_sent(value):
    return jax.tree.map(lambda a: a.astype(jnp.bfloat16) if a.dtype == jnp.float32 else a, value)


def host_tables(width):
    index = np.arange(width, dtype=np.int64)
    angle_index = (index[:, None] * index[None, :] % width).astype(np.float32)
    angle = angle_index * np.float32(2.0 * 3.141592653589793 / width)
    scale = np.float32(1.0) / np.sqrt(np.float32(width))
    return (
        (np.cos(angle) * scale).astype(jnp.bfloat16),
        (np.sin(angle) * scale).astype(jnp.bfloat16),
    )


def make_pupil(row_index, col_index, width):
    row_term = (2 * row_index + 1 - width) * (2 * row_index + 1 - width)
    col_term = (2 * col_index + 1 - width) * (2 * col_index + 1 - width)
    return (row_term[:, None] + col_term[None, :] < width * width).astype(jnp.float32)


def contract(form, left, right):
    return jnp.einsum(form, left, right, preferred_element_type=jnp.float32)


def take_rows(strip, start, width):
    return lax.dynamic_slice_in_dim(strip, start, width, 1)


def place_rows(block, start, total, axis_dim):
    shape = list(block.shape)
    shape[axis_dim] = total
    holder = jnp.zeros(tuple(shape), block.dtype)
    return lax.dynamic_update_slice_in_dim(holder, block, start, axis_dim)


def modulus_step(field_in_re, field_in_im, image, cos_table, sin_table):
    field_re = contract("lka,am->lkm", field_in_re, cos_table) + contract(
        "lka,am->lkm", field_in_im, sin_table
    )
    field_im = contract("lka,am->lkm", field_in_im, cos_table) - contract(
        "lka,am->lkm", field_in_re, sin_table
    )
    factor = jnp.sqrt(image) / jnp.sqrt(field_re * field_re + field_im * field_im + 0.25) - 1.0
    diff_re = (field_re * factor).astype(jnp.bfloat16)
    diff_im = (field_im * factor).astype(jnp.bfloat16)
    back_re = (
        contract("lkm,ma->lka", diff_re, cos_table) - contract("lkm,ma->lka", diff_im, sin_table)
    ).astype(jnp.bfloat16)
    back_im = (
        contract("lkm,ma->lka", diff_im, cos_table) + contract("lkm,ma->lka", diff_re, sin_table)
    ).astype(jnp.bfloat16)
    return (back_re, back_im)


def body_any(spectrum, led_rows, led_cols, images):
    width = images.shape[2]
    slab_rows = spectrum.shape[1]
    columns = spectrum.shape[2]
    slabs = lax.axis_size("slab")
    total_rows = slab_rows * slabs
    position = lax.axis_index("slab")
    cos_table, sin_table = (jnp.asarray(t) for t in host_tables(width))
    own_rows = position * slab_rows + jnp.arange(slab_rows, dtype=jnp.int32)
    col_index = jnp.arange(width, dtype=jnp.int32)

    def take_cols(start):
        return lax.dynamic_slice_in_dim(spectrum, start, width, 2)

    def owner_mask(start):
        return make_pupil(own_rows - start, col_index, width)

    windows = jax.vmap(take_cols)(led_cols)
    masks = jax.vmap(owner_mask)(led_rows)
    win_re = (windows[:, 0] * masks).astype(jnp.bfloat16)
    win_im = (windows[:, 1] * masks).astype(jnp.bfloat16)

    def slice_strip(block, start):
        return take_rows(block, start, width)

    row_re = (
        contract("lgb,bk->lkg", win_re, cos_table) + contract("lgb,bk->lkg", win_im, sin_table)
    ).astype(jnp.bfloat16)
    row_im = (
        contract("lgb,bk->lkg", win_im, cos_table) - contract("lgb,bk->lkg", win_re, sin_table)
    ).astype(jnp.bfloat16)
    col_re, col_im = (
        lax.all_to_all(row_re, "slab", split_axis=1, concat_axis=2, tiled=True),
        lax.all_to_all(row_im, "slab", split_axis=1, concat_axis=2, tiled=True),
    )
    field_in_re = jax.vmap(slice_strip)(col_re, led_rows)
    field_in_im = jax.vmap(slice_strip)(col_im, led_rows)
    back_re, back_im = modulus_step(field_in_re, field_in_im, images, cos_table, sin_table)

    def place_strip(block, start):
        return place_rows(block, start, total_rows, 1)

    full_re = jax.vmap(place_strip)(back_re, led_rows)
    full_im = jax.vmap(place_strip)(back_im, led_rows)
    home_re, home_im = (
        lax.all_to_all(as_sent(full_re), "slab", split_axis=2, concat_axis=1, tiled=True).astype(
            full_re.dtype
        ),
        lax.all_to_all(as_sent(full_im), "slab", split_axis=2, concat_axis=1, tiled=True).astype(
            full_im.dtype
        ),
    )
    upd_re = contract("lkg,kb->lgb", home_re, cos_table) - contract(
        "lkg,kb->lgb", home_im, sin_table
    )
    upd_im = contract("lkg,kb->lgb", home_im, cos_table) + contract(
        "lkg,kb->lgb", home_re, sin_table
    )
    upd_re = upd_re * masks
    upd_im = upd_im * masks

    def add_window(number, gradient):
        start = led_cols[number]
        piece = jnp.stack([upd_re[number], upd_im[number]])
        current = lax.dynamic_slice_in_dim(gradient, start, width, 2)
        return lax.dynamic_update_slice_in_dim(gradient, current + piece, start, 2)

    gradient = lax.fori_loop(
        0, led_rows.shape[0], add_window, jnp.zeros((2, slab_rows, columns), jnp.float32)
    )
    summed = lax.psum_scatter(gradient, "led", scatter_dimension=2, tiled=True)
    share = summed.shape[2]
    own_part = lax.dynamic_slice_in_dim(spectrum, lax.axis_index("led") * share, share, 2)
    return own_part + summed


SLABS = 8
HALF = 4
FIRST, LAST = 0, 7
PASSED = {1: 0, 6: 7}
INNER = (2, 3, 4, 5)


def dot(left, right):
    return jnp.dot(left, right, preferred_element_type=jnp.float32)


def window_mask(first_row, row_start, col_start, rows, first_col, cols, width):
    shape = (rows, cols)
    at_row = lax.broadcasted_iota(jnp.int32, shape, 0) + (first_row - row_start)
    at_col = lax.broadcasted_iota(jnp.int32, shape, 1) + (first_col - col_start)
    wraps = at_col < 0
    at_col = jnp.where(wraps, at_col + width, at_col)
    row_term = 2 * at_row + 1 - width
    col_term = 2 * at_col + 1 - width
    return row_term * row_term + col_term * col_term < width * width, wraps


def row_block(window, table):
    both = dot(window, table)
    half = both.shape[0] // 2
    row_re = both[:half, :LANES] + both[half:, LANES:]
    row_im = both[half:, :LANES] - both[:half, LANES:]
    return row_re.astype(jnp.bfloat16), row_im.astype(jnp.bfloat16)


def store_parts(out, values):
    per = out.shape[0] // 2
    rows = out.shape[1]
    for plane, value in enumerate(values):
        for led in range(per):
            out[plane * per + led] = value[led * rows : (led + 1) * rows]


def is_one_of(position, slabs):
    return functools.reduce(jnp.logical_or, [position == slab for slab in slabs])


def window_kernel(starts, spectrum, window):
    position = lax.axis_index("slab")
    leds = starts.shape[0] // 2
    rows = spectrum.shape[1]
    width = window.shape[1]
    for led in range(leds):
        inside, wraps = window_mask(
            position * rows, starts[led], starts[leds + led], rows, 0, width, width
        )
        for plane in range(2):
            value = jnp.where(wraps, spectrum[plane, :, width:], spectrum[plane, :, :width])
            at = (plane * leds + led) * rows
            window[at : at + rows, :] = jnp.where(inside, value, 0.0).astype(jnp.bfloat16)


def classes_of(position):
    hands_over = is_one_of(position, PASSED)
    return (jnp.where(hands_over, 5, 6), 7, 2, 3, 4, jnp.where(hands_over, 6, 5), 0, 1)


def rows_kernel(which, window, table, *outs):
    position = lax.axis_index("slab")
    for out, d in zip(outs, classes_of(position)[which]):
        store_parts(out, row_block(window[...], table[jnp.bitwise_xor(position, d)]))


def choose_kernel(got, own, out):
    passes = is_one_of(lax.axis_index("slab"), PASSED.values())

    @pl.when(passes)
    def _():
        out[...] = got[...]

    @pl.when(jnp.logical_not(passes))
    def _():
        out[...] = own[...]


def amplitude_kernel(images, table, out, table_out):
    leds, block, width = images.shape
    for led in range(leds):
        for j in range(width // LANES):
            piece = jnp.sqrt(images[led, :, j * LANES : (j + 1) * LANES])
            out[j * LANES : (j + 1) * LANES, led * block : (led + 1) * block] = piece.T
    table_out[...] = table[...]


def field_kernel(amplitude, table, *rest):
    far, near = rest[:5], rest[5 : HALF + 5]
    outs = rest[HALF + 5 : 2 * HALF + 5]
    field_in, diff, strips = rest[2 * HALF + 5 :]
    position = lax.axis_index("slab")
    parts, rows, _ = near[0].shape
    half = parts // 2 * LANES
    width = field_in.shape[0]
    steps = width // LANES
    group = 4
    for d, block in enumerate(near):
        at = pl.multiple_of(jnp.bitwise_and(jnp.bitwise_xor(position, d), HALF - 1) * rows, rows)
        for part in range(parts):
            cols = slice(part * LANES, (part + 1) * LANES)
            field_in[pl.ds(at, rows), cols] = block[part]

    def add(block, origin):
        at = pl.multiple_of(jnp.bitwise_and(origin, HALF - 1) * rows, rows)
        for part in range(parts):
            cols = slice(part * LANES, (part + 1) * LANES)
            field_in[pl.ds(at, rows), cols] += block[part]

    passes = is_one_of(position, PASSED.values())
    hands_over = is_one_of(position, PASSED)
    ends = is_one_of(position, [to ^ 4 for to in PASSED.values()])

    @pl.when(is_one_of(position, INNER))
    def _():
        add(far[0], jnp.bitwise_xor(position, 6))
        add(far[1], jnp.bitwise_xor(position, 7))
        add(far[2], jnp.bitwise_xor(position, jnp.where(ends, 5, 4)))

    @pl.when(jnp.logical_or(passes, hands_over))
    def _():
        add(far[2], jnp.bitwise_xor(position, 4))
        add(far[3], jnp.bitwise_xor(position, jnp.where(hands_over, 7, 6)))
        add(far[4], jnp.bitwise_xor(position, 5))

    for first in range(0, steps, group):
        product = dot(
            table[first : first + group].reshape(group * 2 * LANES, width), field_in[...]
        )
        for j in range(first, first + group):
            both = product[(j - first) * 2 * LANES : (j - first + 1) * 2 * LANES]
            field_re = both[:LANES, :half] + both[LANES:, half:]
            field_im = both[:LANES, half:] - both[LANES:, :half]
            here = pl.ds(j * LANES, LANES)
            factor = (
                amplitude[here, :] * lax.rsqrt(field_re * field_re + field_im * field_im + 0.25)
                - 1.0
            )
            diff[here, :half] = (field_re * factor).astype(jnp.bfloat16)
            diff[here, half:] = (field_im * factor).astype(jnp.bfloat16)
    pieces = rows // LANES
    for i in range(HALF):
        product = dot(
            table[i * pieces : (i + 1) * pieces].reshape(pieces * 2 * LANES, width), diff[...]
        )
        for h in range(pieces):
            both = product[h * 2 * LANES : (h + 1) * 2 * LANES]
            here = pl.ds(h * LANES, LANES)
            back_re = (both[:LANES, :half] - both[LANES:, half:]).astype(jnp.bfloat16)
            back_im = (both[:LANES, half:] + both[LANES:, :half]).astype(jnp.bfloat16)
            for part in range(parts // 2):
                cols = slice(part * LANES, (part + 1) * LANES)
                strips[i, part, here, :] = back_re[:, cols]
                strips[i, parts // 2 + part, here, :] = back_im[:, cols]
    for d, out in enumerate(outs):
        out[...] = strips[jnp.bitwise_and(jnp.bitwise_xor(position, d), HALF - 1)]


def update_columns(own_core, starts, table, back, outs):
    position = lax.axis_index("slab")
    led_at = lax.axis_index("led")
    core = jnp.bitwise_and(led_at, 1)
    plane_x = jnp.right_shift(led_at, 1)
    which_half = jnp.right_shift(position, 2)
    first_row = jnp.bitwise_and(position, HALF - 1)
    leds = starts.shape[0] // 2
    rows = back.shape[0] // (2 * leds)
    depth = back.shape[1]
    width = table.shape[1]
    group = width // LANES // 2
    owner = core if own_core else 1 - core
    shape = (rows, LANES)
    for n in range(group):
        block = owner * group + n
        both = dot(
            back[...], table[block, pl.ds(pl.multiple_of(which_half * depth, depth), depth)]
        )
        half = leds * rows
        update = (
            both[:half, :LANES] - both[half:, LANES:],
            both[half:, :LANES] + both[:half, LANES:],
        )
        sums = [[0.0, 0.0] for _ in outs]
        for led in range(leds):
            at_row = lax.broadcasted_iota(jnp.int32, shape, 0) + (
                first_row * rows - starts[led]
            )
            at_col = lax.broadcasted_iota(jnp.int32, shape, 1) + (
                block * LANES - starts[leds + led]
            )
            row_term = 2 * jnp.where(at_row < 0, at_row + width, at_row) + 1 - width
            col_term = 2 * jnp.where(at_col < 0, at_col + width, at_col) + 1 - width
            inside = row_term * row_term + col_term * col_term < width * width
            this_slab = jnp.where(at_row < 0, 1, 0) == which_half
            this_x = jnp.where(at_col < 0, 1, 0) == plane_x
            for plane in range(2):
                piece = jnp.where(inside, update[plane][led * rows : (led + 1) * rows], 0.0)
                for i, at_slab in enumerate(
                    (jnp.where(this_slab, piece, 0.0), jnp.where(this_slab, 0.0, piece))
                ):
                    sums[2 * i][plane] += jnp.where(this_x, at_slab, 0.0)
                    sums[2 * i + 1][plane] += jnp.where(this_x, 0.0, at_slab)
        cols = slice(n * LANES, (n + 1) * LANES)
        for out, both_planes in zip(outs, sums):
            for plane in range(2):
                out[plane, :, cols] = both_planes[plane].astype(out.dtype)


def sent_kernel(starts, table, *rest):
    blocks = rest[:HALF]
    this_slab, that_slab, back = rest[HALF:]
    position = lax.axis_index("slab")
    parts, rows, _ = blocks[0].shape
    for d, block in enumerate(blocks):
        source = jnp.bitwise_and(jnp.bitwise_xor(position, d), HALF - 1)
        at = pl.multiple_of(source * LANES, LANES)
        for part in range(parts):
            back[part * rows : (part + 1) * rows, pl.ds(at, LANES)] = block[part]
    outs = [out.at[i] for out in (this_slab, that_slab) for i in range(2)]
    update_columns(False, starts, table, back, outs)


def kept_kernel(starts, table, back, *outs):
    update_columns(True, starts, table, back, outs)


def z_first_kernel(that_near, that_far, got_that, out):
    cols = out.shape[3]
    for i, kept in enumerate((that_near, that_far)):
        total = kept[:, :, :cols] + got_that[i, :, :, :cols].astype(jnp.float32)
        out[i] = total.astype(out.dtype)


def x_first_kernel(that_far, got_that, out):
    cols = that_far.shape[2] - out.shape[2]
    total = that_far[:, :, cols:] + got_that[1, :, :, cols:].astype(jnp.float32)
    out[...] = total.astype(out.dtype)


def z_second_kernel(that_near, got_that, got_x, out):
    cols = that_near.shape[2] - out.shape[2]
    total = that_near[:, :, cols:] + got_that[0, :, :, cols:].astype(jnp.float32)
    out[...] = (total + got_x[...].astype(jnp.float32)).astype(out.dtype)


def x_second_kernel(this_far, got_this, got_z, out):
    cols = got_z.shape[3]
    total = this_far[...] + got_this[1].astype(jnp.float32)
    out[:, :, cols:] = total[:, :, cols:].astype(out.dtype)
    out[:, :, :cols] = (total[:, :, :cols] + got_z[1].astype(jnp.float32)).astype(out.dtype)


def local_call(kernel, out_shape, spaces, scratch, flops, moved, name):
    return pl.pallas_call(
        kernel,
        out_shape=out_shape,
        in_specs=[pl.BlockSpec(memory_space=space) for space in spaces],
        out_specs=jax.tree.map(lambda _: pl.BlockSpec(memory_space=pltpu.VMEM), out_shape),
        scratch_shapes=scratch,
        compiler_params=pltpu.CompilerParams(vmem_limit_bytes=32 * 2**20),
        cost_estimate=pl.CostEstimate(flops=flops, bytes_accessed=moved, transcendentals=0),
        name=name,
    )


def body_slabs(spectrum, led_rows, led_cols, images):
    leds, block, width = images.shape
    rows = spectrum.shape[1]
    led_at = lax.axis_index("led")
    bf16 = jnp.bfloat16
    vmem, smem = pltpu.VMEM, pltpu.SMEM
    cos_table, sin_table = host_tables(width)
    steps = width // LANES
    by_col = np.stack(
        [
            np.concatenate([t[:, j * LANES : (j + 1) * LANES] for t in (cos_table, sin_table)], 1)
            for j in range(steps)
        ]
    )
    by_row = jnp.asarray(np.ascontiguousarray(by_col.transpose(0, 2, 1)))
    by_col = jnp.asarray(by_col)
    parts = 2 * leds
    sent_block = jax.ShapeDtypeStruct((parts, rows, LANES), bf16)
    flops = 8 * leds * rows * width * width

    starts = jnp.concatenate([led_rows, led_cols]).astype(jnp.int32)
    window = local_call(
        window_kernel,
        jax.ShapeDtypeStruct((parts * rows, width), bf16),
        [smem, vmem],
        [],
        0,
        6 * 2**20,
        "windows",
    )(starts, spectrum)

    def rows_call(which, name):
        count = which.stop - which.start
        return local_call(
            functools.partial(rows_kernel, which),
            [sent_block] * count,
            [vmem, vmem],
            [],
            flops * count // SLABS,
            5 * 2**20,
            name,
        )(window, by_col)

    first_a, first_b, near_2, near_3 = rows_call(slice(0, 4), "rows_round_1")

    def permute(sent, pairs):
        return lax.ppermute(sent, "slab", pairs)

    def choose(got, own, name):
        return local_call(
            choose_kernel, sent_block, [vmem] * 2, [], 0, 2**19, name
        )(got, own)

    handed = list(PASSED.items())
    windowed = range(FIRST + 1, LAST)
    got_a = permute(first_a, [(s, s ^ 6) for s in INNER] + handed)
    got_b = permute(first_b, [(s, s ^ 7) for s in INNER] + handed)
    near_2 = permute(near_2, [(s, s ^ 2) for s in windowed])
    near_3 = permute(near_3, [(s, s ^ 3) for s in windowed])
    second_a, second_b, near_0, near_1 = rows_call(slice(4, SLABS), "rows_round_2")
    got_a, second_a, second_b, near_1, images = lax.optimization_barrier(
        (got_a, second_a, second_b, near_1, images)
    )
    outer_pairs = [(s, s ^ 6) for s in range(SLABS) if s not in INNER]
    near_1 = permute(near_1, [(s, s ^ 1) for s in windowed])
    near_1, near_2, near_3, got_b = lax.optimization_barrier((near_1, near_2, near_3, got_b))
    far_columns = [
        got_a,
        got_b,
        permute(choose(got_a, second_a, "class_4_blocks"), [(s, s ^ 4) for s in range(SLABS)]),
        permute(choose(got_b, second_b, "class_6_blocks"), outer_pairs),
        permute(second_b, [(s, s ^ 5) for s in INNER]),
    ]
    near_columns = [near_0, near_1, near_2, near_3]
    amplitude, by_row = local_call(
        amplitude_kernel,
        [
            jax.ShapeDtypeStruct((width, leds * block), jnp.float32),
            jax.ShapeDtypeStruct(by_row.shape, bf16),
        ],
        [vmem] * 2,
        [],
        0,
        10 * 2**20,
        "amplitude",
    )(images, by_row)
    strips = local_call(
        field_kernel,
        [sent_block] * HALF,
        [vmem] * 11,
        [pltpu.VMEM((width, parts * block), bf16)] * 2
        + [pltpu.VMEM((HALF,) + sent_block.shape, bf16)],
        16 * leds * block * width * width,
        12 * 2**20,
        "modulus_step",
    )(amplitude, by_row, *far_columns, *near_columns)

    def send_home(d):
        pairs = [(s, (s + d) % SLABS) for s in range(SLABS) if FIRST < (s + d) % SLABS < LAST]
        return permute(strips[d % HALF], pairs)

    home = [strips[0]]
    home += [
        permute(strips[d], [(s, s ^ d) for s in range(SLABS)]) for d in range(1, HALF)
    ]
    share = width // 2
    first = share // 4
    piece = (2, rows, share)
    cores = [(0, 1), (1, 0), (2, 3), (3, 2)]
    planes = [(0, 2), (2, 0), (1, 3), (3, 1)]
    across = [(s, s ^ 4) for s in range(SLABS) if FIRST < s ^ 4 < LAST]
    sent_this, sent_that, back = local_call(
        sent_kernel,
        [
            jax.ShapeDtypeStruct((2,) + piece, bf16),
            jax.ShapeDtypeStruct((2,) + piece, bf16),
            jax.ShapeDtypeStruct((parts * rows, HALF * LANES), bf16),
        ],
        [smem] + [vmem] * (1 + HALF),
        [],
        flops // 4,
        8 * 2**20,
        "update_sent",
    )(starts, by_col, *home)
    got_that = lax.ppermute(sent_that, "led", cores)
    got_this = lax.ppermute(sent_this, "led", cores)
    this_near, this_far, that_near, that_far = local_call(
        kept_kernel,
        [jax.ShapeDtypeStruct(piece, jnp.float32)] * 4,
        [smem, vmem, vmem],
        [],
        flops // 4,
        10 * 2**20,
        "update_kept",
    )(starts, by_col, back)

    def sum_call(kernel, shape, *values):
        out_shape = jax.ShapeDtypeStruct(shape, bf16)
        specs = [vmem] * len(values)
        return local_call(kernel, out_shape, specs, [], 0, 2**20, kernel.__name__)(*values)

    over = sum_call(z_first_kernel, (2, 2, rows, first), that_near, that_far, got_that)
    got_z_first = permute(over, across)
    over = sum_call(x_first_kernel, (2, rows, share - first), that_far, got_that)
    got_x = lax.ppermute(over, "led", planes)
    over = sum_call(z_second_kernel, (2, rows, share - first), that_near, got_that, got_x)
    got_z_second = permute(over, across)
    over = sum_call(x_second_kernel, piece, this_far, got_this, got_z_first)
    got_x = lax.ppermute(over, "led", planes)

    def widen(value, before):
        after = share - before - value.shape[2]
        return jnp.pad(value.astype(jnp.float32), ((0, 0), (0, 0), (before, after)))

    base = lax.dynamic_slice_in_dim(spectrum, led_at * share, share, 2)
    base += this_near + got_this[0].astype(jnp.float32) + widen(got_z_first[0], 0)
    base, got_x = lax.optimization_barrier((base, got_x))
    base += got_x.astype(jnp.float32)
    base, got_z_second = lax.optimization_barrier((base, got_z_second))
    return base + widen(got_z_second, first)


def solution(mesh):
    placed = (P(None, "slab", None), P("led"), P("led"), P("led", "slab", None))
    fits = mesh.shape["slab"] == 8 and mesh.shape["led"] == 4

    def body(spectrum, led_rows, led_cols, images):
        shapes = (spectrum.shape, images.shape)
        if fits and shapes == ((2, 256, 2048), (2, 128, 1024)):
            return body_slabs(spectrum, led_rows, led_cols, images)
        return body_any(spectrum, led_rows, led_cols, images)

    return jax.shard_map(
        body, mesh=mesh, in_specs=placed, out_specs=P(None, "slab", "led"), check_vma=False
    )
```

```python
import functools

import jax
import jax.numpy as jnp
import numpy as np
from jax import lax
from jax.experimental import pallas as pl
from jax.experimental.pallas import tpu as pltpu
from jax.sharding import PartitionSpec as P

LANES = 128


def as_sent(value):
    return jax.tree.map(lambda a: a.astype(jnp.bfloat16) if a.dtype == jnp.float32 else a, value)


def host_tables(width):
    index = np.arange(width, dtype=np.int64)
    angle_index = (index[:, None] * index[None, :] % width).astype(np.float32)
    angle = angle_index * np.float32(2.0 * 3.141592653589793 / width)
    scale = np.float32(1.0) / np.sqrt(np.float32(width))
    return (
        (np.cos(angle) * scale).astype(jnp.bfloat16),
        (np.sin(angle) * scale).astype(jnp.bfloat16),
    )


def make_pupil(row_index, col_index, width):
    row_term = (2 * row_index + 1 - width) * (2 * row_index + 1 - width)
    col_term = (2 * col_index + 1 - width) * (2 * col_index + 1 - width)
    return (row_term[:, None] + col_term[None, :] < width * width).astype(jnp.float32)


def contract(form, left, right):
    return jnp.einsum(form, left, right, preferred_element_type=jnp.float32)


def take_rows(strip, start, width):
    return lax.dynamic_slice_in_dim(strip, start, width, 1)


def place_rows(block, start, total, axis_dim):
    shape = list(block.shape)
    shape[axis_dim] = total
    holder = jnp.zeros(tuple(shape), block.dtype)
    return lax.dynamic_update_slice_in_dim(holder, block, start, axis_dim)


def modulus_step(field_in_re, field_in_im, image, cos_table, sin_table):
    field_re = contract("lka,am->lkm", field_in_re, cos_table) + contract(
        "lka,am->lkm", field_in_im, sin_table
    )
    field_im = contract("lka,am->lkm", field_in_im, cos_table) - contract(
        "lka,am->lkm", field_in_re, sin_table
    )
    factor = jnp.sqrt(image) / jnp.sqrt(field_re * field_re + field_im * field_im + 0.25) - 1.0
    diff_re = (field_re * factor).astype(jnp.bfloat16)
    diff_im = (field_im * factor).astype(jnp.bfloat16)
    back_re = (
        contract("lkm,ma->lka", diff_re, cos_table) - contract("lkm,ma->lka", diff_im, sin_table)
    ).astype(jnp.bfloat16)
    back_im = (
        contract("lkm,ma->lka", diff_im, cos_table) + contract("lkm,ma->lka", diff_re, sin_table)
    ).astype(jnp.bfloat16)
    return (back_re, back_im)


def body_any(spectrum, led_rows, led_cols, images):
    width = images.shape[2]
    slab_rows = spectrum.shape[1]
    columns = spectrum.shape[2]
    slabs = lax.axis_size("slab")
    total_rows = slab_rows * slabs
    position = lax.axis_index("slab")
    cos_table, sin_table = (jnp.asarray(t) for t in host_tables(width))
    own_rows = position * slab_rows + jnp.arange(slab_rows, dtype=jnp.int32)
    col_index = jnp.arange(width, dtype=jnp.int32)

    def take_cols(start):
        return lax.dynamic_slice_in_dim(spectrum, start, width, 2)

    def owner_mask(start):
        return make_pupil(own_rows - start, col_index, width)

    windows = jax.vmap(take_cols)(led_cols)
    masks = jax.vmap(owner_mask)(led_rows)
    win_re = (windows[:, 0] * masks).astype(jnp.bfloat16)
    win_im = (windows[:, 1] * masks).astype(jnp.bfloat16)

    def slice_strip(block, start):
        return take_rows(block, start, width)

    row_re = (
        contract("lgb,bk->lkg", win_re, cos_table) + contract("lgb,bk->lkg", win_im, sin_table)
    ).astype(jnp.bfloat16)
    row_im = (
        contract("lgb,bk->lkg", win_im, cos_table) - contract("lgb,bk->lkg", win_re, sin_table)
    ).astype(jnp.bfloat16)
    col_re, col_im = (
        lax.all_to_all(row_re, "slab", split_axis=1, concat_axis=2, tiled=True),
        lax.all_to_all(row_im, "slab", split_axis=1, concat_axis=2, tiled=True),
    )
    field_in_re = jax.vmap(slice_strip)(col_re, led_rows)
    field_in_im = jax.vmap(slice_strip)(col_im, led_rows)
    back_re, back_im = modulus_step(field_in_re, field_in_im, images, cos_table, sin_table)

    def place_strip(block, start):
        return place_rows(block, start, total_rows, 1)

    full_re = jax.vmap(place_strip)(back_re, led_rows)
    full_im = jax.vmap(place_strip)(back_im, led_rows)
    home_re, home_im = (
        lax.all_to_all(as_sent(full_re), "slab", split_axis=2, concat_axis=1, tiled=True).astype(
            full_re.dtype
        ),
        lax.all_to_all(as_sent(full_im), "slab", split_axis=2, concat_axis=1, tiled=True).astype(
            full_im.dtype
        ),
    )
    upd_re = contract("lkg,kb->lgb", home_re, cos_table) - contract(
        "lkg,kb->lgb", home_im, sin_table
    )
    upd_im = contract("lkg,kb->lgb", home_im, cos_table) + contract(
        "lkg,kb->lgb", home_re, sin_table
    )
    upd_re = upd_re * masks
    upd_im = upd_im * masks

    def add_window(number, gradient):
        start = led_cols[number]
        piece = jnp.stack([upd_re[number], upd_im[number]])
        current = lax.dynamic_slice_in_dim(gradient, start, width, 2)
        return lax.dynamic_update_slice_in_dim(gradient, current + piece, start, 2)

    gradient = lax.fori_loop(
        0, led_rows.shape[0], add_window, jnp.zeros((2, slab_rows, columns), jnp.float32)
    )
    summed = lax.psum_scatter(gradient, "led", scatter_dimension=2, tiled=True)
    share = summed.shape[2]
    own_part = lax.dynamic_slice_in_dim(spectrum, lax.axis_index("led") * share, share, 2)
    return own_part + summed


SLABS = 8
HALF = 4
FIRST, LAST = 0, 7
PASSED = {1: 0, 6: 7}
INNER = (2, 3, 4, 5)


def dot(left, right):
    return jnp.dot(left, right, preferred_element_type=jnp.float32)


def window_mask(first_row, row_start, col_start, rows, first_col, cols, width):
    shape = (rows, cols)
    at_row = lax.broadcasted_iota(jnp.int32, shape, 0) + (first_row - row_start)
    at_col = lax.broadcasted_iota(jnp.int32, shape, 1) + (first_col - col_start)
    wraps = at_col < 0
    at_col = jnp.where(wraps, at_col + width, at_col)
    row_term = 2 * at_row + 1 - width
    col_term = 2 * at_col + 1 - width
    return row_term * row_term + col_term * col_term < width * width, wraps


def row_block(window, table):
    both = dot(window, table)
    half = both.shape[0] // 2
    row_re = both[:half, :LANES] + both[half:, LANES:]
    row_im = both[half:, :LANES] - both[:half, LANES:]
    return row_re.astype(jnp.bfloat16), row_im.astype(jnp.bfloat16)


def store_parts(out, values):
    per = out.shape[0] // 2
    rows = out.shape[1]
    for plane, value in enumerate(values):
        for led in range(per):
            out[plane * per + led] = value[led * rows : (led + 1) * rows]


def is_one_of(position, slabs):
    return functools.reduce(jnp.logical_or, [position == slab for slab in slabs])


def window_kernel(starts, spectrum, window):
    position = lax.axis_index("slab")
    leds = starts.shape[0] // 2
    rows = spectrum.shape[1]
    width = window.shape[1]
    for led in range(leds):
        inside, wraps = window_mask(
            position * rows, starts[led], starts[leds + led], rows, 0, width, width
        )
        for plane in range(2):
            value = jnp.where(wraps, spectrum[plane, :, width:], spectrum[plane, :, :width])
            at = (plane * leds + led) * rows
            window[at : at + rows, :] = jnp.where(inside, value, 0.0).astype(jnp.bfloat16)


def classes_of(position):
    hands_over = is_one_of(position, PASSED)
    return (jnp.where(hands_over, 5, 6), 7, 2, 4, jnp.where(hands_over, 6, 5), 0, 1, 3)


def rows_kernel(which, window, table, *outs):
    position = lax.axis_index("slab")
    for out, d in zip(outs, classes_of(position)[which]):
        store_parts(out, row_block(window[...], table[jnp.bitwise_xor(position, d)]))


def choose_kernel(got, own, out):
    passes = is_one_of(lax.axis_index("slab"), PASSED.values())

    @pl.when(passes)
    def _():
        out[...] = got[...]

    @pl.when(jnp.logical_not(passes))
    def _():
        out[...] = own[...]


def amplitude_kernel(images, table, out, table_out):
    leds, block, width = images.shape
    for led in range(leds):
        for j in range(width // LANES):
            piece = jnp.sqrt(images[led, :, j * LANES : (j + 1) * LANES])
            out[j * LANES : (j + 1) * LANES, led * block : (led + 1) * block] = piece.T
    table_out[...] = table[...]


def field_kernel(amplitude, table, *rest):
    far, near = rest[:5], rest[5 : HALF + 5]
    outs = rest[HALF + 5 : 2 * HALF + 5]
    field_in, diff, strips = rest[2 * HALF + 5 :]
    position = lax.axis_index("slab")
    parts, rows, _ = near[0].shape
    half = parts // 2 * LANES
    width = field_in.shape[0]
    steps = width // LANES
    group = 4
    for d, block in enumerate(near):
        at = pl.multiple_of(jnp.bitwise_and(jnp.bitwise_xor(position, d), HALF - 1) * rows, rows)
        for part in range(parts):
            cols = slice(part * LANES, (part + 1) * LANES)
            field_in[pl.ds(at, rows), cols] = block[part]

    def add(block, origin):
        at = pl.multiple_of(jnp.bitwise_and(origin, HALF - 1) * rows, rows)
        for part in range(parts):
            cols = slice(part * LANES, (part + 1) * LANES)
            field_in[pl.ds(at, rows), cols] += block[part]

    passes = is_one_of(position, PASSED.values())
    hands_over = is_one_of(position, PASSED)
    ends = is_one_of(position, [to ^ 4 for to in PASSED.values()])

    @pl.when(is_one_of(position, INNER))
    def _():
        add(far[1], jnp.bitwise_xor(position, 6))
        add(far[2], jnp.bitwise_xor(position, 7))
        add(far[3], jnp.bitwise_xor(position, jnp.where(ends, 5, 4)))

    @pl.when(jnp.logical_or(passes, hands_over))
    def _():
        add(far[3], jnp.bitwise_xor(position, 4))
        add(far[4], jnp.bitwise_xor(position, jnp.where(hands_over, 7, 6)))
        add(far[0], jnp.bitwise_xor(position, 5))

    for first in range(0, steps, group):
        product = dot(
            table[first : first + group].reshape(group * 2 * LANES, width), field_in[...]
        )
        for j in range(first, first + group):
            both = product[(j - first) * 2 * LANES : (j - first + 1) * 2 * LANES]
            field_re = both[:LANES, :half] + both[LANES:, half:]
            field_im = both[:LANES, half:] - both[LANES:, :half]
            here = pl.ds(j * LANES, LANES)
            factor = (
                amplitude[here, :] * lax.rsqrt(field_re * field_re + field_im * field_im + 0.25)
                - 1.0
            )
            diff[here, :half] = (field_re * factor).astype(jnp.bfloat16)
            diff[here, half:] = (field_im * factor).astype(jnp.bfloat16)
    pieces = rows // LANES
    for i in range(HALF):
        product = dot(
            table[i * pieces : (i + 1) * pieces].reshape(pieces * 2 * LANES, width), diff[...]
        )
        for h in range(pieces):
            both = product[h * 2 * LANES : (h + 1) * 2 * LANES]
            here = pl.ds(h * LANES, LANES)
            back_re = (both[:LANES, :half] - both[LANES:, half:]).astype(jnp.bfloat16)
            back_im = (both[:LANES, half:] + both[LANES:, :half]).astype(jnp.bfloat16)
            for part in range(parts // 2):
                cols = slice(part * LANES, (part + 1) * LANES)
                strips[i, part, here, :] = back_re[:, cols]
                strips[i, parts // 2 + part, here, :] = back_im[:, cols]
    for d, out in enumerate(outs):
        out[...] = strips[jnp.bitwise_and(jnp.bitwise_xor(position, d), HALF - 1)]


def update_columns(own_core, starts, table, back, outs):
    position = lax.axis_index("slab")
    led_at = lax.axis_index("led")
    core = jnp.bitwise_and(led_at, 1)
    plane_x = jnp.right_shift(led_at, 1)
    which_half = jnp.right_shift(position, 2)
    first_row = jnp.bitwise_and(position, HALF - 1)
    leds = starts.shape[0] // 2
    rows = back.shape[0] // (2 * leds)
    depth = back.shape[1]
    width = table.shape[1]
    group = width // LANES // 2
    owner = core if own_core else 1 - core
    shape = (rows, LANES)
    for n in range(group):
        block = owner * group + n
        both = dot(
            back[...], table[block, pl.ds(pl.multiple_of(which_half * depth, depth), depth)]
        )
        half = leds * rows
        update = (
            both[:half, :LANES] - both[half:, LANES:],
            both[half:, :LANES] + both[:half, LANES:],
        )
        sums = [[0.0, 0.0] for _ in outs]
        for led in range(leds):
            at_row = lax.broadcasted_iota(jnp.int32, shape, 0) + (
                first_row * rows - starts[led]
            )
            at_col = lax.broadcasted_iota(jnp.int32, shape, 1) + (
                block * LANES - starts[leds + led]
            )
            row_term = 2 * jnp.where(at_row < 0, at_row + width, at_row) + 1 - width
            col_term = 2 * jnp.where(at_col < 0, at_col + width, at_col) + 1 - width
            inside = row_term * row_term + col_term * col_term < width * width
            this_slab = jnp.where(at_row < 0, 1, 0) == which_half
            this_x = jnp.where(at_col < 0, 1, 0) == plane_x
            for plane in range(2):
                piece = jnp.where(inside, update[plane][led * rows : (led + 1) * rows], 0.0)
                for i, at_slab in enumerate(
                    (jnp.where(this_slab, piece, 0.0), jnp.where(this_slab, 0.0, piece))
                ):
                    sums[2 * i][plane] += jnp.where(this_x, at_slab, 0.0)
                    sums[2 * i + 1][plane] += jnp.where(this_x, 0.0, at_slab)
        cols = slice(n * LANES, (n + 1) * LANES)
        for out, both_planes in zip(outs, sums):
            for plane in range(2):
                out[plane, :, cols] = both_planes[plane].astype(out.dtype)


def sent_kernel(starts, table, *rest):
    blocks = rest[:HALF]
    this_slab, that_slab, back = rest[HALF:]
    position = lax.axis_index("slab")
    parts, rows, _ = blocks[0].shape
    for d, block in enumerate(blocks):
        source = jnp.bitwise_and(jnp.bitwise_xor(position, d), HALF - 1)
        at = pl.multiple_of(source * LANES, LANES)
        for part in range(parts):
            back[part * rows : (part + 1) * rows, pl.ds(at, LANES)] = block[part]
    outs = [out.at[i] for out in (this_slab, that_slab) for i in range(2)]
    update_columns(False, starts, table, back, outs)


def kept_kernel(starts, table, back, *outs):
    update_columns(True, starts, table, back, outs)


def z_first_kernel(that_near, that_far, got_that, out):
    cols = out.shape[3]
    for i, kept in enumerate((that_near, that_far)):
        total = kept[:, :, :cols] + got_that[i, :, :, :cols].astype(jnp.float32)
        out[i] = total.astype(out.dtype)


def x_first_kernel(that_far, got_that, out):
    cols = that_far.shape[2] - out.shape[2]
    total = that_far[:, :, cols:] + got_that[1, :, :, cols:].astype(jnp.float32)
    out[...] = total.astype(out.dtype)


def z_second_kernel(that_near, got_that, got_x, out):
    cols = that_near.shape[2] - out.shape[2]
    total = that_near[:, :, cols:] + got_that[0, :, :, cols:].astype(jnp.float32)
    out[...] = (total + got_x[...].astype(jnp.float32)).astype(out.dtype)


def x_second_kernel(this_far, got_this, got_z, out):
    cols = got_z.shape[3]
    total = this_far[...] + got_this[1].astype(jnp.float32)
    out[:, :, cols:] = total[:, :, cols:].astype(out.dtype)
    out[:, :, :cols] = (total[:, :, :cols] + got_z[1].astype(jnp.float32)).astype(out.dtype)


def local_call(kernel, out_shape, spaces, scratch, flops, moved, name):
    return pl.pallas_call(
        kernel,
        out_shape=out_shape,
        in_specs=[pl.BlockSpec(memory_space=space) for space in spaces],
        out_specs=jax.tree.map(lambda _: pl.BlockSpec(memory_space=pltpu.VMEM), out_shape),
        scratch_shapes=scratch,
        compiler_params=pltpu.CompilerParams(vmem_limit_bytes=32 * 2**20),
        cost_estimate=pl.CostEstimate(flops=flops, bytes_accessed=moved, transcendentals=0),
        name=name,
    )


def body_slabs(spectrum, led_rows, led_cols, images):
    leds, block, width = images.shape
    rows = spectrum.shape[1]
    led_at = lax.axis_index("led")
    bf16 = jnp.bfloat16
    vmem, smem = pltpu.VMEM, pltpu.SMEM
    cos_table, sin_table = host_tables(width)
    steps = width // LANES
    by_col = np.stack(
        [
            np.concatenate([t[:, j * LANES : (j + 1) * LANES] for t in (cos_table, sin_table)], 1)
            for j in range(steps)
        ]
    )
    by_row = jnp.asarray(np.ascontiguousarray(by_col.transpose(0, 2, 1)))
    by_col = jnp.asarray(by_col)
    parts = 2 * leds
    sent_block = jax.ShapeDtypeStruct((parts, rows, LANES), bf16)
    flops = 8 * leds * rows * width * width

    starts = jnp.concatenate([led_rows, led_cols]).astype(jnp.int32)
    window = local_call(
        window_kernel,
        jax.ShapeDtypeStruct((parts * rows, width), bf16),
        [smem, vmem],
        [],
        0,
        6 * 2**20,
        "windows",
    )(starts, spectrum)

    def rows_call(which, name):
        count = which.stop - which.start
        return local_call(
            functools.partial(rows_kernel, which),
            [sent_block] * count,
            [vmem, vmem],
            [],
            flops * count // SLABS,
            5 * 2**20,
            name,
        )(window, by_col)

    first_a, first_b, near_2 = rows_call(slice(0, 3), "rows_round_1")

    def permute(sent, pairs):
        return lax.ppermute(sent, "slab", pairs)

    def choose(got, own, name):
        return local_call(
            choose_kernel, sent_block, [vmem] * 2, [], 0, 2**19, name
        )(got, own)

    handed = list(PASSED.items())
    windowed = range(FIRST + 1, LAST)
    got_a = permute(first_a, [(s, s ^ 6) for s in INNER] + handed)
    got_b = permute(first_b, [(s, s ^ 7) for s in INNER] + handed)
    near_2 = permute(near_2, [(s, s ^ 2) for s in windowed])
    second_a, second_b, near_0, near_1, near_3 = rows_call(slice(3, SLABS), "rows_round_2")
    got_a, near_2, second_a, second_b, near_1, near_3, images = lax.optimization_barrier(
        (got_a, near_2, second_a, second_b, near_1, near_3, images)
    )
    outer_pairs = [(s, s ^ 6) for s in range(SLABS) if s not in INNER]
    inner_5 = permute(second_b, [(s, s ^ 5) for s in INNER])
    near_1 = permute(near_1, [(s, s ^ 1) for s in windowed])
    near_3 = permute(near_3, [(s, s ^ 3) for s in windowed])
    near_1, got_b = lax.optimization_barrier((near_1, got_b))
    class_4 = permute(
        choose(got_a, second_a, "class_4_blocks"), [(s, s ^ 4) for s in range(SLABS)]
    )
    outer_6 = permute(choose(got_b, second_b, "class_6_blocks"), outer_pairs)
    far_columns = [inner_5, got_a, got_b, class_4, outer_6]
    near_columns = [near_0, near_1, near_2, near_3]
    amplitude, by_row = local_call(
        amplitude_kernel,
        [
            jax.ShapeDtypeStruct((width, leds * block), jnp.float32),
            jax.ShapeDtypeStruct(by_row.shape, bf16),
        ],
        [vmem] * 2,
        [],
        0,
        10 * 2**20,
        "amplitude",
    )(images, by_row)
    strips = local_call(
        field_kernel,
        [sent_block] * HALF,
        [vmem] * 11,
        [pltpu.VMEM((width, parts * block), bf16)] * 2
        + [pltpu.VMEM((HALF,) + sent_block.shape, bf16)],
        16 * leds * block * width * width,
        12 * 2**20,
        "modulus_step",
    )(amplitude, by_row, *far_columns, *near_columns)

    def send_home(d):
        pairs = [(s, (s + d) % SLABS) for s in range(SLABS) if FIRST < (s + d) % SLABS < LAST]
        return permute(strips[d % HALF], pairs)

    home = [strips[0]]
    home += [
        permute(strips[d], [(s, s ^ d) for s in range(SLABS)]) for d in range(1, HALF)
    ]
    share = width // 2
    first = share // 4
    piece = (2, rows, share)
    cores = [(0, 1), (1, 0), (2, 3), (3, 2)]
    planes = [(0, 2), (2, 0), (1, 3), (3, 1)]
    across = [(s, s ^ 4) for s in range(SLABS) if FIRST < s ^ 4 < LAST]
    sent_this, sent_that, back = local_call(
        sent_kernel,
        [
            jax.ShapeDtypeStruct((2,) + piece, bf16),
            jax.ShapeDtypeStruct((2,) + piece, bf16),
            jax.ShapeDtypeStruct((parts * rows, HALF * LANES), bf16),
        ],
        [smem] + [vmem] * (1 + HALF),
        [],
        flops // 4,
        8 * 2**20,
        "update_sent",
    )(starts, by_col, *home)
    got_that = lax.ppermute(sent_that, "led", cores)
    got_this = lax.ppermute(sent_this, "led", cores)
    this_near, this_far, that_near, that_far = local_call(
        kept_kernel,
        [jax.ShapeDtypeStruct(piece, jnp.float32)] * 4,
        [smem, vmem, vmem],
        [],
        flops // 4,
        10 * 2**20,
        "update_kept",
    )(starts, by_col, back)

    def sum_call(kernel, shape, *values):
        out_shape = jax.ShapeDtypeStruct(shape, bf16)
        specs = [vmem] * len(values)
        return local_call(kernel, out_shape, specs, [], 0, 2**20, kernel.__name__)(*values)

    over = sum_call(z_first_kernel, (2, 2, rows, first), that_near, that_far, got_that)
    got_z_first = permute(over, across)
    over = sum_call(x_first_kernel, (2, rows, share - first), that_far, got_that)
    got_x = lax.ppermute(over, "led", planes)
    over = sum_call(z_second_kernel, (2, rows, share - first), that_near, got_that, got_x)
    got_z_second = permute(over, across)
    over = sum_call(x_second_kernel, piece, this_far, got_this, got_z_first)
    got_x = lax.ppermute(over, "led", planes)

    def widen(value, before):
        after = share - before - value.shape[2]
        return jnp.pad(value.astype(jnp.float32), ((0, 0), (0, 0), (before, after)))

    base = lax.dynamic_slice_in_dim(spectrum, led_at * share, share, 2)
    base += this_near + got_this[0].astype(jnp.float32) + widen(got_z_first[0], 0)
    base, got_x = lax.optimization_barrier((base, got_x))
    base += got_x.astype(jnp.float32)
    base, got_z_second = lax.optimization_barrier((base, got_z_second))
    return base + widen(got_z_second, first)


def solution(mesh):
    placed = (P(None, "slab", None), P("led"), P("led"), P("led", "slab", None))
    fits = mesh.shape["slab"] == 8 and mesh.shape["led"] == 4

    def body(spectrum, led_rows, led_cols, images):
        shapes = (spectrum.shape, images.shape)
        if fits and shapes == ((2, 256, 2048), (2, 128, 1024)):
            return body_slabs(spectrum, led_rows, led_cols, images)
        return body_any(spectrum, led_rows, led_cols, images)

    return jax.shard_map(
        body, mesh=mesh, in_specs=placed, out_specs=P(None, "slab", "led"), check_vma=False
    )
```

```python
import functools

import jax
import jax.numpy as jnp
import numpy as np
from jax import lax
from jax.experimental import pallas as pl
from jax.experimental.pallas import tpu as pltpu
from jax.sharding import PartitionSpec as P

LANES = 128


def as_sent(value):
    return jax.tree.map(lambda a: a.astype(jnp.bfloat16) if a.dtype == jnp.float32 else a, value)


def host_tables(width):
    index = np.arange(width, dtype=np.int64)
    angle_index = (index[:, None] * index[None, :] % width).astype(np.float32)
    angle = angle_index * np.float32(2.0 * 3.141592653589793 / width)
    scale = np.float32(1.0) / np.sqrt(np.float32(width))
    return (
        (np.cos(angle) * scale).astype(jnp.bfloat16),
        (np.sin(angle) * scale).astype(jnp.bfloat16),
    )


def make_pupil(row_index, col_index, width):
    row_term = (2 * row_index + 1 - width) * (2 * row_index + 1 - width)
    col_term = (2 * col_index + 1 - width) * (2 * col_index + 1 - width)
    return (row_term[:, None] + col_term[None, :] < width * width).astype(jnp.float32)


def contract(form, left, right):
    return jnp.einsum(form, left, right, preferred_element_type=jnp.float32)


def take_rows(strip, start, width):
    return lax.dynamic_slice_in_dim(strip, start, width, 1)


def place_rows(block, start, total, axis_dim):
    shape = list(block.shape)
    shape[axis_dim] = total
    holder = jnp.zeros(tuple(shape), block.dtype)
    return lax.dynamic_update_slice_in_dim(holder, block, start, axis_dim)


def modulus_step(field_in_re, field_in_im, image, cos_table, sin_table):
    field_re = contract("lka,am->lkm", field_in_re, cos_table) + contract(
        "lka,am->lkm", field_in_im, sin_table
    )
    field_im = contract("lka,am->lkm", field_in_im, cos_table) - contract(
        "lka,am->lkm", field_in_re, sin_table
    )
    factor = jnp.sqrt(image) / jnp.sqrt(field_re * field_re + field_im * field_im + 0.25) - 1.0
    diff_re = (field_re * factor).astype(jnp.bfloat16)
    diff_im = (field_im * factor).astype(jnp.bfloat16)
    back_re = (
        contract("lkm,ma->lka", diff_re, cos_table) - contract("lkm,ma->lka", diff_im, sin_table)
    ).astype(jnp.bfloat16)
    back_im = (
        contract("lkm,ma->lka", diff_im, cos_table) + contract("lkm,ma->lka", diff_re, sin_table)
    ).astype(jnp.bfloat16)
    return (back_re, back_im)


def body_any(spectrum, led_rows, led_cols, images):
    width = images.shape[2]
    slab_rows = spectrum.shape[1]
    columns = spectrum.shape[2]
    slabs = lax.axis_size("slab")
    total_rows = slab_rows * slabs
    position = lax.axis_index("slab")
    cos_table, sin_table = (jnp.asarray(t) for t in host_tables(width))
    own_rows = position * slab_rows + jnp.arange(slab_rows, dtype=jnp.int32)
    col_index = jnp.arange(width, dtype=jnp.int32)

    def take_cols(start):
        return lax.dynamic_slice_in_dim(spectrum, start, width, 2)

    def owner_mask(start):
        return make_pupil(own_rows - start, col_index, width)

    windows = jax.vmap(take_cols)(led_cols)
    masks = jax.vmap(owner_mask)(led_rows)
    win_re = (windows[:, 0] * masks).astype(jnp.bfloat16)
    win_im = (windows[:, 1] * masks).astype(jnp.bfloat16)

    def slice_strip(block, start):
        return take_rows(block, start, width)

    row_re = (
        contract("lgb,bk->lkg", win_re, cos_table) + contract("lgb,bk->lkg", win_im, sin_table)
    ).astype(jnp.bfloat16)
    row_im = (
        contract("lgb,bk->lkg", win_im, cos_table) - contract("lgb,bk->lkg", win_re, sin_table)
    ).astype(jnp.bfloat16)
    col_re, col_im = (
        lax.all_to_all(row_re, "slab", split_axis=1, concat_axis=2, tiled=True),
        lax.all_to_all(row_im, "slab", split_axis=1, concat_axis=2, tiled=True),
    )
    field_in_re = jax.vmap(slice_strip)(col_re, led_rows)
    field_in_im = jax.vmap(slice_strip)(col_im, led_rows)
    back_re, back_im = modulus_step(field_in_re, field_in_im, images, cos_table, sin_table)

    def place_strip(block, start):
        return place_rows(block, start, total_rows, 1)

    full_re = jax.vmap(place_strip)(back_re, led_rows)
    full_im = jax.vmap(place_strip)(back_im, led_rows)
    home_re, home_im = (
        lax.all_to_all(as_sent(full_re), "slab", split_axis=2, concat_axis=1, tiled=True).astype(
            full_re.dtype
        ),
        lax.all_to_all(as_sent(full_im), "slab", split_axis=2, concat_axis=1, tiled=True).astype(
            full_im.dtype
        ),
    )
    upd_re = contract("lkg,kb->lgb", home_re, cos_table) - contract(
        "lkg,kb->lgb", home_im, sin_table
    )
    upd_im = contract("lkg,kb->lgb", home_im, cos_table) + contract(
        "lkg,kb->lgb", home_re, sin_table
    )
    upd_re = upd_re * masks
    upd_im = upd_im * masks

    def add_window(number, gradient):
        start = led_cols[number]
        piece = jnp.stack([upd_re[number], upd_im[number]])
        current = lax.dynamic_slice_in_dim(gradient, start, width, 2)
        return lax.dynamic_update_slice_in_dim(gradient, current + piece, start, 2)

    gradient = lax.fori_loop(
        0, led_rows.shape[0], add_window, jnp.zeros((2, slab_rows, columns), jnp.float32)
    )
    summed = lax.psum_scatter(gradient, "led", scatter_dimension=2, tiled=True)
    share = summed.shape[2]
    own_part = lax.dynamic_slice_in_dim(spectrum, lax.axis_index("led") * share, share, 2)
    return own_part + summed


SLABS = 8
HALF = 4
FIRST, LAST = 0, 7
PASSED = {1: 0, 6: 7}
INNER = (2, 3, 4, 5)


def dot(left, right):
    return jnp.dot(left, right, preferred_element_type=jnp.float32)


def window_mask(first_row, row_start, col_start, rows, first_col, cols, width):
    shape = (rows, cols)
    at_row = lax.broadcasted_iota(jnp.int32, shape, 0) + (first_row - row_start)
    at_col = lax.broadcasted_iota(jnp.int32, shape, 1) + (first_col - col_start)
    wraps = at_col < 0
    at_col = jnp.where(wraps, at_col + width, at_col)
    row_term = 2 * at_row + 1 - width
    col_term = 2 * at_col + 1 - width
    return row_term * row_term + col_term * col_term < width * width, wraps


def row_block(window, table):
    both = dot(window, table)
    half = both.shape[0] // 2
    row_re = both[:half, :LANES] + both[half:, LANES:]
    row_im = both[half:, :LANES] - both[:half, LANES:]
    return row_re.astype(jnp.bfloat16), row_im.astype(jnp.bfloat16)


def store_parts(out, values):
    per = out.shape[0] // 2
    rows = out.shape[1]
    for plane, value in enumerate(values):
        for led in range(per):
            out[plane * per + led] = value[led * rows : (led + 1) * rows]


def is_one_of(position, slabs):
    return functools.reduce(jnp.logical_or, [position == slab for slab in slabs])


def window_kernel(starts, spectrum, window):
    position = lax.axis_index("slab")
    leds = starts.shape[0] // 2
    rows = spectrum.shape[1]
    width = window.shape[1]
    for led in range(leds):
        inside, wraps = window_mask(
            position * rows, starts[led], starts[leds + led], rows, 0, width, width
        )
        for plane in range(2):
            value = jnp.where(wraps, spectrum[plane, :, width:], spectrum[plane, :, :width])
            at = (plane * leds + led) * rows
            window[at : at + rows, :] = jnp.where(inside, value, 0.0).astype(jnp.bfloat16)


def classes_of(position):
    hands_over = is_one_of(position, PASSED)
    return (jnp.where(hands_over, 5, 6), 7, 3, 4, jnp.where(hands_over, 6, 5), 0, 1, 2)


def rows_kernel(which, window, table, *outs):
    position = lax.axis_index("slab")
    for out, d in zip(outs, classes_of(position)[which]):
        store_parts(out, row_block(window[...], table[jnp.bitwise_xor(position, d)]))


def choose_kernel(got, own, out):
    passes = is_one_of(lax.axis_index("slab"), PASSED.values())

    @pl.when(passes)
    def _():
        out[...] = got[...]

    @pl.when(jnp.logical_not(passes))
    def _():
        out[...] = own[...]


def amplitude_kernel(images, table, out, table_out):
    leds, block, width = images.shape
    for led in range(leds):
        for j in range(width // LANES):
            piece = jnp.sqrt(images[led, :, j * LANES : (j + 1) * LANES])
            out[j * LANES : (j + 1) * LANES, led * block : (led + 1) * block] = piece.T
    table_out[...] = table[...]


def field_kernel(amplitude, table, *rest):
    far, near = rest[:5], rest[5 : HALF + 5]
    outs = rest[HALF + 5 : 2 * HALF + 5]
    field_in, diff, strips = rest[2 * HALF + 5 :]
    position = lax.axis_index("slab")
    parts, rows, _ = near[0].shape
    half = parts // 2 * LANES
    width = field_in.shape[0]
    steps = width // LANES
    group = 4
    for d, block in enumerate(near):
        at = pl.multiple_of(jnp.bitwise_and(jnp.bitwise_xor(position, d), HALF - 1) * rows, rows)
        for part in range(parts):
            cols = slice(part * LANES, (part + 1) * LANES)
            field_in[pl.ds(at, rows), cols] = block[part]

    def add(block, origin):
        at = pl.multiple_of(jnp.bitwise_and(origin, HALF - 1) * rows, rows)
        for part in range(parts):
            cols = slice(part * LANES, (part + 1) * LANES)
            field_in[pl.ds(at, rows), cols] += block[part]

    passes = is_one_of(position, PASSED.values())
    hands_over = is_one_of(position, PASSED)
    ends = is_one_of(position, [to ^ 4 for to in PASSED.values()])

    @pl.when(is_one_of(position, INNER))
    def _():
        add(far[0], jnp.bitwise_xor(position, 6))
        add(far[1], jnp.bitwise_xor(position, 7))
        add(far[2], jnp.bitwise_xor(position, jnp.where(ends, 5, 4)))

    @pl.when(jnp.logical_or(passes, hands_over))
    def _():
        add(far[2], jnp.bitwise_xor(position, 4))
        add(far[3], jnp.bitwise_xor(position, jnp.where(hands_over, 7, 6)))
        add(far[4], jnp.bitwise_xor(position, 5))

    for first in range(0, steps, group):
        product = dot(
            table[first : first + group].reshape(group * 2 * LANES, width), field_in[...]
        )
        for j in range(first, first + group):
            both = product[(j - first) * 2 * LANES : (j - first + 1) * 2 * LANES]
            field_re = both[:LANES, :half] + both[LANES:, half:]
            field_im = both[:LANES, half:] - both[LANES:, :half]
            here = pl.ds(j * LANES, LANES)
            factor = (
                amplitude[here, :] * lax.rsqrt(field_re * field_re + field_im * field_im + 0.25)
                - 1.0
            )
            diff[here, :half] = (field_re * factor).astype(jnp.bfloat16)
            diff[here, half:] = (field_im * factor).astype(jnp.bfloat16)
    pieces = rows // LANES
    for i in range(HALF):
        product = dot(
            table[i * pieces : (i + 1) * pieces].reshape(pieces * 2 * LANES, width), diff[...]
        )
        for h in range(pieces):
            both = product[h * 2 * LANES : (h + 1) * 2 * LANES]
            here = pl.ds(h * LANES, LANES)
            back_re = (both[:LANES, :half] - both[LANES:, half:]).astype(jnp.bfloat16)
            back_im = (both[:LANES, half:] + both[LANES:, :half]).astype(jnp.bfloat16)
            for part in range(parts // 2):
                cols = slice(part * LANES, (part + 1) * LANES)
                strips[i, part, here, :] = back_re[:, cols]
                strips[i, parts // 2 + part, here, :] = back_im[:, cols]
    for d, out in enumerate(outs):
        out[...] = strips[jnp.bitwise_and(jnp.bitwise_xor(position, d), HALF - 1)]


def update_columns(own_core, starts, table, back, outs):
    position = lax.axis_index("slab")
    led_at = lax.axis_index("led")
    core = jnp.bitwise_and(led_at, 1)
    plane_x = jnp.right_shift(led_at, 1)
    which_half = jnp.right_shift(position, 2)
    first_row = jnp.bitwise_and(position, HALF - 1)
    leds = starts.shape[0] // 2
    rows = back.shape[0] // (2 * leds)
    depth = back.shape[1]
    width = table.shape[1]
    group = width // LANES // 2
    owner = core if own_core else 1 - core
    shape = (rows, LANES)
    for n in range(group):
        block = owner * group + n
        both = dot(
            back[...], table[block, pl.ds(pl.multiple_of(which_half * depth, depth), depth)]
        )
        half = leds * rows
        update = (
            both[:half, :LANES] - both[half:, LANES:],
            both[half:, :LANES] + both[:half, LANES:],
        )
        sums = [[0.0, 0.0] for _ in outs]
        for led in range(leds):
            at_row = lax.broadcasted_iota(jnp.int32, shape, 0) + (
                first_row * rows - starts[led]
            )
            at_col = lax.broadcasted_iota(jnp.int32, shape, 1) + (
                block * LANES - starts[leds + led]
            )
            row_term = 2 * jnp.where(at_row < 0, at_row + width, at_row) + 1 - width
            col_term = 2 * jnp.where(at_col < 0, at_col + width, at_col) + 1 - width
            inside = row_term * row_term + col_term * col_term < width * width
            this_slab = jnp.where(at_row < 0, 1, 0) == which_half
            this_x = jnp.where(at_col < 0, 1, 0) == plane_x
            for plane in range(2):
                piece = jnp.where(inside, update[plane][led * rows : (led + 1) * rows], 0.0)
                for i, at_slab in enumerate(
                    (jnp.where(this_slab, piece, 0.0), jnp.where(this_slab, 0.0, piece))
                ):
                    sums[2 * i][plane] += jnp.where(this_x, at_slab, 0.0)
                    sums[2 * i + 1][plane] += jnp.where(this_x, 0.0, at_slab)
        cols = slice(n * LANES, (n + 1) * LANES)
        for out, both_planes in zip(outs, sums):
            for plane in range(2):
                out[plane, :, cols] = both_planes[plane].astype(out.dtype)


def sent_kernel(starts, table, *rest):
    blocks = rest[:HALF]
    this_slab, that_slab, back = rest[HALF:]
    position = lax.axis_index("slab")
    parts, rows, _ = blocks[0].shape
    for d, block in enumerate(blocks):
        source = jnp.bitwise_and(jnp.bitwise_xor(position, d), HALF - 1)
        at = pl.multiple_of(source * LANES, LANES)
        for part in range(parts):
            back[part * rows : (part + 1) * rows, pl.ds(at, LANES)] = block[part]
    outs = [out.at[i] for out in (this_slab, that_slab) for i in range(2)]
    update_columns(False, starts, table, back, outs)


def kept_kernel(starts, table, back, *outs):
    update_columns(True, starts, table, back, outs)


def z_first_kernel(that_near, that_far, got_that, out):
    cols = out.shape[3]
    for i, kept in enumerate((that_near, that_far)):
        total = kept[:, :, :cols] + got_that[i, :, :, :cols].astype(jnp.float32)
        out[i] = total.astype(out.dtype)


def x_first_kernel(that_far, got_that, out):
    cols = that_far.shape[2] - out.shape[2]
    total = that_far[:, :, cols:] + got_that[1, :, :, cols:].astype(jnp.float32)
    out[...] = total.astype(out.dtype)


def z_second_kernel(that_near, got_that, got_x, out):
    cols = that_near.shape[2] - out.shape[2]
    total = that_near[:, :, cols:] + got_that[0, :, :, cols:].astype(jnp.float32)
    out[...] = (total + got_x[...].astype(jnp.float32)).astype(out.dtype)


def x_second_kernel(this_far, got_this, got_z, out):
    cols = got_z.shape[3]
    total = this_far[...] + got_this[1].astype(jnp.float32)
    out[:, :, cols:] = total[:, :, cols:].astype(out.dtype)
    out[:, :, :cols] = (total[:, :, :cols] + got_z[1].astype(jnp.float32)).astype(out.dtype)


def local_call(kernel, out_shape, spaces, scratch, flops, moved, name, limit=32):
    return pl.pallas_call(
        kernel,
        out_shape=out_shape,
        in_specs=[pl.BlockSpec(memory_space=space) for space in spaces],
        out_specs=jax.tree.map(lambda _: pl.BlockSpec(memory_space=pltpu.VMEM), out_shape),
        scratch_shapes=scratch,
        compiler_params=pltpu.CompilerParams(vmem_limit_bytes=limit * 2**20),
        cost_estimate=pl.CostEstimate(flops=flops, bytes_accessed=moved, transcendentals=0),
        name=name,
    )


def body_slabs(spectrum, led_rows, led_cols, images):
    leds, block, width = images.shape
    rows = spectrum.shape[1]
    led_at = lax.axis_index("led")
    bf16 = jnp.bfloat16
    vmem, smem = pltpu.VMEM, pltpu.SMEM
    cos_table, sin_table = host_tables(width)
    steps = width // LANES
    by_col = np.stack(
        [
            np.concatenate([t[:, j * LANES : (j + 1) * LANES] for t in (cos_table, sin_table)], 1)
            for j in range(steps)
        ]
    )
    by_row = jnp.asarray(np.ascontiguousarray(by_col.transpose(0, 2, 1)))
    by_col = jnp.asarray(by_col)
    parts = 2 * leds
    sent_block = jax.ShapeDtypeStruct((parts, rows, LANES), bf16)
    flops = 8 * leds * rows * width * width

    starts = jnp.concatenate([led_rows, led_cols]).astype(jnp.int32)
    window = local_call(
        window_kernel,
        jax.ShapeDtypeStruct((parts * rows, width), bf16),
        [smem, vmem],
        [],
        0,
        6 * 2**20,
        "windows",
    )(starts, spectrum)

    def rows_call(which, name):
        count = which.stop - which.start
        return local_call(
            functools.partial(rows_kernel, which),
            [sent_block] * count,
            [vmem, vmem],
            [],
            flops * count // SLABS,
            5 * 2**20,
            name,
        )(window, by_col)

    first_a, first_b, near_3 = rows_call(slice(0, 3), "rows_round_1")

    def permute(sent, pairs):
        return lax.ppermute(sent, "slab", pairs)

    def choose(got, own, name):
        return local_call(
            choose_kernel, sent_block, [vmem] * 2, [], 0, 2**19, name
        )(got, own)

    handed = list(PASSED.items())
    windowed = range(FIRST + 1, LAST)
    got_a = permute(first_a, [(s, s ^ 6) for s in INNER] + handed)
    got_b = permute(first_b, [(s, s ^ 7) for s in INNER] + handed)
    near_3 = permute(near_3, [(s, s ^ 3) for s in windowed])
    second_a, second_b, near_0, near_1, near_2 = rows_call(slice(3, SLABS), "rows_round_2")
    got_a, second_a, second_b, near_1, near_2, images = lax.optimization_barrier(
        (got_a, second_a, second_b, near_1, near_2, images)
    )
    outer_pairs = [(s, s ^ 6) for s in range(SLABS) if s not in INNER]
    near_1 = permute(near_1, [(s, s ^ 1) for s in windowed])
    near_2 = permute(near_2, [(s, s ^ 2) for s in windowed])
    near_1, near_3, got_b = lax.optimization_barrier((near_1, near_3, got_b))
    far_columns = [
        got_a,
        got_b,
        permute(choose(got_a, second_a, "class_4_blocks"), [(s, s ^ 4) for s in range(SLABS)]),
        permute(choose(got_b, second_b, "class_6_blocks"), outer_pairs),
        permute(second_b, [(s, s ^ 5) for s in INNER]),
    ]
    near_columns = [near_0, near_1, near_2, near_3]
    amplitude, by_row = local_call(
        amplitude_kernel,
        [
            jax.ShapeDtypeStruct((width, leds * block), jnp.float32),
            jax.ShapeDtypeStruct(by_row.shape, bf16),
        ],
        [vmem] * 2,
        [],
        0,
        10 * 2**20,
        "amplitude",
    )(images, by_row)
    strips = local_call(
        field_kernel,
        [sent_block] * HALF,
        [vmem] * 11,
        [pltpu.VMEM((width, parts * block), bf16)] * 2
        + [pltpu.VMEM((HALF,) + sent_block.shape, bf16)],
        16 * leds * block * width * width,
        12 * 2**20,
        "modulus_step",
    )(amplitude, by_row, *far_columns, *near_columns)

    def send_home(d):
        pairs = [(s, (s + d) % SLABS) for s in range(SLABS) if FIRST < (s + d) % SLABS < LAST]
        return permute(strips[d % HALF], pairs)

    home = [strips[0]]
    home += [
        permute(strips[d], [(s, s ^ d) for s in range(SLABS)]) for d in range(1, HALF)
    ]
    share = width // 2
    first = share // 4
    piece = (2, rows, share)
    cores = [(0, 1), (1, 0), (2, 3), (3, 2)]
    planes = [(0, 2), (2, 0), (1, 3), (3, 1)]
    across = [(s, s ^ 4) for s in range(SLABS) if FIRST < s ^ 4 < LAST]
    sent_this, sent_that, back = local_call(
        sent_kernel,
        [
            jax.ShapeDtypeStruct((2,) + piece, bf16),
            jax.ShapeDtypeStruct((2,) + piece, bf16),
            jax.ShapeDtypeStruct((parts * rows, HALF * LANES), bf16),
        ],
        [smem] + [vmem] * (1 + HALF),
        [],
        flops // 4,
        8 * 2**20,
        "update_sent",
        16,
    )(starts, by_col, *home)
    got_that = lax.ppermute(sent_that, "led", cores)
    got_this = lax.ppermute(sent_this, "led", cores)
    this_near, this_far, that_near, that_far = local_call(
        kept_kernel,
        [jax.ShapeDtypeStruct(piece, jnp.float32)] * 4,
        [smem, vmem, vmem],
        [],
        flops // 4,
        10 * 2**20,
        "update_kept",
        16,
    )(starts, by_col, back)

    def sum_call(kernel, shape, *values):
        out_shape = jax.ShapeDtypeStruct(shape, bf16)
        specs = [vmem] * len(values)
        return local_call(kernel, out_shape, specs, [], 0, 2**20, kernel.__name__, 12)(*values)

    over = sum_call(z_first_kernel, (2, 2, rows, first), that_near, that_far, got_that)
    got_z_first = permute(over, across)
    over = sum_call(x_first_kernel, (2, rows, share - first), that_far, got_that)
    got_x = lax.ppermute(over, "led", planes)
    over = sum_call(z_second_kernel, (2, rows, share - first), that_near, got_that, got_x)
    got_z_second = permute(over, across)
    over = sum_call(x_second_kernel, piece, this_far, got_this, got_z_first)
    got_x = lax.ppermute(over, "led", planes)

    def widen(value, before):
        after = share - before - value.shape[2]
        return jnp.pad(value.astype(jnp.float32), ((0, 0), (0, 0), (before, after)))

    base = lax.dynamic_slice_in_dim(spectrum, led_at * share, share, 2)
    base += this_near + got_this[0].astype(jnp.float32) + widen(got_z_first[0], 0)
    base, got_x = lax.optimization_barrier((base, got_x))
    base += got_x.astype(jnp.float32)
    base, got_z_second = lax.optimization_barrier((base, got_z_second))
    return base + widen(got_z_second, first)


def solution(mesh):
    placed = (P(None, "slab", None), P("led"), P("led"), P("led", "slab", None))
    fits = mesh.shape["slab"] == 8 and mesh.shape["led"] == 4

    def body(spectrum, led_rows, led_cols, images):
        shapes = (spectrum.shape, images.shape)
        if fits and shapes == ((2, 256, 2048), (2, 128, 1024)):
            return body_slabs(spectrum, led_rows, led_cols, images)
        return body_any(spectrum, led_rows, led_cols, images)

    return jax.shard_map(
        body, mesh=mesh, in_specs=placed, out_specs=P(None, "slab", "led"), check_vma=False
    )
```

```python
import functools

import jax
import jax.numpy as jnp
import numpy as np
from jax import lax
from jax.experimental import pallas as pl
from jax.experimental.pallas import tpu as pltpu
from jax.sharding import PartitionSpec as P

LANES = 128


def as_sent(value):
    return jax.tree.map(lambda a: a.astype(jnp.bfloat16) if a.dtype == jnp.float32 else a, value)


def host_tables(width):
    index = np.arange(width, dtype=np.int64)
    angle_index = (index[:, None] * index[None, :] % width).astype(np.float32)
    angle = angle_index * np.float32(2.0 * 3.141592653589793 / width)
    scale = np.float32(1.0) / np.sqrt(np.float32(width))
    return (
        (np.cos(angle) * scale).astype(jnp.bfloat16),
        (np.sin(angle) * scale).astype(jnp.bfloat16),
    )


def make_pupil(row_index, col_index, width):
    row_term = (2 * row_index + 1 - width) * (2 * row_index + 1 - width)
    col_term = (2 * col_index + 1 - width) * (2 * col_index + 1 - width)
    return (row_term[:, None] + col_term[None, :] < width * width).astype(jnp.float32)


def contract(form, left, right):
    return jnp.einsum(form, left, right, preferred_element_type=jnp.float32)


def take_rows(strip, start, width):
    return lax.dynamic_slice_in_dim(strip, start, width, 1)


def place_rows(block, start, total, axis_dim):
    shape = list(block.shape)
    shape[axis_dim] = total
    holder = jnp.zeros(tuple(shape), block.dtype)
    return lax.dynamic_update_slice_in_dim(holder, block, start, axis_dim)


def modulus_step(field_in_re, field_in_im, image, cos_table, sin_table):
    field_re = contract("lka,am->lkm", field_in_re, cos_table) + contract(
        "lka,am->lkm", field_in_im, sin_table
    )
    field_im = contract("lka,am->lkm", field_in_im, cos_table) - contract(
        "lka,am->lkm", field_in_re, sin_table
    )
    factor = jnp.sqrt(image) / jnp.sqrt(field_re * field_re + field_im * field_im + 0.25) - 1.0
    diff_re = (field_re * factor).astype(jnp.bfloat16)
    diff_im = (field_im * factor).astype(jnp.bfloat16)
    back_re = (
        contract("lkm,ma->lka", diff_re, cos_table) - contract("lkm,ma->lka", diff_im, sin_table)
    ).astype(jnp.bfloat16)
    back_im = (
        contract("lkm,ma->lka", diff_im, cos_table) + contract("lkm,ma->lka", diff_re, sin_table)
    ).astype(jnp.bfloat16)
    return (back_re, back_im)


def body_any(spectrum, led_rows, led_cols, images):
    width = images.shape[2]
    slab_rows = spectrum.shape[1]
    columns = spectrum.shape[2]
    slabs = lax.axis_size("slab")
    total_rows = slab_rows * slabs
    position = lax.axis_index("slab")
    cos_table, sin_table = (jnp.asarray(t) for t in host_tables(width))
    own_rows = position * slab_rows + jnp.arange(slab_rows, dtype=jnp.int32)
    col_index = jnp.arange(width, dtype=jnp.int32)

    def take_cols(start):
        return lax.dynamic_slice_in_dim(spectrum, start, width, 2)

    def owner_mask(start):
        return make_pupil(own_rows - start, col_index, width)

    windows = jax.vmap(take_cols)(led_cols)
    masks = jax.vmap(owner_mask)(led_rows)
    win_re = (windows[:, 0] * masks).astype(jnp.bfloat16)
    win_im = (windows[:, 1] * masks).astype(jnp.bfloat16)

    def slice_strip(block, start):
        return take_rows(block, start, width)

    row_re = (
        contract("lgb,bk->lkg", win_re, cos_table) + contract("lgb,bk->lkg", win_im, sin_table)
    ).astype(jnp.bfloat16)
    row_im = (
        contract("lgb,bk->lkg", win_im, cos_table) - contract("lgb,bk->lkg", win_re, sin_table)
    ).astype(jnp.bfloat16)
    col_re, col_im = (
        lax.all_to_all(row_re, "slab", split_axis=1, concat_axis=2, tiled=True),
        lax.all_to_all(row_im, "slab", split_axis=1, concat_axis=2, tiled=True),
    )
    field_in_re = jax.vmap(slice_strip)(col_re, led_rows)
    field_in_im = jax.vmap(slice_strip)(col_im, led_rows)
    back_re, back_im = modulus_step(field_in_re, field_in_im, images, cos_table, sin_table)

    def place_strip(block, start):
        return place_rows(block, start, total_rows, 1)

    full_re = jax.vmap(place_strip)(back_re, led_rows)
    full_im = jax.vmap(place_strip)(back_im, led_rows)
    home_re, home_im = (
        lax.all_to_all(as_sent(full_re), "slab", split_axis=2, concat_axis=1, tiled=True).astype(
            full_re.dtype
        ),
        lax.all_to_all(as_sent(full_im), "slab", split_axis=2, concat_axis=1, tiled=True).astype(
            full_im.dtype
        ),
    )
    upd_re = contract("lkg,kb->lgb", home_re, cos_table) - contract(
        "lkg,kb->lgb", home_im, sin_table
    )
    upd_im = contract("lkg,kb->lgb", home_im, cos_table) + contract(
        "lkg,kb->lgb", home_re, sin_table
    )
    upd_re = upd_re * masks
    upd_im = upd_im * masks

    def add_window(number, gradient):
        start = led_cols[number]
        piece = jnp.stack([upd_re[number], upd_im[number]])
        current = lax.dynamic_slice_in_dim(gradient, start, width, 2)
        return lax.dynamic_update_slice_in_dim(gradient, current + piece, start, 2)

    gradient = lax.fori_loop(
        0, led_rows.shape[0], add_window, jnp.zeros((2, slab_rows, columns), jnp.float32)
    )
    summed = lax.psum_scatter(gradient, "led", scatter_dimension=2, tiled=True)
    share = summed.shape[2]
    own_part = lax.dynamic_slice_in_dim(spectrum, lax.axis_index("led") * share, share, 2)
    return own_part + summed


SLABS = 8
HALF = 4
FIRST, LAST = 0, 7
PASSED = {1: 0, 6: 7}
INNER = (2, 3, 4, 5)


def dot(left, right):
    return jnp.dot(left, right, preferred_element_type=jnp.float32)


def window_mask(first_row, row_start, col_start, rows, first_col, cols, width):
    shape = (rows, cols)
    at_row = lax.broadcasted_iota(jnp.int32, shape, 0) + (first_row - row_start)
    at_col = lax.broadcasted_iota(jnp.int32, shape, 1) + (first_col - col_start)
    wraps = at_col < 0
    at_col = jnp.where(wraps, at_col + width, at_col)
    row_term = 2 * at_row + 1 - width
    col_term = 2 * at_col + 1 - width
    return row_term * row_term + col_term * col_term < width * width, wraps


def row_block(window, table):
    both = dot(window, table)
    half = both.shape[0] // 2
    row_re = both[:half, :LANES] + both[half:, LANES:]
    row_im = both[half:, :LANES] - both[:half, LANES:]
    return row_re.astype(jnp.bfloat16), row_im.astype(jnp.bfloat16)


def store_parts(out, values):
    per = out.shape[0] // 2
    rows = out.shape[1]
    for plane, value in enumerate(values):
        for led in range(per):
            out[plane * per + led] = value[led * rows : (led + 1) * rows]


def is_one_of(position, slabs):
    return functools.reduce(jnp.logical_or, [position == slab for slab in slabs])


def window_kernel(starts, spectrum, window):
    position = lax.axis_index("slab")
    leds = starts.shape[0] // 2
    rows = spectrum.shape[1]
    width = window.shape[1]
    for led in range(leds):
        inside, wraps = window_mask(
            position * rows, starts[led], starts[leds + led], rows, 0, width, width
        )
        for plane in range(2):
            value = jnp.where(wraps, spectrum[plane, :, width:], spectrum[plane, :, :width])
            at = (plane * leds + led) * rows
            window[at : at + rows, :] = jnp.where(inside, value, 0.0).astype(jnp.bfloat16)


def classes_of(position):
    hands_over = is_one_of(position, PASSED)
    return (jnp.where(hands_over, 5, 6), 7, 2, 4, jnp.where(hands_over, 6, 5), 0, 1, 3)


def rows_kernel(which, window, table, *outs):
    position = lax.axis_index("slab")
    for out, d in zip(outs, classes_of(position)[which]):
        store_parts(out, row_block(window[...], table[jnp.bitwise_xor(position, d)]))


def choose_kernel(got, own, out):
    passes = is_one_of(lax.axis_index("slab"), PASSED.values())

    @pl.when(passes)
    def _():
        out[...] = got[...]

    @pl.when(jnp.logical_not(passes))
    def _():
        out[...] = own[...]


def amplitude_kernel(images, table, out, table_out):
    leds, block, width = images.shape
    for led in range(leds):
        for j in range(width // LANES):
            piece = jnp.sqrt(images[led, :, j * LANES : (j + 1) * LANES])
            out[j * LANES : (j + 1) * LANES, led * block : (led + 1) * block] = piece.T
    table_out[...] = table[...]


def field_kernel(amplitude, table, *rest):
    far, near = rest[:5], rest[5 : HALF + 5]
    outs = rest[HALF + 5 : 2 * HALF + 5]
    field_in, diff, strips = rest[2 * HALF + 5 :]
    position = lax.axis_index("slab")
    parts, rows, _ = near[0].shape
    half = parts // 2 * LANES
    width = field_in.shape[0]
    steps = width // LANES
    group = 4
    for d, block in enumerate(near):
        at = pl.multiple_of(jnp.bitwise_and(jnp.bitwise_xor(position, d), HALF - 1) * rows, rows)
        for part in range(parts):
            cols = slice(part * LANES, (part + 1) * LANES)
            field_in[pl.ds(at, rows), cols] = block[part]

    def add(block, origin):
        at = pl.multiple_of(jnp.bitwise_and(origin, HALF - 1) * rows, rows)
        for part in range(parts):
            cols = slice(part * LANES, (part + 1) * LANES)
            field_in[pl.ds(at, rows), cols] += block[part]

    passes = is_one_of(position, PASSED.values())
    hands_over = is_one_of(position, PASSED)
    ends = is_one_of(position, [to ^ 4 for to in PASSED.values()])

    @pl.when(is_one_of(position, INNER))
    def _():
        add(far[0], jnp.bitwise_xor(position, 6))
        add(far[1], jnp.bitwise_xor(position, 7))
        add(far[2], jnp.bitwise_xor(position, jnp.where(ends, 5, 4)))

    @pl.when(jnp.logical_or(passes, hands_over))
    def _():
        add(far[2], jnp.bitwise_xor(position, 4))
        add(far[3], jnp.bitwise_xor(position, jnp.where(hands_over, 7, 6)))
        add(far[4], jnp.bitwise_xor(position, 5))

    for first in range(0, steps, group):
        product = dot(
            table[first : first + group].reshape(group * 2 * LANES, width), field_in[...]
        )
        for j in range(first, first + group):
            both = product[(j - first) * 2 * LANES : (j - first + 1) * 2 * LANES]
            field_re = both[:LANES, :half] + both[LANES:, half:]
            field_im = both[:LANES, half:] - both[LANES:, :half]
            here = pl.ds(j * LANES, LANES)
            factor = (
                amplitude[here, :] * lax.rsqrt(field_re * field_re + field_im * field_im + 0.25)
                - 1.0
            )
            diff[here, :half] = (field_re * factor).astype(jnp.bfloat16)
            diff[here, half:] = (field_im * factor).astype(jnp.bfloat16)
    pieces = rows // LANES
    for i in range(HALF):
        product = dot(
            table[i * pieces : (i + 1) * pieces].reshape(pieces * 2 * LANES, width), diff[...]
        )
        for h in range(pieces):
            both = product[h * 2 * LANES : (h + 1) * 2 * LANES]
            here = pl.ds(h * LANES, LANES)
            back_re = (both[:LANES, :half] - both[LANES:, half:]).astype(jnp.bfloat16)
            back_im = (both[:LANES, half:] + both[LANES:, :half]).astype(jnp.bfloat16)
            for part in range(parts // 2):
                cols = slice(part * LANES, (part + 1) * LANES)
                strips[i, part, here, :] = back_re[:, cols]
                strips[i, parts // 2 + part, here, :] = back_im[:, cols]
    for d, out in enumerate(outs):
        out[...] = strips[jnp.bitwise_and(jnp.bitwise_xor(position, d), HALF - 1)]


def update_columns(own_core, starts, table, back, outs):
    position = lax.axis_index("slab")
    led_at = lax.axis_index("led")
    core = jnp.bitwise_and(led_at, 1)
    plane_x = jnp.right_shift(led_at, 1)
    which_half = jnp.right_shift(position, 2)
    first_row = jnp.bitwise_and(position, HALF - 1)
    leds = starts.shape[0] // 2
    rows = back.shape[0] // (2 * leds)
    depth = back.shape[1]
    width = table.shape[1]
    group = width // LANES // 2
    owner = core if own_core else 1 - core
    shape = (rows, LANES)
    for n in range(group):
        block = owner * group + n
        both = dot(
            back[...], table[block, pl.ds(pl.multiple_of(which_half * depth, depth), depth)]
        )
        half = leds * rows
        update = (
            both[:half, :LANES] - both[half:, LANES:],
            both[half:, :LANES] + both[:half, LANES:],
        )
        sums = [[0.0, 0.0] for _ in outs]
        for led in range(leds):
            at_row = lax.broadcasted_iota(jnp.int32, shape, 0) + (
                first_row * rows - starts[led]
            )
            at_col = lax.broadcasted_iota(jnp.int32, shape, 1) + (
                block * LANES - starts[leds + led]
            )
            row_term = 2 * jnp.where(at_row < 0, at_row + width, at_row) + 1 - width
            col_term = 2 * jnp.where(at_col < 0, at_col + width, at_col) + 1 - width
            inside = row_term * row_term + col_term * col_term < width * width
            this_slab = jnp.where(at_row < 0, 1, 0) == which_half
            this_x = jnp.where(at_col < 0, 1, 0) == plane_x
            for plane in range(2):
                piece = jnp.where(inside, update[plane][led * rows : (led + 1) * rows], 0.0)
                for i, at_slab in enumerate(
                    (jnp.where(this_slab, piece, 0.0), jnp.where(this_slab, 0.0, piece))
                ):
                    sums[2 * i][plane] += jnp.where(this_x, at_slab, 0.0)
                    sums[2 * i + 1][plane] += jnp.where(this_x, 0.0, at_slab)
        cols = slice(n * LANES, (n + 1) * LANES)
        for out, both_planes in zip(outs, sums):
            for plane in range(2):
                out[plane, :, cols] = both_planes[plane].astype(out.dtype)


def sent_kernel(starts, table, *rest):
    blocks = rest[:HALF]
    this_slab, that_slab, back = rest[HALF:]
    position = lax.axis_index("slab")
    parts, rows, _ = blocks[0].shape
    for d, block in enumerate(blocks):
        source = jnp.bitwise_and(jnp.bitwise_xor(position, d), HALF - 1)
        at = pl.multiple_of(source * LANES, LANES)
        for part in range(parts):
            back[part * rows : (part + 1) * rows, pl.ds(at, LANES)] = block[part]
    outs = [out.at[i] for out in (this_slab, that_slab) for i in range(2)]
    update_columns(False, starts, table, back, outs)


def kept_kernel(starts, table, back, *outs):
    update_columns(True, starts, table, back, outs)


def first_kernel(that_near, that_far, got_that, z_out, x_out):
    cols = z_out.shape[3]
    near = that_near[:, :, :cols] + got_that[0, :, :, :cols].astype(jnp.float32)
    far = that_far[...] + got_that[1].astype(jnp.float32)
    z_out[0] = near.astype(z_out.dtype)
    z_out[1] = far[:, :, :cols].astype(z_out.dtype)
    x_out[...] = far[:, :, cols:].astype(x_out.dtype)


def z_second_kernel(that_near, got_that, got_x, out):
    cols = that_near.shape[2] - out.shape[2]
    total = that_near[:, :, cols:] + got_that[0, :, :, cols:].astype(jnp.float32)
    out[...] = (total + got_x[...].astype(jnp.float32)).astype(out.dtype)


def x_own_kernel(this_far, got_this, out):
    cols = this_far.shape[2] - out.shape[2]
    total = this_far[:, :, cols:] + got_this[1, :, :, cols:].astype(jnp.float32)
    out[...] = total.astype(out.dtype)


def x_last_kernel(this_far, got_this, got_z, out):
    cols = out.shape[2]
    total = this_far[:, :, :cols] + got_this[1, :, :, :cols].astype(jnp.float32)
    out[...] = (total + got_z[1].astype(jnp.float32)).astype(out.dtype)


def local_call(kernel, out_shape, spaces, scratch, flops, moved, name, limit=32):
    return pl.pallas_call(
        kernel,
        out_shape=out_shape,
        in_specs=[pl.BlockSpec(memory_space=space) for space in spaces],
        out_specs=jax.tree.map(lambda _: pl.BlockSpec(memory_space=pltpu.VMEM), out_shape),
        scratch_shapes=scratch,
        compiler_params=pltpu.CompilerParams(vmem_limit_bytes=limit * 2**20),
        cost_estimate=pl.CostEstimate(flops=flops, bytes_accessed=moved, transcendentals=0),
        name=name,
    )


def body_slabs(spectrum, led_rows, led_cols, images):
    leds, block, width = images.shape
    rows = spectrum.shape[1]
    led_at = lax.axis_index("led")
    bf16 = jnp.bfloat16
    vmem, smem = pltpu.VMEM, pltpu.SMEM
    cos_table, sin_table = host_tables(width)
    steps = width // LANES
    by_col = np.stack(
        [
            np.concatenate([t[:, j * LANES : (j + 1) * LANES] for t in (cos_table, sin_table)], 1)
            for j in range(steps)
        ]
    )
    by_row = jnp.asarray(np.ascontiguousarray(by_col.transpose(0, 2, 1)))
    by_col = jnp.asarray(by_col)
    parts = 2 * leds
    sent_block = jax.ShapeDtypeStruct((parts, rows, LANES), bf16)
    flops = 8 * leds * rows * width * width

    starts = jnp.concatenate([led_rows, led_cols]).astype(jnp.int32)
    window = local_call(
        window_kernel,
        jax.ShapeDtypeStruct((parts * rows, width), bf16),
        [smem, vmem],
        [],
        0,
        6 * 2**20,
        "windows",
    )(starts, spectrum)

    def rows_call(which, name):
        count = which.stop - which.start
        return local_call(
            functools.partial(rows_kernel, which),
            [sent_block] * count,
            [vmem, vmem],
            [],
            flops * count // SLABS,
            5 * 2**20,
            name,
        )(window, by_col)

    first_a, first_b, near_2 = rows_call(slice(0, 3), "rows_round_1")

    def permute(sent, pairs):
        return lax.ppermute(sent, "slab", pairs)

    def choose(got, own, name):
        return local_call(
            choose_kernel, sent_block, [vmem] * 2, [], 0, 2**19, name
        )(got, own)

    handed = list(PASSED.items())
    windowed = range(FIRST + 1, LAST)
    got_a = permute(first_a, [(s, s ^ 6) for s in INNER] + handed)
    got_b = permute(first_b, [(s, s ^ 7) for s in INNER] + handed)
    near_2 = permute(near_2, [(s, s ^ 2) for s in windowed])
    second_a, second_b, near_0, near_1, near_3 = rows_call(slice(3, SLABS), "rows_round_2")
    got_a, near_2, second_a, second_b, near_1, near_3, images = lax.optimization_barrier(
        (got_a, near_2, second_a, second_b, near_1, near_3, images)
    )
    outer_pairs = [(s, s ^ 6) for s in range(SLABS) if s not in INNER]
    near_1 = permute(near_1, [(s, s ^ 1) for s in windowed])
    near_3 = permute(near_3, [(s, s ^ 3) for s in windowed])
    near_1, got_b = lax.optimization_barrier((near_1, got_b))
    far_columns = [
        got_a,
        got_b,
        permute(choose(got_a, second_a, "class_4_blocks"), [(s, s ^ 4) for s in range(SLABS)]),
        permute(choose(got_b, second_b, "class_6_blocks"), outer_pairs),
        permute(second_b, [(s, s ^ 5) for s in INNER]),
    ]
    near_columns = [near_0, near_1, near_2, near_3]
    amplitude, by_row = local_call(
        amplitude_kernel,
        [
            jax.ShapeDtypeStruct((width, leds * block), jnp.float32),
            jax.ShapeDtypeStruct(by_row.shape, bf16),
        ],
        [vmem] * 2,
        [],
        0,
        10 * 2**20,
        "amplitude",
    )(images, by_row)
    strips = local_call(
        field_kernel,
        [sent_block] * HALF,
        [vmem] * 11,
        [pltpu.VMEM((width, parts * block), bf16)] * 2
        + [pltpu.VMEM((HALF,) + sent_block.shape, bf16)],
        16 * leds * block * width * width,
        12 * 2**20,
        "modulus_step",
    )(amplitude, by_row, *far_columns, *near_columns)

    def send_home(d):
        pairs = [(s, (s + d) % SLABS) for s in range(SLABS) if FIRST < (s + d) % SLABS < LAST]
        return permute(strips[d % HALF], pairs)

    home = [strips[0]]
    home += [
        permute(strips[d], [(s, s ^ d) for s in range(SLABS)]) for d in range(1, HALF)
    ]
    share = width // 2
    first = share // 4
    piece = (2, rows, share)
    cores = [(0, 1), (1, 0), (2, 3), (3, 2)]
    planes = [(0, 2), (2, 0), (1, 3), (3, 1)]
    across = [(s, s ^ 4) for s in range(SLABS) if FIRST < s ^ 4 < LAST]
    sent_this, sent_that, back = local_call(
        sent_kernel,
        [
            jax.ShapeDtypeStruct((2,) + piece, bf16),
            jax.ShapeDtypeStruct((2,) + piece, bf16),
            jax.ShapeDtypeStruct((parts * rows, HALF * LANES), bf16),
        ],
        [smem] + [vmem] * (1 + HALF),
        [],
        flops // 4,
        8 * 2**20,
        "update_sent",
        16,
    )(starts, by_col, *home)
    got_that = lax.ppermute(sent_that, "led", cores)
    got_this = lax.ppermute(sent_this, "led", cores)
    this_near, this_far, that_near, that_far = local_call(
        kept_kernel,
        [jax.ShapeDtypeStruct(piece, jnp.float32)] * 4,
        [smem, vmem, vmem],
        [],
        flops // 4,
        10 * 2**20,
        "update_kept",
        16,
    )(starts, by_col, back)

    def sum_call(kernel, shapes, *values):
        out_shape = [jax.ShapeDtypeStruct(shape, bf16) for shape in shapes]
        specs = [vmem] * len(values)
        return local_call(kernel, out_shape, specs, [], 0, 2**20, kernel.__name__, 12)(*values)

    rest = (2, rows, share - first)
    over_z, over_x = sum_call(
        first_kernel, [(2, 2, rows, first), rest], that_near, that_far, got_that
    )
    got_z_first = permute(over_z, across)
    got_x = lax.ppermute(over_x, "led", planes)
    (over_z,) = sum_call(z_second_kernel, [rest], that_near, got_that, got_x)
    got_z_second = permute(over_z, across)
    (over,) = sum_call(x_own_kernel, [rest], this_far, got_this)
    got_x_own = lax.ppermute(over, "led", planes)
    over, got_z_first = lax.optimization_barrier((over_z, got_z_first))
    (over,) = sum_call(x_last_kernel, [(2, rows, first)], this_far, got_this, got_z_first)
    got_x_last = lax.ppermute(over, "led", planes)

    def widen(value, before):
        after = share - before - value.shape[2]
        return jnp.pad(value.astype(jnp.float32), ((0, 0), (0, 0), (before, after)))

    base = lax.dynamic_slice_in_dim(spectrum, led_at * share, share, 2)
    base += this_near + got_this[0].astype(jnp.float32) + widen(got_z_first[0], 0)
    base, got_x_own, got_x_last = lax.optimization_barrier((base, got_x_own, got_x_last))
    base += widen(got_x_own, first) + widen(got_x_last, 0)
    base, got_z_second = lax.optimization_barrier((base, got_z_second))
    return base + widen(got_z_second, first)


def solution(mesh):
    placed = (P(None, "slab", None), P("led"), P("led"), P("led", "slab", None))
    fits = mesh.shape["slab"] == 8 and mesh.shape["led"] == 4

    def body(spectrum, led_rows, led_cols, images):
        shapes = (spectrum.shape, images.shape)
        if fits and shapes == ((2, 256, 2048), (2, 128, 1024)):
            return body_slabs(spectrum, led_rows, led_cols, images)
        return body_any(spectrum, led_rows, led_cols, images)

    return jax.shard_map(
        body, mesh=mesh, in_specs=placed, out_specs=P(None, "slab", "led"), check_vma=False
    )
```

```python
import functools

import jax
import jax.numpy as jnp
import numpy as np
from jax import lax
from jax.experimental import pallas as pl
from jax.experimental.pallas import tpu as pltpu
from jax.sharding import PartitionSpec as P

LANES = 128


def as_sent(value):
    return jax.tree.map(lambda a: a.astype(jnp.bfloat16) if a.dtype == jnp.float32 else a, value)


def host_tables(width):
    index = np.arange(width, dtype=np.int64)
    angle_index = (index[:, None] * index[None, :] % width).astype(np.float32)
    angle = angle_index * np.float32(2.0 * 3.141592653589793 / width)
    scale = np.float32(1.0) / np.sqrt(np.float32(width))
    return (
        (np.cos(angle) * scale).astype(jnp.bfloat16),
        (np.sin(angle) * scale).astype(jnp.bfloat16),
    )


def make_pupil(row_index, col_index, width):
    row_term = (2 * row_index + 1 - width) * (2 * row_index + 1 - width)
    col_term = (2 * col_index + 1 - width) * (2 * col_index + 1 - width)
    return (row_term[:, None] + col_term[None, :] < width * width).astype(jnp.float32)


def contract(form, left, right):
    return jnp.einsum(form, left, right, preferred_element_type=jnp.float32)


def take_rows(strip, start, width):
    return lax.dynamic_slice_in_dim(strip, start, width, 1)


def place_rows(block, start, total, axis_dim):
    shape = list(block.shape)
    shape[axis_dim] = total
    holder = jnp.zeros(tuple(shape), block.dtype)
    return lax.dynamic_update_slice_in_dim(holder, block, start, axis_dim)


def modulus_step(field_in_re, field_in_im, image, cos_table, sin_table):
    field_re = contract("lka,am->lkm", field_in_re, cos_table) + contract(
        "lka,am->lkm", field_in_im, sin_table
    )
    field_im = contract("lka,am->lkm", field_in_im, cos_table) - contract(
        "lka,am->lkm", field_in_re, sin_table
    )
    factor = jnp.sqrt(image) / jnp.sqrt(field_re * field_re + field_im * field_im + 0.25) - 1.0
    diff_re = (field_re * factor).astype(jnp.bfloat16)
    diff_im = (field_im * factor).astype(jnp.bfloat16)
    back_re = (
        contract("lkm,ma->lka", diff_re, cos_table) - contract("lkm,ma->lka", diff_im, sin_table)
    ).astype(jnp.bfloat16)
    back_im = (
        contract("lkm,ma->lka", diff_im, cos_table) + contract("lkm,ma->lka", diff_re, sin_table)
    ).astype(jnp.bfloat16)
    return (back_re, back_im)


def body_any(spectrum, led_rows, led_cols, images):
    width = images.shape[2]
    slab_rows = spectrum.shape[1]
    columns = spectrum.shape[2]
    slabs = lax.axis_size("slab")
    total_rows = slab_rows * slabs
    position = lax.axis_index("slab")
    cos_table, sin_table = (jnp.asarray(t) for t in host_tables(width))
    own_rows = position * slab_rows + jnp.arange(slab_rows, dtype=jnp.int32)
    col_index = jnp.arange(width, dtype=jnp.int32)

    def take_cols(start):
        return lax.dynamic_slice_in_dim(spectrum, start, width, 2)

    def owner_mask(start):
        return make_pupil(own_rows - start, col_index, width)

    windows = jax.vmap(take_cols)(led_cols)
    masks = jax.vmap(owner_mask)(led_rows)
    win_re = (windows[:, 0] * masks).astype(jnp.bfloat16)
    win_im = (windows[:, 1] * masks).astype(jnp.bfloat16)

    def slice_strip(block, start):
        return take_rows(block, start, width)

    row_re = (
        contract("lgb,bk->lkg", win_re, cos_table) + contract("lgb,bk->lkg", win_im, sin_table)
    ).astype(jnp.bfloat16)
    row_im = (
        contract("lgb,bk->lkg", win_im, cos_table) - contract("lgb,bk->lkg", win_re, sin_table)
    ).astype(jnp.bfloat16)
    col_re, col_im = (
        lax.all_to_all(row_re, "slab", split_axis=1, concat_axis=2, tiled=True),
        lax.all_to_all(row_im, "slab", split_axis=1, concat_axis=2, tiled=True),
    )
    field_in_re = jax.vmap(slice_strip)(col_re, led_rows)
    field_in_im = jax.vmap(slice_strip)(col_im, led_rows)
    back_re, back_im = modulus_step(field_in_re, field_in_im, images, cos_table, sin_table)

    def place_strip(block, start):
        return place_rows(block, start, total_rows, 1)

    full_re = jax.vmap(place_strip)(back_re, led_rows)
    full_im = jax.vmap(place_strip)(back_im, led_rows)
    home_re, home_im = (
        lax.all_to_all(as_sent(full_re), "slab", split_axis=2, concat_axis=1, tiled=True).astype(
            full_re.dtype
        ),
        lax.all_to_all(as_sent(full_im), "slab", split_axis=2, concat_axis=1, tiled=True).astype(
            full_im.dtype
        ),
    )
    upd_re = contract("lkg,kb->lgb", home_re, cos_table) - contract(
        "lkg,kb->lgb", home_im, sin_table
    )
    upd_im = contract("lkg,kb->lgb", home_im, cos_table) + contract(
        "lkg,kb->lgb", home_re, sin_table
    )
    upd_re = upd_re * masks
    upd_im = upd_im * masks

    def add_window(number, gradient):
        start = led_cols[number]
        piece = jnp.stack([upd_re[number], upd_im[number]])
        current = lax.dynamic_slice_in_dim(gradient, start, width, 2)
        return lax.dynamic_update_slice_in_dim(gradient, current + piece, start, 2)

    gradient = lax.fori_loop(
        0, led_rows.shape[0], add_window, jnp.zeros((2, slab_rows, columns), jnp.float32)
    )
    summed = lax.psum_scatter(gradient, "led", scatter_dimension=2, tiled=True)
    share = summed.shape[2]
    own_part = lax.dynamic_slice_in_dim(spectrum, lax.axis_index("led") * share, share, 2)
    return own_part + summed


SLABS = 8
HALF = 4
FIRST, LAST = 0, 7
PASSED = {1: 0, 6: 7}
INNER = (2, 3, 4, 5)


def dot(left, right):
    return jnp.dot(left, right, preferred_element_type=jnp.float32)


def window_mask(first_row, row_start, col_start, rows, first_col, cols, width):
    shape = (rows, cols)
    at_row = lax.broadcasted_iota(jnp.int32, shape, 0) + (first_row - row_start)
    at_col = lax.broadcasted_iota(jnp.int32, shape, 1) + (first_col - col_start)
    wraps = at_col < 0
    at_col = jnp.where(wraps, at_col + width, at_col)
    row_term = 2 * at_row + 1 - width
    col_term = 2 * at_col + 1 - width
    return row_term * row_term + col_term * col_term < width * width, wraps


def row_block(window, table):
    both = dot(window, table)
    half = both.shape[0] // 2
    row_re = both[:half, :LANES] + both[half:, LANES:]
    row_im = both[half:, :LANES] - both[:half, LANES:]
    return row_re.astype(jnp.bfloat16), row_im.astype(jnp.bfloat16)


def store_parts(out, values):
    per = out.shape[0] // 2
    rows = out.shape[1]
    for plane, value in enumerate(values):
        for led in range(per):
            out[plane * per + led] = value[led * rows : (led + 1) * rows]


def is_one_of(position, slabs):
    return functools.reduce(jnp.logical_or, [position == slab for slab in slabs])


def window_kernel(starts, spectrum, window):
    position = lax.axis_index("slab")
    leds = starts.shape[0] // 2
    rows = spectrum.shape[1]
    width = window.shape[1]
    for led in range(leds):
        inside, wraps = window_mask(
            position * rows, starts[led], starts[leds + led], rows, 0, width, width
        )
        for plane in range(2):
            value = jnp.where(wraps, spectrum[plane, :, width:], spectrum[plane, :, :width])
            at = (plane * leds + led) * rows
            window[at : at + rows, :] = jnp.where(inside, value, 0.0).astype(jnp.bfloat16)


def classes_of(position):
    hands_over = is_one_of(position, PASSED)
    return (jnp.where(hands_over, 5, 6), 7, 2, 4, jnp.where(hands_over, 6, 5), 0, 1, 3)


def rows_kernel(which, window, table, *outs):
    position = lax.axis_index("slab")
    for out, d in zip(outs, classes_of(position)[which]):
        store_parts(out, row_block(window[...], table[jnp.bitwise_xor(position, d)]))


def choose_kernel(got, own, out):
    passes = is_one_of(lax.axis_index("slab"), PASSED.values())

    @pl.when(passes)
    def _():
        out[...] = got[...]

    @pl.when(jnp.logical_not(passes))
    def _():
        out[...] = own[...]


def amplitude_kernel(images, table, out, table_out):
    leds, block, width = images.shape
    for led in range(leds):
        for j in range(width // LANES):
            piece = jnp.sqrt(images[led, :, j * LANES : (j + 1) * LANES])
            out[j * LANES : (j + 1) * LANES, led * block : (led + 1) * block] = piece.T
    table_out[...] = table[...]


def field_kernel(amplitude, table, *rest):
    far, near = rest[:5], rest[5 : HALF + 5]
    outs = rest[HALF + 5 : 2 * HALF + 5]
    field_in, diff, strips = rest[2 * HALF + 5 :]
    position = lax.axis_index("slab")
    parts, rows, _ = near[0].shape
    half = parts // 2 * LANES
    width = field_in.shape[0]
    steps = width // LANES
    group = 4
    for d, block in enumerate(near):
        at = pl.multiple_of(jnp.bitwise_and(jnp.bitwise_xor(position, d), HALF - 1) * rows, rows)
        for part in range(parts):
            cols = slice(part * LANES, (part + 1) * LANES)
            field_in[pl.ds(at, rows), cols] = block[part]

    def add(block, origin):
        at = pl.multiple_of(jnp.bitwise_and(origin, HALF - 1) * rows, rows)
        for part in range(parts):
            cols = slice(part * LANES, (part + 1) * LANES)
            field_in[pl.ds(at, rows), cols] += block[part]

    passes = is_one_of(position, PASSED.values())
    hands_over = is_one_of(position, PASSED)
    ends = is_one_of(position, [to ^ 4 for to in PASSED.values()])

    @pl.when(is_one_of(position, INNER))
    def _():
        add(far[0], jnp.bitwise_xor(position, 6))
        add(far[1], jnp.bitwise_xor(position, 7))
        add(far[2], jnp.bitwise_xor(position, jnp.where(ends, 5, 4)))

    @pl.when(jnp.logical_or(passes, hands_over))
    def _():
        add(far[2], jnp.bitwise_xor(position, 4))
        add(far[3], jnp.bitwise_xor(position, jnp.where(hands_over, 7, 6)))
        add(far[4], jnp.bitwise_xor(position, 5))

    for first in range(0, steps, group):
        product = dot(
            table[first : first + group].reshape(group * 2 * LANES, width), field_in[...]
        )
        for j in range(first, first + group):
            both = product[(j - first) * 2 * LANES : (j - first + 1) * 2 * LANES]
            field_re = both[:LANES, :half] + both[LANES:, half:]
            field_im = both[:LANES, half:] - both[LANES:, :half]
            here = pl.ds(j * LANES, LANES)
            factor = (
                amplitude[here, :] * lax.rsqrt(field_re * field_re + field_im * field_im + 0.25)
                - 1.0
            )
            diff[here, :half] = (field_re * factor).astype(jnp.bfloat16)
            diff[here, half:] = (field_im * factor).astype(jnp.bfloat16)
    pieces = rows // LANES
    for i in range(HALF):
        product = dot(
            table[i * pieces : (i + 1) * pieces].reshape(pieces * 2 * LANES, width), diff[...]
        )
        for h in range(pieces):
            both = product[h * 2 * LANES : (h + 1) * 2 * LANES]
            here = pl.ds(h * LANES, LANES)
            back_re = (both[:LANES, :half] - both[LANES:, half:]).astype(jnp.bfloat16)
            back_im = (both[:LANES, half:] + both[LANES:, :half]).astype(jnp.bfloat16)
            for part in range(parts // 2):
                cols = slice(part * LANES, (part + 1) * LANES)
                strips[i, part, here, :] = back_re[:, cols]
                strips[i, parts // 2 + part, here, :] = back_im[:, cols]
    for d, out in enumerate(outs):
        out[...] = strips[jnp.bitwise_and(jnp.bitwise_xor(position, d), HALF - 1)]


def update_columns(own_core, starts, table, back, outs):
    position = lax.axis_index("slab")
    led_at = lax.axis_index("led")
    core = jnp.bitwise_and(led_at, 1)
    plane_x = jnp.right_shift(led_at, 1)
    which_half = jnp.right_shift(position, 2)
    first_row = jnp.bitwise_and(position, HALF - 1)
    leds = starts.shape[0] // 2
    rows = back.shape[0] // (2 * leds)
    depth = back.shape[1]
    width = table.shape[1]
    group = width // LANES // 2
    owner = core if own_core else 1 - core
    shape = (rows, LANES)
    for n in range(group):
        block = owner * group + n
        both = dot(
            back[...], table[block, pl.ds(pl.multiple_of(which_half * depth, depth), depth)]
        )
        half = leds * rows
        update = (
            both[:half, :LANES] - both[half:, LANES:],
            both[half:, :LANES] + both[:half, LANES:],
        )
        sums = [[0.0, 0.0] for _ in outs]
        for led in range(leds):
            at_row = lax.broadcasted_iota(jnp.int32, shape, 0) + (
                first_row * rows - starts[led]
            )
            at_col = lax.broadcasted_iota(jnp.int32, shape, 1) + (
                block * LANES - starts[leds + led]
            )
            row_term = 2 * jnp.where(at_row < 0, at_row + width, at_row) + 1 - width
            col_term = 2 * jnp.where(at_col < 0, at_col + width, at_col) + 1 - width
            inside = row_term * row_term + col_term * col_term < width * width
            this_slab = jnp.where(at_row < 0, 1, 0) == which_half
            this_x = jnp.where(at_col < 0, 1, 0) == plane_x
            for plane in range(2):
                piece = jnp.where(inside, update[plane][led * rows : (led + 1) * rows], 0.0)
                for i, at_slab in enumerate(
                    (jnp.where(this_slab, piece, 0.0), jnp.where(this_slab, 0.0, piece))
                ):
                    sums[2 * i][plane] += jnp.where(this_x, at_slab, 0.0)
                    sums[2 * i + 1][plane] += jnp.where(this_x, 0.0, at_slab)
        cols = slice(n * LANES, (n + 1) * LANES)
        for out, both_planes in zip(outs, sums):
            for plane in range(2):
                out[plane, :, cols] = both_planes[plane].astype(out.dtype)


def sent_kernel(starts, table, *rest):
    blocks = rest[:HALF]
    this_slab, that_slab, back = rest[HALF:]
    position = lax.axis_index("slab")
    parts, rows, _ = blocks[0].shape
    for d, block in enumerate(blocks):
        source = jnp.bitwise_and(jnp.bitwise_xor(position, d), HALF - 1)
        at = pl.multiple_of(source * LANES, LANES)
        for part in range(parts):
            back[part * rows : (part + 1) * rows, pl.ds(at, LANES)] = block[part]
    outs = [out.at[i] for out in (this_slab, that_slab) for i in range(2)]
    update_columns(False, starts, table, back, outs)


def kept_kernel(starts, table, back, *outs):
    update_columns(True, starts, table, back, outs)


def first_kernel(that_near, that_far, got_that, z_out, x_out):
    cols = z_out.shape[3]
    near = that_near[:, :, :cols].astype(jnp.float32) + got_that[0, :, :, :cols].astype(jnp.float32)
    far = that_far[...].astype(jnp.float32) + got_that[1].astype(jnp.float32)
    z_out[0] = near.astype(z_out.dtype)
    z_out[1] = far[:, :, :cols].astype(z_out.dtype)
    x_out[...] = far[:, :, cols:].astype(x_out.dtype)


def z_second_kernel(that_near, got_that, got_x, out):
    cols = that_near.shape[2] - out.shape[2]
    total = that_near[:, :, cols:].astype(jnp.float32) + got_that[0, :, :, cols:].astype(jnp.float32)
    out[...] = (total + got_x[...].astype(jnp.float32)).astype(out.dtype)


def x_own_kernel(this_far, got_this, out):
    cols = this_far.shape[2] - out.shape[2]
    total = this_far[:, :, cols:].astype(jnp.float32) + got_this[1, :, :, cols:].astype(jnp.float32)
    out[...] = total.astype(out.dtype)


def x_last_kernel(this_far, got_this, got_z, out):
    cols = out.shape[2]
    total = this_far[:, :, :cols].astype(jnp.float32) + got_this[1, :, :, :cols].astype(jnp.float32)
    out[...] = (total + got_z[1].astype(jnp.float32)).astype(out.dtype)


def local_call(kernel, out_shape, spaces, scratch, flops, moved, name, limit=32):
    return pl.pallas_call(
        kernel,
        out_shape=out_shape,
        in_specs=[pl.BlockSpec(memory_space=space) for space in spaces],
        out_specs=jax.tree.map(lambda _: pl.BlockSpec(memory_space=pltpu.VMEM), out_shape),
        scratch_shapes=scratch,
        compiler_params=pltpu.CompilerParams(vmem_limit_bytes=limit * 2**20),
        cost_estimate=pl.CostEstimate(flops=flops, bytes_accessed=moved, transcendentals=0),
        name=name,
    )


def body_slabs(spectrum, led_rows, led_cols, images):
    leds, block, width = images.shape
    rows = spectrum.shape[1]
    led_at = lax.axis_index("led")
    bf16 = jnp.bfloat16
    vmem, smem = pltpu.VMEM, pltpu.SMEM
    cos_table, sin_table = host_tables(width)
    steps = width // LANES
    by_col = np.stack(
        [
            np.concatenate([t[:, j * LANES : (j + 1) * LANES] for t in (cos_table, sin_table)], 1)
            for j in range(steps)
        ]
    )
    by_row = jnp.asarray(np.ascontiguousarray(by_col.transpose(0, 2, 1)))
    by_col = jnp.asarray(by_col)
    parts = 2 * leds
    sent_block = jax.ShapeDtypeStruct((parts, rows, LANES), bf16)
    flops = 8 * leds * rows * width * width

    starts = jnp.concatenate([led_rows, led_cols]).astype(jnp.int32)
    window = local_call(
        window_kernel,
        jax.ShapeDtypeStruct((parts * rows, width), bf16),
        [smem, vmem],
        [],
        0,
        6 * 2**20,
        "windows",
    )(starts, spectrum)

    def rows_call(which, name):
        count = which.stop - which.start
        return local_call(
            functools.partial(rows_kernel, which),
            [sent_block] * count,
            [vmem, vmem],
            [],
            flops * count // SLABS,
            5 * 2**20,
            name,
        )(window, by_col)

    first_a, first_b, near_2 = rows_call(slice(0, 3), "rows_round_1")

    def permute(sent, pairs):
        return lax.ppermute(sent, "slab", pairs)

    def choose(got, own, name):
        return local_call(
            choose_kernel, sent_block, [vmem] * 2, [], 0, 2**19, name
        )(got, own)

    handed = list(PASSED.items())
    windowed = range(FIRST + 1, LAST)
    got_a = permute(first_a, [(s, s ^ 6) for s in INNER] + handed)
    got_b = permute(first_b, [(s, s ^ 7) for s in INNER] + handed)
    near_2 = permute(near_2, [(s, s ^ 2) for s in windowed])
    second_a, second_b, near_0, near_1, near_3 = rows_call(slice(3, SLABS), "rows_round_2")
    got_a, near_2, second_a, second_b, near_1, near_3, images = lax.optimization_barrier(
        (got_a, near_2, second_a, second_b, near_1, near_3, images)
    )
    outer_pairs = [(s, s ^ 6) for s in range(SLABS) if s not in INNER]
    near_1 = permute(near_1, [(s, s ^ 1) for s in windowed])
    near_3 = permute(near_3, [(s, s ^ 3) for s in windowed])
    near_1, got_b = lax.optimization_barrier((near_1, got_b))
    far_columns = [
        got_a,
        got_b,
        permute(choose(got_a, second_a, "class_4_blocks"), [(s, s ^ 4) for s in range(SLABS)]),
        permute(choose(got_b, second_b, "class_6_blocks"), outer_pairs),
        permute(second_b, [(s, s ^ 5) for s in INNER]),
    ]
    near_columns = [near_0, near_1, near_2, near_3]
    amplitude, by_row = local_call(
        amplitude_kernel,
        [
            jax.ShapeDtypeStruct((width, leds * block), jnp.float32),
            jax.ShapeDtypeStruct(by_row.shape, bf16),
        ],
        [vmem] * 2,
        [],
        0,
        10 * 2**20,
        "amplitude",
    )(images, by_row)
    strips = local_call(
        field_kernel,
        [sent_block] * HALF,
        [vmem] * 11,
        [pltpu.VMEM((width, parts * block), bf16)] * 2
        + [pltpu.VMEM((HALF,) + sent_block.shape, bf16)],
        16 * leds * block * width * width,
        12 * 2**20,
        "modulus_step",
    )(amplitude, by_row, *far_columns, *near_columns)

    def send_home(d):
        pairs = [(s, (s + d) % SLABS) for s in range(SLABS) if FIRST < (s + d) % SLABS < LAST]
        return permute(strips[d % HALF], pairs)

    home = [strips[0]]
    home += [
        permute(strips[d], [(s, s ^ d) for s in range(SLABS)]) for d in range(1, HALF)
    ]
    share = width // 2
    first = share // 4
    piece = (2, rows, share)
    cores = [(0, 1), (1, 0), (2, 3), (3, 2)]
    planes = [(0, 2), (2, 0), (1, 3), (3, 1)]
    across = [(s, s ^ 4) for s in range(SLABS) if FIRST < s ^ 4 < LAST]
    sent_this, sent_that, back = local_call(
        sent_kernel,
        [
            jax.ShapeDtypeStruct((2,) + piece, bf16),
            jax.ShapeDtypeStruct((2,) + piece, bf16),
            jax.ShapeDtypeStruct((parts * rows, HALF * LANES), bf16),
        ],
        [smem] + [vmem] * (1 + HALF),
        [],
        flops // 4,
        8 * 2**20,
        "update_sent",
        16,
    )(starts, by_col, *home)
    got_that = lax.ppermute(sent_that, "led", cores)
    got_this = lax.ppermute(sent_this, "led", cores)
    this_near, this_far, that_near, that_far = local_call(
        kept_kernel,
        [jax.ShapeDtypeStruct(piece, jnp.float32)] + [jax.ShapeDtypeStruct(piece, bf16)] * 3,
        [smem, vmem, vmem],
        [],
        flops // 4,
        10 * 2**20,
        "update_kept",
        16,
    )(starts, by_col, back)

    def sum_call(kernel, shapes, *values):
        out_shape = [jax.ShapeDtypeStruct(shape, bf16) for shape in shapes]
        specs = [vmem] * len(values)
        return local_call(kernel, out_shape, specs, [], 0, 2**20, kernel.__name__, 12)(*values)

    rest = (2, rows, share - first)
    over_z, over_x = sum_call(
        first_kernel, [(2, 2, rows, first), rest], that_near, that_far, got_that
    )
    got_z_first = permute(over_z, across)
    got_x = lax.ppermute(over_x, "led", planes)
    (over_z,) = sum_call(z_second_kernel, [rest], that_near, got_that, got_x)
    got_z_second = permute(over_z, across)
    (over,) = sum_call(x_own_kernel, [rest], this_far, got_this)
    got_x_own = lax.ppermute(over, "led", planes)
    over, got_z_first = lax.optimization_barrier((over_z, got_z_first))
    (over,) = sum_call(x_last_kernel, [(2, rows, first)], this_far, got_this, got_z_first)
    got_x_last = lax.ppermute(over, "led", planes)

    def widen(value, before):
        after = share - before - value.shape[2]
        return jnp.pad(value.astype(jnp.float32), ((0, 0), (0, 0), (before, after)))

    base = lax.dynamic_slice_in_dim(spectrum, led_at * share, share, 2)
    base += this_near + got_this[0].astype(jnp.float32) + widen(got_z_first[0], 0)
    base, got_x_own, got_x_last = lax.optimization_barrier((base, got_x_own, got_x_last))
    base += widen(got_x_own, first) + widen(got_x_last, 0)
    base, got_z_second = lax.optimization_barrier((base, got_z_second))
    return base + widen(got_z_second, first)


def solution(mesh):
    placed = (P(None, "slab", None), P("led"), P("led"), P("led", "slab", None))
    fits = mesh.shape["slab"] == 8 and mesh.shape["led"] == 4

    def body(spectrum, led_rows, led_cols, images):
        shapes = (spectrum.shape, images.shape)
        if fits and shapes == ((2, 256, 2048), (2, 128, 1024)):
            return body_slabs(spectrum, led_rows, led_cols, images)
        return body_any(spectrum, led_rows, led_cols, images)

    return jax.shard_map(
        body, mesh=mesh, in_specs=placed, out_specs=P(None, "slab", "led"), check_vma=False
    )
```

```python
import functools

import jax
import jax.numpy as jnp
import numpy as np
from jax import lax
from jax.experimental import pallas as pl
from jax.experimental.pallas import tpu as pltpu
from jax.sharding import PartitionSpec as P

LANES = 128


def as_sent(value):
    return jax.tree.map(lambda a: a.astype(jnp.bfloat16) if a.dtype == jnp.float32 else a, value)


def host_tables(width):
    index = np.arange(width, dtype=np.int64)
    angle_index = (index[:, None] * index[None, :] % width).astype(np.float32)
    angle = angle_index * np.float32(2.0 * 3.141592653589793 / width)
    scale = np.float32(1.0) / np.sqrt(np.float32(width))
    return (
        (np.cos(angle) * scale).astype(jnp.bfloat16),
        (np.sin(angle) * scale).astype(jnp.bfloat16),
    )


def make_pupil(row_index, col_index, width):
    row_term = (2 * row_index + 1 - width) * (2 * row_index + 1 - width)
    col_term = (2 * col_index + 1 - width) * (2 * col_index + 1 - width)
    return (row_term[:, None] + col_term[None, :] < width * width).astype(jnp.float32)


def contract(form, left, right):
    return jnp.einsum(form, left, right, preferred_element_type=jnp.float32)


def take_rows(strip, start, width):
    return lax.dynamic_slice_in_dim(strip, start, width, 1)


def place_rows(block, start, total, axis_dim):
    shape = list(block.shape)
    shape[axis_dim] = total
    holder = jnp.zeros(tuple(shape), block.dtype)
    return lax.dynamic_update_slice_in_dim(holder, block, start, axis_dim)


def modulus_step(field_in_re, field_in_im, image, cos_table, sin_table):
    field_re = contract("lka,am->lkm", field_in_re, cos_table) + contract(
        "lka,am->lkm", field_in_im, sin_table
    )
    field_im = contract("lka,am->lkm", field_in_im, cos_table) - contract(
        "lka,am->lkm", field_in_re, sin_table
    )
    factor = jnp.sqrt(image) / jnp.sqrt(field_re * field_re + field_im * field_im + 0.25) - 1.0
    diff_re = (field_re * factor).astype(jnp.bfloat16)
    diff_im = (field_im * factor).astype(jnp.bfloat16)
    back_re = (
        contract("lkm,ma->lka", diff_re, cos_table) - contract("lkm,ma->lka", diff_im, sin_table)
    ).astype(jnp.bfloat16)
    back_im = (
        contract("lkm,ma->lka", diff_im, cos_table) + contract("lkm,ma->lka", diff_re, sin_table)
    ).astype(jnp.bfloat16)
    return (back_re, back_im)


def body_any(spectrum, led_rows, led_cols, images):
    width = images.shape[2]
    slab_rows = spectrum.shape[1]
    columns = spectrum.shape[2]
    slabs = lax.axis_size("slab")
    total_rows = slab_rows * slabs
    position = lax.axis_index("slab")
    cos_table, sin_table = (jnp.asarray(t) for t in host_tables(width))
    own_rows = position * slab_rows + jnp.arange(slab_rows, dtype=jnp.int32)
    col_index = jnp.arange(width, dtype=jnp.int32)

    def take_cols(start):
        return lax.dynamic_slice_in_dim(spectrum, start, width, 2)

    def owner_mask(start):
        return make_pupil(own_rows - start, col_index, width)

    windows = jax.vmap(take_cols)(led_cols)
    masks = jax.vmap(owner_mask)(led_rows)
    win_re = (windows[:, 0] * masks).astype(jnp.bfloat16)
    win_im = (windows[:, 1] * masks).astype(jnp.bfloat16)

    def slice_strip(block, start):
        return take_rows(block, start, width)

    row_re = (
        contract("lgb,bk->lkg", win_re, cos_table) + contract("lgb,bk->lkg", win_im, sin_table)
    ).astype(jnp.bfloat16)
    row_im = (
        contract("lgb,bk->lkg", win_im, cos_table) - contract("lgb,bk->lkg", win_re, sin_table)
    ).astype(jnp.bfloat16)
    col_re, col_im = (
        lax.all_to_all(row_re, "slab", split_axis=1, concat_axis=2, tiled=True),
        lax.all_to_all(row_im, "slab", split_axis=1, concat_axis=2, tiled=True),
    )
    field_in_re = jax.vmap(slice_strip)(col_re, led_rows)
    field_in_im = jax.vmap(slice_strip)(col_im, led_rows)
    back_re, back_im = modulus_step(field_in_re, field_in_im, images, cos_table, sin_table)

    def place_strip(block, start):
        return place_rows(block, start, total_rows, 1)

    full_re = jax.vmap(place_strip)(back_re, led_rows)
    full_im = jax.vmap(place_strip)(back_im, led_rows)
    home_re, home_im = (
        lax.all_to_all(as_sent(full_re), "slab", split_axis=2, concat_axis=1, tiled=True).astype(
            full_re.dtype
        ),
        lax.all_to_all(as_sent(full_im), "slab", split_axis=2, concat_axis=1, tiled=True).astype(
            full_im.dtype
        ),
    )
    upd_re = contract("lkg,kb->lgb", home_re, cos_table) - contract(
        "lkg,kb->lgb", home_im, sin_table
    )
    upd_im = contract("lkg,kb->lgb", home_im, cos_table) + contract(
        "lkg,kb->lgb", home_re, sin_table
    )
    upd_re = upd_re * masks
    upd_im = upd_im * masks

    def add_window(number, gradient):
        start = led_cols[number]
        piece = jnp.stack([upd_re[number], upd_im[number]])
        current = lax.dynamic_slice_in_dim(gradient, start, width, 2)
        return lax.dynamic_update_slice_in_dim(gradient, current + piece, start, 2)

    gradient = lax.fori_loop(
        0, led_rows.shape[0], add_window, jnp.zeros((2, slab_rows, columns), jnp.float32)
    )
    summed = lax.psum_scatter(gradient, "led", scatter_dimension=2, tiled=True)
    share = summed.shape[2]
    own_part = lax.dynamic_slice_in_dim(spectrum, lax.axis_index("led") * share, share, 2)
    return own_part + summed


SLABS = 8
HALF = 4
FIRST, LAST = 0, 7
PASSED = {1: 0, 6: 7}
INNER = (2, 3, 4, 5)


def dot(left, right):
    return jnp.dot(left, right, preferred_element_type=jnp.float32)


def window_mask(first_row, row_start, col_start, rows, first_col, cols, width):
    shape = (rows, cols)
    at_row = lax.broadcasted_iota(jnp.int32, shape, 0) + (first_row - row_start)
    at_col = lax.broadcasted_iota(jnp.int32, shape, 1) + (first_col - col_start)
    wraps = at_col < 0
    at_col = jnp.where(wraps, at_col + width, at_col)
    row_term = 2 * at_row + 1 - width
    col_term = 2 * at_col + 1 - width
    return row_term * row_term + col_term * col_term < width * width, wraps


def row_block(window, table):
    both = dot(window, table)
    half = both.shape[0] // 2
    row_re = both[:half, :LANES] + both[half:, LANES:]
    row_im = both[half:, :LANES] - both[:half, LANES:]
    return row_re.astype(jnp.bfloat16), row_im.astype(jnp.bfloat16)


def store_parts(out, values):
    per = out.shape[0] // 2
    rows = out.shape[1]
    for plane, value in enumerate(values):
        for led in range(per):
            out[plane * per + led] = value[led * rows : (led + 1) * rows]


def is_one_of(position, slabs):
    return functools.reduce(jnp.logical_or, [position == slab for slab in slabs])


def window_kernel(starts, spectrum, window):
    position = lax.axis_index("slab")
    leds = starts.shape[0] // 2
    rows = spectrum.shape[1]
    width = window.shape[1]
    for led in range(leds):
        inside, wraps = window_mask(
            position * rows, starts[led], starts[leds + led], rows, 0, width, width
        )
        for plane in range(2):
            value = jnp.where(wraps, spectrum[plane, :, width:], spectrum[plane, :, :width])
            at = (plane * leds + led) * rows
            window[at : at + rows, :] = jnp.where(inside, value, 0.0).astype(jnp.bfloat16)


def classes_of(position):
    hands_over = is_one_of(position, PASSED)
    return (jnp.where(hands_over, 5, 6), 7, 2, 4, jnp.where(hands_over, 6, 5), 0, 1, 3)


def rows_kernel(which, window, table, *outs):
    position = lax.axis_index("slab")
    for out, d in zip(outs, classes_of(position)[which]):
        store_parts(out, row_block(window[...], table[jnp.bitwise_xor(position, d)]))


def choose_kernel(got, own, out):
    passes = is_one_of(lax.axis_index("slab"), PASSED.values())

    @pl.when(passes)
    def _():
        out[...] = got[...]

    @pl.when(jnp.logical_not(passes))
    def _():
        out[...] = own[...]


def amplitude_kernel(images, table, out, table_out):
    leds, block, width = images.shape
    for led in range(leds):
        for j in range(width // LANES):
            piece = jnp.sqrt(images[led, :, j * LANES : (j + 1) * LANES])
            out[j * LANES : (j + 1) * LANES, led * block : (led + 1) * block] = piece.T
    table_out[...] = table[...]


def field_kernel(amplitude, table, *rest):
    far, near = rest[:5], rest[5 : HALF + 5]
    outs = rest[HALF + 5 : 2 * HALF + 5]
    field_in, diff, strips = rest[2 * HALF + 5 :]
    position = lax.axis_index("slab")
    parts, rows, _ = near[0].shape
    half = parts // 2 * LANES
    width = field_in.shape[0]
    steps = width // LANES
    group = 4
    for d, block in enumerate(near):
        at = pl.multiple_of(jnp.bitwise_and(jnp.bitwise_xor(position, d), HALF - 1) * rows, rows)
        for part in range(parts):
            cols = slice(part * LANES, (part + 1) * LANES)
            field_in[pl.ds(at, rows), cols] = block[part]

    def add(block, origin):
        at = pl.multiple_of(jnp.bitwise_and(origin, HALF - 1) * rows, rows)
        for part in range(parts):
            cols = slice(part * LANES, (part + 1) * LANES)
            field_in[pl.ds(at, rows), cols] += block[part]

    passes = is_one_of(position, PASSED.values())
    hands_over = is_one_of(position, PASSED)
    ends = is_one_of(position, [to ^ 4 for to in PASSED.values()])

    @pl.when(is_one_of(position, INNER))
    def _():
        add(far[0], jnp.bitwise_xor(position, 6))
        add(far[1], jnp.bitwise_xor(position, 7))
        add(far[2], jnp.bitwise_xor(position, jnp.where(ends, 5, 4)))

    @pl.when(jnp.logical_or(passes, hands_over))
    def _():
        add(far[2], jnp.bitwise_xor(position, 4))
        add(far[3], jnp.bitwise_xor(position, jnp.where(hands_over, 7, 6)))
        add(far[4], jnp.bitwise_xor(position, 5))

    for first in range(0, steps, group):
        product = dot(
            table[first : first + group].reshape(group * 2 * LANES, width), field_in[...]
        )
        for j in range(first, first + group):
            both = product[(j - first) * 2 * LANES : (j - first + 1) * 2 * LANES]
            field_re = both[:LANES, :half] + both[LANES:, half:]
            field_im = both[:LANES, half:] - both[LANES:, :half]
            here = pl.ds(j * LANES, LANES)
            factor = (
                amplitude[here, :] * lax.rsqrt(field_re * field_re + field_im * field_im + 0.25)
                - 1.0
            )
            diff[here, :half] = (field_re * factor).astype(jnp.bfloat16)
            diff[here, half:] = (field_im * factor).astype(jnp.bfloat16)
    pieces = rows // LANES
    for i in range(HALF):
        product = dot(
            table[i * pieces : (i + 1) * pieces].reshape(pieces * 2 * LANES, width), diff[...]
        )
        for h in range(pieces):
            both = product[h * 2 * LANES : (h + 1) * 2 * LANES]
            here = pl.ds(h * LANES, LANES)
            back_re = (both[:LANES, :half] - both[LANES:, half:]).astype(jnp.bfloat16)
            back_im = (both[:LANES, half:] + both[LANES:, :half]).astype(jnp.bfloat16)
            for part in range(parts // 2):
                cols = slice(part * LANES, (part + 1) * LANES)
                strips[i, part, here, :] = back_re[:, cols]
                strips[i, parts // 2 + part, here, :] = back_im[:, cols]
    for d, out in enumerate(outs):
        out[...] = strips[jnp.bitwise_and(jnp.bitwise_xor(position, d), HALF - 1)]


def update_columns(own_core, starts, table, back, outs):
    position = lax.axis_index("slab")
    led_at = lax.axis_index("led")
    core = jnp.bitwise_and(led_at, 1)
    plane_x = jnp.right_shift(led_at, 1)
    which_half = jnp.right_shift(position, 2)
    first_row = jnp.bitwise_and(position, HALF - 1)
    leds = starts.shape[0] // 2
    rows = back.shape[0] // (2 * leds)
    depth = back.shape[1]
    width = table.shape[1]
    group = width // LANES // 2
    owner = core if own_core else 1 - core
    shape = (rows, LANES)
    for n in range(group):
        block = owner * group + n
        both = dot(
            back[...], table[block, pl.ds(pl.multiple_of(which_half * depth, depth), depth)]
        )
        half = leds * rows
        update = (
            both[:half, :LANES] - both[half:, LANES:],
            both[half:, :LANES] + both[:half, LANES:],
        )
        sums = [[0.0, 0.0] for _ in outs]
        for led in range(leds):
            at_row = lax.broadcasted_iota(jnp.int32, shape, 0) + (
                first_row * rows - starts[led]
            )
            at_col = lax.broadcasted_iota(jnp.int32, shape, 1) + (
                block * LANES - starts[leds + led]
            )
            row_term = 2 * jnp.where(at_row < 0, at_row + width, at_row) + 1 - width
            col_term = 2 * jnp.where(at_col < 0, at_col + width, at_col) + 1 - width
            inside = row_term * row_term + col_term * col_term < width * width
            this_slab = jnp.where(at_row < 0, 1, 0) == which_half
            this_x = jnp.where(at_col < 0, 1, 0) == plane_x
            for plane in range(2):
                piece = jnp.where(inside, update[plane][led * rows : (led + 1) * rows], 0.0)
                for i, at_slab in enumerate(
                    (jnp.where(this_slab, piece, 0.0), jnp.where(this_slab, 0.0, piece))
                ):
                    sums[2 * i][plane] += jnp.where(this_x, at_slab, 0.0)
                    sums[2 * i + 1][plane] += jnp.where(this_x, 0.0, at_slab)
        cols = slice(n * LANES, (n + 1) * LANES)
        for out, both_planes in zip(outs, sums):
            for plane in range(2):
                out[plane, :, cols] = both_planes[plane].astype(out.dtype)


def sent_kernel(starts, table, *rest):
    blocks = rest[:HALF]
    this_slab, that_slab, back = rest[HALF:]
    position = lax.axis_index("slab")
    parts, rows, _ = blocks[0].shape
    for d, block in enumerate(blocks):
        source = jnp.bitwise_and(jnp.bitwise_xor(position, d), HALF - 1)
        at = pl.multiple_of(source * LANES, LANES)
        for part in range(parts):
            back[part * rows : (part + 1) * rows, pl.ds(at, LANES)] = block[part]
    outs = [out.at[i] for out in (this_slab, that_slab) for i in range(2)]
    update_columns(False, starts, table, back, outs)


def kept_kernel(starts, table, back, *outs):
    update_columns(True, starts, table, back, outs)


def z_first_kernel(that_near, that_far, got_that, out):
    cols = out.shape[3]
    for i, kept in enumerate((that_near, that_far)):
        total = kept[:, :, :cols] + got_that[i, :, :, :cols].astype(jnp.float32)
        out[i] = total.astype(out.dtype)


def x_first_kernel(that_far, got_that, out):
    cols = that_far.shape[2] - out.shape[2]
    total = that_far[:, :, cols:] + got_that[1, :, :, cols:].astype(jnp.float32)
    out[...] = total.astype(out.dtype)


def z_second_kernel(that_near, got_that, got_x, out):
    cols = that_near.shape[2] - out.shape[2]
    total = that_near[:, :, cols:] + got_that[0, :, :, cols:].astype(jnp.float32)
    out[...] = (total + got_x[...].astype(jnp.float32)).astype(out.dtype)


def x_second_kernel(this_far, got_this, got_z, out):
    cols = got_z.shape[3]
    total = this_far[...] + got_this[1].astype(jnp.float32)
    out[:, :, cols:] = total[:, :, cols:].astype(out.dtype)
    out[:, :, :cols] = (total[:, :, :cols] + got_z[1].astype(jnp.float32)).astype(out.dtype)


def local_call(kernel, out_shape, spaces, scratch, flops, moved, name):
    return pl.pallas_call(
        kernel,
        out_shape=out_shape,
        in_specs=[pl.BlockSpec(memory_space=space) for space in spaces],
        out_specs=jax.tree.map(lambda _: pl.BlockSpec(memory_space=pltpu.VMEM), out_shape),
        scratch_shapes=scratch,
        compiler_params=pltpu.CompilerParams(vmem_limit_bytes=32 * 2**20),
        cost_estimate=pl.CostEstimate(flops=flops, bytes_accessed=moved, transcendentals=0),
        name=name,
    )


def body_slabs(spectrum, led_rows, led_cols, images):
    leds, block, width = images.shape
    rows = spectrum.shape[1]
    led_at = lax.axis_index("led")
    bf16 = jnp.bfloat16
    vmem, smem = pltpu.VMEM, pltpu.SMEM
    cos_table, sin_table = host_tables(width)
    steps = width // LANES
    by_col = np.stack(
        [
            np.concatenate([t[:, j * LANES : (j + 1) * LANES] for t in (cos_table, sin_table)], 1)
            for j in range(steps)
        ]
    )
    by_row = jnp.asarray(np.ascontiguousarray(by_col.transpose(0, 2, 1)))
    by_col = jnp.asarray(by_col)
    parts = 2 * leds
    sent_block = jax.ShapeDtypeStruct((parts, rows, LANES), bf16)
    flops = 8 * leds * rows * width * width

    starts = jnp.concatenate([led_rows, led_cols]).astype(jnp.int32)
    window = local_call(
        window_kernel,
        jax.ShapeDtypeStruct((parts * rows, width), bf16),
        [smem, vmem],
        [],
        0,
        6 * 2**20,
        "windows",
    )(starts, spectrum)

    def rows_call(which, name):
        count = which.stop - which.start
        return local_call(
            functools.partial(rows_kernel, which),
            [sent_block] * count,
            [vmem, vmem],
            [],
            flops * count // SLABS,
            5 * 2**20,
            name,
        )(window, by_col)

    first_a, first_b, near_2 = rows_call(slice(0, 3), "rows_round_1")

    def permute(sent, pairs):
        return lax.ppermute(sent, "slab", pairs)

    def choose(got, own, name):
        return local_call(
            choose_kernel, sent_block, [vmem] * 2, [], 0, 2**19, name
        )(got, own)

    handed = list(PASSED.items())
    windowed = range(FIRST + 1, LAST)
    got_a = permute(first_a, [(s, s ^ 6) for s in INNER] + handed)
    got_b = permute(first_b, [(s, s ^ 7) for s in INNER] + handed)
    near_2 = permute(near_2, [(s, s ^ 2) for s in windowed])
    second_a, second_b, near_0, near_1, near_3 = rows_call(slice(3, SLABS), "rows_round_2")
    got_a, near_2, second_a, second_b, near_1, near_3, images = lax.optimization_barrier(
        (got_a, near_2, second_a, second_b, near_1, near_3, images)
    )
    outer_pairs = [(s, s ^ 6) for s in range(SLABS) if s not in INNER]
    near_1 = permute(near_1, [(s, s ^ 1) for s in windowed])
    near_3 = permute(near_3, [(s, s ^ 3) for s in windowed])
    near_3, got_b = lax.optimization_barrier((near_3, got_b))
    far_columns = [
        got_a,
        got_b,
        permute(choose(got_a, second_a, "class_4_blocks"), [(s, s ^ 4) for s in range(SLABS)]),
        permute(choose(got_b, second_b, "class_6_blocks"), outer_pairs),
        permute(second_b, [(s, s ^ 5) for s in INNER]),
    ]
    near_columns = [near_0, near_1, near_2, near_3]
    amplitude, by_row = local_call(
        amplitude_kernel,
        [
            jax.ShapeDtypeStruct((width, leds * block), jnp.float32),
            jax.ShapeDtypeStruct(by_row.shape, bf16),
        ],
        [vmem] * 2,
        [],
        0,
        10 * 2**20,
        "amplitude",
    )(images, by_row)
    strips = local_call(
        field_kernel,
        [sent_block] * HALF,
        [vmem] * 11,
        [pltpu.VMEM((width, parts * block), bf16)] * 2
        + [pltpu.VMEM((HALF,) + sent_block.shape, bf16)],
        16 * leds * block * width * width,
        12 * 2**20,
        "modulus_step",
    )(amplitude, by_row, *far_columns, *near_columns)

    def send_home(d):
        pairs = [(s, (s + d) % SLABS) for s in range(SLABS) if FIRST < (s + d) % SLABS < LAST]
        return permute(strips[d % HALF], pairs)

    home = [strips[0]]
    home += [
        permute(strips[d], [(s, s ^ d) for s in range(SLABS)]) for d in range(1, HALF)
    ]
    share = width // 2
    first = share // 4
    piece = (2, rows, share)
    cores = [(0, 1), (1, 0), (2, 3), (3, 2)]
    planes = [(0, 2), (2, 0), (1, 3), (3, 1)]
    across = [(s, s ^ 4) for s in range(SLABS) if FIRST < s ^ 4 < LAST]
    sent_this, sent_that, back = local_call(
        sent_kernel,
        [
            jax.ShapeDtypeStruct((2,) + piece, bf16),
            jax.ShapeDtypeStruct((2,) + piece, bf16),
            jax.ShapeDtypeStruct((parts * rows, HALF * LANES), bf16),
        ],
        [smem] + [vmem] * (1 + HALF),
        [],
        flops // 4,
        8 * 2**20,
        "update_sent",
    )(starts, by_col, *home)
    got_that = lax.ppermute(sent_that, "led", cores)
    got_this = lax.ppermute(sent_this, "led", cores)
    this_near, this_far, that_near, that_far = local_call(
        kept_kernel,
        [jax.ShapeDtypeStruct(piece, jnp.float32)] * 4,
        [smem, vmem, vmem],
        [],
        flops // 4,
        10 * 2**20,
        "update_kept",
    )(starts, by_col, back)

    def sum_call(kernel, shape, *values):
        out_shape = jax.ShapeDtypeStruct(shape, bf16)
        specs = [vmem] * len(values)
        return local_call(kernel, out_shape, specs, [], 0, 2**20, kernel.__name__)(*values)

    over = sum_call(z_first_kernel, (2, 2, rows, first), that_near, that_far, got_that)
    got_z_first = permute(over, across)
    over = sum_call(x_first_kernel, (2, rows, share - first), that_far, got_that)
    got_x = lax.ppermute(over, "led", planes)
    over = sum_call(z_second_kernel, (2, rows, share - first), that_near, got_that, got_x)
    got_z_second = permute(over, across)
    over = sum_call(x_second_kernel, piece, this_far, got_this, got_z_first)
    got_x = lax.ppermute(over, "led", planes)

    def widen(value, before):
        after = share - before - value.shape[2]
        return jnp.pad(value.astype(jnp.float32), ((0, 0), (0, 0), (before, after)))

    base = lax.dynamic_slice_in_dim(spectrum, led_at * share, share, 2)
    base += this_near + got_this[0].astype(jnp.float32) + widen(got_z_first[0], 0)
    base, got_x = lax.optimization_barrier((base, got_x))
    base += got_x.astype(jnp.float32)
    base, got_z_second = lax.optimization_barrier((base, got_z_second))
    return base + widen(got_z_second, first)


def solution(mesh):
    placed = (P(None, "slab", None), P("led"), P("led"), P("led", "slab", None))
    fits = mesh.shape["slab"] == 8 and mesh.shape["led"] == 4

    def body(spectrum, led_rows, led_cols, images):
        shapes = (spectrum.shape, images.shape)
        if fits and shapes == ((2, 256, 2048), (2, 128, 1024)):
            return body_slabs(spectrum, led_rows, led_cols, images)
        return body_any(spectrum, led_rows, led_cols, images)

    return jax.shard_map(
        body, mesh=mesh, in_specs=placed, out_specs=P(None, "slab", "led"), check_vma=False
    )
```

```python
import functools

import jax
import jax.numpy as jnp
import numpy as np
from jax import lax
from jax.experimental import pallas as pl
from jax.experimental.pallas import tpu as pltpu
from jax.sharding import PartitionSpec as P

LANES = 128


def as_sent(value):
    return jax.tree.map(lambda a: a.astype(jnp.bfloat16) if a.dtype == jnp.float32 else a, value)


def host_tables(width):
    index = np.arange(width, dtype=np.int64)
    angle_index = (index[:, None] * index[None, :] % width).astype(np.float32)
    angle = angle_index * np.float32(2.0 * 3.141592653589793 / width)
    scale = np.float32(1.0) / np.sqrt(np.float32(width))
    return (
        (np.cos(angle) * scale).astype(jnp.bfloat16),
        (np.sin(angle) * scale).astype(jnp.bfloat16),
    )


def make_pupil(row_index, col_index, width):
    row_term = (2 * row_index + 1 - width) * (2 * row_index + 1 - width)
    col_term = (2 * col_index + 1 - width) * (2 * col_index + 1 - width)
    return (row_term[:, None] + col_term[None, :] < width * width).astype(jnp.float32)


def contract(form, left, right):
    return jnp.einsum(form, left, right, preferred_element_type=jnp.float32)


def take_rows(strip, start, width):
    return lax.dynamic_slice_in_dim(strip, start, width, 1)


def place_rows(block, start, total, axis_dim):
    shape = list(block.shape)
    shape[axis_dim] = total
    holder = jnp.zeros(tuple(shape), block.dtype)
    return lax.dynamic_update_slice_in_dim(holder, block, start, axis_dim)


def modulus_step(field_in_re, field_in_im, image, cos_table, sin_table):
    field_re = contract("lka,am->lkm", field_in_re, cos_table) + contract(
        "lka,am->lkm", field_in_im, sin_table
    )
    field_im = contract("lka,am->lkm", field_in_im, cos_table) - contract(
        "lka,am->lkm", field_in_re, sin_table
    )
    factor = jnp.sqrt(image) / jnp.sqrt(field_re * field_re + field_im * field_im + 0.25) - 1.0
    diff_re = (field_re * factor).astype(jnp.bfloat16)
    diff_im = (field_im * factor).astype(jnp.bfloat16)
    back_re = (
        contract("lkm,ma->lka", diff_re, cos_table) - contract("lkm,ma->lka", diff_im, sin_table)
    ).astype(jnp.bfloat16)
    back_im = (
        contract("lkm,ma->lka", diff_im, cos_table) + contract("lkm,ma->lka", diff_re, sin_table)
    ).astype(jnp.bfloat16)
    return (back_re, back_im)


def body_any(spectrum, led_rows, led_cols, images):
    width = images.shape[2]
    slab_rows = spectrum.shape[1]
    columns = spectrum.shape[2]
    slabs = lax.axis_size("slab")
    total_rows = slab_rows * slabs
    position = lax.axis_index("slab")
    cos_table, sin_table = (jnp.asarray(t) for t in host_tables(width))
    own_rows = position * slab_rows + jnp.arange(slab_rows, dtype=jnp.int32)
    col_index = jnp.arange(width, dtype=jnp.int32)

    def take_cols(start):
        return lax.dynamic_slice_in_dim(spectrum, start, width, 2)

    def owner_mask(start):
        return make_pupil(own_rows - start, col_index, width)

    windows = jax.vmap(take_cols)(led_cols)
    masks = jax.vmap(owner_mask)(led_rows)
    win_re = (windows[:, 0] * masks).astype(jnp.bfloat16)
    win_im = (windows[:, 1] * masks).astype(jnp.bfloat16)

    def slice_strip(block, start):
        return take_rows(block, start, width)

    row_re = (
        contract("lgb,bk->lkg", win_re, cos_table) + contract("lgb,bk->lkg", win_im, sin_table)
    ).astype(jnp.bfloat16)
    row_im = (
        contract("lgb,bk->lkg", win_im, cos_table) - contract("lgb,bk->lkg", win_re, sin_table)
    ).astype(jnp.bfloat16)
    col_re, col_im = (
        lax.all_to_all(row_re, "slab", split_axis=1, concat_axis=2, tiled=True),
        lax.all_to_all(row_im, "slab", split_axis=1, concat_axis=2, tiled=True),
    )
    field_in_re = jax.vmap(slice_strip)(col_re, led_rows)
    field_in_im = jax.vmap(slice_strip)(col_im, led_rows)
    back_re, back_im = modulus_step(field_in_re, field_in_im, images, cos_table, sin_table)

    def place_strip(block, start):
        return place_rows(block, start, total_rows, 1)

    full_re = jax.vmap(place_strip)(back_re, led_rows)
    full_im = jax.vmap(place_strip)(back_im, led_rows)
    home_re, home_im = (
        lax.all_to_all(as_sent(full_re), "slab", split_axis=2, concat_axis=1, tiled=True).astype(
            full_re.dtype
        ),
        lax.all_to_all(as_sent(full_im), "slab", split_axis=2, concat_axis=1, tiled=True).astype(
            full_im.dtype
        ),
    )
    upd_re = contract("lkg,kb->lgb", home_re, cos_table) - contract(
        "lkg,kb->lgb", home_im, sin_table
    )
    upd_im = contract("lkg,kb->lgb", home_im, cos_table) + contract(
        "lkg,kb->lgb", home_re, sin_table
    )
    upd_re = upd_re * masks
    upd_im = upd_im * masks

    def add_window(number, gradient):
        start = led_cols[number]
        piece = jnp.stack([upd_re[number], upd_im[number]])
        current = lax.dynamic_slice_in_dim(gradient, start, width, 2)
        return lax.dynamic_update_slice_in_dim(gradient, current + piece, start, 2)

    gradient = lax.fori_loop(
        0, led_rows.shape[0], add_window, jnp.zeros((2, slab_rows, columns), jnp.float32)
    )
    summed = lax.psum_scatter(gradient, "led", scatter_dimension=2, tiled=True)
    share = summed.shape[2]
    own_part = lax.dynamic_slice_in_dim(spectrum, lax.axis_index("led") * share, share, 2)
    return own_part + summed


SLABS = 8
HALF = 4
FIRST, LAST = 0, 7
PASSED = {1: 0, 6: 7}
INNER = (2, 3, 4, 5)


def dot(left, right):
    return jnp.dot(left, right, preferred_element_type=jnp.float32)


def window_mask(first_row, row_start, col_start, rows, first_col, cols, width):
    shape = (rows, cols)
    at_row = lax.broadcasted_iota(jnp.int32, shape, 0) + (first_row - row_start)
    at_col = lax.broadcasted_iota(jnp.int32, shape, 1) + (first_col - col_start)
    wraps = at_col < 0
    at_col = jnp.where(wraps, at_col + width, at_col)
    row_term = 2 * at_row + 1 - width
    col_term = 2 * at_col + 1 - width
    return row_term * row_term + col_term * col_term < width * width, wraps


def row_block(window, table):
    both = dot(window, table)
    half = both.shape[0] // 2
    row_re = both[:half, :LANES] + both[half:, LANES:]
    row_im = both[half:, :LANES] - both[:half, LANES:]
    return row_re.astype(jnp.bfloat16), row_im.astype(jnp.bfloat16)


def store_parts(out, values):
    per = out.shape[0] // 2
    rows = out.shape[1]
    for plane, value in enumerate(values):
        for led in range(per):
            out[plane * per + led] = value[led * rows : (led + 1) * rows]


def is_one_of(position, slabs):
    return functools.reduce(jnp.logical_or, [position == slab for slab in slabs])


def window_kernel(starts, spectrum, window):
    position = lax.axis_index("slab")
    leds = starts.shape[0] // 2
    rows = spectrum.shape[1]
    width = window.shape[1]
    for led in range(leds):
        inside, wraps = window_mask(
            position * rows, starts[led], starts[leds + led], rows, 0, width, width
        )
        for plane in range(2):
            value = jnp.where(wraps, spectrum[plane, :, width:], spectrum[plane, :, :width])
            at = (plane * leds + led) * rows
            window[at : at + rows, :] = jnp.where(inside, value, 0.0).astype(jnp.bfloat16)


def classes_of(position):
    hands_over = is_one_of(position, PASSED)
    return (jnp.where(hands_over, 5, 6), 7, 2, 4, jnp.where(hands_over, 6, 5), 0, 1, 3)


def rows_kernel(which, window, table, *outs):
    position = lax.axis_index("slab")
    for out, d in zip(outs, classes_of(position)[which]):
        store_parts(out, row_block(window[...], table[jnp.bitwise_xor(position, d)]))


def choose_kernel(got, own, out):
    passes = is_one_of(lax.axis_index("slab"), PASSED.values())

    @pl.when(passes)
    def _():
        out[...] = got[...]

    @pl.when(jnp.logical_not(passes))
    def _():
        out[...] = own[...]


def amplitude_kernel(images, table, out, table_out):
    leds, block, width = images.shape
    for led in range(leds):
        for j in range(width // LANES):
            piece = jnp.sqrt(images[led, :, j * LANES : (j + 1) * LANES])
            out[j * LANES : (j + 1) * LANES, led * block : (led + 1) * block] = piece.T
    table_out[...] = table[...]


def field_kernel(amplitude, table, *rest):
    far, near = rest[:5], rest[5 : HALF + 5]
    outs = rest[HALF + 5 : 2 * HALF + 5]
    field_in, diff, strips = rest[2 * HALF + 5 :]
    position = lax.axis_index("slab")
    parts, rows, _ = near[0].shape
    half = parts // 2 * LANES
    width = field_in.shape[0]
    steps = width // LANES
    group = 4
    for d, block in enumerate(near):
        at = pl.multiple_of(jnp.bitwise_and(jnp.bitwise_xor(position, d), HALF - 1) * rows, rows)
        for part in range(parts):
            cols = slice(part * LANES, (part + 1) * LANES)
            field_in[pl.ds(at, rows), cols] = block[part]

    def add(block, origin):
        at = pl.multiple_of(jnp.bitwise_and(origin, HALF - 1) * rows, rows)
        for part in range(parts):
            cols = slice(part * LANES, (part + 1) * LANES)
            field_in[pl.ds(at, rows), cols] += block[part]

    passes = is_one_of(position, PASSED.values())
    hands_over = is_one_of(position, PASSED)
    ends = is_one_of(position, [to ^ 4 for to in PASSED.values()])

    @pl.when(is_one_of(position, INNER))
    def _():
        add(far[0], jnp.bitwise_xor(position, 6))
        add(far[1], jnp.bitwise_xor(position, 7))
        add(far[2], jnp.bitwise_xor(position, jnp.where(ends, 5, 4)))

    @pl.when(jnp.logical_or(passes, hands_over))
    def _():
        add(far[2], jnp.bitwise_xor(position, 4))
        add(far[3], jnp.bitwise_xor(position, jnp.where(hands_over, 7, 6)))
        add(far[4], jnp.bitwise_xor(position, 5))

    for first in range(0, steps, group):
        product = dot(
            table[first : first + group].reshape(group * 2 * LANES, width), field_in[...]
        )
        for j in range(first, first + group):
            both = product[(j - first) * 2 * LANES : (j - first + 1) * 2 * LANES]
            field_re = both[:LANES, :half] + both[LANES:, half:]
            field_im = both[:LANES, half:] - both[LANES:, :half]
            here = pl.ds(j * LANES, LANES)
            factor = (
                amplitude[here, :] * lax.rsqrt(field_re * field_re + field_im * field_im + 0.25)
                - 1.0
            )
            diff[here, :half] = (field_re * factor).astype(jnp.bfloat16)
            diff[here, half:] = (field_im * factor).astype(jnp.bfloat16)
    pieces = rows // LANES
    for i in range(HALF):
        product = dot(
            table[i * pieces : (i + 1) * pieces].reshape(pieces * 2 * LANES, width), diff[...]
        )
        for h in range(pieces):
            both = product[h * 2 * LANES : (h + 1) * 2 * LANES]
            here = pl.ds(h * LANES, LANES)
            back_re = (both[:LANES, :half] - both[LANES:, half:]).astype(jnp.bfloat16)
            back_im = (both[:LANES, half:] + both[LANES:, :half]).astype(jnp.bfloat16)
            for part in range(parts // 2):
                cols = slice(part * LANES, (part + 1) * LANES)
                strips[i, part, here, :] = back_re[:, cols]
                strips[i, parts // 2 + part, here, :] = back_im[:, cols]
    for d, out in enumerate(outs):
        out[...] = strips[jnp.bitwise_and(jnp.bitwise_xor(position, d), HALF - 1)]


def update_columns(own_core, starts, table, back, outs):
    position = lax.axis_index("slab")
    led_at = lax.axis_index("led")
    core = jnp.bitwise_and(led_at, 1)
    plane_x = jnp.right_shift(led_at, 1)
    which_half = jnp.right_shift(position, 2)
    first_row = jnp.bitwise_and(position, HALF - 1)
    leds = starts.shape[0] // 2
    rows = back.shape[0] // (2 * leds)
    depth = back.shape[1]
    width = table.shape[1]
    group = width // LANES // 2
    owner = core if own_core else 1 - core
    shape = (rows, LANES)
    for n in range(group):
        block = owner * group + n
        both = dot(
            back[...], table[block, pl.ds(pl.multiple_of(which_half * depth, depth), depth)]
        )
        half = leds * rows
        update = (
            both[:half, :LANES] - both[half:, LANES:],
            both[half:, :LANES] + both[:half, LANES:],
        )
        sums = [[0.0, 0.0] for _ in outs]
        for led in range(leds):
            at_row = lax.broadcasted_iota(jnp.int32, shape, 0) + (
                first_row * rows - starts[led]
            )
            at_col = lax.broadcasted_iota(jnp.int32, shape, 1) + (
                block * LANES - starts[leds + led]
            )
            row_term = 2 * jnp.where(at_row < 0, at_row + width, at_row) + 1 - width
            col_term = 2 * jnp.where(at_col < 0, at_col + width, at_col) + 1 - width
            inside = row_term * row_term + col_term * col_term < width * width
            this_slab = jnp.where(at_row < 0, 1, 0) == which_half
            this_x = jnp.where(at_col < 0, 1, 0) == plane_x
            for plane in range(2):
                piece = jnp.where(inside, update[plane][led * rows : (led + 1) * rows], 0.0)
                for i, at_slab in enumerate(
                    (jnp.where(this_slab, piece, 0.0), jnp.where(this_slab, 0.0, piece))
                ):
                    sums[2 * i][plane] += jnp.where(this_x, at_slab, 0.0)
                    sums[2 * i + 1][plane] += jnp.where(this_x, 0.0, at_slab)
        cols = slice(n * LANES, (n + 1) * LANES)
        for out, both_planes in zip(outs, sums):
            for plane in range(2):
                out[plane, :, cols] = both_planes[plane].astype(out.dtype)


def sent_kernel(starts, table, *rest):
    blocks = rest[:HALF]
    this_slab, that_slab, back = rest[HALF:]
    position = lax.axis_index("slab")
    parts, rows, _ = blocks[0].shape
    for d, block in enumerate(blocks):
        source = jnp.bitwise_and(jnp.bitwise_xor(position, d), HALF - 1)
        at = pl.multiple_of(source * LANES, LANES)
        for part in range(parts):
            back[part * rows : (part + 1) * rows, pl.ds(at, LANES)] = block[part]
    outs = [out.at[i] for out in (this_slab, that_slab) for i in range(2)]
    update_columns(False, starts, table, back, outs)


def kept_kernel(starts, table, back, *outs):
    update_columns(True, starts, table, back, outs)


def z_first_kernel(that_near, that_far, got_that, out):
    cols = out.shape[3]
    for i, kept in enumerate((that_near, that_far)):
        total = kept[:, :, :cols] + got_that[i, :, :, :cols].astype(jnp.float32)
        out[i] = total.astype(out.dtype)


def x_first_kernel(that_far, got_that, out):
    cols = that_far.shape[2] - out.shape[2]
    total = that_far[:, :, cols:] + got_that[1, :, :, cols:].astype(jnp.float32)
    out[...] = total.astype(out.dtype)


def z_second_kernel(that_near, got_that, got_x, out):
    cols = that_near.shape[2] - out.shape[2]
    total = that_near[:, :, cols:] + got_that[0, :, :, cols:].astype(jnp.float32)
    out[...] = (total + got_x[...].astype(jnp.float32)).astype(out.dtype)


def x_second_kernel(this_far, got_this, got_z, out):
    cols = got_z.shape[3]
    total = this_far[...] + got_this[1].astype(jnp.float32)
    out[:, :, cols:] = total[:, :, cols:].astype(out.dtype)
    out[:, :, :cols] = (total[:, :, :cols] + got_z[1].astype(jnp.float32)).astype(out.dtype)


def local_call(kernel, out_shape, spaces, scratch, flops, moved, name):
    return pl.pallas_call(
        kernel,
        out_shape=out_shape,
        in_specs=[pl.BlockSpec(memory_space=space) for space in spaces],
        out_specs=jax.tree.map(lambda _: pl.BlockSpec(memory_space=pltpu.VMEM), out_shape),
        scratch_shapes=scratch,
        compiler_params=pltpu.CompilerParams(vmem_limit_bytes=32 * 2**20),
        cost_estimate=pl.CostEstimate(flops=flops, bytes_accessed=moved, transcendentals=0),
        name=name,
    )


def body_slabs(spectrum, led_rows, led_cols, images):
    leds, block, width = images.shape
    rows = spectrum.shape[1]
    led_at = lax.axis_index("led")
    bf16 = jnp.bfloat16
    vmem, smem = pltpu.VMEM, pltpu.SMEM
    cos_table, sin_table = host_tables(width)
    steps = width // LANES
    by_col = np.stack(
        [
            np.concatenate([t[:, j * LANES : (j + 1) * LANES] for t in (cos_table, sin_table)], 1)
            for j in range(steps)
        ]
    )
    by_row = jnp.asarray(np.ascontiguousarray(by_col.transpose(0, 2, 1)))
    by_col = jnp.asarray(by_col)
    parts = 2 * leds
    sent_block = jax.ShapeDtypeStruct((parts, rows, LANES), bf16)
    flops = 8 * leds * rows * width * width

    starts = jnp.concatenate([led_rows, led_cols]).astype(jnp.int32)
    window = local_call(
        window_kernel,
        jax.ShapeDtypeStruct((parts * rows, width), bf16),
        [smem, vmem],
        [],
        0,
        6 * 2**20,
        "windows",
    )(starts, spectrum)

    def rows_call(which, name):
        count = which.stop - which.start
        return local_call(
            functools.partial(rows_kernel, which),
            [sent_block] * count,
            [vmem, vmem],
            [],
            flops * count // SLABS,
            5 * 2**20,
            name,
        )(window, by_col)

    first_a, first_b, near_2 = rows_call(slice(0, 3), "rows_round_1")

    def permute(sent, pairs):
        return lax.ppermute(sent, "slab", pairs)

    def choose(got, own, name):
        return local_call(
            choose_kernel, sent_block, [vmem] * 2, [], 0, 2**19, name
        )(got, own)

    handed = list(PASSED.items())
    windowed = range(FIRST + 1, LAST)
    got_a = permute(first_a, [(s, s ^ 6) for s in INNER] + handed)
    got_b = permute(first_b, [(s, s ^ 7) for s in INNER] + handed)
    near_2 = permute(near_2, [(s, s ^ 2) for s in windowed])
    second_a, second_b, near_0, near_1, near_3 = rows_call(slice(3, SLABS), "rows_round_2")
    got_a, near_2, second_a, second_b, near_1, near_3, images = lax.optimization_barrier(
        (got_a, near_2, second_a, second_b, near_1, near_3, images)
    )
    outer_pairs = [(s, s ^ 6) for s in range(SLABS) if s not in INNER]
    near_1 = permute(near_1, [(s, s ^ 1) for s in windowed])
    near_3 = permute(near_3, [(s, s ^ 3) for s in windowed])
    near_3, got_b = lax.optimization_barrier((near_3, got_b))
    third = choose(got_a, second_b, "class_5_blocks")
    inner_5 = permute(third, [(s, s ^ 5) for s in INNER])
    third, second_a = lax.optimization_barrier((third, second_a))
    far_columns = [
        got_a,
        got_b,
        permute(choose(got_a, second_a, "class_4_blocks"), [(s, s ^ 4) for s in range(SLABS)]),
        permute(choose(got_b, second_b, "class_6_blocks"), outer_pairs),
        inner_5,
    ]
    near_columns = [near_0, near_1, near_2, near_3]
    amplitude, by_row = local_call(
        amplitude_kernel,
        [
            jax.ShapeDtypeStruct((width, leds * block), jnp.float32),
            jax.ShapeDtypeStruct(by_row.shape, bf16),
        ],
        [vmem] * 2,
        [],
        0,
        10 * 2**20,
        "amplitude",
    )(images, by_row)
    strips = local_call(
        field_kernel,
        [sent_block] * HALF,
        [vmem] * 11,
        [pltpu.VMEM((width, parts * block), bf16)] * 2
        + [pltpu.VMEM((HALF,) + sent_block.shape, bf16)],
        16 * leds * block * width * width,
        12 * 2**20,
        "modulus_step",
    )(amplitude, by_row, *far_columns, *near_columns)

    def send_home(d):
        pairs = [(s, (s + d) % SLABS) for s in range(SLABS) if FIRST < (s + d) % SLABS < LAST]
        return permute(strips[d % HALF], pairs)

    home = [strips[0]]
    home += [
        permute(strips[d], [(s, s ^ d) for s in range(SLABS)]) for d in range(1, HALF)
    ]
    share = width // 2
    first = share // 4
    piece = (2, rows, share)
    cores = [(0, 1), (1, 0), (2, 3), (3, 2)]
    planes = [(0, 2), (2, 0), (1, 3), (3, 1)]
    across = [(s, s ^ 4) for s in range(SLABS) if FIRST < s ^ 4 < LAST]
    sent_this, sent_that, back = local_call(
        sent_kernel,
        [
            jax.ShapeDtypeStruct((2,) + piece, bf16),
            jax.ShapeDtypeStruct((2,) + piece, bf16),
            jax.ShapeDtypeStruct((parts * rows, HALF * LANES), bf16),
        ],
        [smem] + [vmem] * (1 + HALF),
        [],
        flops // 4,
        8 * 2**20,
        "update_sent",
    )(starts, by_col, *home)
    got_that = lax.ppermute(sent_that, "led", cores)
    got_this = lax.ppermute(sent_this, "led", cores)
    this_near, this_far, that_near, that_far = local_call(
        kept_kernel,
        [jax.ShapeDtypeStruct(piece, jnp.float32)] * 4,
        [smem, vmem, vmem],
        [],
        flops // 4,
        10 * 2**20,
        "update_kept",
    )(starts, by_col, back)

    def sum_call(kernel, shape, *values):
        out_shape = jax.ShapeDtypeStruct(shape, bf16)
        specs = [vmem] * len(values)
        return local_call(kernel, out_shape, specs, [], 0, 2**20, kernel.__name__)(*values)

    over = sum_call(z_first_kernel, (2, 2, rows, first), that_near, that_far, got_that)
    got_z_first = permute(over, across)
    over = sum_call(x_first_kernel, (2, rows, share - first), that_far, got_that)
    got_x = lax.ppermute(over, "led", planes)
    over = sum_call(z_second_kernel, (2, rows, share - first), that_near, got_that, got_x)
    got_z_second = permute(over, across)
    over = sum_call(x_second_kernel, piece, this_far, got_this, got_z_first)
    got_x = lax.ppermute(over, "led", planes)

    def widen(value, before):
        after = share - before - value.shape[2]
        return jnp.pad(value.astype(jnp.float32), ((0, 0), (0, 0), (before, after)))

    base = lax.dynamic_slice_in_dim(spectrum, led_at * share, share, 2)
    base += this_near + got_this[0].astype(jnp.float32) + widen(got_z_first[0], 0)
    base, got_x = lax.optimization_barrier((base, got_x))
    base += got_x.astype(jnp.float32)
    base, got_z_second = lax.optimization_barrier((base, got_z_second))
    return base + widen(got_z_second, first)


def solution(mesh):
    placed = (P(None, "slab", None), P("led"), P("led"), P("led", "slab", None))
    fits = mesh.shape["slab"] == 8 and mesh.shape["led"] == 4

    def body(spectrum, led_rows, led_cols, images):
        shapes = (spectrum.shape, images.shape)
        if fits and shapes == ((2, 256, 2048), (2, 128, 1024)):
            return body_slabs(spectrum, led_rows, led_cols, images)
        return body_any(spectrum, led_rows, led_cols, images)

    return jax.shard_map(
        body, mesh=mesh, in_specs=placed, out_specs=P(None, "slab", "led"), check_vma=False
    )
```

```python
import functools

import jax
import jax.numpy as jnp
import numpy as np
from jax import lax
from jax.experimental import pallas as pl
from jax.experimental.pallas import tpu as pltpu
from jax.sharding import PartitionSpec as P

LANES = 128


def as_sent(value):
    return jax.tree.map(lambda a: a.astype(jnp.bfloat16) if a.dtype == jnp.float32 else a, value)


def host_tables(width):
    index = np.arange(width, dtype=np.int64)
    angle_index = (index[:, None] * index[None, :] % width).astype(np.float32)
    angle = angle_index * np.float32(2.0 * 3.141592653589793 / width)
    scale = np.float32(1.0) / np.sqrt(np.float32(width))
    return (
        (np.cos(angle) * scale).astype(jnp.bfloat16),
        (np.sin(angle) * scale).astype(jnp.bfloat16),
    )


def make_pupil(row_index, col_index, width):
    row_term = (2 * row_index + 1 - width) * (2 * row_index + 1 - width)
    col_term = (2 * col_index + 1 - width) * (2 * col_index + 1 - width)
    return (row_term[:, None] + col_term[None, :] < width * width).astype(jnp.float32)


def contract(form, left, right):
    return jnp.einsum(form, left, right, preferred_element_type=jnp.float32)


def take_rows(strip, start, width):
    return lax.dynamic_slice_in_dim(strip, start, width, 1)


def place_rows(block, start, total, axis_dim):
    shape = list(block.shape)
    shape[axis_dim] = total
    holder = jnp.zeros(tuple(shape), block.dtype)
    return lax.dynamic_update_slice_in_dim(holder, block, start, axis_dim)


def modulus_step(field_in_re, field_in_im, image, cos_table, sin_table):
    field_re = contract("lka,am->lkm", field_in_re, cos_table) + contract(
        "lka,am->lkm", field_in_im, sin_table
    )
    field_im = contract("lka,am->lkm", field_in_im, cos_table) - contract(
        "lka,am->lkm", field_in_re, sin_table
    )
    factor = jnp.sqrt(image) / jnp.sqrt(field_re * field_re + field_im * field_im + 0.25) - 1.0
    diff_re = (field_re * factor).astype(jnp.bfloat16)
    diff_im = (field_im * factor).astype(jnp.bfloat16)
    back_re = (
        contract("lkm,ma->lka", diff_re, cos_table) - contract("lkm,ma->lka", diff_im, sin_table)
    ).astype(jnp.bfloat16)
    back_im = (
        contract("lkm,ma->lka", diff_im, cos_table) + contract("lkm,ma->lka", diff_re, sin_table)
    ).astype(jnp.bfloat16)
    return (back_re, back_im)


def body_any(spectrum, led_rows, led_cols, images):
    width = images.shape[2]
    slab_rows = spectrum.shape[1]
    columns = spectrum.shape[2]
    slabs = lax.axis_size("slab")
    total_rows = slab_rows * slabs
    position = lax.axis_index("slab")
    cos_table, sin_table = (jnp.asarray(t) for t in host_tables(width))
    own_rows = position * slab_rows + jnp.arange(slab_rows, dtype=jnp.int32)
    col_index = jnp.arange(width, dtype=jnp.int32)

    def take_cols(start):
        return lax.dynamic_slice_in_dim(spectrum, start, width, 2)

    def owner_mask(start):
        return make_pupil(own_rows - start, col_index, width)

    windows = jax.vmap(take_cols)(led_cols)
    masks = jax.vmap(owner_mask)(led_rows)
    win_re = (windows[:, 0] * masks).astype(jnp.bfloat16)
    win_im = (windows[:, 1] * masks).astype(jnp.bfloat16)

    def slice_strip(block, start):
        return take_rows(block, start, width)

    row_re = (
        contract("lgb,bk->lkg", win_re, cos_table) + contract("lgb,bk->lkg", win_im, sin_table)
    ).astype(jnp.bfloat16)
    row_im = (
        contract("lgb,bk->lkg", win_im, cos_table) - contract("lgb,bk->lkg", win_re, sin_table)
    ).astype(jnp.bfloat16)
    col_re, col_im = (
        lax.all_to_all(row_re, "slab", split_axis=1, concat_axis=2, tiled=True),
        lax.all_to_all(row_im, "slab", split_axis=1, concat_axis=2, tiled=True),
    )
    field_in_re = jax.vmap(slice_strip)(col_re, led_rows)
    field_in_im = jax.vmap(slice_strip)(col_im, led_rows)
    back_re, back_im = modulus_step(field_in_re, field_in_im, images, cos_table, sin_table)

    def place_strip(block, start):
        return place_rows(block, start, total_rows, 1)

    full_re = jax.vmap(place_strip)(back_re, led_rows)
    full_im = jax.vmap(place_strip)(back_im, led_rows)
    home_re, home_im = (
        lax.all_to_all(as_sent(full_re), "slab", split_axis=2, concat_axis=1, tiled=True).astype(
            full_re.dtype
        ),
        lax.all_to_all(as_sent(full_im), "slab", split_axis=2, concat_axis=1, tiled=True).astype(
            full_im.dtype
        ),
    )
    upd_re = contract("lkg,kb->lgb", home_re, cos_table) - contract(
        "lkg,kb->lgb", home_im, sin_table
    )
    upd_im = contract("lkg,kb->lgb", home_im, cos_table) + contract(
        "lkg,kb->lgb", home_re, sin_table
    )
    upd_re = upd_re * masks
    upd_im = upd_im * masks

    def add_window(number, gradient):
        start = led_cols[number]
        piece = jnp.stack([upd_re[number], upd_im[number]])
        current = lax.dynamic_slice_in_dim(gradient, start, width, 2)
        return lax.dynamic_update_slice_in_dim(gradient, current + piece, start, 2)

    gradient = lax.fori_loop(
        0, led_rows.shape[0], add_window, jnp.zeros((2, slab_rows, columns), jnp.float32)
    )
    summed = lax.psum_scatter(gradient, "led", scatter_dimension=2, tiled=True)
    share = summed.shape[2]
    own_part = lax.dynamic_slice_in_dim(spectrum, lax.axis_index("led") * share, share, 2)
    return own_part + summed


SLABS = 8
HALF = 4
FIRST, LAST = 0, 7
PASSED = {1: 0, 6: 7}
INNER = (2, 3, 4, 5)


def dot(left, right):
    return jnp.dot(left, right, preferred_element_type=jnp.float32)


def window_mask(first_row, row_start, col_start, rows, first_col, cols, width):
    shape = (rows, cols)
    at_row = lax.broadcasted_iota(jnp.int32, shape, 0) + (first_row - row_start)
    at_col = lax.broadcasted_iota(jnp.int32, shape, 1) + (first_col - col_start)
    wraps = at_col < 0
    at_col = jnp.where(wraps, at_col + width, at_col)
    row_term = 2 * at_row + 1 - width
    col_term = 2 * at_col + 1 - width
    return row_term * row_term + col_term * col_term < width * width, wraps


def row_block(window, table):
    both = dot(window, table)
    half = both.shape[0] // 2
    row_re = both[:half, :LANES] + both[half:, LANES:]
    row_im = both[half:, :LANES] - both[:half, LANES:]
    return row_re.astype(jnp.bfloat16), row_im.astype(jnp.bfloat16)


def store_parts(out, values):
    per = out.shape[0] // 2
    rows = out.shape[1]
    for plane, value in enumerate(values):
        for led in range(per):
            out[plane * per + led] = value[led * rows : (led + 1) * rows]


def is_one_of(position, slabs):
    return functools.reduce(jnp.logical_or, [position == slab for slab in slabs])


def window_kernel(starts, spectrum, window):
    position = lax.axis_index("slab")
    leds = starts.shape[0] // 2
    rows = spectrum.shape[1]
    width = window.shape[1]
    for led in range(leds):
        inside, wraps = window_mask(
            position * rows, starts[led], starts[leds + led], rows, 0, width, width
        )
        for plane in range(2):
            value = jnp.where(wraps, spectrum[plane, :, width:], spectrum[plane, :, :width])
            at = (plane * leds + led) * rows
            window[at : at + rows, :] = jnp.where(inside, value, 0.0).astype(jnp.bfloat16)


def classes_of(position):
    hands_over = is_one_of(position, PASSED)
    return (jnp.where(hands_over, 5, 6), 7, 2, 4, jnp.where(hands_over, 6, 5), 0, 1, 3)


def rows_kernel(which, window, table, *outs):
    position = lax.axis_index("slab")
    for out, d in zip(outs, classes_of(position)[which]):
        store_parts(out, row_block(window[...], table[jnp.bitwise_xor(position, d)]))


def choose_kernel(got, own, out):
    passes = is_one_of(lax.axis_index("slab"), PASSED.values())

    @pl.when(passes)
    def _():
        out[...] = got[...]

    @pl.when(jnp.logical_not(passes))
    def _():
        out[...] = own[...]


def amplitude_kernel(images, table, out, table_out):
    leds, block, width = images.shape
    for led in range(leds):
        for j in range(width // LANES):
            piece = jnp.sqrt(images[led, :, j * LANES : (j + 1) * LANES])
            out[j * LANES : (j + 1) * LANES, led * block : (led + 1) * block] = piece.T
    table_out[...] = table[...]


def field_kernel(amplitude, table, *rest):
    far, near = rest[:5], rest[5 : HALF + 5]
    outs = rest[HALF + 5 : 2 * HALF + 5]
    field_in, diff, strips = rest[2 * HALF + 5 :]
    position = lax.axis_index("slab")
    parts, rows, _ = near[0].shape
    half = parts // 2 * LANES
    width = field_in.shape[0]
    steps = width // LANES
    group = 4
    for d, block in enumerate(near):
        at = pl.multiple_of(jnp.bitwise_and(jnp.bitwise_xor(position, d), HALF - 1) * rows, rows)
        for part in range(parts):
            cols = slice(part * LANES, (part + 1) * LANES)
            field_in[pl.ds(at, rows), cols] = block[part]

    def add(block, origin):
        at = pl.multiple_of(jnp.bitwise_and(origin, HALF - 1) * rows, rows)
        for part in range(parts):
            cols = slice(part * LANES, (part + 1) * LANES)
            field_in[pl.ds(at, rows), cols] += block[part]

    passes = is_one_of(position, PASSED.values())
    hands_over = is_one_of(position, PASSED)
    ends = is_one_of(position, [to ^ 4 for to in PASSED.values()])

    @pl.when(is_one_of(position, INNER))
    def _():
        add(far[0], jnp.bitwise_xor(position, 6))
        add(far[1], jnp.bitwise_xor(position, 7))
        add(far[2], jnp.bitwise_xor(position, jnp.where(ends, 5, 4)))

    @pl.when(jnp.logical_or(passes, hands_over))
    def _():
        add(far[2], jnp.bitwise_xor(position, 4))
        add(far[3], jnp.bitwise_xor(position, jnp.where(hands_over, 7, 6)))
        add(far[4], jnp.bitwise_xor(position, 5))

    for first in range(0, steps, group):
        product = dot(
            table[first : first + group].reshape(group * 2 * LANES, width), field_in[...]
        )
        for j in range(first, first + group):
            both = product[(j - first) * 2 * LANES : (j - first + 1) * 2 * LANES]
            field_re = both[:LANES, :half] + both[LANES:, half:]
            field_im = both[:LANES, half:] - both[LANES:, :half]
            here = pl.ds(j * LANES, LANES)
            factor = (
                amplitude[here, :] * lax.rsqrt(field_re * field_re + field_im * field_im + 0.25)
                - 1.0
            )
            diff[here, :half] = (field_re * factor).astype(jnp.bfloat16)
            diff[here, half:] = (field_im * factor).astype(jnp.bfloat16)
    pieces = rows // LANES
    for i in range(HALF):
        product = dot(
            table[i * pieces : (i + 1) * pieces].reshape(pieces * 2 * LANES, width), diff[...]
        )
        for h in range(pieces):
            both = product[h * 2 * LANES : (h + 1) * 2 * LANES]
            here = pl.ds(h * LANES, LANES)
            back_re = (both[:LANES, :half] - both[LANES:, half:]).astype(jnp.bfloat16)
            back_im = (both[:LANES, half:] + both[LANES:, :half]).astype(jnp.bfloat16)
            for part in range(parts // 2):
                cols = slice(part * LANES, (part + 1) * LANES)
                strips[i, part, here, :] = back_re[:, cols]
                strips[i, parts // 2 + part, here, :] = back_im[:, cols]
    for d, out in enumerate(outs):
        out[...] = strips[jnp.bitwise_and(jnp.bitwise_xor(position, d), HALF - 1)]


def update_columns(own_core, starts, table, back, outs):
    position = lax.axis_index("slab")
    led_at = lax.axis_index("led")
    core = jnp.bitwise_and(led_at, 1)
    plane_x = jnp.right_shift(led_at, 1)
    which_half = jnp.right_shift(position, 2)
    first_row = jnp.bitwise_and(position, HALF - 1)
    leds = starts.shape[0] // 2
    rows = back.shape[0] // (2 * leds)
    depth = back.shape[1]
    width = table.shape[1]
    group = width // LANES // 2
    owner = core if own_core else 1 - core
    shape = (rows, LANES)
    for n in range(group):
        block = owner * group + n
        both = dot(
            back[...], table[block, pl.ds(pl.multiple_of(which_half * depth, depth), depth)]
        )
        half = leds * rows
        update = (
            both[:half, :LANES] - both[half:, LANES:],
            both[half:, :LANES] + both[:half, LANES:],
        )
        sums = [[0.0, 0.0] for _ in outs]
        for led in range(leds):
            at_row = lax.broadcasted_iota(jnp.int32, shape, 0) + (
                first_row * rows - starts[led]
            )
            at_col = lax.broadcasted_iota(jnp.int32, shape, 1) + (
                block * LANES - starts[leds + led]
            )
            row_term = 2 * jnp.where(at_row < 0, at_row + width, at_row) + 1 - width
            col_term = 2 * jnp.where(at_col < 0, at_col + width, at_col) + 1 - width
            inside = row_term * row_term + col_term * col_term < width * width
            this_slab = jnp.where(at_row < 0, 1, 0) == which_half
            this_x = jnp.where(at_col < 0, 1, 0) == plane_x
            for plane in range(2):
                piece = jnp.where(inside, update[plane][led * rows : (led + 1) * rows], 0.0)
                for i, at_slab in enumerate(
                    (jnp.where(this_slab, piece, 0.0), jnp.where(this_slab, 0.0, piece))
                ):
                    sums[2 * i][plane] += jnp.where(this_x, at_slab, 0.0)
                    sums[2 * i + 1][plane] += jnp.where(this_x, 0.0, at_slab)
        cols = slice(n * LANES, (n + 1) * LANES)
        for out, both_planes in zip(outs, sums):
            for plane in range(2):
                out[plane, :, cols] = both_planes[plane].astype(out.dtype)


def sent_kernel(starts, table, *rest):
    blocks = rest[:HALF]
    this_slab, that_slab, back = rest[HALF:]
    position = lax.axis_index("slab")
    parts, rows, _ = blocks[0].shape
    for d, block in enumerate(blocks):
        source = jnp.bitwise_and(jnp.bitwise_xor(position, d), HALF - 1)
        at = pl.multiple_of(source * LANES, LANES)
        for part in range(parts):
            back[part * rows : (part + 1) * rows, pl.ds(at, LANES)] = block[part]
    outs = [out.at[i] for out in (this_slab, that_slab) for i in range(2)]
    update_columns(False, starts, table, back, outs)


def kept_kernel(starts, table, back, *outs):
    update_columns(True, starts, table, back, outs)


def z_first_kernel(that_near, that_far, got_that, out):
    cols = out.shape[3]
    for i, kept in enumerate((that_near, that_far)):
        total = kept[:, :, :cols] + got_that[i, :, :, :cols].astype(jnp.float32)
        out[i] = total.astype(out.dtype)


def x_first_kernel(that_far, got_that, out):
    cols = that_far.shape[2] - out.shape[2]
    total = that_far[:, :, cols:] + got_that[1, :, :, cols:].astype(jnp.float32)
    out[...] = total.astype(out.dtype)


def z_second_kernel(that_near, got_that, got_x, out):
    cols = that_near.shape[2] - out.shape[2]
    total = that_near[:, :, cols:] + got_that[0, :, :, cols:].astype(jnp.float32)
    out[...] = (total + got_x[...].astype(jnp.float32)).astype(out.dtype)


def x_second_kernel(this_far, got_this, got_z, out):
    cols = got_z.shape[3]
    total = this_far[...] + got_this[1].astype(jnp.float32)
    out[:, :, cols:] = total[:, :, cols:].astype(out.dtype)
    out[:, :, :cols] = (total[:, :, :cols] + got_z[1].astype(jnp.float32)).astype(out.dtype)


def local_call(kernel, out_shape, spaces, scratch, flops, moved, name):
    return pl.pallas_call(
        kernel,
        out_shape=out_shape,
        in_specs=[pl.BlockSpec(memory_space=space) for space in spaces],
        out_specs=jax.tree.map(lambda _: pl.BlockSpec(memory_space=pltpu.VMEM), out_shape),
        scratch_shapes=scratch,
        compiler_params=pltpu.CompilerParams(vmem_limit_bytes=32 * 2**20),
        cost_estimate=pl.CostEstimate(flops=flops, bytes_accessed=moved, transcendentals=0),
        name=name,
    )


def body_slabs(spectrum, led_rows, led_cols, images):
    leds, block, width = images.shape
    rows = spectrum.shape[1]
    led_at = lax.axis_index("led")
    bf16 = jnp.bfloat16
    vmem, smem = pltpu.VMEM, pltpu.SMEM
    cos_table, sin_table = host_tables(width)
    steps = width // LANES
    by_col = np.stack(
        [
            np.concatenate([t[:, j * LANES : (j + 1) * LANES] for t in (cos_table, sin_table)], 1)
            for j in range(steps)
        ]
    )
    by_row = jnp.asarray(np.ascontiguousarray(by_col.transpose(0, 2, 1)))
    by_col = jnp.asarray(by_col)
    parts = 2 * leds
    sent_block = jax.ShapeDtypeStruct((parts, rows, LANES), bf16)
    flops = 8 * leds * rows * width * width

    starts = jnp.concatenate([led_rows, led_cols]).astype(jnp.int32)
    window = local_call(
        window_kernel,
        jax.ShapeDtypeStruct((parts * rows, width), bf16),
        [smem, vmem],
        [],
        0,
        6 * 2**20,
        "windows",
    )(starts, spectrum)

    def rows_call(which, name):
        count = which.stop - which.start
        return local_call(
            functools.partial(rows_kernel, which),
            [sent_block] * count,
            [vmem, vmem],
            [],
            flops * count // SLABS,
            5 * 2**20,
            name,
        )(window, by_col)

    first_a, first_b, near_2 = rows_call(slice(0, 3), "rows_round_1")

    def permute(sent, pairs):
        return lax.ppermute(sent, "slab", pairs)

    def choose(got, own, name):
        return local_call(
            choose_kernel, sent_block, [vmem] * 2, [], 0, 2**19, name
        )(got, own)

    handed = list(PASSED.items())
    windowed = range(FIRST + 1, LAST)
    got_a = permute(first_a, [(s, s ^ 6) for s in INNER] + handed)
    got_b = permute(first_b, [(s, s ^ 7) for s in INNER] + handed)
    near_2 = permute(near_2, [(s, s ^ 2) for s in windowed])
    second_a, second_b, near_0, near_1, near_3 = rows_call(slice(3, SLABS), "rows_round_2")
    got_a, second_a, near_3, images = lax.optimization_barrier((got_a, second_a, near_3, images))
    _, near_2, second_b, near_1 = lax.optimization_barrier((got_a, near_2, second_b, near_1))
    outer_pairs = [(s, s ^ 6) for s in range(SLABS) if s not in INNER]
    near_1 = permute(near_1, [(s, s ^ 1) for s in windowed])
    near_3 = permute(near_3, [(s, s ^ 3) for s in windowed])
    near_3, got_b = lax.optimization_barrier((near_3, got_b))
    far_columns = [
        got_a,
        got_b,
        permute(choose(got_a, second_a, "class_4_blocks"), [(s, s ^ 4) for s in range(SLABS)]),
        permute(choose(got_b, second_b, "class_6_blocks"), outer_pairs),
        permute(second_b, [(s, s ^ 5) for s in INNER]),
    ]
    near_columns = [near_0, near_1, near_2, near_3]
    amplitude, by_row = local_call(
        amplitude_kernel,
        [
            jax.ShapeDtypeStruct((width, leds * block), jnp.float32),
            jax.ShapeDtypeStruct(by_row.shape, bf16),
        ],
        [vmem] * 2,
        [],
        0,
        10 * 2**20,
        "amplitude",
    )(images, by_row)
    strips = local_call(
        field_kernel,
        [sent_block] * HALF,
        [vmem] * 11,
        [pltpu.VMEM((width, parts * block), bf16)] * 2
        + [pltpu.VMEM((HALF,) + sent_block.shape, bf16)],
        16 * leds * block * width * width,
        12 * 2**20,
        "modulus_step",
    )(amplitude, by_row, *far_columns, *near_columns)

    def send_home(d):
        pairs = [(s, (s + d) % SLABS) for s in range(SLABS) if FIRST < (s + d) % SLABS < LAST]
        return permute(strips[d % HALF], pairs)

    home = [strips[0]]
    home += [
        permute(strips[d], [(s, s ^ d) for s in range(SLABS)]) for d in range(1, HALF)
    ]
    share = width // 2
    first = share // 4
    piece = (2, rows, share)
    cores = [(0, 1), (1, 0), (2, 3), (3, 2)]
    planes = [(0, 2), (2, 0), (1, 3), (3, 1)]
    across = [(s, s ^ 4) for s in range(SLABS) if FIRST < s ^ 4 < LAST]
    sent_this, sent_that, back = local_call(
        sent_kernel,
        [
            jax.ShapeDtypeStruct((2,) + piece, bf16),
            jax.ShapeDtypeStruct((2,) + piece, bf16),
            jax.ShapeDtypeStruct((parts * rows, HALF * LANES), bf16),
        ],
        [smem] + [vmem] * (1 + HALF),
        [],
        flops // 4,
        8 * 2**20,
        "update_sent",
    )(starts, by_col, *home)
    got_that = lax.ppermute(sent_that, "led", cores)
    got_this = lax.ppermute(sent_this, "led", cores)
    this_near, this_far, that_near, that_far = local_call(
        kept_kernel,
        [jax.ShapeDtypeStruct(piece, jnp.float32)] * 4,
        [smem, vmem, vmem],
        [],
        flops // 4,
        10 * 2**20,
        "update_kept",
    )(starts, by_col, back)

    def sum_call(kernel, shape, *values):
        out_shape = jax.ShapeDtypeStruct(shape, bf16)
        specs = [vmem] * len(values)
        return local_call(kernel, out_shape, specs, [], 0, 2**20, kernel.__name__)(*values)

    over = sum_call(z_first_kernel, (2, 2, rows, first), that_near, that_far, got_that)
    got_z_first = permute(over, across)
    over = sum_call(x_first_kernel, (2, rows, share - first), that_far, got_that)
    got_x = lax.ppermute(over, "led", planes)
    over = sum_call(z_second_kernel, (2, rows, share - first), that_near, got_that, got_x)
    got_z_second = permute(over, across)
    over = sum_call(x_second_kernel, piece, this_far, got_this, got_z_first)
    got_x = lax.ppermute(over, "led", planes)

    def widen(value, before):
        after = share - before - value.shape[2]
        return jnp.pad(value.astype(jnp.float32), ((0, 0), (0, 0), (before, after)))

    base = lax.dynamic_slice_in_dim(spectrum, led_at * share, share, 2)
    base += this_near + got_this[0].astype(jnp.float32) + widen(got_z_first[0], 0)
    base, got_x = lax.optimization_barrier((base, got_x))
    base += got_x.astype(jnp.float32)
    base, got_z_second = lax.optimization_barrier((base, got_z_second))
    return base + widen(got_z_second, first)


def solution(mesh):
    placed = (P(None, "slab", None), P("led"), P("led"), P("led", "slab", None))
    fits = mesh.shape["slab"] == 8 and mesh.shape["led"] == 4

    def body(spectrum, led_rows, led_cols, images):
        shapes = (spectrum.shape, images.shape)
        if fits and shapes == ((2, 256, 2048), (2, 128, 1024)):
            return body_slabs(spectrum, led_rows, led_cols, images)
        return body_any(spectrum, led_rows, led_cols, images)

    return jax.shard_map(
        body, mesh=mesh, in_specs=placed, out_specs=P(None, "slab", "led"), check_vma=False
    )
```

```python
import functools

import jax
import jax.numpy as jnp
import numpy as np
from jax import lax
from jax.experimental import pallas as pl
from jax.experimental.pallas import tpu as pltpu
from jax.sharding import PartitionSpec as P

LANES = 128


def as_sent(value):
    return jax.tree.map(lambda a: a.astype(jnp.bfloat16) if a.dtype == jnp.float32 else a, value)


def host_tables(width):
    index = np.arange(width, dtype=np.int64)
    angle_index = (index[:, None] * index[None, :] % width).astype(np.float32)
    angle = angle_index * np.float32(2.0 * 3.141592653589793 / width)
    scale = np.float32(1.0) / np.sqrt(np.float32(width))
    return (
        (np.cos(angle) * scale).astype(jnp.bfloat16),
        (np.sin(angle) * scale).astype(jnp.bfloat16),
    )


def make_pupil(row_index, col_index, width):
    row_term = (2 * row_index + 1 - width) * (2 * row_index + 1 - width)
    col_term = (2 * col_index + 1 - width) * (2 * col_index + 1 - width)
    return (row_term[:, None] + col_term[None, :] < width * width).astype(jnp.float32)


def contract(form, left, right):
    return jnp.einsum(form, left, right, preferred_element_type=jnp.float32)


def take_rows(strip, start, width):
    return lax.dynamic_slice_in_dim(strip, start, width, 1)


def place_rows(block, start, total, axis_dim):
    shape = list(block.shape)
    shape[axis_dim] = total
    holder = jnp.zeros(tuple(shape), block.dtype)
    return lax.dynamic_update_slice_in_dim(holder, block, start, axis_dim)


def modulus_step(field_in_re, field_in_im, image, cos_table, sin_table):
    field_re = contract("lka,am->lkm", field_in_re, cos_table) + contract(
        "lka,am->lkm", field_in_im, sin_table
    )
    field_im = contract("lka,am->lkm", field_in_im, cos_table) - contract(
        "lka,am->lkm", field_in_re, sin_table
    )
    factor = jnp.sqrt(image) / jnp.sqrt(field_re * field_re + field_im * field_im + 0.25) - 1.0
    diff_re = (field_re * factor).astype(jnp.bfloat16)
    diff_im = (field_im * factor).astype(jnp.bfloat16)
    back_re = (
        contract("lkm,ma->lka", diff_re, cos_table) - contract("lkm,ma->lka", diff_im, sin_table)
    ).astype(jnp.bfloat16)
    back_im = (
        contract("lkm,ma->lka", diff_im, cos_table) + contract("lkm,ma->lka", diff_re, sin_table)
    ).astype(jnp.bfloat16)
    return (back_re, back_im)


def body_any(spectrum, led_rows, led_cols, images):
    width = images.shape[2]
    slab_rows = spectrum.shape[1]
    columns = spectrum.shape[2]
    slabs = lax.axis_size("slab")
    total_rows = slab_rows * slabs
    position = lax.axis_index("slab")
    cos_table, sin_table = (jnp.asarray(t) for t in host_tables(width))
    own_rows = position * slab_rows + jnp.arange(slab_rows, dtype=jnp.int32)
    col_index = jnp.arange(width, dtype=jnp.int32)

    def take_cols(start):
        return lax.dynamic_slice_in_dim(spectrum, start, width, 2)

    def owner_mask(start):
        return make_pupil(own_rows - start, col_index, width)

    windows = jax.vmap(take_cols)(led_cols)
    masks = jax.vmap(owner_mask)(led_rows)
    win_re = (windows[:, 0] * masks).astype(jnp.bfloat16)
    win_im = (windows[:, 1] * masks).astype(jnp.bfloat16)

    def slice_strip(block, start):
        return take_rows(block, start, width)

    row_re = (
        contract("lgb,bk->lkg", win_re, cos_table) + contract("lgb,bk->lkg", win_im, sin_table)
    ).astype(jnp.bfloat16)
    row_im = (
        contract("lgb,bk->lkg", win_im, cos_table) - contract("lgb,bk->lkg", win_re, sin_table)
    ).astype(jnp.bfloat16)
    col_re, col_im = (
        lax.all_to_all(row_re, "slab", split_axis=1, concat_axis=2, tiled=True),
        lax.all_to_all(row_im, "slab", split_axis=1, concat_axis=2, tiled=True),
    )
    field_in_re = jax.vmap(slice_strip)(col_re, led_rows)
    field_in_im = jax.vmap(slice_strip)(col_im, led_rows)
    back_re, back_im = modulus_step(field_in_re, field_in_im, images, cos_table, sin_table)

    def place_strip(block, start):
        return place_rows(block, start, total_rows, 1)

    full_re = jax.vmap(place_strip)(back_re, led_rows)
    full_im = jax.vmap(place_strip)(back_im, led_rows)
    home_re, home_im = (
        lax.all_to_all(as_sent(full_re), "slab", split_axis=2, concat_axis=1, tiled=True).astype(
            full_re.dtype
        ),
        lax.all_to_all(as_sent(full_im), "slab", split_axis=2, concat_axis=1, tiled=True).astype(
            full_im.dtype
        ),
    )
    upd_re = contract("lkg,kb->lgb", home_re, cos_table) - contract(
        "lkg,kb->lgb", home_im, sin_table
    )
    upd_im = contract("lkg,kb->lgb", home_im, cos_table) + contract(
        "lkg,kb->lgb", home_re, sin_table
    )
    upd_re = upd_re * masks
    upd_im = upd_im * masks

    def add_window(number, gradient):
        start = led_cols[number]
        piece = jnp.stack([upd_re[number], upd_im[number]])
        current = lax.dynamic_slice_in_dim(gradient, start, width, 2)
        return lax.dynamic_update_slice_in_dim(gradient, current + piece, start, 2)

    gradient = lax.fori_loop(
        0, led_rows.shape[0], add_window, jnp.zeros((2, slab_rows, columns), jnp.float32)
    )
    summed = lax.psum_scatter(gradient, "led", scatter_dimension=2, tiled=True)
    share = summed.shape[2]
    own_part = lax.dynamic_slice_in_dim(spectrum, lax.axis_index("led") * share, share, 2)
    return own_part + summed


SLABS = 8
HALF = 4
FIRST, LAST = 0, 7
PASSED = {1: 0, 6: 7}
INNER = (2, 3, 4, 5)


def dot(left, right):
    return jnp.dot(left, right, preferred_element_type=jnp.float32)


def window_mask(first_row, row_start, col_start, rows, first_col, cols, width):
    shape = (rows, cols)
    at_row = lax.broadcasted_iota(jnp.int32, shape, 0) + (first_row - row_start)
    at_col = lax.broadcasted_iota(jnp.int32, shape, 1) + (first_col - col_start)
    wraps = at_col < 0
    at_col = jnp.where(wraps, at_col + width, at_col)
    row_term = 2 * at_row + 1 - width
    col_term = 2 * at_col + 1 - width
    return row_term * row_term + col_term * col_term < width * width, wraps


def row_block(window, table):
    both = dot(window, table)
    half = both.shape[0] // 2
    row_re = both[:half, :LANES] + both[half:, LANES:]
    row_im = both[half:, :LANES] - both[:half, LANES:]
    return row_re.astype(jnp.bfloat16), row_im.astype(jnp.bfloat16)


def store_parts(out, values):
    per = out.shape[0] // 2
    rows = out.shape[1]
    for plane, value in enumerate(values):
        for led in range(per):
            out[plane * per + led] = value[led * rows : (led + 1) * rows]


def is_one_of(position, slabs):
    return functools.reduce(jnp.logical_or, [position == slab for slab in slabs])


def window_kernel(starts, spectrum, window):
    position = lax.axis_index("slab")
    leds = starts.shape[0] // 2
    rows = spectrum.shape[1]
    width = window.shape[1]
    for led in range(leds):
        inside, wraps = window_mask(
            position * rows, starts[led], starts[leds + led], rows, 0, width, width
        )
        for plane in range(2):
            value = jnp.where(wraps, spectrum[plane, :, width:], spectrum[plane, :, :width])
            at = (plane * leds + led) * rows
            window[at : at + rows, :] = jnp.where(inside, value, 0.0).astype(jnp.bfloat16)


def classes_of(position):
    hands_over = is_one_of(position, PASSED)
    return (jnp.where(hands_over, 5, 6), 7, 2, 4, jnp.where(hands_over, 6, 5), 0, 1, 3)


def rows_kernel(which, window, table, *outs):
    position = lax.axis_index("slab")
    for out, d in zip(outs, classes_of(position)[which]):
        store_parts(out, row_block(window[...], table[jnp.bitwise_xor(position, d)]))


def choose_kernel(got, own, out):
    passes = is_one_of(lax.axis_index("slab"), PASSED.values())

    @pl.when(passes)
    def _():
        out[...] = got[...]

    @pl.when(jnp.logical_not(passes))
    def _():
        out[...] = own[...]


def amplitude_kernel(images, table, out, table_out):
    leds, block, width = images.shape
    for led in range(leds):
        for j in range(width // LANES):
            piece = jnp.sqrt(images[led, :, j * LANES : (j + 1) * LANES])
            out[j * LANES : (j + 1) * LANES, led * block : (led + 1) * block] = piece.T
    table_out[...] = table[...]


def field_kernel(amplitude, table, *rest):
    far, near = rest[:5], rest[5 : HALF + 5]
    outs = rest[HALF + 5 : 2 * HALF + 5]
    field_in, diff, strips = rest[2 * HALF + 5 :]
    position = lax.axis_index("slab")
    parts, rows, _ = near[0].shape
    half = parts // 2 * LANES
    width = field_in.shape[0]
    steps = width // LANES
    group = 4
    for d, block in enumerate(near):
        at = pl.multiple_of(jnp.bitwise_and(jnp.bitwise_xor(position, d), HALF - 1) * rows, rows)
        for part in range(parts):
            cols = slice(part * LANES, (part + 1) * LANES)
            field_in[pl.ds(at, rows), cols] = block[part]

    def add(block, origin):
        at = pl.multiple_of(jnp.bitwise_and(origin, HALF - 1) * rows, rows)
        for part in range(parts):
            cols = slice(part * LANES, (part + 1) * LANES)
            field_in[pl.ds(at, rows), cols] += block[part]

    passes = is_one_of(position, PASSED.values())
    hands_over = is_one_of(position, PASSED)
    ends = is_one_of(position, [to ^ 4 for to in PASSED.values()])

    @pl.when(is_one_of(position, INNER))
    def _():
        add(far[0], jnp.bitwise_xor(position, 6))
        add(far[1], jnp.bitwise_xor(position, 7))
        add(far[2], jnp.bitwise_xor(position, jnp.where(ends, 5, 4)))

    @pl.when(jnp.logical_or(passes, hands_over))
    def _():
        add(far[2], jnp.bitwise_xor(position, 4))
        add(far[3], jnp.bitwise_xor(position, jnp.where(hands_over, 7, 6)))
        add(far[4], jnp.bitwise_xor(position, 5))

    for first in range(0, steps, group):
        product = dot(
            table[first : first + group].reshape(group * 2 * LANES, width), field_in[...]
        )
        for j in range(first, first + group):
            both = product[(j - first) * 2 * LANES : (j - first + 1) * 2 * LANES]
            field_re = both[:LANES, :half] + both[LANES:, half:]
            field_im = both[:LANES, half:] - both[LANES:, :half]
            here = pl.ds(j * LANES, LANES)
            factor = (
                amplitude[here, :] * lax.rsqrt(field_re * field_re + field_im * field_im + 0.25)
                - 1.0
            )
            diff[here, :half] = (field_re * factor).astype(jnp.bfloat16)
            diff[here, half:] = (field_im * factor).astype(jnp.bfloat16)
    pieces = rows // LANES
    for i in range(HALF):
        product = dot(
            table[i * pieces : (i + 1) * pieces].reshape(pieces * 2 * LANES, width), diff[...]
        )
        for h in range(pieces):
            both = product[h * 2 * LANES : (h + 1) * 2 * LANES]
            here = pl.ds(h * LANES, LANES)
            back_re = (both[:LANES, :half] - both[LANES:, half:]).astype(jnp.bfloat16)
            back_im = (both[:LANES, half:] + both[LANES:, :half]).astype(jnp.bfloat16)
            for part in range(parts // 2):
                cols = slice(part * LANES, (part + 1) * LANES)
                strips[i, part, here, :] = back_re[:, cols]
                strips[i, parts // 2 + part, here, :] = back_im[:, cols]
    for d, out in enumerate(outs):
        out[...] = strips[jnp.bitwise_and(jnp.bitwise_xor(position, d), HALF - 1)]


def update_columns(own_core, starts, table, back, outs):
    position = lax.axis_index("slab")
    led_at = lax.axis_index("led")
    core = jnp.bitwise_and(led_at, 1)
    plane_x = jnp.right_shift(led_at, 1)
    which_half = jnp.right_shift(position, 2)
    first_row = jnp.bitwise_and(position, HALF - 1)
    leds = starts.shape[0] // 2
    rows = back.shape[0] // (2 * leds)
    depth = back.shape[1]
    width = table.shape[1]
    group = width // LANES // 2
    owner = core if own_core else 1 - core
    shape = (rows, LANES)
    for n in range(group):
        block = owner * group + n
        both = dot(
            back[...], table[block, pl.ds(pl.multiple_of(which_half * depth, depth), depth)]
        )
        half = leds * rows
        update = (
            both[:half, :LANES] - both[half:, LANES:],
            both[half:, :LANES] + both[:half, LANES:],
        )
        sums = [[0.0, 0.0] for _ in outs]
        for led in range(leds):
            at_row = lax.broadcasted_iota(jnp.int32, shape, 0) + (
                first_row * rows - starts[led]
            )
            at_col = lax.broadcasted_iota(jnp.int32, shape, 1) + (
                block * LANES - starts[leds + led]
            )
            row_term = 2 * jnp.where(at_row < 0, at_row + width, at_row) + 1 - width
            col_term = 2 * jnp.where(at_col < 0, at_col + width, at_col) + 1 - width
            inside = row_term * row_term + col_term * col_term < width * width
            this_slab = jnp.where(at_row < 0, 1, 0) == which_half
            this_x = jnp.where(at_col < 0, 1, 0) == plane_x
            for plane in range(2):
                piece = jnp.where(inside, update[plane][led * rows : (led + 1) * rows], 0.0)
                for i, at_slab in enumerate(
                    (jnp.where(this_slab, piece, 0.0), jnp.where(this_slab, 0.0, piece))
                ):
                    sums[2 * i][plane] += jnp.where(this_x, at_slab, 0.0)
                    sums[2 * i + 1][plane] += jnp.where(this_x, 0.0, at_slab)
        cols = slice(n * LANES, (n + 1) * LANES)
        for out, both_planes in zip(outs, sums):
            for plane in range(2):
                out[plane, :, cols] = both_planes[plane].astype(out.dtype)


def sent_kernel(starts, table, *rest):
    blocks = rest[:HALF]
    this_slab, that_slab, back = rest[HALF:]
    position = lax.axis_index("slab")
    parts, rows, _ = blocks[0].shape
    for d, block in enumerate(blocks):
        source = jnp.bitwise_and(jnp.bitwise_xor(position, d), HALF - 1)
        at = pl.multiple_of(source * LANES, LANES)
        for part in range(parts):
            back[part * rows : (part + 1) * rows, pl.ds(at, LANES)] = block[part]
    outs = [out.at[i] for out in (this_slab, that_slab) for i in range(2)]
    update_columns(False, starts, table, back, outs)


def kept_kernel(starts, table, back, *outs):
    update_columns(True, starts, table, back, outs)


def z_first_kernel(that_near, that_far, got_that, out):
    cols = out.shape[3]
    for i, kept in enumerate((that_near, that_far)):
        total = kept[:, :, :cols].astype(jnp.float32) + got_that[i, :, :, :cols].astype(jnp.float32)
        out[i] = total.astype(out.dtype)


def x_first_kernel(that_far, got_that, out):
    cols = that_far.shape[2] - out.shape[2]
    total = that_far[:, :, cols:].astype(jnp.float32) + got_that[1, :, :, cols:].astype(jnp.float32)
    out[...] = total.astype(out.dtype)


def z_second_kernel(that_near, got_that, got_x, out):
    cols = that_near.shape[2] - out.shape[2]
    total = that_near[:, :, cols:].astype(jnp.float32) + got_that[0, :, :, cols:].astype(jnp.float32)
    out[...] = (total + got_x[...].astype(jnp.float32)).astype(out.dtype)


def x_second_kernel(this_far, got_this, got_z, out):
    cols = got_z.shape[3]
    total = this_far[...].astype(jnp.float32) + got_this[1].astype(jnp.float32)
    out[:, :, cols:] = total[:, :, cols:].astype(out.dtype)
    out[:, :, :cols] = (total[:, :, :cols] + got_z[1].astype(jnp.float32)).astype(out.dtype)


def local_call(kernel, out_shape, spaces, scratch, flops, moved, name):
    return pl.pallas_call(
        kernel,
        out_shape=out_shape,
        in_specs=[pl.BlockSpec(memory_space=space) for space in spaces],
        out_specs=jax.tree.map(lambda _: pl.BlockSpec(memory_space=pltpu.VMEM), out_shape),
        scratch_shapes=scratch,
        compiler_params=pltpu.CompilerParams(vmem_limit_bytes=32 * 2**20),
        cost_estimate=pl.CostEstimate(flops=flops, bytes_accessed=moved, transcendentals=0),
        name=name,
    )


def body_slabs(spectrum, led_rows, led_cols, images):
    leds, block, width = images.shape
    rows = spectrum.shape[1]
    led_at = lax.axis_index("led")
    bf16 = jnp.bfloat16
    vmem, smem = pltpu.VMEM, pltpu.SMEM
    cos_table, sin_table = host_tables(width)
    steps = width // LANES
    by_col = np.stack(
        [
            np.concatenate([t[:, j * LANES : (j + 1) * LANES] for t in (cos_table, sin_table)], 1)
            for j in range(steps)
        ]
    )
    by_row = jnp.asarray(np.ascontiguousarray(by_col.transpose(0, 2, 1)))
    by_col = jnp.asarray(by_col)
    parts = 2 * leds
    sent_block = jax.ShapeDtypeStruct((parts, rows, LANES), bf16)
    flops = 8 * leds * rows * width * width

    starts = jnp.concatenate([led_rows, led_cols]).astype(jnp.int32)
    window = local_call(
        window_kernel,
        jax.ShapeDtypeStruct((parts * rows, width), bf16),
        [smem, vmem],
        [],
        0,
        6 * 2**20,
        "windows",
    )(starts, spectrum)

    def rows_call(which, name):
        count = which.stop - which.start
        return local_call(
            functools.partial(rows_kernel, which),
            [sent_block] * count,
            [vmem, vmem],
            [],
            flops * count // SLABS,
            5 * 2**20,
            name,
        )(window, by_col)

    first_a, first_b, near_2 = rows_call(slice(0, 3), "rows_round_1")

    def permute(sent, pairs):
        return lax.ppermute(sent, "slab", pairs)

    def choose(got, own, name):
        return local_call(
            choose_kernel, sent_block, [vmem] * 2, [], 0, 2**19, name
        )(got, own)

    handed = list(PASSED.items())
    windowed = range(FIRST + 1, LAST)
    got_a = permute(first_a, [(s, s ^ 6) for s in INNER] + handed)
    got_b = permute(first_b, [(s, s ^ 7) for s in INNER] + handed)
    near_2 = permute(near_2, [(s, s ^ 2) for s in windowed])
    second_a, second_b, near_0, near_1, near_3 = rows_call(slice(3, SLABS), "rows_round_2")
    got_a, near_2, second_a, second_b, near_1, near_3, images = lax.optimization_barrier(
        (got_a, near_2, second_a, second_b, near_1, near_3, images)
    )
    outer_pairs = [(s, s ^ 6) for s in range(SLABS) if s not in INNER]
    near_1 = permute(near_1, [(s, s ^ 1) for s in windowed])
    near_3 = permute(near_3, [(s, s ^ 3) for s in windowed])
    near_3, got_b = lax.optimization_barrier((near_3, got_b))
    far_columns = [
        got_a,
        got_b,
        permute(choose(got_a, second_a, "class_4_blocks"), [(s, s ^ 4) for s in range(SLABS)]),
        permute(choose(got_b, second_b, "class_6_blocks"), outer_pairs),
        permute(second_b, [(s, s ^ 5) for s in INNER]),
    ]
    near_columns = [near_0, near_1, near_2, near_3]
    amplitude, by_row = local_call(
        amplitude_kernel,
        [
            jax.ShapeDtypeStruct((width, leds * block), jnp.float32),
            jax.ShapeDtypeStruct(by_row.shape, bf16),
        ],
        [vmem] * 2,
        [],
        0,
        10 * 2**20,
        "amplitude",
    )(images, by_row)
    strips = local_call(
        field_kernel,
        [sent_block] * HALF,
        [vmem] * 11,
        [pltpu.VMEM((width, parts * block), bf16)] * 2
        + [pltpu.VMEM((HALF,) + sent_block.shape, bf16)],
        16 * leds * block * width * width,
        12 * 2**20,
        "modulus_step",
    )(amplitude, by_row, *far_columns, *near_columns)

    def send_home(d):
        pairs = [(s, (s + d) % SLABS) for s in range(SLABS) if FIRST < (s + d) % SLABS < LAST]
        return permute(strips[d % HALF], pairs)

    home = [strips[0]]
    home += [
        permute(strips[d], [(s, s ^ d) for s in range(SLABS)]) for d in range(1, HALF)
    ]
    share = width // 2
    first = share // 4
    piece = (2, rows, share)
    cores = [(0, 1), (1, 0), (2, 3), (3, 2)]
    planes = [(0, 2), (2, 0), (1, 3), (3, 1)]
    across = [(s, s ^ 4) for s in range(SLABS) if FIRST < s ^ 4 < LAST]
    sent_this, sent_that, back = local_call(
        sent_kernel,
        [
            jax.ShapeDtypeStruct((2,) + piece, bf16),
            jax.ShapeDtypeStruct((2,) + piece, bf16),
            jax.ShapeDtypeStruct((parts * rows, HALF * LANES), bf16),
        ],
        [smem] + [vmem] * (1 + HALF),
        [],
        flops // 4,
        8 * 2**20,
        "update_sent",
    )(starts, by_col, *home)
    got_that = lax.ppermute(sent_that, "led", cores)
    got_this = lax.ppermute(sent_this, "led", cores)
    this_near, this_far, that_near, that_far = local_call(
        kept_kernel,
        [jax.ShapeDtypeStruct(piece, jnp.float32)] + [jax.ShapeDtypeStruct(piece, bf16)] * 3,
        [smem, vmem, vmem],
        [],
        flops // 4,
        10 * 2**20,
        "update_kept",
    )(starts, by_col, back)

    def sum_call(kernel, shape, *values):
        out_shape = jax.ShapeDtypeStruct(shape, bf16)
        specs = [vmem] * len(values)
        return local_call(kernel, out_shape, specs, [], 0, 2**20, kernel.__name__)(*values)

    over = sum_call(z_first_kernel, (2, 2, rows, first), that_near, that_far, got_that)
    got_z_first = permute(over, across)
    over = sum_call(x_first_kernel, (2, rows, share - first), that_far, got_that)
    got_x = lax.ppermute(over, "led", planes)
    over = sum_call(z_second_kernel, (2, rows, share - first), that_near, got_that, got_x)
    got_z_second = permute(over, across)
    over = sum_call(x_second_kernel, piece, this_far, got_this, got_z_first)
    got_x = lax.ppermute(over, "led", planes)

    def widen(value, before):
        after = share - before - value.shape[2]
        return jnp.pad(value.astype(jnp.float32), ((0, 0), (0, 0), (before, after)))

    base = lax.dynamic_slice_in_dim(spectrum, led_at * share, share, 2)
    base += this_near + got_this[0].astype(jnp.float32) + widen(got_z_first[0], 0)
    base, got_x = lax.optimization_barrier((base, got_x))
    base += got_x.astype(jnp.float32)
    base, got_z_second = lax.optimization_barrier((base, got_z_second))
    return base + widen(got_z_second, first)


def solution(mesh):
    placed = (P(None, "slab", None), P("led"), P("led"), P("led", "slab", None))
    fits = mesh.shape["slab"] == 8 and mesh.shape["led"] == 4

    def body(spectrum, led_rows, led_cols, images):
        shapes = (spectrum.shape, images.shape)
        if fits and shapes == ((2, 256, 2048), (2, 128, 1024)):
            return body_slabs(spectrum, led_rows, led_cols, images)
        return body_any(spectrum, led_rows, led_cols, images)

    return jax.shard_map(
        body, mesh=mesh, in_specs=placed, out_specs=P(None, "slab", "led"), check_vma=False
    )
```

```python
import functools

import jax
import jax.numpy as jnp
import numpy as np
from jax import lax
from jax.experimental import pallas as pl
from jax.experimental.pallas import tpu as pltpu
from jax.sharding import PartitionSpec as P

LANES = 128


def as_sent(value):
    return jax.tree.map(lambda a: a.astype(jnp.bfloat16) if a.dtype == jnp.float32 else a, value)


def host_tables(width):
    index = np.arange(width, dtype=np.int64)
    angle_index = (index[:, None] * index[None, :] % width).astype(np.float32)
    angle = angle_index * np.float32(2.0 * 3.141592653589793 / width)
    scale = np.float32(1.0) / np.sqrt(np.float32(width))
    return (
        (np.cos(angle) * scale).astype(jnp.bfloat16),
        (np.sin(angle) * scale).astype(jnp.bfloat16),
    )


def make_pupil(row_index, col_index, width):
    row_term = (2 * row_index + 1 - width) * (2 * row_index + 1 - width)
    col_term = (2 * col_index + 1 - width) * (2 * col_index + 1 - width)
    return (row_term[:, None] + col_term[None, :] < width * width).astype(jnp.float32)


def contract(form, left, right):
    return jnp.einsum(form, left, right, preferred_element_type=jnp.float32)


def take_rows(strip, start, width):
    return lax.dynamic_slice_in_dim(strip, start, width, 1)


def place_rows(block, start, total, axis_dim):
    shape = list(block.shape)
    shape[axis_dim] = total
    holder = jnp.zeros(tuple(shape), block.dtype)
    return lax.dynamic_update_slice_in_dim(holder, block, start, axis_dim)


def modulus_step(field_in_re, field_in_im, image, cos_table, sin_table):
    field_re = contract("lka,am->lkm", field_in_re, cos_table) + contract(
        "lka,am->lkm", field_in_im, sin_table
    )
    field_im = contract("lka,am->lkm", field_in_im, cos_table) - contract(
        "lka,am->lkm", field_in_re, sin_table
    )
    factor = jnp.sqrt(image) / jnp.sqrt(field_re * field_re + field_im * field_im + 0.25) - 1.0
    diff_re = (field_re * factor).astype(jnp.bfloat16)
    diff_im = (field_im * factor).astype(jnp.bfloat16)
    back_re = (
        contract("lkm,ma->lka", diff_re, cos_table) - contract("lkm,ma->lka", diff_im, sin_table)
    ).astype(jnp.bfloat16)
    back_im = (
        contract("lkm,ma->lka", diff_im, cos_table) + contract("lkm,ma->lka", diff_re, sin_table)
    ).astype(jnp.bfloat16)
    return (back_re, back_im)


def body_any(spectrum, led_rows, led_cols, images):
    width = images.shape[2]
    slab_rows = spectrum.shape[1]
    columns = spectrum.shape[2]
    slabs = lax.axis_size("slab")
    total_rows = slab_rows * slabs
    position = lax.axis_index("slab")
    cos_table, sin_table = (jnp.asarray(t) for t in host_tables(width))
    own_rows = position * slab_rows + jnp.arange(slab_rows, dtype=jnp.int32)
    col_index = jnp.arange(width, dtype=jnp.int32)

    def take_cols(start):
        return lax.dynamic_slice_in_dim(spectrum, start, width, 2)

    def owner_mask(start):
        return make_pupil(own_rows - start, col_index, width)

    windows = jax.vmap(take_cols)(led_cols)
    masks = jax.vmap(owner_mask)(led_rows)
    win_re = (windows[:, 0] * masks).astype(jnp.bfloat16)
    win_im = (windows[:, 1] * masks).astype(jnp.bfloat16)

    def slice_strip(block, start):
        return take_rows(block, start, width)

    row_re = (
        contract("lgb,bk->lkg", win_re, cos_table) + contract("lgb,bk->lkg", win_im, sin_table)
    ).astype(jnp.bfloat16)
    row_im = (
        contract("lgb,bk->lkg", win_im, cos_table) - contract("lgb,bk->lkg", win_re, sin_table)
    ).astype(jnp.bfloat16)
    col_re, col_im = (
        lax.all_to_all(row_re, "slab", split_axis=1, concat_axis=2, tiled=True),
        lax.all_to_all(row_im, "slab", split_axis=1, concat_axis=2, tiled=True),
    )
    field_in_re = jax.vmap(slice_strip)(col_re, led_rows)
    field_in_im = jax.vmap(slice_strip)(col_im, led_rows)
    back_re, back_im = modulus_step(field_in_re, field_in_im, images, cos_table, sin_table)

    def place_strip(block, start):
        return place_rows(block, start, total_rows, 1)

    full_re = jax.vmap(place_strip)(back_re, led_rows)
    full_im = jax.vmap(place_strip)(back_im, led_rows)
    home_re, home_im = (
        lax.all_to_all(as_sent(full_re), "slab", split_axis=2, concat_axis=1, tiled=True).astype(
            full_re.dtype
        ),
        lax.all_to_all(as_sent(full_im), "slab", split_axis=2, concat_axis=1, tiled=True).astype(
            full_im.dtype
        ),
    )
    upd_re = contract("lkg,kb->lgb", home_re, cos_table) - contract(
        "lkg,kb->lgb", home_im, sin_table
    )
    upd_im = contract("lkg,kb->lgb", home_im, cos_table) + contract(
        "lkg,kb->lgb", home_re, sin_table
    )
    upd_re = upd_re * masks
    upd_im = upd_im * masks

    def add_window(number, gradient):
        start = led_cols[number]
        piece = jnp.stack([upd_re[number], upd_im[number]])
        current = lax.dynamic_slice_in_dim(gradient, start, width, 2)
        return lax.dynamic_update_slice_in_dim(gradient, current + piece, start, 2)

    gradient = lax.fori_loop(
        0, led_rows.shape[0], add_window, jnp.zeros((2, slab_rows, columns), jnp.float32)
    )
    summed = lax.psum_scatter(gradient, "led", scatter_dimension=2, tiled=True)
    share = summed.shape[2]
    own_part = lax.dynamic_slice_in_dim(spectrum, lax.axis_index("led") * share, share, 2)
    return own_part + summed


SLABS = 8
HALF = 4
FIRST, LAST = 0, 7
PASSED = {1: 0, 6: 7}
INNER = (2, 3, 4, 5)


def dot(left, right):
    return jnp.dot(left, right, preferred_element_type=jnp.float32)


def window_mask(first_row, row_start, col_start, rows, first_col, cols, width):
    shape = (rows, cols)
    at_row = lax.broadcasted_iota(jnp.int32, shape, 0) + (first_row - row_start)
    at_col = lax.broadcasted_iota(jnp.int32, shape, 1) + (first_col - col_start)
    wraps = at_col < 0
    at_col = jnp.where(wraps, at_col + width, at_col)
    row_term = 2 * at_row + 1 - width
    col_term = 2 * at_col + 1 - width
    return row_term * row_term + col_term * col_term < width * width, wraps


def row_block(window, table):
    both = dot(window, table)
    half = both.shape[0] // 2
    row_re = both[:half, :LANES] + both[half:, LANES:]
    row_im = both[half:, :LANES] - both[:half, LANES:]
    return row_re.astype(jnp.bfloat16), row_im.astype(jnp.bfloat16)


def store_parts(out, values):
    per = out.shape[0] // 2
    rows = out.shape[1]
    for plane, value in enumerate(values):
        for led in range(per):
            out[plane * per + led] = value[led * rows : (led + 1) * rows]


def is_one_of(position, slabs):
    return functools.reduce(jnp.logical_or, [position == slab for slab in slabs])


def window_kernel(starts, spectrum, window):
    position = lax.axis_index("slab")
    leds = starts.shape[0] // 2
    rows = spectrum.shape[1]
    width = window.shape[1]
    for led in range(leds):
        inside, wraps = window_mask(
            position * rows, starts[led], starts[leds + led], rows, 0, width, width
        )
        for plane in range(2):
            value = jnp.where(wraps, spectrum[plane, :, width:], spectrum[plane, :, :width])
            at = (plane * leds + led) * rows
            window[at : at + rows, :] = jnp.where(inside, value, 0.0).astype(jnp.bfloat16)


def classes_of(position):
    hands_over = is_one_of(position, PASSED)
    return (jnp.where(hands_over, 5, 6), 7, 2, 4, jnp.where(hands_over, 6, 5), 0, 1, 3)


def rows_kernel(which, window, table, *outs):
    position = lax.axis_index("slab")
    for out, d in zip(outs, classes_of(position)[which]):
        store_parts(out, row_block(window[...], table[jnp.bitwise_xor(position, d)]))


def choose_kernel(got, own, out):
    passes = is_one_of(lax.axis_index("slab"), PASSED.values())

    @pl.when(passes)
    def _():
        out[...] = got[...]

    @pl.when(jnp.logical_not(passes))
    def _():
        out[...] = own[...]


def amplitude_kernel(images, table, out, table_out):
    leds, block, width = images.shape
    for led in range(leds):
        for j in range(width // LANES):
            piece = jnp.sqrt(images[led, :, j * LANES : (j + 1) * LANES])
            out[j * LANES : (j + 1) * LANES, led * block : (led + 1) * block] = piece.T
    table_out[...] = table[...]


def field_kernel(amplitude, table, *rest):
    far, near = rest[:5], rest[5 : HALF + 5]
    outs = rest[HALF + 5 : 2 * HALF + 5]
    field_in, diff, strips = rest[2 * HALF + 5 :]
    position = lax.axis_index("slab")
    parts, rows, _ = near[0].shape
    half = parts // 2 * LANES
    width = field_in.shape[0]
    steps = width // LANES
    group = 4
    for d, block in enumerate(near):
        at = pl.multiple_of(jnp.bitwise_and(jnp.bitwise_xor(position, d), HALF - 1) * rows, rows)
        for part in range(parts):
            cols = slice(part * LANES, (part + 1) * LANES)
            field_in[pl.ds(at, rows), cols] = block[part]

    def add(block, origin):
        at = pl.multiple_of(jnp.bitwise_and(origin, HALF - 1) * rows, rows)
        for part in range(parts):
            cols = slice(part * LANES, (part + 1) * LANES)
            field_in[pl.ds(at, rows), cols] += block[part]

    passes = is_one_of(position, PASSED.values())
    hands_over = is_one_of(position, PASSED)
    ends = is_one_of(position, [to ^ 4 for to in PASSED.values()])

    @pl.when(is_one_of(position, INNER))
    def _():
        add(far[0], jnp.bitwise_xor(position, 6))
        add(far[1], jnp.bitwise_xor(position, 7))
        add(far[2], jnp.bitwise_xor(position, jnp.where(ends, 5, 4)))

    @pl.when(jnp.logical_or(passes, hands_over))
    def _():
        add(far[2], jnp.bitwise_xor(position, 4))
        add(far[3], jnp.bitwise_xor(position, jnp.where(hands_over, 7, 6)))
        add(far[4], jnp.bitwise_xor(position, 5))

    for first in range(0, steps, group):
        product = dot(
            table[first : first + group].reshape(group * 2 * LANES, width), field_in[...]
        )
        for j in range(first, first + group):
            both = product[(j - first) * 2 * LANES : (j - first + 1) * 2 * LANES]
            field_re = both[:LANES, :half] + both[LANES:, half:]
            field_im = both[:LANES, half:] - both[LANES:, :half]
            here = pl.ds(j * LANES, LANES)
            factor = (
                amplitude[here, :] * lax.rsqrt(field_re * field_re + field_im * field_im + 0.25)
                - 1.0
            )
            diff[here, :half] = (field_re * factor).astype(jnp.bfloat16)
            diff[here, half:] = (field_im * factor).astype(jnp.bfloat16)
    pieces = rows // LANES
    for i in range(HALF):
        product = dot(
            table[i * pieces : (i + 1) * pieces].reshape(pieces * 2 * LANES, width), diff[...]
        )
        for h in range(pieces):
            both = product[h * 2 * LANES : (h + 1) * 2 * LANES]
            here = pl.ds(h * LANES, LANES)
            back_re = (both[:LANES, :half] - both[LANES:, half:]).astype(jnp.bfloat16)
            back_im = (both[:LANES, half:] + both[LANES:, :half]).astype(jnp.bfloat16)
            for part in range(parts // 2):
                cols = slice(part * LANES, (part + 1) * LANES)
                strips[i, part, here, :] = back_re[:, cols]
                strips[i, parts // 2 + part, here, :] = back_im[:, cols]
    for d, out in enumerate(outs):
        out[...] = strips[jnp.bitwise_and(jnp.bitwise_xor(position, d), HALF - 1)]


def update_columns(own_core, starts, table, back, outs):
    position = lax.axis_index("slab")
    led_at = lax.axis_index("led")
    core = jnp.bitwise_and(led_at, 1)
    plane_x = jnp.right_shift(led_at, 1)
    which_half = jnp.right_shift(position, 2)
    first_row = jnp.bitwise_and(position, HALF - 1)
    leds = starts.shape[0] // 2
    rows = back.shape[0] // (2 * leds)
    depth = back.shape[1]
    width = table.shape[1]
    group = width // LANES // 2
    owner = core if own_core else 1 - core
    shape = (rows, LANES)
    for n in range(group):
        block = owner * group + n
        both = dot(
            back[...], table[block, pl.ds(pl.multiple_of(which_half * depth, depth), depth)]
        )
        half = leds * rows
        update = (
            both[:half, :LANES] - both[half:, LANES:],
            both[half:, :LANES] + both[:half, LANES:],
        )
        sums = [[0.0, 0.0] for _ in outs]
        for led in range(leds):
            at_row = lax.broadcasted_iota(jnp.int32, shape, 0) + (
                first_row * rows - starts[led]
            )
            at_col = lax.broadcasted_iota(jnp.int32, shape, 1) + (
                block * LANES - starts[leds + led]
            )
            row_term = 2 * jnp.where(at_row < 0, at_row + width, at_row) + 1 - width
            col_term = 2 * jnp.where(at_col < 0, at_col + width, at_col) + 1 - width
            inside = row_term * row_term + col_term * col_term < width * width
            this_slab = jnp.where(at_row < 0, 1, 0) == which_half
            this_x = jnp.where(at_col < 0, 1, 0) == plane_x
            for plane in range(2):
                piece = jnp.where(inside, update[plane][led * rows : (led + 1) * rows], 0.0)
                for i, at_slab in enumerate(
                    (jnp.where(this_slab, piece, 0.0), jnp.where(this_slab, 0.0, piece))
                ):
                    sums[2 * i][plane] += jnp.where(this_x, at_slab, 0.0)
                    sums[2 * i + 1][plane] += jnp.where(this_x, 0.0, at_slab)
        cols = slice(n * LANES, (n + 1) * LANES)
        for out, both_planes in zip(outs, sums):
            for plane in range(2):
                out[plane, :, cols] = both_planes[plane].astype(out.dtype)


def sent_kernel(starts, table, *rest):
    blocks = rest[:HALF]
    this_slab, that_slab, back = rest[HALF:]
    position = lax.axis_index("slab")
    parts, rows, _ = blocks[0].shape
    for d, block in enumerate(blocks):
        source = jnp.bitwise_and(jnp.bitwise_xor(position, d), HALF - 1)
        at = pl.multiple_of(source * LANES, LANES)
        for part in range(parts):
            back[part * rows : (part + 1) * rows, pl.ds(at, LANES)] = block[part]
    outs = [out.at[i] for out in (this_slab, that_slab) for i in range(2)]
    update_columns(False, starts, table, back, outs)


def kept_kernel(starts, table, back, *outs):
    update_columns(True, starts, table, back, outs)


def z_first_kernel(that_near, that_far, got_that, out):
    cols = out.shape[3]
    for i, kept in enumerate((that_near, that_far)):
        total = kept[:, :, :cols] + got_that[i, :, :, :cols].astype(jnp.float32)
        out[i] = total.astype(out.dtype)


def x_first_kernel(that_far, got_that, out):
    cols = that_far.shape[2] - out.shape[2]
    total = that_far[:, :, cols:] + got_that[1, :, :, cols:].astype(jnp.float32)
    out[...] = total.astype(out.dtype)


def z_second_kernel(that_near, got_that, got_x, out):
    cols = that_near.shape[2] - out.shape[2]
    total = that_near[:, :, cols:] + got_that[0, :, :, cols:].astype(jnp.float32)
    out[...] = (total + got_x[...].astype(jnp.float32)).astype(out.dtype)


def x_own_kernel(this_far, got_this, out):
    cols = this_far.shape[2] - out.shape[2]
    total = this_far[:, :, cols:] + got_this[1, :, :, cols:].astype(jnp.float32)
    out[...] = total.astype(out.dtype)


def x_last_kernel(this_far, got_this, got_z, out):
    cols = out.shape[2]
    total = this_far[:, :, :cols] + got_this[1, :, :, :cols].astype(jnp.float32)
    out[...] = (total + got_z[1].astype(jnp.float32)).astype(out.dtype)


def local_call(kernel, out_shape, spaces, scratch, flops, moved, name):
    return pl.pallas_call(
        kernel,
        out_shape=out_shape,
        in_specs=[pl.BlockSpec(memory_space=space) for space in spaces],
        out_specs=jax.tree.map(lambda _: pl.BlockSpec(memory_space=pltpu.VMEM), out_shape),
        scratch_shapes=scratch,
        compiler_params=pltpu.CompilerParams(vmem_limit_bytes=32 * 2**20),
        cost_estimate=pl.CostEstimate(flops=flops, bytes_accessed=moved, transcendentals=0),
        name=name,
    )


def body_slabs(spectrum, led_rows, led_cols, images):
    leds, block, width = images.shape
    rows = spectrum.shape[1]
    led_at = lax.axis_index("led")
    bf16 = jnp.bfloat16
    vmem, smem = pltpu.VMEM, pltpu.SMEM
    cos_table, sin_table = host_tables(width)
    steps = width // LANES
    by_col = np.stack(
        [
            np.concatenate([t[:, j * LANES : (j + 1) * LANES] for t in (cos_table, sin_table)], 1)
            for j in range(steps)
        ]
    )
    by_row = jnp.asarray(np.ascontiguousarray(by_col.transpose(0, 2, 1)))
    by_col = jnp.asarray(by_col)
    parts = 2 * leds
    sent_block = jax.ShapeDtypeStruct((parts, rows, LANES), bf16)
    flops = 8 * leds * rows * width * width

    starts = jnp.concatenate([led_rows, led_cols]).astype(jnp.int32)
    window = local_call(
        window_kernel,
        jax.ShapeDtypeStruct((parts * rows, width), bf16),
        [smem, vmem],
        [],
        0,
        6 * 2**20,
        "windows",
    )(starts, spectrum)

    def rows_call(which, name):
        count = which.stop - which.start
        return local_call(
            functools.partial(rows_kernel, which),
            [sent_block] * count,
            [vmem, vmem],
            [],
            flops * count // SLABS,
            5 * 2**20,
            name,
        )(window, by_col)

    first_a, first_b, near_2 = rows_call(slice(0, 3), "rows_round_1")

    def permute(sent, pairs):
        return lax.ppermute(sent, "slab", pairs)

    def choose(got, own, name):
        return local_call(
            choose_kernel, sent_block, [vmem] * 2, [], 0, 2**19, name
        )(got, own)

    handed = list(PASSED.items())
    windowed = range(FIRST + 1, LAST)
    got_a = permute(first_a, [(s, s ^ 6) for s in INNER] + handed)
    got_b = permute(first_b, [(s, s ^ 7) for s in INNER] + handed)
    near_2 = permute(near_2, [(s, s ^ 2) for s in windowed])
    second_a, second_b, near_0, near_1, near_3 = rows_call(slice(3, SLABS), "rows_round_2")
    got_a, near_2, second_a, second_b, near_1, near_3, images = lax.optimization_barrier(
        (got_a, near_2, second_a, second_b, near_1, near_3, images)
    )
    outer_pairs = [(s, s ^ 6) for s in range(SLABS) if s not in INNER]
    near_1 = permute(near_1, [(s, s ^ 1) for s in windowed])
    near_3 = permute(near_3, [(s, s ^ 3) for s in windowed])
    near_3, got_b = lax.optimization_barrier((near_3, got_b))
    far_columns = [
        got_a,
        got_b,
        permute(choose(got_a, second_a, "class_4_blocks"), [(s, s ^ 4) for s in range(SLABS)]),
        permute(choose(got_b, second_b, "class_6_blocks"), outer_pairs),
        permute(second_b, [(s, s ^ 5) for s in INNER]),
    ]
    near_columns = [near_0, near_1, near_2, near_3]
    amplitude, by_row = local_call(
        amplitude_kernel,
        [
            jax.ShapeDtypeStruct((width, leds * block), jnp.float32),
            jax.ShapeDtypeStruct(by_row.shape, bf16),
        ],
        [vmem] * 2,
        [],
        0,
        10 * 2**20,
        "amplitude",
    )(images, by_row)
    strips = local_call(
        field_kernel,
        [sent_block] * HALF,
        [vmem] * 11,
        [pltpu.VMEM((width, parts * block), bf16)] * 2
        + [pltpu.VMEM((HALF,) + sent_block.shape, bf16)],
        16 * leds * block * width * width,
        12 * 2**20,
        "modulus_step",
    )(amplitude, by_row, *far_columns, *near_columns)

    def send_home(d):
        pairs = [(s, (s + d) % SLABS) for s in range(SLABS) if FIRST < (s + d) % SLABS < LAST]
        return permute(strips[d % HALF], pairs)

    home = [strips[0]]
    home += [
        permute(strips[d], [(s, s ^ d) for s in range(SLABS)]) for d in range(1, HALF)
    ]
    share = width // 2
    first = share // 4
    piece = (2, rows, share)
    cores = [(0, 1), (1, 0), (2, 3), (3, 2)]
    planes = [(0, 2), (2, 0), (1, 3), (3, 1)]
    across = [(s, s ^ 4) for s in range(SLABS) if FIRST < s ^ 4 < LAST]
    sent_this, sent_that, back = local_call(
        sent_kernel,
        [
            jax.ShapeDtypeStruct((2,) + piece, bf16),
            jax.ShapeDtypeStruct((2,) + piece, bf16),
            jax.ShapeDtypeStruct((parts * rows, HALF * LANES), bf16),
        ],
        [smem] + [vmem] * (1 + HALF),
        [],
        flops // 4,
        8 * 2**20,
        "update_sent",
    )(starts, by_col, *home)
    got_that = lax.ppermute(sent_that, "led", cores)
    got_this = lax.ppermute(sent_this, "led", cores)
    this_near, this_far, that_near, that_far = local_call(
        kept_kernel,
        [jax.ShapeDtypeStruct(piece, jnp.float32)] * 4,
        [smem, vmem, vmem],
        [],
        flops // 4,
        10 * 2**20,
        "update_kept",
    )(starts, by_col, back)

    def sum_call(kernel, shape, *values):
        out_shape = jax.ShapeDtypeStruct(shape, bf16)
        specs = [vmem] * len(values)
        return local_call(kernel, out_shape, specs, [], 0, 2**20, kernel.__name__)(*values)

    over = sum_call(z_first_kernel, (2, 2, rows, first), that_near, that_far, got_that)
    got_z_first = permute(over, across)
    over = sum_call(x_first_kernel, (2, rows, share - first), that_far, got_that)
    got_x = lax.ppermute(over, "led", planes)
    over = sum_call(z_second_kernel, (2, rows, share - first), that_near, got_that, got_x)
    got_z_second = permute(over, across)
    over = sum_call(x_own_kernel, (2, rows, share - first), this_far, got_this)
    got_x_own = lax.ppermute(over, "led", planes)
    over = sum_call(x_last_kernel, (2, rows, first), this_far, got_this, got_z_first)
    got_x_last = lax.ppermute(over, "led", planes)

    def widen(value, before):
        after = share - before - value.shape[2]
        return jnp.pad(value.astype(jnp.float32), ((0, 0), (0, 0), (before, after)))

    base = lax.dynamic_slice_in_dim(spectrum, led_at * share, share, 2)
    base += this_near + got_this[0].astype(jnp.float32) + widen(got_z_first[0], 0)
    base, got_x_own, got_x_last = lax.optimization_barrier((base, got_x_own, got_x_last))
    base += widen(got_x_own, first) + widen(got_x_last, 0)
    base, got_z_second = lax.optimization_barrier((base, got_z_second))
    return base + widen(got_z_second, first)


def solution(mesh):
    placed = (P(None, "slab", None), P("led"), P("led"), P("led", "slab", None))
    fits = mesh.shape["slab"] == 8 and mesh.shape["led"] == 4

    def body(spectrum, led_rows, led_cols, images):
        shapes = (spectrum.shape, images.shape)
        if fits and shapes == ((2, 256, 2048), (2, 128, 1024)):
            return body_slabs(spectrum, led_rows, led_cols, images)
        return body_any(spectrum, led_rows, led_cols, images)

    return jax.shard_map(
        body, mesh=mesh, in_specs=placed, out_specs=P(None, "slab", "led"), check_vma=False
    )
```
